32 devices in a mesh: seq: 4 (over z), rows: 8 (over y, x, core).
Axes of the slice: x: 2, y: 2, z: 4, core: 2. Of those that a mesh axis runs over, the one named last changes fastest.
Arguments:
- tokens: bfloat16 [16, 1024, 1024], P('rows', 'seq'), may hold values from -6 to 6
- cotangent: bfloat16 [16, 1024, 1024], P('rows', 'seq'), may hold values from -6 to 6
- lengths: int32 [16], P('rows'), may hold values from 32 to 1024, as said below
- owner_perm: int32 [768], replicated, may hold values from 0 to 767, as said below
- master: float32 [768, 128, 128], P(('seq', 'rows'))
- norm_gains: float32 [2, 1024], replicated, may hold values from 0.5 to 1.5
- stat_left: float32 [768, 128, 128], P(('seq', 'rows'))
- stat_right: float32 [768, 128, 128], P(('seq', 'rows'))
- root_left: float32 [768, 128, 128], P(('seq', 'rows'))
- root_right: float32 [768, 128, 128], P(('seq', 'rows'))
- moment_first: float32 [2, 1024], replicated, may hold values from -40 to 40
- moment_second: float32 [2, 1024], replicated, may hold values from 2.048 to 32.768
Outputs:
- layer_out: bfloat16 [16, 1024, 1024], P('rows', 'seq')
- input_grad: float32 [16, 1024, 1024], P('rows', 'seq')
- grad_blocks: float32 [768, 128, 128], P(('seq', 'rows'))
- stat_left_new: float32 [768, 128, 128], P(('seq', 'rows'))
- stat_right_new: float32 [768, 128, 128], P(('seq', 'rows'))
- master_new: float32 [768, 128, 128], P(('seq', 'rows'))
- first_new: float32 [2, 1024], replicated
- second_new: float32 [2, 1024], replicated
- gains_new: float32 [2, 1024], replicated
The draws below stay inside these ranges and needn't reach their ends.
Inputs may be any that keep to these rules, and one draw needn't show every extreme that they name: `lengths`: in each aligned block of 2 rows one row, drawn from the seed, is longer than 768; the first such row has length 1024. `owner_perm`: each block number appears once.
All inputs are finite; a program needn't handle non-finite values.
Results may differ from the reference program's by a relative error of at most 0.015.
Values may be sent and summed in bfloat16 or wider, within the bound.
No kernel may reach another device: no remote copies, remote signals or barrier semaphores. Data moves between devices by JAX's collectives and lax.ppermute only.
A program may use at most 256 MiB of HBM per device.

```python
import math
import jax
import jax.numpy as jnp
from jax import lax

D = 1024
H = 16
HD = 64
FF = 4096
BLK = 128
SLOTS = 1024
MINLEN = 32
STEP = 10
ROW_DEV = 2
ROWS = 16
NB = 768


def owner_order(key):
    return jax.random.permutation(jax.random.fold_in(key, 101), NB).astype(jnp.int32)


def matrix_kind(block_order):
    first_mark = D // BLK * (3 * D // BLK)
    second_mark = first_mark + D // BLK * (D // BLK)
    third_mark = second_mark + D // BLK * (FF // BLK)
    return (block_order >= first_mark).astype(jnp.int32) + (block_order >= second_mark).astype(jnp.int32) + (block_order >= third_mark).astype(jnp.int32)


def draw_owner_perm(key, part):
    return owner_order(key)


def draw_master(key, part):
    kinds = matrix_kind(owner_order(key))
    key = jax.random.fold_in(key, 1)
    scales = jnp.array([D ** (-0.5), 8.0 * D ** (-0.5), D ** (-0.5), FF ** (-0.5)], jnp.float32)
    noise_draw = jax.random.normal(key, (NB, BLK, BLK), jnp.float32)
    return noise_draw * scales[kinds][:, None, None]


def statistic(key, salt_value):
    kinds = matrix_kind(owner_order(key))
    key = jax.random.fold_in(key, salt_value)
    sizes_sq = jnp.array([0.25, 0.0144, 0.0324, 0.16], jnp.float32) * (BLK * ROWS * SLOTS)
    diagonal = jnp.exp(jax.random.uniform(key, (NB, BLK), jnp.float32, 0.0, math.log(4.0)))
    diagonal = diagonal * sizes_sq[kinds][:, None]
    return diagonal[:, :, None] * jnp.eye(BLK, dtype=jnp.float32)[None, :, :]


def draw_stat_left(key, part):
    return statistic(key, 2)


def draw_stat_right(key, part):
    return statistic(key, 3)


def inverse_root(key, salt_value):
    key = jax.random.fold_in(key, salt_value)
    first_key, second_key = jax.random.split(key)
    diagonal = jnp.exp(jax.random.uniform(first_key, (NB, BLK), jnp.float32, 0.0, math.log(4.0)))
    off_diag = jax.random.normal(second_key, (NB, BLK, BLK), jnp.float32) / 28.0
    return off_diag + diagonal[:, :, None] * jnp.eye(BLK, dtype=jnp.float32)[None, :, :]


def draw_root_left(key, part):
    return inverse_root(key, 4)


def draw_root_right(key, part):
    return inverse_root(key, 5)


def draw_lengths(key, part):
    key = jax.random.fold_in(key, 7)
    first_key, second_key, third_key = jax.random.split(key, 3)
    base_len = jax.random.randint(first_key, (ROWS,), MINLEN, SLOTS + 1)
    long_len = jax.random.randint(third_key, (ROWS,), SLOTS - SLOTS // 4 + 1, SLOTS + 1)
    chosen = jax.random.randint(second_key, (ROWS // ROW_DEV,), 0, ROW_DEV)
    full_row = (jnp.arange(ROW_DEV)[None, :] == chosen[:, None]).reshape(ROWS)
    result = jnp.where(full_row, long_len, base_len)
    result = jnp.where(jnp.arange(ROWS) == chosen[0], SLOTS, result)
    return result.astype(jnp.int32)


def levels(key, extent, shards, least, high):
    level = 1.0
    for dim, blocks in shards:
        heights = jax.random.uniform(jax.random.fold_in(jax.random.fold_in(key, 6), dim), (blocks,), jnp.float32, least / len(shards), high / len(shards))
        level = level * jnp.repeat(jnp.exp(heights), extent[dim] // blocks).reshape((-1,) + (1,) * (len(extent) - 1 - dim))
    return level


def normal_values(stream_key, dims, deviation, reach, cuts=(), kind=jnp.bfloat16):
    factor_of = levels(stream_key, dims, cuts, -0.22, 0.18) if cuts else 1.0
    values = jax.random.normal(stream_key, dims, jnp.float32) * deviation * factor_of
    return jnp.minimum(jnp.maximum(values, -reach), reach).astype(kind)


def setup_inputs(seed: int = 0) -> dict:
    keys = jax.random.split(jax.random.key(seed), 13)
    tokens = normal_values(keys[0], (ROWS, SLOTS, D), 1.0, 6.0, ((0, 8), (1, 4)))
    cotangent = normal_values(keys[1], (ROWS, SLOTS, D), 1.0, 6.0, ((0, 8), (1, 4)))
    lengths = draw_lengths(jax.random.fold_in(keys[12], 71), 0)
    owner_perm = draw_owner_perm(jax.random.fold_in(keys[12], 71), 0)
    master = draw_master(jax.random.fold_in(keys[12], 71), 0)
    norm_gains = jnp.clip(1.0 + 0.1 * jax.random.normal(keys[5], (2, D), jnp.float32), 0.5, 1.5)
    stat_left = draw_stat_left(jax.random.fold_in(keys[12], 71), 0)
    stat_right = draw_stat_right(jax.random.fold_in(keys[12], 71), 0)
    root_left = draw_root_left(jax.random.fold_in(keys[12], 71), 0)
    root_right = draw_root_right(jax.random.fold_in(keys[12], 71), 0)
    moment_first = normal_values(keys[10], (2, D), (0.055 * (ROWS * SLOTS) ** 0.5), 40.0, (), jnp.float32)
    moment_second = jnp.clip(jnp.exp(jax.random.uniform(keys[11], (2, D), jnp.float32, math.log(2.048), math.log(32.768))), 2.048, 32.768)
    return dict(tokens=tokens, cotangent=cotangent, lengths=lengths, owner_perm=owner_perm, master=master, norm_gains=norm_gains, stat_left=stat_left, stat_right=stat_right, root_left=root_left, root_right=root_right, moment_first=moment_first, moment_second=moment_second)


norm_eps = 1e-05
score_scale = 0.125
masked_score = -1e+30
pair_rows = 2

@jax.custom_vjp
def low(v):
    return lax.optimization_barrier(v.astype(jnp.bfloat16)).astype(jnp.float32)

@jax.custom_vjp
def low_back(v):
    return v

def low_keep(v):
    return (low(v), None)

def low_pass(kept, grad):
    return (grad,)

def back_keep(v):
    return (v, None)

def back_low(kept, grad):
    return (low(grad),)
low.defvjp(low_keep, low_pass)
low_back.defvjp(back_keep, back_low)

def join_blocks(blocks, height, breadth):
    block_len = blocks.shape[-1]
    return blocks.reshape(height // block_len, breadth // block_len, block_len, block_len).transpose(0, 2, 1, 3).reshape(height, breadth)

def split_blocks(matrix):
    height, breadth = matrix.shape
    return matrix.reshape(height // BLK, BLK, breadth // BLK, BLK).transpose(0, 2, 1, 3).reshape(-1, BLK, BLK)

def unpack(blocks):
    shapes_list = [(D, 3 * D), (D, D), (D, FF), (FF, D)]
    result = []
    offset = 0
    for height, breadth in shapes_list:
        number = height // BLK * (breadth // BLK)
        result.append(join_blocks(blocks[offset:offset + number], height, breadth))
        offset = offset + number
    return tuple(result)

def unit_norm(values):
    row_mean = lax.optimization_barrier(jnp.mean(values, -1, keepdims=True))
    centered = values - row_mean
    row_var = lax.optimization_barrier(jnp.mean(centered * centered, -1, keepdims=True))
    return centered * lax.rsqrt(row_var + norm_eps)

def group_layer(group_in, group_lens, weights, norm_gains):
    highest = lax.Precision.HIGHEST
    w_qkv, w_out, w_up, w_down = weights
    group_count = group_in.shape[0]
    flat_rows = group_in.reshape(group_count * SLOTS, D)
    normed1 = low(unit_norm(flat_rows) * norm_gains[0])
    projected = low_back(low(jnp.dot(normed1, w_qkv, precision=highest)))
    queries = projected[:, :D].reshape(group_count, SLOTS, H, HD)
    key_all = projected[:, D:2 * D].reshape(group_count, SLOTS, H, HD)
    values = projected[:, 2 * D:].reshape(group_count, SLOTS, H, HD)
    scores = low_back(jnp.einsum('gqhd,gkhd->ghqk', queries, key_all, precision=highest) * score_scale)
    key_live = (jnp.arange(SLOTS, dtype=jnp.int32)[None, :] < group_lens[:, None])[:, None, None, :]
    scores = jnp.where(key_live, scores, masked_score)
    row_max = lax.optimization_barrier(jnp.max(scores, -1, keepdims=True))
    expos = jnp.exp(scores - row_max)
    probs = low(expos / lax.optimization_barrier(jnp.sum(expos, -1, keepdims=True)))
    attended = jnp.einsum('ghqk,gkhd->gqhd', probs, values, precision=highest).reshape(group_count * SLOTS, D)
    attended = low_back(low(attended))
    middle = flat_rows + low_back(jnp.dot(attended, w_out, precision=highest))
    normed2 = low(unit_norm(middle) * norm_gains[1])
    hidden = low_back(jnp.dot(normed2, w_up, precision=highest))
    activated = low(jax.nn.gelu(hidden, approximate=False))
    result = middle + low_back(jnp.dot(activated, w_down, precision=highest))
    return result.reshape(group_count, SLOTS, D)

def reference(tokens, cotangent, lengths, owner_perm, master, norm_gains, stat_left, stat_right, root_left, root_right, moment_first, moment_second):
    highest = lax.Precision.HIGHEST
    inverse = jnp.zeros((NB,), jnp.int32).at[owner_perm].set(jnp.arange(NB, dtype=jnp.int32))
    weights = unpack(master[inverse])
    live_mask = (jnp.arange(SLOTS, dtype=jnp.int32)[None, :] < lengths[:, None]).astype(jnp.float32)
    grad_top = cotangent.astype(jnp.float32) * live_mask[:, :, None]
    inputs_f = tokens.astype(jnp.float32)
    group_lens = lengths.reshape(ROWS // pair_rows, pair_rows)

    def forward(layer_in, layer_weights, gain_pair):
        rounded = tuple((low(matrix) for matrix in layer_weights))
        grouped = layer_in.reshape(ROWS // pair_rows, pair_rows, SLOTS, D)

        def one_group(carried, item_now):
            return (carried, group_layer(item_now[0], item_now[1], rounded, gain_pair))
        _ignored, outputs = lax.scan(jax.checkpoint(one_group), jnp.float32(0.0), (grouped, group_lens))
        return outputs.reshape(ROWS, SLOTS, D)
    layer_f32, pullback = jax.vjp(forward, inputs_f, weights, norm_gains)
    input_grad, grad_weights, gain_grad = pullback(grad_top)
    layer_out = layer_f32.astype(jnp.bfloat16)
    pieces = jnp.concatenate([split_blocks(matrix) for matrix in grad_weights], 0)
    grad_blocks = pieces[owner_perm]
    stat_left_new = stat_left + jnp.einsum('nij,nkj->nik', grad_blocks, grad_blocks, precision=highest)
    stat_right_new = stat_right + jnp.einsum('nji,njk->nik', grad_blocks, grad_blocks, precision=highest)
    direction = jnp.einsum('nij,njk->nik', root_left, grad_blocks, precision=highest)
    direction = jnp.einsum('nij,njk->nik', direction, root_right, precision=highest)
    weight_rms = jnp.sqrt(lax.optimization_barrier(jnp.mean(master * master, (1, 2))) + 1e-06)
    step_inv = lax.rsqrt(lax.optimization_barrier(jnp.mean(direction * direction, (1, 2))) + 1e-06)
    master_new = master - 0.3 * (weight_rms * step_inv)[:, None, None] * direction
    first_new = 0.9 * moment_first + 0.1 * gain_grad
    second_new = 0.999 * moment_second + 0.001 * gain_grad * gain_grad
    first_hat = first_new / (1.0 - 0.9 ** STEP)
    second_hat = second_new / (1.0 - 0.999 ** STEP)
    gains_new = norm_gains - 0.5 * first_hat / (jnp.sqrt(second_hat) + 1e-08)
    return (layer_out, input_grad, grad_blocks, stat_left_new, stat_right_new, master_new, first_new, second_new, gains_new)
```

```python
import jax
import jax.numpy as jnp
from jax import lax
from jax.sharding import Mesh
from jax.sharding import PartitionSpec as P

D = 1024
HD = 64
FF = 4096
BLK = 128
STEP = 10


norm_eps = 1e-05
score_scale = 0.125
masked_score = -1e30


def join_blocks(blocks, height, breadth):
    block_len = blocks.shape[-1]
    return (
        blocks.reshape(height // block_len, breadth // block_len, block_len, block_len)
        .transpose(0, 2, 1, 3)
        .reshape(height, breadth)
    )


def split_blocks(matrix):
    height, breadth = matrix.shape
    return (
        matrix.reshape(height // BLK, BLK, breadth // BLK, BLK)
        .transpose(0, 2, 1, 3)
        .reshape(-1, BLK, BLK)
    )


def unpack(blocks):
    shapes_list = [(D, 3 * D), (D, D), (D, FF), (FF, D)]
    result = []
    offset = 0
    for height, breadth in shapes_list:
        number = height // BLK * (breadth // BLK)
        result.append(join_blocks(blocks[offset : offset + number], height, breadth))
        offset = offset + number
    return tuple(result)


def normalize(values):
    row_mean = jnp.mean(values, -1, keepdims=True)
    centered = values - row_mean
    row_var = jnp.mean(centered * centered, -1, keepdims=True)
    inv_std = lax.rsqrt(row_var + norm_eps)
    return (centered * inv_std, inv_std)


def norm_back(gradient, unit_vals, inv_std):
    grad_mean = jnp.mean(gradient, -1, keepdims=True)
    cross_mean = jnp.mean(gradient * unit_vals, -1, keepdims=True)
    return inv_std * (gradient - grad_mean - unit_vals * cross_mean)


def gelu_slope(hidden):
    return (
        0.5 * (1.0 + jax.scipy.special.erf(hidden * 0.7071067811865476))
        + hidden * jnp.exp(-0.5 * hidden * hidden) * 0.3989422804014327
    )


def contract_rows(left_mat, right_mat):
    return lax.dot_general(
        left_mat, right_mat, (((0,), (0,)), ((), ())), preferred_element_type=jnp.float32
    )


def contract_cols(left_mat, right_mat):
    return lax.dot_general(
        left_mat, right_mat, (((1,), (1,)), ((), ())), preferred_element_type=jnp.float32
    )


def by_blocks(step_fn, loop_state, key_parts, block_len):
    full_len = key_parts[0].shape[1]
    piece_len = min(full_len, block_len)
    piece_count = full_len // piece_len
    stacked = tuple(
        (
            part_array.reshape(
                part_array.shape[0], piece_count, piece_len, part_array.shape[2]
            ).swapaxes(0, 1)
            for part_array in key_parts
        )
    )

    def inner(carried, item_now):
        block_parts, item_index = item_now
        return (step_fn(carried, block_parts, item_index * piece_len), None)

    final_state, _ignored = lax.scan(
        inner, loop_state, (stacked, jnp.arange(piece_count, dtype=jnp.int32))
    )
    return final_state


def pair_moves():
    moves_same, moves_cross = [], []
    for z in range(4):
        for c in range(2):
            for moves, bit in ((moves_same, z % 2), (moves_cross, 1 - z % 2)):
                moves.append((z * 2 + c, (2 * c + bit) * 2 + z // 2))
    return moves_same, moves_cross


def spread_rows(values, parity):
    moves_same, moves_cross = pair_moves()
    kept = lax.dynamic_index_in_dim(values, parity, 0, False)
    crossed = lax.dynamic_index_in_dim(values, 1 - parity, 0, False)
    kept = lax.ppermute(kept, ("seq", "core"), moves_same)
    crossed = lax.ppermute(crossed, ("seq", "core"), moves_cross)
    low_part = jnp.where(parity == 0, kept, crossed)
    high_part = jnp.where(parity == 0, crossed, kept)
    return jnp.concatenate([low_part, high_part], 0)[None]


def gather_rows(values, parity):
    moves_same, moves_cross = pair_moves()
    length = values.shape[1] // 2
    parts = values.reshape(2, length, values.shape[2])
    kept = lax.dynamic_index_in_dim(parts, parity, 0, False)
    crossed = lax.dynamic_index_in_dim(parts, 1 - parity, 0, False)
    kept = lax.ppermute(kept, ("seq", "core"), [(b, a) for a, b in moves_same])
    crossed = lax.ppermute(crossed, ("seq", "core"), [(b, a) for a, b in moves_cross])
    return jnp.stack([jnp.where(parity == 0, kept, crossed), jnp.where(parity == 0, crossed, kept)], 0)


def local(
    tokens,
    cotangent,
    lengths,
    owner_perm,
    master,
    norm_gains,
    stat_left,
    stat_right,
    root_left,
    root_right,
    moment_first,
    moment_second,
):
    core = lax.axis_index("core")
    place_z = lax.axis_index("seq")
    parity = place_z % 2
    lengths = lax.dynamic_slice_in_dim(lax.all_gather(lengths, "core", axis=0, tiled=True), place_z, 1, 0)
    tokens = spread_rows(tokens, parity)
    cotangent = spread_rows(cotangent, parity)
    row_count, local_len, model_width = tokens.shape
    head_count = model_width // HD
    block_count = owner_perm.shape[0]
    owned_count = master.shape[0]
    half = block_count // 2
    near = lax.all_gather(master.astype(jnp.bfloat16), ("seq", "chip"), axis=0, tiled=True)
    far = lax.ppermute(near, "core", [(0, 1), (1, 0)])
    gathered = jnp.concatenate([near, far], 0)
    slots = jnp.arange(block_count, dtype=jnp.int32)
    slot_dev = slots // owned_count
    slot_place = (slot_dev // 2) * owned_count + slots % owned_count + jnp.where(slot_dev % 2 == core, 0, half)
    inverse = jnp.zeros((block_count,), jnp.int32).at[owner_perm].set(slot_place)
    send_perm = jnp.zeros((block_count,), jnp.int32).at[slot_place].set(owner_perm)
    w_qkv, w_out, w_up, w_down = unpack(gathered[inverse])
    flat_rows = tokens.reshape(row_count * local_len, model_width).astype(jnp.float32)
    unit_first, inv_first = normalize(flat_rows)
    normed1 = (unit_first * norm_gains[0]).astype(jnp.bfloat16)
    projected = jnp.dot(normed1, w_qkv, preferred_element_type=jnp.float32).astype(jnp.bfloat16)
    queries = (
        projected[:, :model_width]
        .reshape(row_count, local_len, head_count, HD)
        .transpose(0, 2, 1, 3)
    )
    key_all = projected[:, model_width : 2 * model_width].reshape(row_count, local_len, model_width)
    values = projected[:, 2 * model_width :].reshape(row_count, local_len, model_width)
    places = core * local_len + jnp.arange(local_len, dtype=jnp.int32)
    live_mask = (places[None, :] < lengths[:, None]).astype(jnp.float32)
    key_span = local_len * 2

    gathered_keys = lax.all_gather(key_all, "core", axis=1, tiled=True)
    gathered_values = lax.all_gather(values, "core", axis=1, tiled=True)

    def key_mask(offset, block_len):
        return ((offset + jnp.arange(block_len, dtype=jnp.int32))[None, :] < lengths[:, None])[
            :, None, None, :
        ]

    def forward_block(loop_state, block_parts, offset):
        run_max, run_total, run_sum = loop_state
        key_block, value_block = block_parts
        block_len = key_block.shape[1]
        key_heads = key_block.reshape(row_count, block_len, head_count, HD)
        value_heads = value_block.reshape(row_count, block_len, head_count, HD)
        scores = (
            jnp.einsum("rhqd,rkhd->rhqk", queries, key_heads, preferred_element_type=jnp.float32)
            * score_scale
        )
        key_live = key_mask(offset, block_len)
        scores = jnp.where(key_live, scores, masked_score)
        new_max = jnp.maximum(run_max, jnp.max(scores, -1))
        factor = jnp.exp(run_max - new_max)
        expos = jnp.where(key_live, jnp.exp(scores - new_max[..., None]), 0.0)
        run_total = run_total * factor + jnp.sum(expos, -1)
        run_sum = run_sum * factor[..., None] + jnp.einsum(
            "rhqk,rkhd->rhqd",
            expos.astype(jnp.bfloat16),
            value_heads,
            preferred_element_type=jnp.float32,
        )
        return (new_max, run_total, run_sum)

    start_state = (
        jnp.full((row_count, head_count, local_len), masked_score, jnp.float32),
        jnp.zeros((row_count, head_count, local_len), jnp.float32),
        jnp.zeros((row_count, head_count, local_len, HD), jnp.float32),
    )
    run_max, run_total, run_sum = by_blocks(
        forward_block,
        start_state,
        (
            gathered_keys,
            gathered_values,
        ),
        local_len,
    )
    attended_heads = run_sum / run_total[..., None]
    log_total = run_max + jnp.log(run_total)
    attended = (
        attended_heads.transpose(0, 2, 1, 3)
        .reshape(row_count * local_len, model_width)
        .astype(jnp.bfloat16)
    )
    middle = flat_rows + jnp.dot(attended, w_out, preferred_element_type=jnp.float32)
    unit_second, inv_second = normalize(middle)
    normed2 = (unit_second * norm_gains[1]).astype(jnp.bfloat16)
    hidden = jnp.dot(normed2, w_up, preferred_element_type=jnp.float32)
    activated = jax.nn.gelu(hidden, approximate=False).astype(jnp.bfloat16)
    layer_f32 = middle + jnp.dot(activated, w_down, preferred_element_type=jnp.float32)
    layer_out = layer_f32.reshape(row_count, local_len, model_width).astype(jnp.bfloat16)
    grad_top = (
        cotangent.reshape(row_count * local_len, model_width).astype(jnp.float32)
        * live_mask.reshape(-1)[:, None]
    )
    back_top = grad_top.astype(jnp.bfloat16)
    grad_down = contract_rows(activated, back_top)
    grad_act = contract_cols(back_top, w_down)
    grad_hidden = (grad_act * gelu_slope(hidden)).astype(jnp.bfloat16)
    grad_up = contract_rows(normed2, grad_hidden)
    grad_normed2 = contract_cols(grad_hidden, w_up)
    gain_second = jnp.sum(grad_normed2 * unit_second, 0)
    grad_middle = grad_top + norm_back(grad_normed2 * norm_gains[1], unit_second, inv_second)
    back_middle = grad_middle.astype(jnp.bfloat16)
    grad_out_w = contract_rows(attended, back_middle)
    grad_attended = contract_cols(back_middle, w_out).astype(jnp.bfloat16)
    grad_heads = grad_attended.reshape(row_count, local_len, head_count, HD).transpose(0, 2, 1, 3)
    row_delta = jnp.sum(grad_heads.astype(jnp.float32) * attended_heads, -1)

    def backward_block(loop_state, block_parts, offset):
        grad_query, key_total, value_total = loop_state
        key_block, value_block = block_parts
        block_len = key_block.shape[1]
        key_heads = key_block.reshape(row_count, block_len, head_count, HD)
        value_heads = value_block.reshape(row_count, block_len, head_count, HD)
        scores = (
            jnp.einsum("rhqd,rkhd->rhqk", queries, key_heads, preferred_element_type=jnp.float32)
            * score_scale
        )
        key_live = key_mask(offset, block_len)
        probs = jnp.where(key_live, jnp.exp(scores - log_total[..., None]), 0.0)
        grad_probs = jnp.einsum(
            "rhqd,rkhd->rhqk", grad_heads, value_heads, preferred_element_type=jnp.float32
        )
        grad_scores = (probs * (grad_probs - row_delta[..., None])).astype(jnp.bfloat16)
        grad_query = (
            grad_query
            + jnp.einsum(
                "rhqk,rkhd->rhqd", grad_scores, key_heads, preferred_element_type=jnp.float32
            )
            * score_scale
        )
        key_part = (
            jnp.einsum("rhqk,rhqd->rkhd", grad_scores, queries, preferred_element_type=jnp.float32)
            * score_scale
        )
        value_part = jnp.einsum(
            "rhqk,rhqd->rkhd",
            probs.astype(jnp.bfloat16),
            grad_heads,
            preferred_element_type=jnp.float32,
        )
        key_old = lax.dynamic_slice_in_dim(key_total, offset, block_len, 1)
        value_old = lax.dynamic_slice_in_dim(value_total, offset, block_len, 1)
        key_total = lax.dynamic_update_slice_in_dim(
            key_total, key_old + key_part.reshape(row_count, block_len, model_width), offset, 1
        )
        value_total = lax.dynamic_update_slice_in_dim(
            value_total,
            value_old + value_part.reshape(row_count, block_len, model_width),
            offset,
            1,
        )
        return (grad_query, key_total, value_total)

    back_start = (
        jnp.zeros((row_count, head_count, local_len, HD), jnp.float32),
        jnp.zeros((row_count, key_span, model_width), jnp.float32),
        jnp.zeros((row_count, key_span, model_width), jnp.float32),
    )
    grad_query, key_total, value_total = by_blocks(
        backward_block,
        back_start,
        (
            gathered_keys,
            gathered_values,
        ),
        local_len,
    )
    grad_keys, grad_values = (
        lax.psum_scatter(
            key_total.astype(jnp.bfloat16), "core", scatter_dimension=1, tiled=True
        ).astype(jnp.float32),
        lax.psum_scatter(
            value_total.astype(jnp.bfloat16), "core", scatter_dimension=1, tiled=True
        ).astype(jnp.float32),
    )
    grad_query_flat = grad_query.transpose(0, 2, 1, 3).reshape(row_count * local_len, model_width)
    grad_qkv = jnp.concatenate(
        [grad_query_flat, grad_keys.reshape(-1, model_width), grad_values.reshape(-1, model_width)],
        1,
    ).astype(jnp.bfloat16)
    grad_in_w = contract_rows(normed1, grad_qkv)
    grad_normed1 = contract_cols(grad_qkv, w_qkv)
    gain_first = jnp.sum(grad_normed1 * unit_first, 0)
    input_grad = grad_middle + norm_back(grad_normed1 * norm_gains[0], unit_first, inv_first)
    input_grad = gather_rows(
        input_grad.reshape(row_count, local_len, model_width).astype(jnp.bfloat16), parity
    ).astype(jnp.float32)
    layer_out = gather_rows(layer_out, parity)
    gain_grad = lax.psum(jnp.stack([gain_first, gain_second]), ("seq", "chip", "core"))
    pieces = jnp.concatenate(
        [
            split_blocks(grad_in_w),
            split_blocks(grad_out_w),
            split_blocks(grad_up),
            split_blocks(grad_down),
        ],
        0,
    )
    owned_grad = pieces.astype(jnp.bfloat16)[send_perm]
    other_half = lax.ppermute(owned_grad[half:], "core", [(0, 1), (1, 0)])
    chip_grad = (owned_grad[:half].astype(jnp.float32) + other_half.astype(jnp.float32)).astype(jnp.bfloat16)
    grad_blocks = lax.psum_scatter(
        chip_grad, ("seq", "chip"), scatter_dimension=0, tiled=True
    ).astype(jnp.float32)
    highest = lax.Precision.HIGHEST
    stat_left_new = stat_left + jnp.einsum(
        "nij,nkj->nik", grad_blocks, grad_blocks, precision=highest
    )
    stat_right_new = stat_right + jnp.einsum(
        "nji,njk->nik", grad_blocks, grad_blocks, precision=highest
    )
    direction = jnp.einsum("nij,njk->nik", root_left, grad_blocks, precision=highest)
    direction = jnp.einsum("nij,njk->nik", direction, root_right, precision=highest)
    weight_rms = jnp.sqrt(jnp.mean(master * master, (1, 2)) + 1e-06)
    step_inv = lax.rsqrt(jnp.mean(direction * direction, (1, 2)) + 1e-06)
    master_new = master - 0.3 * (weight_rms * step_inv)[:, None, None] * direction
    first_new = 0.9 * moment_first + 0.1 * gain_grad
    second_new = 0.999 * moment_second + 0.001 * gain_grad * gain_grad
    first_hat = first_new / (1.0 - 0.9**STEP)
    second_hat = second_new / (1.0 - 0.999**STEP)
    gains_new = norm_gains - 0.5 * first_hat / (jnp.sqrt(second_hat) + 1e-08)
    return (
        layer_out,
        input_grad,
        grad_blocks,
        stat_left_new,
        stat_right_new,
        master_new,
        first_new,
        second_new,
        gains_new,
    )


def solution(mesh):
    seq_size, rows_size = mesh.shape["seq"], mesh.shape["rows"]
    mesh = Mesh(mesh.devices.reshape(seq_size, rows_size // 2, 2), ("seq", "chip", "core"))
    placed = (
        P(("chip", "core"), "seq", None),
        P(("chip", "core"), "seq", None),
        P(("chip", "core")),
        P(),
        P(("seq", "chip", "core"), None, None),
        P(),
        P(("seq", "chip", "core"), None, None),
        P(("seq", "chip", "core"), None, None),
        P(("seq", "chip", "core"), None, None),
        P(("seq", "chip", "core"), None, None),
        P(),
        P(),
    )
    return jax.shard_map(
        local,
        mesh=mesh,
        in_specs=placed,
        out_specs=(
            P(("chip", "core"), "seq", None),
            P(("chip", "core"), "seq", None),
            P(("seq", "chip", "core"), None, None),
            P(("seq", "chip", "core"), None, None),
            P(("seq", "chip", "core"), None, None),
            P(("seq", "chip", "core"), None, None),
            P(),
            P(),
            P(),
        ),
        check_vma=False,
    )
```

```python
import functools
import jax
import jax.numpy as jnp
from jax import lax
from jax.experimental import pallas as pl
from jax.experimental.pallas import tpu as pltpu
from jax.sharding import Mesh
from jax.sharding import PartitionSpec as P

D = 1024
HD = 64
FF = 4096
BLK = 128
STEP = 10
COLS = 512
BF = jnp.bfloat16
F32 = jnp.float32
MIB = 1024 * 1024

norm_eps = 1e-05
score_scale = 0.125
masked_score = -1e30


def params(limit=56, semantics=1):
    return pltpu.CompilerParams(
        vmem_limit_bytes=limit * MIB, dimension_semantics=("arbitrary",) * semantics
    )


def mul_nn(left, right):
    return jnp.dot(left, right, preferred_element_type=F32)


def mul_nt(left, right):
    return lax.dot_general(left, right, (((1,), (1,)), ((), ())), preferred_element_type=F32)


def mul_tn(left, right):
    return lax.dot_general(left, right, (((0,), (0,)), ((), ())), preferred_element_type=F32)


def join_tile(ref):
    rows, cols = ref.shape[0], ref.shape[1]
    return jnp.concatenate([ref[:, j].reshape(rows * BLK, BLK) for j in range(cols)], axis=1)


def split_tile(ref, matrix):
    rows, cols = ref.shape[0], ref.shape[1]
    for j in range(cols):
        ref[:, j] = matrix[:, j * BLK : (j + 1) * BLK].reshape(rows, BLK, BLK).astype(ref.dtype)


def normalize(values):
    row_mean = jnp.mean(values, -1, keepdims=True)
    centered = values - row_mean
    row_var = jnp.mean(centered * centered, -1, keepdims=True)
    inv_std = lax.rsqrt(row_var + norm_eps)
    return centered * inv_std, inv_std


def norm_back(gradient, unit_vals, inv_std):
    grad_mean = jnp.mean(gradient, -1, keepdims=True)
    cross_mean = jnp.mean(gradient * unit_vals, -1, keepdims=True)
    return inv_std * (gradient - grad_mean - unit_vals * cross_mean)


def place_body(near_table, far_table, near_ref, far_ref, out_ref, sem):
    for table, src in ((near_table, near_ref), (far_table, far_ref)):

        @pl.loop(0, src.shape[0])
        def _(slot):
            pltpu.make_async_copy(src.at[slot], out_ref.at[table[slot]], sem).start()

    pltpu.make_async_copy(out_ref, out_ref, sem).wait()


def place_blocks(near_table, far_table, near, far):
    smem = pl.BlockSpec(memory_space=pltpu.SMEM)
    hbm = pl.BlockSpec(memory_space=pl.ANY)
    return pl.pallas_call(
        place_body,
        out_shape=jax.ShapeDtypeStruct((near.shape[0] * 2, BLK, BLK), BF),
        in_specs=[smem, smem, hbm, hbm],
        out_specs=hbm,
        scratch_shapes=[pltpu.SemaphoreType.DMA],
        compiler_params=pltpu.CompilerParams(vmem_limit_bytes=4 * MIB),
        name="place_weights",
    )(near_table, far_table, near, far)


def owner_body(starts, table, *refs):
    count = len(starts)
    sources = refs[:count]
    mine, other, sem = refs[-3:]
    half = mine.shape[0]
    for start, src in zip(starts, sources):

        @pl.loop(0, src.shape[0])
        def _(slot):
            dest = table[start + slot]

            @pl.when(dest < half)
            def _():
                pltpu.make_async_copy(src.at[slot], mine.at[dest], sem).start()

            @pl.when(dest >= half)
            def _():
                pltpu.make_async_copy(src.at[slot], other.at[dest - half], sem).start()

    for src in sources:
        pltpu.make_async_copy(src, src, sem).wait()


def owner_blocks(table, starts, sources, kept=None):
    smem = pl.BlockSpec(memory_space=pltpu.SMEM)
    hbm = pl.BlockSpec(memory_space=pl.ANY)
    half = table.shape[0] // 2
    shape = jax.ShapeDtypeStruct((half, BLK, BLK), BF)
    kept = () if kept is None else kept

    def body(table_ref, *refs):
        owner_body(starts, table_ref, *refs[: len(sources)], *refs[-3:])

    return pl.pallas_call(
        body,
        out_shape=[shape, shape],
        in_specs=[smem] + [hbm] * (len(sources) + len(kept)),
        out_specs=[hbm, hbm],
        scratch_shapes=[pltpu.SemaphoreType.DMA],
        input_output_aliases={1 + len(sources) + i: i for i in range(len(kept))},
        compiler_params=pltpu.CompilerParams(vmem_limit_bytes=4 * MIB),
        name="owner_order",
    )(table, *sources, *kept)


def qkv_body(own_ref, other_ref, gains_ref, w_ref, own_out, other_out, normed):
    step = pl.program_id(0)
    span = own_ref.shape[0]

    @pl.when(step == 0)
    def _():
        gain = gains_ref[0:1]
        normed[:span] = (normalize(own_ref[...].astype(F32))[0] * gain).astype(BF)
        normed[span:] = (normalize(other_ref[...].astype(F32))[0] * gain).astype(BF)

    weight = join_tile(w_ref)
    own_out[...] = mul_nn(normed[:span], weight).astype(BF)

    @pl.when(step >= D // COLS)
    def _():
        other_out[...] = mul_nn(normed[span:], weight).astype(BF)


def project(own, other, gains, weights):
    span = own.shape[0]
    skip = D // COLS
    whole = lambda j: (0, 0)
    return pl.pallas_call(
        qkv_body,
        grid=(3 * D // COLS,),
        in_specs=[
            pl.BlockSpec((span, D), whole),
            pl.BlockSpec((span, D), whole),
            pl.BlockSpec((2, D), whole),
            pl.BlockSpec((D // BLK, COLS // BLK, BLK, BLK), lambda j: (0, j, 0, 0)),
        ],
        out_specs=[
            pl.BlockSpec((span, COLS), lambda j: (0, j)),
            pl.BlockSpec((span, COLS), lambda j: (0, jnp.maximum(j - skip, 0))),
        ],
        out_shape=[
            jax.ShapeDtypeStruct((span, 3 * D), BF),
            jax.ShapeDtypeStruct((span, 2 * D), BF),
        ],
        scratch_shapes=[pltpu.VMEM((2 * span, D), BF)],
        compiler_params=params(),
        name="qkv_projection",
    )(own, other, gains, weights.reshape(-1, 3 * D // BLK, BLK, BLK))


def lane_masks(head):
    lane = lax.broadcasted_iota(jnp.int32, (1, BLK), 1)
    first = HD * (1 - head)
    keep = (lane // HD == head).astype(F32)
    dead_lane = (lane == first).astype(F32)
    terms = [(lane == first + 1 + i).astype(F32) for i in range(3)]
    return keep, dead_lane, terms


def three_terms(values):
    high = values.astype(BF).astype(F32)
    rest = values - high
    middle = rest.astype(BF).astype(F32)
    return high, middle, rest - middle


def key_bias(span, live_count):
    row = lax.broadcasted_iota(jnp.int32, (span, 1), 0)
    return jnp.where(row < live_count, 0.0, masked_score).astype(F32)


def attend_body(live_ref, q_ref, ko_ref, vo_ref, kx_ref, vx_ref, out_ref, aug_ref):
    span = q_ref.shape[0]
    bias_own = key_bias(span, live_ref[0])
    bias_other = key_bias(span, live_ref[1])
    queries = q_ref[...].astype(F32) * score_scale
    k_own, k_other = ko_ref[...].astype(F32), kx_ref[...].astype(F32)
    results = []
    for head in range(2):
        keep, dead_lane, terms = lane_masks(head)
        q_head = (queries * keep + dead_lane).astype(BF)
        s_own = mul_nt(q_head, (k_own * keep + bias_own * dead_lane).astype(BF))
        s_other = mul_nt(q_head, (k_other * keep + bias_other * dead_lane).astype(BF))
        top = jnp.maximum(
            jnp.max(s_own, -1, keepdims=True), jnp.max(s_other, -1, keepdims=True)
        )
        p_own = jnp.exp(s_own - top)
        p_other = jnp.exp(s_other - top)
        total = jnp.sum(p_own, -1, keepdims=True) + jnp.sum(p_other, -1, keepdims=True)
        mixed = mul_nn(p_own.astype(BF), vo_ref[...]) + mul_nn(p_other.astype(BF), vx_ref[...])
        results.append(mixed / total * keep)
        parts = three_terms(-(top + jnp.log(total)))
        stats = sum(part * lane for part, lane in zip(parts, terms))
        aug_ref[:, head * BLK : (head + 1) * BLK] = (q_head.astype(F32) + stats).astype(BF)
    out_ref[...] = (results[0] + results[1]).astype(BF)


def attend(live, own, other):
    span = own.shape[0]
    pairs = D // BLK
    col = lambda shift: pl.BlockSpec((span, BLK), lambda p: (0, p + shift))
    return pl.pallas_call(
        attend_body,
        grid=(pairs,),
        in_specs=[
            pl.BlockSpec(memory_space=pltpu.SMEM),
            col(0),
            col(pairs),
            col(2 * pairs),
            col(0),
            col(pairs),
        ],
        out_specs=[col(0), pl.BlockSpec((span, 2 * BLK), lambda p: (0, p))],
        out_shape=[
            jax.ShapeDtypeStruct((span, D), BF),
            jax.ShapeDtypeStruct((span, 2 * D), BF),
        ],
        compiler_params=params(),
        name="attention",
    )(live, own, own, own, other, other)


def attend_back_body(
    live_ref, aug_ref, ko_ref, vo_ref, kx_ref, vx_ref, at_ref, g_ref, dq_ref, own_ref, other_ref
):
    span = at_ref.shape[0]
    grads = g_ref[...].astype(F32)
    product = grads * at_ref[...].astype(F32)
    keeps, g_augs, q_augs = [], [], []
    for head in range(2):
        keep, dead_lane, terms = lane_masks(head)
        delta = jnp.sum(product * keep, -1, keepdims=True)
        parts = three_terms(-delta)
        stats = sum(part * lane for part, lane in zip(parts, terms))
        g_augs.append((grads * keep + stats).astype(BF))
        q_augs.append(aug_ref[:, head * BLK : (head + 1) * BLK])
    d_query = [None, None]
    for k_ref, v_ref, out_ref, live in (
        (ko_ref, vo_ref, own_ref, live_ref[0]),
        (kx_ref, vx_ref, other_ref, live_ref[1]),
    ):
        bias = key_bias(span, live)
        keys = k_ref[...]
        keys_f, values_f = keys.astype(F32), v_ref[...].astype(F32)
        d_keys = d_values = None
        for head in range(2):
            keep, dead_lane, terms = lane_masks(head)
            ones = terms[0] + terms[1] + terms[2]
            k_aug = (keys_f * keep + (bias * dead_lane + ones)).astype(BF)
            v_aug = (values_f * keep + ones).astype(BF)
            probs = jnp.exp(mul_nt(k_aug, q_augs[head]))
            d_scores = (probs * mul_nt(v_aug, g_augs[head])).astype(BF)
            value_part = mul_nn(probs.astype(BF), g_augs[head]) * keep
            key_part = mul_nn(d_scores, q_augs[head]) * keep
            query_part = mul_tn(d_scores, keys) * (keep * score_scale)
            d_query[head] = query_part if d_query[head] is None else d_query[head] + query_part
            d_values = value_part if d_values is None else d_values + value_part
            d_keys = key_part if d_keys is None else d_keys + key_part
        out_ref[0] = d_keys.astype(out_ref.dtype)
        out_ref[1] = d_values.astype(out_ref.dtype)
    dq_ref[...] = (d_query[0] + d_query[1]).astype(BF)


def attend_back(live, aug, own, other, attended, grads):
    span = own.shape[0]
    pairs = D // BLK
    col = lambda shift: pl.BlockSpec((span, BLK), lambda p: (0, p + shift))
    pair_out = pl.BlockSpec((2, span, BLK), lambda p: (0, 0, p))
    return pl.pallas_call(
        attend_back_body,
        grid=(pairs,),
        in_specs=[
            pl.BlockSpec(memory_space=pltpu.SMEM),
            pl.BlockSpec((span, 2 * BLK), lambda p: (0, p)),
            col(pairs),
            col(2 * pairs),
            col(0),
            col(pairs),
            col(0),
            col(0),
        ],
        out_specs=[col(0), pair_out, pair_out],
        out_shape=[
            jax.ShapeDtypeStruct((span, D), BF),
            jax.ShapeDtypeStruct((2, span, D), F32),
            jax.ShapeDtypeStruct((2, span, D), BF),
        ],
        compiler_params=params(),
        name="attention_backward",
    )(live, aug, own, own, other, other, attended, grads)


def feed_body(
    live_ref,
    tokens_ref,
    attended_ref,
    cot_ref,
    gains_ref,
    wo_ref,
    wu_ref,
    wd_ref,
    layer_ref,
    gu_ref,
    gd_ref,
    go_ref,
    gm_ref,
    ga_ref,
    gain_ref,
    unit,
    inv,
    normed,
    top,
    acc_out,
    acc_back,
):
    step = pl.program_id(0)
    span = tokens_ref.shape[0]

    @pl.when(step == 0)
    def _():
        weight = join_tile(wo_ref)
        middle = tokens_ref[...].astype(F32) + mul_nn(attended_ref[...], weight)
        unit_vals, inv_std = normalize(middle)
        unit[...] = unit_vals
        inv[...] = inv_std
        normed[...] = (unit_vals * gains_ref[1:2]).astype(BF)
        row = lax.broadcasted_iota(jnp.int32, (span, 1), 0)
        top[...] = jnp.where(row < live_ref[2], cot_ref[...].astype(F32), 0.0).astype(BF)
        acc_out[...] = middle
        acc_back[...] = jnp.zeros_like(acc_back)

    w_up = join_tile(wu_ref)
    w_down = join_tile(wd_ref)
    hidden = mul_nn(normed[...], w_up)
    grad_act = mul_nt(top[...], w_down)
    erf_part = 0.5 * (1.0 + lax.erf(hidden * 0.7071067811865476))
    activated = (hidden * erf_part).astype(BF)
    slope = erf_part + hidden * jnp.exp(-0.5 * hidden * hidden) * 0.3989422804014327
    grad_hidden = (grad_act * slope).astype(BF)
    acc_out[...] += mul_nn(activated, w_down)
    acc_back[...] += mul_nt(grad_hidden, w_up)
    split_tile(gd_ref, mul_tn(activated, top[...]))
    split_tile(gu_ref, mul_tn(normed[...], grad_hidden))

    @pl.when(step == pl.num_programs(0) - 1)
    def _():
        layer_ref[...] = acc_out[...].astype(BF)
        unit_vals = unit[...]
        back = acc_back[...]
        gain_ref[...] = jnp.sum(back * unit_vals, 0, keepdims=True)
        grad_middle = top[...].astype(F32) + norm_back(back * gains_ref[1:2], unit_vals, inv[...])
        gm_ref[...] = grad_middle
        back_middle = grad_middle.astype(BF)
        split_tile(go_ref, mul_tn(attended_ref[...], back_middle))
        ga_ref[...] = mul_nt(back_middle, join_tile(wo_ref)).astype(BF)


def feed(live, tokens, attended, cotangent, gains, weights):
    span = tokens.shape[0]
    side, width = D // BLK, COLS // BLK
    whole = lambda j: (0, 0)
    act = pl.BlockSpec((span, D), whole)
    per_row = weights.reshape(-1, side, BLK, BLK)
    per_up = weights.reshape(-1, FF // BLK, BLK, BLK)
    out_row = (3 * side * side) // side // side
    up_row = 4 * side * side // (FF // BLK) // side
    down_row = (4 * side * side + side * FF // BLK) // side // width
    return pl.pallas_call(
        feed_body,
        grid=(FF // COLS,),
        in_specs=[
            pl.BlockSpec(memory_space=pltpu.SMEM),
            act,
            act,
            act,
            pl.BlockSpec((2, D), whole),
            pl.BlockSpec((side, side, BLK, BLK), lambda j: (out_row, 0, 0, 0)),
            pl.BlockSpec((side, width, BLK, BLK), lambda j: (up_row, j, 0, 0)),
            pl.BlockSpec((width, side, BLK, BLK), lambda j: (down_row + j, 0, 0, 0)),
        ],
        out_specs=[
            act,
            pl.BlockSpec((side, width, BLK, BLK), lambda j: (0, j, 0, 0)),
            pl.BlockSpec((width, side, BLK, BLK), lambda j: (j, 0, 0, 0)),
            pl.BlockSpec((side, side, BLK, BLK), lambda j: (0, 0, 0, 0)),
            act,
            act,
            pl.BlockSpec((1, D), whole),
        ],
        out_shape=[
            jax.ShapeDtypeStruct((span, D), BF),
            jax.ShapeDtypeStruct((side, FF // BLK, BLK, BLK), BF),
            jax.ShapeDtypeStruct((FF // BLK, side, BLK, BLK), BF),
            jax.ShapeDtypeStruct((side, side, BLK, BLK), BF),
            jax.ShapeDtypeStruct((span, D), F32),
            jax.ShapeDtypeStruct((span, D), BF),
            jax.ShapeDtypeStruct((1, D), F32),
        ],
        scratch_shapes=[
            pltpu.VMEM((span, D), F32),
            pltpu.VMEM((span, 1), F32),
            pltpu.VMEM((span, D), BF),
            pltpu.VMEM((span, D), BF),
            pltpu.VMEM((span, D), F32),
            pltpu.VMEM((span, D), F32),
        ],
        compiler_params=params(),
        name="feed_forward",
    )(live, tokens, attended, cotangent, gains, per_row, per_up, per_row)


def input_body(
    tokens_ref, gains_ref, dq_ref, own_ref, recv_ref, gm_ref, w_ref, gq_ref, out_ref, gain_ref,
    unit, inv, normed, acc, tile
):
    step = pl.program_id(0)

    @pl.when(step == 0)
    def _():
        unit_vals, inv_std = normalize(tokens_ref[...].astype(F32))
        unit[...] = unit_vals
        inv[...] = inv_std
        normed[...] = (unit_vals * gains_ref[0:1]).astype(BF)
        acc[...] = jnp.zeros_like(acc)

    @pl.when(step < D // COLS)
    def _():
        tile[...] = dq_ref[...]

    @pl.when(step >= D // COLS)
    def _():
        tile[...] = (own_ref[0] + recv_ref[0].astype(F32)).astype(BF)

    grad = tile[...]
    split_tile(gq_ref, mul_tn(normed[...], grad))
    acc[...] += mul_nt(grad, join_tile(w_ref))

    @pl.when(step == pl.num_programs(0) - 1)
    def _():
        unit_vals = unit[...]
        back = acc[...]
        gain_ref[...] = jnp.sum(back * unit_vals, 0, keepdims=True)
        out_ref[...] = (
            gm_ref[...] + norm_back(back * gains_ref[0:1], unit_vals, inv[...])
        ).astype(BF)


def input_back(tokens, gains, d_query, own, received, grad_middle, weights):
    span = tokens.shape[0]
    side, width = D // BLK, COLS // BLK
    per = D // COLS
    whole = lambda j: (0, 0)
    act = pl.BlockSpec((span, D), whole)
    later = lambda j: (jnp.maximum(j - per, 0) // per, 0, jnp.maximum(j - per, 0) % per)
    tile = pl.BlockSpec((side, width, BLK, BLK), lambda j: (0, j, 0, 0))
    return pl.pallas_call(
        input_body,
        grid=(3 * per,),
        in_specs=[
            act,
            pl.BlockSpec((2, D), whole),
            pl.BlockSpec((span, COLS), lambda j: (0, jnp.minimum(j, per - 1))),
            pl.BlockSpec((1, span, COLS), later),
            pl.BlockSpec((1, span, COLS), later),
            act,
            tile,
        ],
        out_specs=[tile, act, pl.BlockSpec((1, D), whole)],
        out_shape=[
            jax.ShapeDtypeStruct((side, 3 * side, BLK, BLK), BF),
            jax.ShapeDtypeStruct((span, D), BF),
            jax.ShapeDtypeStruct((1, D), F32),
        ],
        scratch_shapes=[
            pltpu.VMEM((span, D), F32),
            pltpu.VMEM((span, 1), F32),
            pltpu.VMEM((span, D), BF),
            pltpu.VMEM((span, D), F32),
            pltpu.VMEM((span, COLS), BF),
        ],
        compiler_params=params(),
        name="qkv_backward",
    )(
        tokens, gains, d_query, own, received, grad_middle,
        weights.reshape(-1, 3 * side, BLK, BLK),
    )


def update_body(g_ref, m_ref, sl_ref, sr_ref, rl_ref, rr_ref, sl_out, sr_out, m_out):
    highest = lax.Precision.HIGHEST
    for i in range(g_ref.shape[0]):
        grad = g_ref[i]
        dot = functools.partial(
            lax.dot_general, precision=highest, preferred_element_type=F32
        )
        sl_out[i] = sl_ref[i] + dot(grad, grad, (((1,), (1,)), ((), ())))
        sr_out[i] = sr_ref[i] + dot(grad, grad, (((0,), (0,)), ((), ())))
        inner = dot(rl_ref[i], grad, (((1,), (0,)), ((), ())))
        direction = dot(inner, rr_ref[i], (((1,), (0,)), ((), ())))
        master = m_ref[i]
        scale = jnp.sqrt(jnp.mean(master * master, keepdims=True) + 1e-06)
        scale = scale * lax.rsqrt(jnp.mean(direction * direction, keepdims=True) + 1e-06)
        m_out[i] = master - 0.3 * scale * direction


def update(grads, master, stat_left, stat_right, root_left, root_right):
    count = grads.shape[0]
    group = 3 if count % 3 == 0 else 1
    block = pl.BlockSpec((group, BLK, BLK), lambda i: (i, 0, 0))
    shape = jax.ShapeDtypeStruct(grads.shape, F32)
    return pl.pallas_call(
        update_body,
        grid=(count // group,),
        in_specs=[block] * 6,
        out_specs=[block] * 3,
        out_shape=[shape] * 3,
        compiler_params=params(),
        name="block_update",
    )(grads, master, stat_left, stat_right, root_left, root_right)


def pair_moves():
    moves_same, moves_cross = [], []
    for z in range(4):
        for c in range(2):
            for moves, bit in ((moves_same, z % 2), (moves_cross, 1 - z % 2)):
                moves.append((z * 2 + c, (2 * c + bit) * 2 + z // 2))
    return moves_same, moves_cross


def spread_rows(values, parity):
    moves_same, moves_cross = pair_moves()
    kept = lax.dynamic_index_in_dim(values, parity, 0, False)
    crossed = lax.dynamic_index_in_dim(values, 1 - parity, 0, False)
    kept = lax.ppermute(kept, ("seq", "core"), moves_same)
    crossed = lax.ppermute(crossed, ("seq", "core"), moves_cross)
    low_part = jnp.where(parity == 0, kept, crossed)
    high_part = jnp.where(parity == 0, crossed, kept)
    return jnp.concatenate([low_part, high_part], 0)


def gather_rows(values, parity):
    moves_same, moves_cross = pair_moves()
    parts = values.reshape(2, values.shape[0] // 2, values.shape[1])
    kept = lax.dynamic_index_in_dim(parts, parity, 0, False)
    crossed = lax.dynamic_index_in_dim(parts, 1 - parity, 0, False)
    kept = lax.ppermute(kept, ("seq", "core"), [(b, a) for a, b in moves_same])
    crossed = lax.ppermute(crossed, ("seq", "core"), [(b, a) for a, b in moves_cross])
    return jnp.stack([jnp.where(parity == 0, kept, crossed), jnp.where(parity == 0, crossed, kept)], 0)


def swap_cores(values):
    return lax.ppermute(values, "core", [(0, 1), (1, 0)])


def sum_all(values):
    axes = ("seq", "chip", "core")
    count = lax.axis_size(axes)
    bit = 1
    while bit < count:
        values = values + lax.ppermute(values, axes, [(i, i ^ bit) for i in range(count)])
        bit *= 2
    return values


def local(
    tokens,
    cotangent,
    lengths,
    owner_perm,
    master,
    norm_gains,
    stat_left,
    stat_right,
    root_left,
    root_right,
    moment_first,
    moment_second,
):
    core = lax.axis_index("core")
    place_z = lax.axis_index("seq")
    parity = place_z % 2
    block_count = owner_perm.shape[0]
    owned = master.shape[0]
    half = block_count // 2

    near = lax.all_gather(master.astype(BF), ("seq", "chip"), axis=0, tiled=True)
    far = swap_cores(near)

    length = lax.dynamic_index_in_dim(
        lax.all_gather(lengths, "core", axis=0, tiled=True), place_z, 0, False
    )
    own_tokens = spread_rows(tokens, parity)
    other_tokens = swap_cores(own_tokens)
    own_cot = spread_rows(cotangent, parity)
    span = own_tokens.shape[0]
    live = jnp.stack([length - core * span, length - (1 - core) * span, length - core * span])

    by_core = owner_perm.reshape(half // owned, 2, owned)
    near_table = lax.dynamic_index_in_dim(by_core, core, 1, False).reshape(half)
    far_table = lax.dynamic_index_in_dim(by_core, 1 - core, 1, False).reshape(half)
    slot_places = jnp.zeros((block_count,), jnp.int32).at[
        jnp.concatenate([near_table, far_table])
    ].set(jnp.arange(block_count, dtype=jnp.int32))

    weights = place_blocks(near_table, far_table, near, far)
    own_qkv, other_kv = project(own_tokens, other_tokens, norm_gains, weights)
    attended, q_aug = attend(live, own_qkv, other_kv)
    layer, g_up, g_down, g_out, grad_middle, grad_attended, gain_second = feed(
        live, own_tokens, attended, own_cot, norm_gains, weights
    )
    layer_out = gather_rows(layer, parity)
    d_query, d_own, d_other = attend_back(live, q_aug, own_qkv, other_kv, attended, grad_attended)
    received = swap_cores(d_other)
    side = D // BLK
    flat = lambda g: g.reshape(-1, BLK, BLK)
    first_rest = 3 * side * side
    sends = owner_blocks(
        slot_places,
        (first_rest, first_rest + side * side, first_rest + side * side + side * FF // BLK),
        (flat(g_out), flat(g_up), flat(g_down)),
    )
    g_qkv, grad_in, gain_first = input_back(
        own_tokens, norm_gains, d_query, d_own, received, grad_middle, weights
    )
    input_grad = gather_rows(grad_in, parity).astype(F32)
    gain_grad = sum_all(jnp.concatenate([gain_first, gain_second], 0))
    mine, other = owner_blocks(slot_places, (0,), (flat(g_qkv),), tuple(sends))
    chip_grad = (mine.astype(F32) + swap_cores(other).astype(F32)).astype(BF)
    grad_blocks = lax.psum_scatter(
        chip_grad, ("seq", "chip"), scatter_dimension=0, tiled=True
    ).astype(F32)
    stat_left_new, stat_right_new, master_new = update(
        grad_blocks, master, stat_left, stat_right, root_left, root_right
    )
    first_new = 0.9 * moment_first + 0.1 * gain_grad
    second_new = 0.999 * moment_second + 0.001 * gain_grad * gain_grad
    first_hat = first_new / (1.0 - 0.9**STEP)
    second_hat = second_new / (1.0 - 0.999**STEP)
    gains_new = norm_gains - 0.5 * first_hat / (jnp.sqrt(second_hat) + 1e-08)
    return (
        layer_out,
        input_grad,
        grad_blocks,
        stat_left_new,
        stat_right_new,
        master_new,
        first_new,
        second_new,
        gains_new,
    )


def solution(mesh):
    seq_size, rows_size = mesh.shape["seq"], mesh.shape["rows"]
    mesh = Mesh(mesh.devices.reshape(seq_size, rows_size // 2, 2), ("seq", "chip", "core"))
    activation = P(("chip", "core"), "seq", None)
    blocks = P(("seq", "chip", "core"), None, None)
    return jax.shard_map(
        local,
        mesh=mesh,
        in_specs=(
            activation, activation, P(("chip", "core")), P(), blocks, P(),
            blocks, blocks, blocks, blocks, P(), P(),
        ),
        out_specs=(activation, activation, blocks, blocks, blocks, blocks, P(), P(), P()),
        check_vma=False,
    )
```

```python
import functools
import jax
import jax.numpy as jnp
import numpy as np
from jax import lax
from jax.experimental import pallas as pl
from jax.experimental.pallas import tpu as pltpu
from jax.sharding import Mesh
from jax.sharding import PartitionSpec as P

D = 1024
HD = 64
FF = 4096
BLK = 128
STEP = 10
COLS = 512
BF = jnp.bfloat16
F32 = jnp.float32
MIB = 1024 * 1024

norm_eps = 1e-05
score_scale = 0.125
masked_score = -1e30


def params():
    return pltpu.CompilerParams(vmem_limit_bytes=56 * MIB)


def mul_nn(left, right):
    return jnp.dot(left, right, preferred_element_type=F32)


def mul_nt(left, right):
    return lax.dot_general(left, right, (((1,), (1,)), ((), ())), preferred_element_type=F32)


def mul_tn(left, right):
    return lax.dot_general(left, right, (((0,), (0,)), ((), ())), preferred_element_type=F32)


def join_tile(ref):
    rows, cols = ref.shape[0], ref.shape[1]
    return jnp.concatenate([ref[:, j].reshape(rows * BLK, BLK) for j in range(cols)], axis=1)


def split_tile(ref, matrix):
    rows, cols = ref.shape[0], ref.shape[1]
    for j in range(cols):
        ref[:, j] = matrix[:, j * BLK : (j + 1) * BLK].reshape(rows, BLK, BLK).astype(ref.dtype)


def normalize(values):
    row_mean = jnp.mean(values, -1, keepdims=True)
    centered = values - row_mean
    row_var = jnp.mean(centered * centered, -1, keepdims=True)
    inv_std = lax.rsqrt(row_var + norm_eps)
    return centered * inv_std, inv_std


def norm_back(gradient, unit_vals, inv_std):
    grad_mean = jnp.mean(gradient, -1, keepdims=True)
    cross_mean = jnp.mean(gradient * unit_vals, -1, keepdims=True)
    return inv_std * (gradient - grad_mean - unit_vals * cross_mean)


def place_body(first, table, near_ref, far_ref, *refs):
    out_ref, sem = refs[-2:]
    count = near_ref.shape[0]
    half = table.shape[0] // 2
    for start, src in ((first, near_ref), (half + first, far_ref)):

        @pl.loop(0, count)
        def _(slot):
            pltpu.make_async_copy(src.at[slot], out_ref.at[table[start + slot]], sem).start()

    done = out_ref.at[pl.ds(0, 2 * count)]
    pltpu.make_async_copy(done, done, sem).wait()


def place_blocks(table, first, near, far, kept):
    smem = pl.BlockSpec(memory_space=pltpu.SMEM)
    hbm = pl.BlockSpec(memory_space=pltpu.HBM)
    kept = () if kept is None else (kept,)
    return pl.pallas_call(
        functools.partial(place_body, first),
        out_shape=jax.ShapeDtypeStruct((table.shape[0], BLK, BLK), BF),
        in_specs=[smem, hbm, hbm] + [hbm] * len(kept),
        out_specs=hbm,
        scratch_shapes=[pltpu.SemaphoreType.DMA],
        input_output_aliases={3: 0} if kept else {},
        compiler_params=params(),
        name="place_weights",
    )(table, near, far, *kept)


def qkv_body(own_ref, other_ref, gains_ref, w_ref, own_out, other_out, normed):
    step = pl.program_id(0)
    span = own_ref.shape[0]

    @pl.when(step == 0)
    def _():
        gain = gains_ref[0:1]
        normed[:span] = (normalize(own_ref[...].astype(F32))[0] * gain).astype(BF)
        normed[span:] = (normalize(other_ref[...].astype(F32))[0] * gain).astype(BF)

    weight = join_tile(w_ref)
    own_out[...] = mul_nn(normed[:span], weight).astype(BF)

    @pl.when(step >= D // COLS)
    def _():
        other_out[...] = mul_nn(normed[span:], weight).astype(BF)


def project(own, other, gains, weights):
    span = own.shape[0]
    skip = D // COLS
    whole = lambda j: (0, 0)
    return pl.pallas_call(
        qkv_body,
        grid=(3 * D // COLS,),
        in_specs=[
            pl.BlockSpec((span, D), whole),
            pl.BlockSpec((span, D), whole),
            pl.BlockSpec((2, D), whole),
            pl.BlockSpec((D // BLK, COLS // BLK, BLK, BLK), lambda j: (0, j, 0, 0)),
        ],
        out_specs=[
            pl.BlockSpec((span, COLS), lambda j: (0, j)),
            pl.BlockSpec((span, COLS), lambda j: (0, jnp.maximum(j - skip, 0))),
        ],
        out_shape=[
            jax.ShapeDtypeStruct((span, 3 * D), BF),
            jax.ShapeDtypeStruct((span, 2 * D), BF),
        ],
        scratch_shapes=[pltpu.VMEM((2 * span, D), BF)],
        compiler_params=params(),
        name="qkv_projection",
    )(own, other, gains, weights.reshape(-1, 3 * D // BLK, BLK, BLK))


def lane_masks(head):
    lane = lax.broadcasted_iota(jnp.int32, (1, BLK), 1)
    first = HD * (1 - head)
    keep = (lane // HD == head).astype(F32)
    dead_lane = (lane == first).astype(F32)
    terms = [(lane == first + 1 + i).astype(F32) for i in range(3)]
    return keep, dead_lane, terms


def three_terms(values):
    high = values.astype(BF).astype(F32)
    rest = values - high
    middle = rest.astype(BF).astype(F32)
    return high, middle, rest - middle


def key_bias(span, live_count):
    row = lax.broadcasted_iota(jnp.int32, (span, 1), 0)
    return jnp.where(row < live_count, 0.0, masked_score).astype(F32)


def attend_body(live_ref, q_ref, ko_ref, vo_ref, kx_ref, vx_ref, out_ref, aug_ref):
    span = q_ref.shape[0]
    bias_own = key_bias(span, live_ref[0])
    bias_other = key_bias(span, live_ref[1])
    queries = q_ref[...].astype(F32) * score_scale
    k_own, k_other = ko_ref[...].astype(F32), kx_ref[...].astype(F32)
    results = []
    for head in range(2):
        keep, dead_lane, terms = lane_masks(head)
        q_head = (queries * keep + dead_lane).astype(BF)
        s_own = mul_nt(q_head, (k_own * keep + bias_own * dead_lane).astype(BF))
        s_other = mul_nt(q_head, (k_other * keep + bias_other * dead_lane).astype(BF))
        top = jnp.maximum(
            jnp.max(s_own, -1, keepdims=True), jnp.max(s_other, -1, keepdims=True)
        )
        p_own = jnp.exp(s_own - top)
        p_other = jnp.exp(s_other - top)
        total = jnp.sum(p_own, -1, keepdims=True) + jnp.sum(p_other, -1, keepdims=True)
        mixed = mul_nn(p_own.astype(BF), vo_ref[...]) + mul_nn(p_other.astype(BF), vx_ref[...])
        results.append(mixed / total * keep)
        parts = three_terms(-(top + jnp.log(total)))
        stats = sum(part * lane for part, lane in zip(parts, terms))
        aug_ref[:, head * BLK : (head + 1) * BLK] = (q_head.astype(F32) + stats).astype(BF)
    out_ref[...] = (results[0] + results[1]).astype(BF)


def attend(live, own, other):
    span = own.shape[0]
    pairs = D // BLK
    col = lambda shift: pl.BlockSpec((span, BLK), lambda p: (0, p + shift))
    return pl.pallas_call(
        attend_body,
        grid=(pairs,),
        in_specs=[
            pl.BlockSpec(memory_space=pltpu.SMEM),
            col(0),
            col(pairs),
            col(2 * pairs),
            col(0),
            col(pairs),
        ],
        out_specs=[col(0), pl.BlockSpec((span, 2 * BLK), lambda p: (0, p))],
        out_shape=[
            jax.ShapeDtypeStruct((span, D), BF),
            jax.ShapeDtypeStruct((span, 2 * D), BF),
        ],
        compiler_params=params(),
        name="attention",
    )(live, own, own, own, other, other)


def attend_back_body(
    starts, live_ref, aug_ref, ko_ref, vo_ref, kx_ref, vx_ref, at_ref, g_ref, table, *refs
):
    sources = refs[: len(starts)]
    dq_ref, own_ref, other_ref, buffer, sem = refs[len(starts) :]
    span = at_ref.shape[0]
    step, steps = pl.program_id(0), D // BLK
    for start, src in zip(starts, sources):
        share = src.shape[0] // steps
        for i in range(share):
            slot = step * share + i
            pltpu.make_async_copy(src.at[slot], buffer.at[table[start + slot]], sem).start()
    grads = g_ref[...].astype(F32)
    product = grads * at_ref[...].astype(F32)
    keeps, g_augs, q_augs = [], [], []
    for head in range(2):
        keep, dead_lane, terms = lane_masks(head)
        delta = jnp.sum(product * keep, -1, keepdims=True)
        parts = three_terms(-delta)
        stats = sum(part * lane for part, lane in zip(parts, terms))
        g_augs.append((grads * keep + stats).astype(BF))
        q_augs.append(aug_ref[:, head * BLK : (head + 1) * BLK])
    d_query = [None, None]
    for k_ref, v_ref, out_ref, live in (
        (ko_ref, vo_ref, own_ref, live_ref[0]),
        (kx_ref, vx_ref, other_ref, live_ref[1]),
    ):
        bias = key_bias(span, live)
        keys = k_ref[...]
        keys_f, values_f = keys.astype(F32), v_ref[...].astype(F32)
        d_keys = d_values = None
        for head in range(2):
            keep, dead_lane, terms = lane_masks(head)
            ones = terms[0] + terms[1] + terms[2]
            k_aug = (keys_f * keep + (bias * dead_lane + ones)).astype(BF)
            v_aug = (values_f * keep + ones).astype(BF)
            probs = jnp.exp(mul_nt(k_aug, q_augs[head]))
            d_scores = (probs * mul_nt(v_aug, g_augs[head])).astype(BF)
            value_part = mul_nn(probs.astype(BF), g_augs[head]) * keep
            key_part = mul_nn(d_scores, q_augs[head]) * keep
            query_part = mul_tn(d_scores, keys) * (keep * score_scale)
            d_query[head] = query_part if d_query[head] is None else d_query[head] + query_part
            d_values = value_part if d_values is None else d_values + value_part
            d_keys = key_part if d_keys is None else d_keys + key_part
        out_ref[0] = d_keys.astype(out_ref.dtype)
        out_ref[1] = d_values.astype(out_ref.dtype)
    dq_ref[...] = (d_query[0] + d_query[1]).astype(BF)

    @pl.when(step == steps - 1)
    def _():
        for src in sources:
            pltpu.make_async_copy(src, src, sem).wait()


def attend_back(live, aug, own, other, attended, grads, table, starts, sources):
    span = own.shape[0]
    hbm = pl.BlockSpec(memory_space=pltpu.HBM)
    pairs = D // BLK
    col = lambda shift: pl.BlockSpec((span, BLK), lambda p: (0, p + shift))
    pair_out = pl.BlockSpec((2, span, BLK), lambda p: (0, 0, p))
    return pl.pallas_call(
        functools.partial(attend_back_body, starts),
        grid=(pairs,),
        in_specs=[
            pl.BlockSpec(memory_space=pltpu.SMEM),
            pl.BlockSpec((span, 2 * BLK), lambda p: (0, p)),
            col(pairs),
            col(2 * pairs),
            col(0),
            col(pairs),
            col(0),
            col(0),
            pl.BlockSpec(memory_space=pltpu.SMEM),
        ]
        + [hbm] * len(sources),
        out_specs=[col(0), pair_out, pair_out, hbm],
        out_shape=[
            jax.ShapeDtypeStruct((span, D), BF),
            jax.ShapeDtypeStruct((2, span, D), F32),
            jax.ShapeDtypeStruct((2, span, D), BF),
            jax.ShapeDtypeStruct((table.shape[0], BLK, BLK), BF),
        ],
        scratch_shapes=[pltpu.SemaphoreType.DMA],
        compiler_params=params(),
        name="attention_backward",
    )(live, aug, own, own, other, other, attended, grads, table, *sources)


def feed_body(
    live_ref,
    tokens_ref,
    attended_ref,
    cot_ref,
    gains_ref,
    wo_ref,
    wu_ref,
    wd_ref,
    layer_ref,
    gu_ref,
    gd_ref,
    go_ref,
    gm_ref,
    ga_ref,
    gain_ref,
    unit,
    inv,
    normed,
    top,
    acc_out,
    acc_back,
):
    step = pl.program_id(0)
    span = tokens_ref.shape[0]

    @pl.when(step == 0)
    def _():
        weight = join_tile(wo_ref)
        middle = tokens_ref[...].astype(F32) + mul_nn(attended_ref[...], weight)
        unit_vals, inv_std = normalize(middle)
        unit[...] = unit_vals
        inv[...] = inv_std
        normed[...] = (unit_vals * gains_ref[1:2]).astype(BF)
        row = lax.broadcasted_iota(jnp.int32, (span, 1), 0)
        top[...] = jnp.where(row < live_ref[2], cot_ref[...].astype(F32), 0.0).astype(BF)
        acc_out[...] = middle
        acc_back[...] = jnp.zeros_like(acc_back)

    w_up = join_tile(wu_ref)
    w_down = join_tile(wd_ref)
    hidden = mul_nn(normed[...], w_up)
    grad_act = mul_nt(top[...], w_down)
    erf_part = 0.5 * (1.0 + lax.erf(hidden * 0.7071067811865476))
    activated = (hidden * erf_part).astype(BF)
    slope = erf_part + hidden * jnp.exp(-0.5 * hidden * hidden) * 0.3989422804014327
    grad_hidden = (grad_act * slope).astype(BF)
    acc_out[...] += mul_nn(activated, w_down)
    acc_back[...] += mul_nt(grad_hidden, w_up)
    split_tile(gd_ref, mul_tn(activated, top[...]))
    split_tile(gu_ref, mul_tn(normed[...], grad_hidden))

    @pl.when(step == pl.num_programs(0) - 1)
    def _():
        layer_ref[...] = acc_out[...].astype(BF)
        unit_vals = unit[...]
        back = acc_back[...]
        gain_ref[...] = jnp.sum(back * unit_vals, 0, keepdims=True)
        grad_middle = top[...].astype(F32) + norm_back(back * gains_ref[1:2], unit_vals, inv[...])
        gm_ref[...] = grad_middle
        back_middle = grad_middle.astype(BF)
        split_tile(go_ref, mul_tn(attended_ref[...], back_middle))
        ga_ref[...] = mul_nt(back_middle, join_tile(wo_ref)).astype(BF)


def feed(live, tokens, attended, cotangent, gains, weights):
    span = tokens.shape[0]
    side, width = D // BLK, COLS // BLK
    whole = lambda j: (0, 0)
    act = pl.BlockSpec((span, D), whole)
    per_row = weights.reshape(-1, side, BLK, BLK)
    per_up = weights.reshape(-1, FF // BLK, BLK, BLK)
    out_row = (3 * side * side) // side // side
    up_row = 4 * side * side // (FF // BLK) // side
    down_row = (4 * side * side + side * FF // BLK) // side // width
    return pl.pallas_call(
        feed_body,
        grid=(FF // COLS,),
        in_specs=[
            pl.BlockSpec(memory_space=pltpu.SMEM),
            act,
            act,
            act,
            pl.BlockSpec((2, D), whole),
            pl.BlockSpec((side, side, BLK, BLK), lambda j: (out_row, 0, 0, 0)),
            pl.BlockSpec((side, width, BLK, BLK), lambda j: (up_row, j, 0, 0)),
            pl.BlockSpec((width, side, BLK, BLK), lambda j: (down_row + j, 0, 0, 0)),
        ],
        out_specs=[
            act,
            pl.BlockSpec((side, width, BLK, BLK), lambda j: (0, j, 0, 0)),
            pl.BlockSpec((width, side, BLK, BLK), lambda j: (j, 0, 0, 0)),
            pl.BlockSpec((side, side, BLK, BLK), lambda j: (0, 0, 0, 0)),
            act,
            act,
            pl.BlockSpec((1, D), whole),
        ],
        out_shape=[
            jax.ShapeDtypeStruct((span, D), BF),
            jax.ShapeDtypeStruct((side, FF // BLK, BLK, BLK), BF),
            jax.ShapeDtypeStruct((FF // BLK, side, BLK, BLK), BF),
            jax.ShapeDtypeStruct((side, side, BLK, BLK), BF),
            jax.ShapeDtypeStruct((span, D), F32),
            jax.ShapeDtypeStruct((span, D), BF),
            jax.ShapeDtypeStruct((1, D), F32),
        ],
        scratch_shapes=[
            pltpu.VMEM((span, D), F32),
            pltpu.VMEM((span, 1), F32),
            pltpu.VMEM((span, D), BF),
            pltpu.VMEM((span, D), BF),
            pltpu.VMEM((span, D), F32),
            pltpu.VMEM((span, D), F32),
        ],
        compiler_params=params(),
        name="feed_forward",
    )(live, tokens, attended, cotangent, gains, per_row, per_up, per_row)


def input_body(
    tokens_ref, gains_ref, dq_ref, own_ref, recv_ref, gm_ref, w_ref, table, kept_ref,
    buffer, out_ref, gain_ref, unit, inv, normed, acc, tile, stage, sems
):
    step = pl.program_id(0)
    last = pl.num_programs(0) - 1
    place = step % 2

    def drain(which):
        pltpu.make_async_copy(stage.at[which], stage.at[which], sems.at[which]).wait()

    @pl.when(step == 0)
    def _():
        unit_vals, inv_std = normalize(tokens_ref[...].astype(F32))
        unit[...] = unit_vals
        inv[...] = inv_std
        normed[...] = (unit_vals * gains_ref[0:1]).astype(BF)
        acc[...] = jnp.zeros_like(acc)

    @pl.when(step < D // COLS)
    def _():
        tile[...] = dq_ref[...]

    @pl.when(step >= D // COLS)
    def _():
        tile[...] = (own_ref[0] + recv_ref[0].astype(F32)).astype(BF)

    grad = tile[...]
    acc[...] += mul_nt(grad, join_tile(w_ref))

    @pl.when(step >= 2)
    def _():
        drain(place)

    split_tile(stage.at[place], mul_tn(normed[...], grad))
    rows, cols = stage.shape[1], stage.shape[2]
    for i in range(rows):
        for j in range(cols):
            dest = table[i * (3 * D // BLK) + step * cols + j]
            pltpu.make_async_copy(stage.at[place, i, j], buffer.at[dest], sems.at[place]).start()

    @pl.when(step == last)
    def _():
        drain(1 - place)
        drain(place)
        unit_vals = unit[...]
        back = acc[...]
        gain_ref[...] = jnp.sum(back * unit_vals, 0, keepdims=True)
        out_ref[...] = (
            gm_ref[...] + norm_back(back * gains_ref[0:1], unit_vals, inv[...])
        ).astype(BF)


def input_back(tokens, gains, d_query, own, received, grad_middle, weights, table, kept):
    span = tokens.shape[0]
    hbm = pl.BlockSpec(memory_space=pltpu.HBM)
    side, width = D // BLK, COLS // BLK
    per = D // COLS
    whole = lambda j: (0, 0)
    act = pl.BlockSpec((span, D), whole)
    later = lambda j: (jnp.maximum(j - per, 0) // per, 0, jnp.maximum(j - per, 0) % per)
    tile = pl.BlockSpec((side, width, BLK, BLK), lambda j: (0, j, 0, 0))
    return pl.pallas_call(
        input_body,
        grid=(3 * per,),
        in_specs=[
            act,
            pl.BlockSpec((2, D), whole),
            pl.BlockSpec((span, COLS), lambda j: (0, jnp.minimum(j, per - 1))),
            pl.BlockSpec((1, span, COLS), later),
            pl.BlockSpec((1, span, COLS), later),
            act,
            tile,
            pl.BlockSpec(memory_space=pltpu.SMEM),
            hbm,
        ],
        out_specs=[hbm, act, pl.BlockSpec((1, D), whole)],
        input_output_aliases={8: 0},
        out_shape=[
            jax.ShapeDtypeStruct(kept.shape, BF),
            jax.ShapeDtypeStruct((span, D), BF),
            jax.ShapeDtypeStruct((1, D), F32),
        ],
        scratch_shapes=[
            pltpu.VMEM((span, D), F32),
            pltpu.VMEM((span, 1), F32),
            pltpu.VMEM((span, D), BF),
            pltpu.VMEM((span, D), F32),
            pltpu.VMEM((span, COLS), BF),
            pltpu.VMEM((2, side, width, BLK, BLK), BF),
            pltpu.SemaphoreType.DMA((2,)),
        ],
        compiler_params=params(),
        name="qkv_backward",
    )(
        tokens, gains, d_query, own, received, grad_middle,
        weights.reshape(-1, 3 * side, BLK, BLK), table, kept,
    )


def two_terms(values):
    high = values.astype(BF)
    return high, (values - high.astype(F32)).astype(BF)


def update_body(g_ref, m_ref, sl_ref, sr_ref, rl_ref, rr_ref, sl_out, sr_out, m_out):
    def long_left(terms, axis):
        return jnp.concatenate([terms[0], terms[0], terms[1]], axis)

    def long_right(terms, axis):
        return jnp.concatenate([terms[0], terms[1], terms[0]], axis)

    for i in range(g_ref.shape[0]):
        grad = two_terms(g_ref[i])
        sl_out[i] = sl_ref[i] + mul_nt(long_left(grad, 1), long_right(grad, 1))
        tall = long_right(grad, 0)
        sr_out[i] = sr_ref[i] + mul_tn(long_left(grad, 0), tall)
        inner = mul_nn(long_left(two_terms(rl_ref[i]), 1), tall)
        direction = mul_nn(
            long_left(two_terms(inner), 1), long_right(two_terms(rr_ref[i]), 0)
        )
        master = m_ref[i]
        scale = jnp.sqrt(jnp.mean(master * master, keepdims=True) + 1e-06)
        scale = scale * lax.rsqrt(jnp.mean(direction * direction, keepdims=True) + 1e-06)
        m_out[i] = master - 0.3 * scale * direction


def update(grads, master, stat_left, stat_right, root_left, root_right):
    count = grads.shape[0]
    group = 3 if count % 3 == 0 else 1
    block = pl.BlockSpec((group, BLK, BLK), lambda i: (i, 0, 0))
    shape = jax.ShapeDtypeStruct(grads.shape, F32)
    return pl.pallas_call(
        update_body,
        grid=(count // group,),
        in_specs=[block] * 6,
        out_specs=[block] * 3,
        out_shape=[shape] * 3,
        compiler_params=params(),
        name="block_update",
    )(grads, master, stat_left, stat_right, root_left, root_right)


def pair_moves():
    moves_same, moves_cross = [], []
    for z in range(4):
        for c in range(2):
            for moves, bit in ((moves_same, z % 2), (moves_cross, 1 - z % 2)):
                moves.append((z * 2 + c, (2 * c + bit) * 2 + z // 2))
    return moves_same, moves_cross


def spread_rows(values, parity):
    moves_same, moves_cross = pair_moves()
    kept = lax.dynamic_index_in_dim(values, parity, 0, False)
    crossed = lax.dynamic_index_in_dim(values, 1 - parity, 0, False)
    kept = lax.ppermute(kept, ("seq", "core"), moves_same)
    crossed = lax.ppermute(crossed, ("seq", "core"), moves_cross)
    low_part = jnp.where(parity == 0, kept, crossed)
    high_part = jnp.where(parity == 0, crossed, kept)
    return jnp.concatenate([low_part, high_part], 0)


def gather_rows(values, parity):
    moves_same, moves_cross = pair_moves()
    parts = values.reshape(2, values.shape[0] // 2, values.shape[1])
    kept = lax.dynamic_index_in_dim(parts, parity, 0, False)
    crossed = lax.dynamic_index_in_dim(parts, 1 - parity, 0, False)
    kept = lax.ppermute(kept, ("seq", "core"), [(b, a) for a, b in moves_same])
    crossed = lax.ppermute(crossed, ("seq", "core"), [(b, a) for a, b in moves_cross])
    return jnp.stack([jnp.where(parity == 0, kept, crossed), jnp.where(parity == 0, crossed, kept)], 0)


def swap_cores(values):
    return lax.ppermute(values, "core", [(0, 1), (1, 0)])


def sum_all(values):
    axes = ("seq", "chip", "core")
    count = lax.axis_size(axes)
    bit = 1
    while bit < count:
        values = values + lax.ppermute(values, axes, [(i, i ^ bit) for i in range(count)])
        bit *= 2
    return values


def chip_orders(chips):
    bits = [1 << i for i in range(chips.bit_length() - 1)]
    return bits, bits[::-1]


def offsets(order):
    result = [0]
    for bit in order:
        result = result + [o ^ bit for o in result]
    return result


def place_lists(chips, owned, planes):
    halves = ((0, owned // 2), (owned // 2, owned))
    lists = []
    for k in range(planes):
        for order, (low, high) in zip(chip_orders(chips), halves):
            for offset in offsets(order):
                lists += [(k, offset, slot) for slot in range(low, high)]
    return np.array(lists, np.int32).T


def swap_chips(values, bit):
    chips = lax.axis_size("chip")
    return lax.ppermute(values, "chip", [(i, i ^ bit) for i in range(chips)])


def move_planes(values, shift):
    planes = lax.axis_size("seq")
    return lax.ppermute(values, "seq", [(i, (i + shift) % planes) for i in range(planes)])


def gather_plane(values):
    middle = values.shape[0] // 2
    parts = []
    for part, order in zip((values[:middle], values[middle:]), chip_orders(lax.axis_size("chip"))):
        for bit in order:
            part = jnp.concatenate([part, swap_chips(part, bit)], 0)
        parts.append(part)
    return jnp.concatenate(parts, 0)


def add_halves(kept, came):
    return (kept.astype(F32) + came.astype(F32)).astype(BF)


def scatter_plane(values, owned):
    chips = lax.axis_size("chip")
    middle = owned // 2 * chips
    parts = []
    for part, order in zip((values[:middle], values[middle:]), chip_orders(chips)):
        for bit in order[::-1]:
            count = part.shape[0] // 2
            part = add_halves(part[:count], swap_chips(part[count:], bit))
        parts.append(part)
    return jnp.concatenate(parts, 0)


def local(
    tokens,
    cotangent,
    lengths,
    owner_perm,
    master,
    norm_gains,
    stat_left,
    stat_right,
    root_left,
    root_right,
    moment_first,
    moment_second,
):
    core = lax.axis_index("core")
    place_z = lax.axis_index("seq")
    parity = place_z % 2
    block_count = owner_perm.shape[0]
    owned = master.shape[0]
    half = block_count // 2

    chips, planes = lax.axis_size("chip"), lax.axis_size("seq")
    me = lax.axis_index("chip")

    own_tokens = spread_rows(tokens, parity)
    other_tokens = swap_cores(own_tokens)
    own_cot = spread_rows(cotangent, parity)
    pair_lengths = jnp.stack([lengths, swap_cores(lengths)])
    pair_lengths = jnp.where(core == 0, pair_lengths, pair_lengths[::-1]).reshape(-1)
    length = lax.dynamic_index_in_dim(pair_lengths, place_z, 0, False)
    span = own_tokens.shape[0]
    live = jnp.stack([length - core * span, length - (1 - core) * span, length - core * span])

    distance, offset, slot = place_lists(chips, owned, planes)
    device = ((place_z - distance) % planes * chips + (me ^ offset)) * 2
    near_slots = (device + core) * owned + slot
    far_slots = (device + 1 - core) * owned + slot
    table = owner_perm[jnp.concatenate([near_slots, far_slots])]
    inverse = jnp.zeros((block_count,), jnp.int32).at[table].set(
        jnp.arange(block_count, dtype=jnp.int32)
    )

    shard = master.astype(BF)
    shards = [shard] + [move_planes(shard, k) for k in range(1, planes)]
    (shards[-1], own_tokens, other_tokens, own_cot, live, table, inverse) = lax.optimization_barrier(
        (shards[-1], own_tokens, other_tokens, own_cot, live, table, inverse)
    )
    weights = None
    per_plane = chips * owned
    for k in range(planes):
        near = gather_plane(shards[k])
        weights = place_blocks(table, k * per_plane, near, swap_cores(near), weights)

    own_qkv, other_kv = project(own_tokens, other_tokens, norm_gains, weights)
    attended, q_aug = attend(live, own_qkv, other_kv)
    layer, g_up, g_down, g_out, grad_middle, grad_attended, gain_second = feed(
        live, own_tokens, attended, own_cot, norm_gains, weights
    )
    layer_out = gather_rows(layer, parity)
    side = D // BLK
    flat = lambda g: g.reshape(-1, BLK, BLK)
    first_rest = 3 * side * side
    starts = (first_rest, first_rest + side * side, first_rest + side * side + side * FF // BLK)
    d_query, d_own, d_other, sends = attend_back(
        live, q_aug, own_qkv, other_kv, attended, grad_attended,
        inverse, starts, (flat(g_out), flat(g_up), flat(g_down)),
    )
    received = swap_cores(d_other)
    sends, grad_in, gain_first = input_back(
        own_tokens, norm_gains, d_query, d_own, received, grad_middle, weights, inverse, sends
    )
    input_grad = gather_rows(grad_in, parity).astype(F32)
    gain_grad = sum_all(jnp.concatenate([gain_first, gain_second], 0))
    grad_blocks = None
    for k in [2, 1, 3, 0]:
        mine = sends[k * per_plane : (k + 1) * per_plane]
        other = sends[half + k * per_plane : half + (k + 1) * per_plane]
        part = scatter_plane(add_halves(mine, swap_cores(other)), owned)
        if k:
            part = move_planes(part, -k)
        part = part.astype(F32)
        grad_blocks = part if grad_blocks is None else grad_blocks + part
    stat_left_new, stat_right_new, master_new = update(
        grad_blocks, master, stat_left, stat_right, root_left, root_right
    )
    first_new = 0.9 * moment_first + 0.1 * gain_grad
    second_new = 0.999 * moment_second + 0.001 * gain_grad * gain_grad
    first_hat = first_new / (1.0 - 0.9**STEP)
    second_hat = second_new / (1.0 - 0.999**STEP)
    gains_new = norm_gains - 0.5 * first_hat / (jnp.sqrt(second_hat) + 1e-08)
    return (
        layer_out,
        input_grad,
        grad_blocks,
        stat_left_new,
        stat_right_new,
        master_new,
        first_new,
        second_new,
        gains_new,
    )


def solution(mesh):
    seq_size, rows_size = mesh.shape["seq"], mesh.shape["rows"]
    mesh = Mesh(mesh.devices.reshape(seq_size, rows_size // 2, 2), ("seq", "chip", "core"))
    activation = P(("chip", "core"), "seq", None)
    blocks = P(("seq", "chip", "core"), None, None)
    return jax.shard_map(
        local,
        mesh=mesh,
        in_specs=(
            activation, activation, P(("chip", "core")), P(), blocks, P(),
            blocks, blocks, blocks, blocks, P(), P(),
        ),
        out_specs=(activation, activation, blocks, blocks, blocks, blocks, P(), P(), P()),
        check_vma=False,
    )
```

```python
import functools
import jax
import jax.numpy as jnp
import numpy as np
from jax import lax
from jax.experimental import pallas as pl
from jax.experimental.pallas import tpu as pltpu
from jax.sharding import Mesh
from jax.sharding import PartitionSpec as P

D = 1024
HD = 64
FF = 4096
BLK = 128
STEP = 10
COLS = 512
BF = jnp.bfloat16
F32 = jnp.float32
MIB = 1024 * 1024

norm_eps = 1e-05
score_scale = 0.125
masked_score = -1e30


def params():
    return pltpu.CompilerParams(vmem_limit_bytes=56 * MIB)


def cost(flops, nbytes):
    return pl.CostEstimate(flops=int(flops), bytes_accessed=int(nbytes), transcendentals=0)


def mul_nn(left, right):
    return jnp.dot(left, right, preferred_element_type=F32)


def mul_nt(left, right):
    return lax.dot_general(left, right, (((1,), (1,)), ((), ())), preferred_element_type=F32)


def mul_tn(left, right):
    return lax.dot_general(left, right, (((0,), (0,)), ((), ())), preferred_element_type=F32)


def join_tile(ref):
    rows, cols = ref.shape[0], ref.shape[1]
    return jnp.concatenate([ref[:, j].reshape(rows * BLK, BLK) for j in range(cols)], axis=1)


def split_tile(ref, matrix):
    rows, cols = ref.shape[0], ref.shape[1]
    for j in range(cols):
        ref[:, j] = matrix[:, j * BLK : (j + 1) * BLK].reshape(rows, BLK, BLK).astype(ref.dtype)


def normalize(values):
    row_mean = jnp.mean(values, -1, keepdims=True)
    centered = values - row_mean
    row_var = jnp.mean(centered * centered, -1, keepdims=True)
    inv_std = lax.rsqrt(row_var + norm_eps)
    return centered * inv_std, inv_std


def norm_back(gradient, unit_vals, inv_std):
    grad_mean = jnp.mean(gradient, -1, keepdims=True)
    cross_mean = jnp.mean(gradient * unit_vals, -1, keepdims=True)
    return inv_std * (gradient - grad_mean - unit_vals * cross_mean)


def place_body(first, table, near_ref, far_ref, *refs):
    out_ref, sem = refs[-2:]
    count = near_ref.shape[0]
    half = table.shape[0] // 2
    start = first + pl.program_id(0) * count
    for slot in range(count):
        pltpu.make_async_copy(near_ref.at[slot], out_ref.at[table[start + slot]], sem).start()
        far_place = table[half + start + slot]
        pltpu.make_async_copy(far_ref.at[slot], out_ref.at[far_place], sem).start()
    done = out_ref.at[pl.ds(0, 2 * count)]
    pltpu.make_async_copy(done, done, sem).wait()


def place_blocks(table, first, near, far, kept):
    smem = pl.BlockSpec(memory_space=pltpu.SMEM)
    hbm = pl.BlockSpec(memory_space=pltpu.HBM)
    steps = 4
    part = pl.BlockSpec((near.shape[0] // steps, BLK, BLK), lambda i: (i, 0, 0))
    kept = () if kept is None else (kept,)
    return pl.pallas_call(
        functools.partial(place_body, first),
        grid=(steps,),
        out_shape=jax.ShapeDtypeStruct((table.shape[0], BLK, BLK), BF),
        in_specs=[smem, part, part] + [hbm] * len(kept),
        out_specs=hbm,
        scratch_shapes=[pltpu.SemaphoreType.DMA],
        input_output_aliases={3: 0} if kept else {},
        compiler_params=params(),
        cost_estimate=cost(0, 4 * near.size * 2),
        name="place_weights",
    )(table, near, far, *kept)


def qkv_body(own_ref, other_ref, gains_ref, w_ref, own_out, other_out, normed):
    step = pl.program_id(0)
    span = own_ref.shape[0]

    @pl.when(step == 0)
    def _():
        gain = gains_ref[0:1]
        normed[:span] = (normalize(own_ref[...].astype(F32))[0] * gain).astype(BF)
        normed[span:] = (normalize(other_ref[...].astype(F32))[0] * gain).astype(BF)

    weight = join_tile(w_ref)
    own_out[...] = mul_nn(normed[:span], weight).astype(BF)

    @pl.when(step >= D // COLS)
    def _():
        other_out[...] = mul_nn(normed[span:], weight).astype(BF)


def project(own, other, gains, weights):
    span = own.shape[0]
    skip = D // COLS
    whole = lambda j: (0, 0)
    return pl.pallas_call(
        qkv_body,
        grid=(3 * D // COLS,),
        in_specs=[
            pl.BlockSpec((span, D), whole),
            pl.BlockSpec((span, D), whole),
            pl.BlockSpec((2, D), whole),
            pl.BlockSpec((D // BLK, COLS // BLK, BLK, BLK), lambda j: (0, j, 0, 0)),
        ],
        out_specs=[
            pl.BlockSpec((span, COLS), lambda j: (0, j)),
            pl.BlockSpec((span, COLS), lambda j: (0, jnp.maximum(j - skip, 0))),
        ],
        out_shape=[
            jax.ShapeDtypeStruct((span, 3 * D), BF),
            jax.ShapeDtypeStruct((span, 2 * D), BF),
        ],
        scratch_shapes=[pltpu.VMEM((2 * span, D), BF)],
        compiler_params=params(),
        cost_estimate=cost(10 * span * D * D, 12 * MIB),
        name="qkv_projection",
    )(own, other, gains, weights.reshape(-1, 3 * D // BLK, BLK, BLK))


def lane_masks(head):
    lane = lax.broadcasted_iota(jnp.int32, (1, BLK), 1)
    first = HD * (1 - head)
    keep = (lane // HD == head).astype(F32)
    dead_lane = (lane == first).astype(F32)
    terms = [(lane == first + 1 + i).astype(F32) for i in range(3)]
    return keep, dead_lane, terms


def three_terms(values):
    high = values.astype(BF).astype(F32)
    rest = values - high
    middle = rest.astype(BF).astype(F32)
    return high, middle, rest - middle


def key_bias(span, live_count):
    row = lax.broadcasted_iota(jnp.int32, (span, 1), 0)
    return jnp.where(row < live_count, 0.0, masked_score).astype(F32)


def attend_body(live_ref, q_ref, ko_ref, vo_ref, kx_ref, vx_ref, out_ref, aug_ref):
    span = q_ref.shape[0]
    bias_own = key_bias(span, live_ref[0])
    bias_other = key_bias(span, live_ref[1])
    queries = q_ref[...].astype(F32) * score_scale
    k_own, k_other = ko_ref[...].astype(F32), kx_ref[...].astype(F32)
    results = []
    for head in range(2):
        keep, dead_lane, terms = lane_masks(head)
        q_head = (queries * keep + dead_lane).astype(BF)
        s_own = mul_nt(q_head, (k_own * keep + bias_own * dead_lane).astype(BF))
        s_other = mul_nt(q_head, (k_other * keep + bias_other * dead_lane).astype(BF))
        top = jnp.maximum(
            jnp.max(s_own, -1, keepdims=True), jnp.max(s_other, -1, keepdims=True)
        )
        p_own = jnp.exp(s_own - top)
        p_other = jnp.exp(s_other - top)
        total = jnp.sum(p_own, -1, keepdims=True) + jnp.sum(p_other, -1, keepdims=True)
        mixed = mul_nn(p_own.astype(BF), vo_ref[...]) + mul_nn(p_other.astype(BF), vx_ref[...])
        results.append(mixed / total * keep)
        parts = three_terms(-(top + jnp.log(total)))
        stats = sum(part * lane for part, lane in zip(parts, terms))
        aug_ref[:, head * BLK : (head + 1) * BLK] = (q_head.astype(F32) + stats).astype(BF)
    out_ref[...] = (results[0] + results[1]).astype(BF)


def attend(live, own, other):
    span = own.shape[0]
    pairs = D // BLK
    col = lambda shift: pl.BlockSpec((span, BLK), lambda p: (0, p + shift))
    return pl.pallas_call(
        attend_body,
        grid=(pairs,),
        in_specs=[
            pl.BlockSpec(memory_space=pltpu.SMEM),
            col(0),
            col(pairs),
            col(2 * pairs),
            col(0),
            col(pairs),
        ],
        out_specs=[col(0), pl.BlockSpec((span, 2 * BLK), lambda p: (0, p))],
        out_shape=[
            jax.ShapeDtypeStruct((span, D), BF),
            jax.ShapeDtypeStruct((span, 2 * D), BF),
        ],
        compiler_params=params(),
        cost_estimate=cost(40 * span * span * D, 8 * MIB),
        name="attention",
    )(live, own, own, own, other, other)


def attend_back_body(
    starts, live_ref, aug_ref, ko_ref, vo_ref, kx_ref, vx_ref, at_ref, g_ref, table, *refs
):
    sources = refs[: len(starts)]
    dq_ref, own_ref, other_ref, buffer, sem = refs[len(starts) :]
    span = at_ref.shape[0]
    step = pl.program_id(0)
    for start, src in zip(starts, sources):
        share = src.shape[0]
        for i in range(share):
            dest = table[start + step * share + i]
            pltpu.make_async_copy(src.at[i], buffer.at[dest], sem).start()
    grads = g_ref[...].astype(F32)
    product = grads * at_ref[...].astype(F32)
    keeps, g_augs, q_augs = [], [], []
    for head in range(2):
        keep, dead_lane, terms = lane_masks(head)
        delta = jnp.sum(product * keep, -1, keepdims=True)
        parts = three_terms(-delta)
        stats = sum(part * lane for part, lane in zip(parts, terms))
        g_augs.append((grads * keep + stats).astype(BF))
        q_augs.append(aug_ref[:, head * BLK : (head + 1) * BLK])
    d_query = [None, None]
    for k_ref, v_ref, out_ref, live in (
        (ko_ref, vo_ref, own_ref, live_ref[0]),
        (kx_ref, vx_ref, other_ref, live_ref[1]),
    ):
        bias = key_bias(span, live)
        keys = k_ref[...]
        keys_f, values_f = keys.astype(F32), v_ref[...].astype(F32)
        d_keys = d_values = None
        for head in range(2):
            keep, dead_lane, terms = lane_masks(head)
            ones = terms[0] + terms[1] + terms[2]
            k_aug = (keys_f * keep + (bias * dead_lane + ones)).astype(BF)
            v_aug = (values_f * keep + ones).astype(BF)
            probs = jnp.exp(mul_nt(k_aug, q_augs[head]))
            d_scores = (probs * mul_nt(v_aug, g_augs[head])).astype(BF)
            value_part = mul_nn(probs.astype(BF), g_augs[head]) * keep
            key_part = mul_nn(d_scores, q_augs[head]) * keep
            query_part = mul_tn(d_scores, keys) * (keep * score_scale)
            d_query[head] = query_part if d_query[head] is None else d_query[head] + query_part
            d_values = value_part if d_values is None else d_values + value_part
            d_keys = key_part if d_keys is None else d_keys + key_part
        out_ref[0] = d_keys.astype(out_ref.dtype)
        out_ref[1] = d_values.astype(out_ref.dtype)
    dq_ref[...] = (d_query[0] + d_query[1]).astype(BF)
    for src in sources:
        pltpu.make_async_copy(src, src, sem).wait()


def attend_back(live, aug, own, other, attended, grads, table, starts, sources):
    span = own.shape[0]
    hbm = pl.BlockSpec(memory_space=pltpu.HBM)
    pairs = D // BLK
    col = lambda shift: pl.BlockSpec((span, BLK), lambda p: (0, p + shift))
    pair_out = pl.BlockSpec((2, span, BLK), lambda p: (0, 0, p))
    return pl.pallas_call(
        functools.partial(attend_back_body, starts),
        grid=(pairs,),
        in_specs=[
            pl.BlockSpec(memory_space=pltpu.SMEM),
            pl.BlockSpec((span, 2 * BLK), lambda p: (0, p)),
            col(pairs),
            col(2 * pairs),
            col(0),
            col(pairs),
            col(0),
            col(0),
            pl.BlockSpec(memory_space=pltpu.SMEM),
        ]
        + [
            pl.BlockSpec((src.shape[0] // pairs, BLK, BLK), lambda p: (p, 0, 0))
            for src in sources
        ],
        out_specs=[col(0), pair_out, pair_out, hbm],
        out_shape=[
            jax.ShapeDtypeStruct((span, D), BF),
            jax.ShapeDtypeStruct((2, span, D), F32),
            jax.ShapeDtypeStruct((2, span, D), BF),
            jax.ShapeDtypeStruct((table.shape[0], BLK, BLK), BF),
        ],
        scratch_shapes=[pltpu.SemaphoreType.DMA],
        compiler_params=params(),
        cost_estimate=cost(60 * span * span * D, 50 * MIB),
        name="attention_backward",
    )(live, aug, own, own, other, other, attended, grads, table, *sources)


def feed_body(
    live_ref,
    tokens_ref,
    attended_ref,
    cot_ref,
    gains_ref,
    wo_ref,
    wu_ref,
    wd_ref,
    layer_ref,
    gu_ref,
    gd_ref,
    go_ref,
    gm_ref,
    ga_ref,
    gain_ref,
    unit,
    inv,
    normed,
    top,
    acc_out,
    acc_back,
):
    step = pl.program_id(0)
    span = tokens_ref.shape[0]

    @pl.when(step == 0)
    def _():
        weight = join_tile(wo_ref)
        middle = tokens_ref[...].astype(F32) + mul_nn(attended_ref[...], weight)
        unit_vals, inv_std = normalize(middle)
        unit[...] = unit_vals
        inv[...] = inv_std
        normed[...] = (unit_vals * gains_ref[1:2]).astype(BF)
        row = lax.broadcasted_iota(jnp.int32, (span, 1), 0)
        top[...] = jnp.where(row < live_ref[2], cot_ref[...].astype(F32), 0.0).astype(BF)
        acc_out[...] = middle
        acc_back[...] = jnp.zeros_like(acc_back)

    w_up = join_tile(wu_ref)
    w_down = join_tile(wd_ref)
    hidden = mul_nn(normed[...], w_up)
    grad_act = mul_nt(top[...], w_down)
    erf_part = 0.5 * (1.0 + lax.erf(hidden * 0.7071067811865476))
    activated = (hidden * erf_part).astype(BF)
    slope = erf_part + hidden * jnp.exp(-0.5 * hidden * hidden) * 0.3989422804014327
    grad_hidden = (grad_act * slope).astype(BF)
    acc_out[...] += mul_nn(activated, w_down)
    acc_back[...] += mul_nt(grad_hidden, w_up)
    split_tile(gd_ref, mul_tn(activated, top[...]))
    split_tile(gu_ref, mul_tn(normed[...], grad_hidden))

    @pl.when(step == pl.num_programs(0) - 1)
    def _():
        layer_ref[...] = acc_out[...].astype(BF)
        unit_vals = unit[...]
        back = acc_back[...]
        gain_ref[...] = jnp.sum(back * unit_vals, 0, keepdims=True)
        grad_middle = top[...].astype(F32) + norm_back(back * gains_ref[1:2], unit_vals, inv[...])
        gm_ref[...] = grad_middle
        back_middle = grad_middle.astype(BF)
        split_tile(go_ref, mul_tn(attended_ref[...], back_middle))
        ga_ref[...] = mul_nt(back_middle, join_tile(wo_ref)).astype(BF)


def feed(live, tokens, attended, cotangent, gains, weights):
    span = tokens.shape[0]
    side, width = D // BLK, COLS // BLK
    whole = lambda j: (0, 0)
    act = pl.BlockSpec((span, D), whole)
    per_row = weights.reshape(-1, side, BLK, BLK)
    per_up = weights.reshape(-1, FF // BLK, BLK, BLK)
    out_row = (3 * side * side) // side // side
    up_row = 4 * side * side // (FF // BLK) // side
    down_row = (4 * side * side + side * FF // BLK) // side // width
    return pl.pallas_call(
        feed_body,
        grid=(FF // COLS,),
        in_specs=[
            pl.BlockSpec(memory_space=pltpu.SMEM),
            act,
            act,
            act,
            pl.BlockSpec((2, D), whole),
            pl.BlockSpec((side, side, BLK, BLK), lambda j: (out_row, 0, 0, 0)),
            pl.BlockSpec((side, width, BLK, BLK), lambda j: (up_row, j, 0, 0)),
            pl.BlockSpec((width, side, BLK, BLK), lambda j: (down_row + j, 0, 0, 0)),
        ],
        out_specs=[
            act,
            pl.BlockSpec((side, width, BLK, BLK), lambda j: (0, j, 0, 0)),
            pl.BlockSpec((width, side, BLK, BLK), lambda j: (j, 0, 0, 0)),
            pl.BlockSpec((side, side, BLK, BLK), lambda j: (0, 0, 0, 0)),
            act,
            act,
            pl.BlockSpec((1, D), whole),
        ],
        out_shape=[
            jax.ShapeDtypeStruct((span, D), BF),
            jax.ShapeDtypeStruct((side, FF // BLK, BLK, BLK), BF),
            jax.ShapeDtypeStruct((FF // BLK, side, BLK, BLK), BF),
            jax.ShapeDtypeStruct((side, side, BLK, BLK), BF),
            jax.ShapeDtypeStruct((span, D), F32),
            jax.ShapeDtypeStruct((span, D), BF),
            jax.ShapeDtypeStruct((1, D), F32),
        ],
        scratch_shapes=[
            pltpu.VMEM((span, D), F32),
            pltpu.VMEM((span, 1), F32),
            pltpu.VMEM((span, D), BF),
            pltpu.VMEM((span, D), BF),
            pltpu.VMEM((span, D), F32),
            pltpu.VMEM((span, D), F32),
        ],
        compiler_params=params(),
        cost_estimate=cost(14 * span * D * FF, 50 * MIB),
        name="feed_forward",
    )(live, tokens, attended, cotangent, gains, per_row, per_up, per_row)


def input_body(
    tokens_ref, gains_ref, dq_ref, own_ref, recv_ref, gm_ref, w_ref, table, kept_ref,
    buffer, out_ref, gain_ref, unit, inv, normed, acc, tile, stage, sems
):
    step = pl.program_id(0)
    last = pl.num_programs(0) - 1
    place = step % 2

    def drain(which):
        pltpu.make_async_copy(stage.at[which], stage.at[which], sems.at[which]).wait()

    @pl.when(step == 0)
    def _():
        unit_vals, inv_std = normalize(tokens_ref[...].astype(F32))
        unit[...] = unit_vals
        inv[...] = inv_std
        normed[...] = (unit_vals * gains_ref[0:1]).astype(BF)
        acc[...] = jnp.zeros_like(acc)

    @pl.when(step < D // COLS)
    def _():
        tile[...] = dq_ref[...]

    @pl.when(step >= D // COLS)
    def _():
        tile[...] = (own_ref[0] + recv_ref[0].astype(F32)).astype(BF)

    grad = tile[...]
    acc[...] += mul_nt(grad, join_tile(w_ref))

    @pl.when(step >= 2)
    def _():
        drain(place)

    split_tile(stage.at[place], mul_tn(normed[...], grad))
    rows, cols = stage.shape[1], stage.shape[2]
    for i in range(rows):
        for j in range(cols):
            dest = table[i * (3 * D // BLK) + step * cols + j]
            pltpu.make_async_copy(stage.at[place, i, j], buffer.at[dest], sems.at[place]).start()

    @pl.when(step == last)
    def _():
        drain(1 - place)
        drain(place)
        unit_vals = unit[...]
        back = acc[...]
        gain_ref[...] = jnp.sum(back * unit_vals, 0, keepdims=True)
        out_ref[...] = (
            gm_ref[...] + norm_back(back * gains_ref[0:1], unit_vals, inv[...])
        ).astype(BF)


def input_back(tokens, gains, d_query, own, received, grad_middle, weights, table, kept):
    span = tokens.shape[0]
    hbm = pl.BlockSpec(memory_space=pltpu.HBM)
    side, width = D // BLK, COLS // BLK
    per = D // COLS
    whole = lambda j: (0, 0)
    act = pl.BlockSpec((span, D), whole)
    later = lambda j: (jnp.maximum(j - per, 0) // per, 0, jnp.maximum(j - per, 0) % per)
    tile = pl.BlockSpec((side, width, BLK, BLK), lambda j: (0, j, 0, 0))
    return pl.pallas_call(
        input_body,
        grid=(3 * per,),
        in_specs=[
            act,
            pl.BlockSpec((2, D), whole),
            pl.BlockSpec((span, COLS), lambda j: (0, jnp.minimum(j, per - 1))),
            pl.BlockSpec((1, span, COLS), later),
            pl.BlockSpec((1, span, COLS), later),
            act,
            tile,
            pl.BlockSpec(memory_space=pltpu.SMEM),
            hbm,
        ],
        out_specs=[hbm, act, pl.BlockSpec((1, D), whole)],
        input_output_aliases={8: 0},
        out_shape=[
            jax.ShapeDtypeStruct(kept.shape, BF),
            jax.ShapeDtypeStruct((span, D), BF),
            jax.ShapeDtypeStruct((1, D), F32),
        ],
        scratch_shapes=[
            pltpu.VMEM((span, D), F32),
            pltpu.VMEM((span, 1), F32),
            pltpu.VMEM((span, D), BF),
            pltpu.VMEM((span, D), F32),
            pltpu.VMEM((span, COLS), BF),
            pltpu.VMEM((2, side, width, BLK, BLK), BF),
            pltpu.SemaphoreType.DMA((2,)),
        ],
        compiler_params=params(),
        cost_estimate=cost(14 * span * D * D, 25 * MIB),
        name="qkv_backward",
    )(
        tokens, gains, d_query, own, received, grad_middle,
        weights.reshape(-1, 3 * side, BLK, BLK), table, kept,
    )


def two_terms(values):
    high = values.astype(BF)
    return high, (values - high.astype(F32)).astype(BF)


def update_body(g_ref, m_ref, sl_ref, sr_ref, rl_ref, rr_ref, sl_out, sr_out, m_out):
    def long_left(terms, axis):
        return jnp.concatenate([terms[0], terms[0], terms[1]], axis)

    def long_right(terms, axis):
        return jnp.concatenate([terms[0], terms[1], terms[0]], axis)

    for i in range(g_ref.shape[0]):
        grad = two_terms(g_ref[i])
        sl_out[i] = sl_ref[i] + mul_nt(long_left(grad, 1), long_right(grad, 1))
        tall = long_right(grad, 0)
        sr_out[i] = sr_ref[i] + mul_tn(long_left(grad, 0), tall)
        inner = mul_nn(long_left(two_terms(rl_ref[i]), 1), tall)
        direction = mul_nn(
            long_left(two_terms(inner), 1), long_right(two_terms(rr_ref[i]), 0)
        )
        master = m_ref[i]
        scale = jnp.sqrt(jnp.mean(master * master, keepdims=True) + 1e-06)
        scale = scale * lax.rsqrt(jnp.mean(direction * direction, keepdims=True) + 1e-06)
        m_out[i] = master - 0.3 * scale * direction


def update(grads, master, stat_left, stat_right, root_left, root_right):
    count = grads.shape[0]
    group = 3 if count % 3 == 0 else 1
    block = pl.BlockSpec((group, BLK, BLK), lambda i: (i, 0, 0))
    shape = jax.ShapeDtypeStruct(grads.shape, F32)
    return pl.pallas_call(
        update_body,
        grid=(count // group,),
        in_specs=[block] * 6,
        out_specs=[block] * 3,
        out_shape=[shape] * 3,
        compiler_params=params(),
        cost_estimate=cost(48 * count * BLK**3, 15 * MIB),
        name="block_update",
    )(grads, master, stat_left, stat_right, root_left, root_right)


def pair_moves():
    moves_same, moves_cross = [], []
    for z in range(4):
        for c in range(2):
            for moves, bit in ((moves_same, z % 2), (moves_cross, 1 - z % 2)):
                moves.append((z * 2 + c, (2 * c + bit) * 2 + z // 2))
    return moves_same, moves_cross


def spread_rows(values, parity):
    moves_same, moves_cross = pair_moves()
    kept = lax.dynamic_index_in_dim(values, parity, 0, False)
    crossed = lax.dynamic_index_in_dim(values, 1 - parity, 0, False)
    kept = lax.ppermute(kept, ("seq", "core"), moves_same)
    crossed = lax.ppermute(crossed, ("seq", "core"), moves_cross)
    low_part = jnp.where(parity == 0, kept, crossed)
    high_part = jnp.where(parity == 0, crossed, kept)
    return jnp.concatenate([low_part, high_part], 0)


def gather_rows(values, parity):
    moves_same, moves_cross = pair_moves()
    parts = values.reshape(2, values.shape[0] // 2, values.shape[1])
    kept = lax.dynamic_index_in_dim(parts, parity, 0, False)
    crossed = lax.dynamic_index_in_dim(parts, 1 - parity, 0, False)
    kept = lax.ppermute(kept, ("seq", "core"), [(b, a) for a, b in moves_same])
    crossed = lax.ppermute(crossed, ("seq", "core"), [(b, a) for a, b in moves_cross])
    return jnp.stack([jnp.where(parity == 0, kept, crossed), jnp.where(parity == 0, crossed, kept)], 0)


def swap_cores(values):
    return lax.ppermute(values, "core", [(0, 1), (1, 0)])


def sum_all(values):
    axes = ("seq", "chip", "core")
    count = lax.axis_size(axes)
    bit = 1
    while bit < count:
        values = values + lax.ppermute(values, axes, [(i, i ^ bit) for i in range(count)])
        bit *= 2
    return values


def chip_orders(chips):
    bits = [1 << i for i in range(chips.bit_length() - 1)]
    return bits, bits[::-1]


def offsets(order):
    result = [0]
    for bit in order:
        result = result + [o ^ bit for o in result]
    return result


def place_lists(chips, owned, planes):
    halves = ((0, owned // 2), (owned // 2, owned))
    lists = []
    for k in range(planes):
        for order, (low, high) in zip(chip_orders(chips), halves):
            for offset in offsets(order):
                lists += [(k, offset, slot) for slot in range(low, high)]
    return np.array(lists, np.int32).T


def swap_chips(values, bit):
    chips = lax.axis_size("chip")
    return lax.ppermute(values, "chip", [(i, i ^ bit) for i in range(chips)])


def move_planes(values, shift):
    planes = lax.axis_size("seq")
    return lax.ppermute(values, "seq", [(i, (i + shift) % planes) for i in range(planes)])


def after(value, *deps):
    return lax.optimization_barrier((value, *deps))[0]


def gather_plane(values, deps):
    middle = values.shape[0] // 2
    values = after(values, *deps)
    parts = [values[:middle], values[middle:]]
    orders = chip_orders(lax.axis_size("chip"))
    first = None
    for bits in zip(*orders):
        came = [swap_chips(part, bit) for part, bit in zip(parts, bits)]
        first = first or came
        parts = [jnp.concatenate(pair, 0) for pair in zip(parts, came)]
    return jnp.concatenate(parts, 0), first


def add_halves(kept, came):
    return (kept.astype(F32) + came.astype(F32)).astype(BF)


def scatter_plane(values, owned, deps):
    chips = lax.axis_size("chip")
    middle = owned // 2 * chips
    values = after(values, *deps)
    parts = [values[:middle], values[middle:]]
    orders = chip_orders(chips)
    first = None
    for bits in zip(*(order[::-1] for order in orders)):
        counts = [part.shape[0] // 2 for part in parts]
        came = [swap_chips(part[n:], bit) for part, n, bit in zip(parts, counts, bits)]
        first = first or came
        parts = [add_halves(part[:n], new) for part, n, new in zip(parts, counts, came)]
    return jnp.concatenate(parts, 0), first


def local(
    tokens,
    cotangent,
    lengths,
    owner_perm,
    master,
    norm_gains,
    stat_left,
    stat_right,
    root_left,
    root_right,
    moment_first,
    moment_second,
):
    core = lax.axis_index("core")
    place_z = lax.axis_index("seq")
    parity = place_z % 2
    block_count = owner_perm.shape[0]
    owned = master.shape[0]
    half = block_count // 2

    chips, planes = lax.axis_size("chip"), lax.axis_size("seq")
    me = lax.axis_index("chip")

    pair_lengths = jnp.stack([lengths, swap_cores(lengths)])
    pair_lengths = jnp.where(core == 0, pair_lengths, pair_lengths[::-1]).reshape(-1)
    length = lax.dynamic_index_in_dim(pair_lengths, place_z, 0, False)
    span = tokens.shape[0] * tokens.shape[1]
    live = jnp.stack([length - core * span, length - (1 - core) * span, length - core * span])

    distance, offset, slot = place_lists(chips, owned, planes)
    device = ((place_z - distance) % planes * chips + (me ^ offset)) * 2
    near_slots = (device + core) * owned + slot
    far_slots = (device + 1 - core) * owned + slot
    table = owner_perm[jnp.concatenate([near_slots, far_slots])]
    inverse = jnp.zeros((block_count,), jnp.int32).at[table].set(
        jnp.arange(block_count, dtype=jnp.int32)
    )

    shard = master.astype(BF)
    shards = {0: shard}
    shards[1] = move_planes(shard, 1)
    shards[3] = move_planes(after(shard, shards[1]), 3)
    shards[2] = move_planes(after(shard, shards[3]), 2)
    own_tokens = spread_rows(after(tokens, shards[2]), parity)
    other_tokens = swap_cores(own_tokens)
    per_plane = chips * owned
    weights, deps = None, (table, inverse, live)
    for k in (0, 1, 3, 2):
        near, deps = gather_plane(shards[k], deps)
        weights = place_blocks(table, k * per_plane, near, swap_cores(near), weights)
    own_cot = spread_rows(after(cotangent, near), parity)

    own_qkv, other_kv = project(own_tokens, other_tokens, norm_gains, weights)
    attended, q_aug = attend(live, own_qkv, other_kv)
    layer, g_up, g_down, g_out, grad_middle, grad_attended, gain_second = feed(
        live, own_tokens, attended, own_cot, norm_gains, weights
    )
    layer_out = gather_rows(layer, parity)
    side = D // BLK
    flat = lambda g: g.reshape(-1, BLK, BLK)
    first_rest = 3 * side * side
    starts = (first_rest, first_rest + side * side, first_rest + side * side + side * FF // BLK)
    d_query, d_own, d_other, sends = attend_back(
        live, q_aug, own_qkv, other_kv, attended, grad_attended,
        inverse, starts, (flat(g_out), flat(g_up), flat(g_down)),
    )
    received = swap_cores(after(d_other, layer_out))
    sends, grad_in, gain_first = input_back(
        own_tokens, norm_gains, d_query, d_own, received, grad_middle, weights, inverse, sends
    )
    input_grad = gather_rows(grad_in, parity).astype(F32)
    grad_blocks, swap_deps, chip_deps = None, (), ()
    gain_grad = jnp.concatenate([gain_first, gain_second], 0)
    for turn, k in enumerate((2, 1, 3, 0)):
        sends = after(sends, *swap_deps)
        mine = sends[k * per_plane : (k + 1) * per_plane]
        other = swap_cores(sends[half + k * per_plane : half + (k + 1) * per_plane])
        swap_deps = (other,)
        if turn == 2:
            chip_deps = (*chip_deps, input_grad)
        part, chip_deps = scatter_plane(add_halves(mine, other), owned, chip_deps)
        if turn == 0:
            gain_grad = sum_all(after(gain_grad, *chip_deps))
        if k:
            part = move_planes(part, -k)
        part = part.astype(F32)
        grad_blocks = part if grad_blocks is None else grad_blocks + part
    stat_left_new, stat_right_new, master_new = update(
        grad_blocks, master, stat_left, stat_right, root_left, root_right
    )
    first_new = 0.9 * moment_first + 0.1 * gain_grad
    second_new = 0.999 * moment_second + 0.001 * gain_grad * gain_grad
    first_hat = first_new / (1.0 - 0.9**STEP)
    second_hat = second_new / (1.0 - 0.999**STEP)
    gains_new = norm_gains - 0.5 * first_hat / (jnp.sqrt(second_hat) + 1e-08)
    return (
        layer_out,
        input_grad,
        grad_blocks,
        stat_left_new,
        stat_right_new,
        master_new,
        first_new,
        second_new,
        gains_new,
    )


def solution(mesh):
    seq_size, rows_size = mesh.shape["seq"], mesh.shape["rows"]
    mesh = Mesh(mesh.devices.reshape(seq_size, rows_size // 2, 2), ("seq", "chip", "core"))
    activation = P(("chip", "core"), "seq", None)
    blocks = P(("seq", "chip", "core"), None, None)
    return jax.shard_map(
        local,
        mesh=mesh,
        in_specs=(
            activation, activation, P(("chip", "core")), P(), blocks, P(),
            blocks, blocks, blocks, blocks, P(), P(),
        ),
        out_specs=(activation, activation, blocks, blocks, blocks, blocks, P(), P(), P()),
        check_vma=False,
    )
```

```python
import functools
import jax
import jax.numpy as jnp
import numpy as np
from jax import lax
from jax.experimental import pallas as pl
from jax.experimental.pallas import tpu as pltpu
from jax.sharding import Mesh
from jax.sharding import PartitionSpec as P

D = 1024
HD = 64
FF = 4096
BLK = 128
STEP = 10
COLS = 512
BF = jnp.bfloat16
F32 = jnp.float32
MIB = 1024 * 1024

norm_eps = 1e-05
score_scale = 0.125
masked_score = -1e30


def params():
    return pltpu.CompilerParams(vmem_limit_bytes=56 * MIB)


def cost(flops, nbytes):
    return pl.CostEstimate(flops=int(flops), bytes_accessed=int(nbytes), transcendentals=0)


def mul_nn(left, right):
    return jnp.dot(left, right, preferred_element_type=F32)


def mul_nt(left, right):
    return lax.dot_general(left, right, (((1,), (1,)), ((), ())), preferred_element_type=F32)


def mul_tn(left, right):
    return lax.dot_general(left, right, (((0,), (0,)), ((), ())), preferred_element_type=F32)


def join_tile(ref):
    rows, cols = ref.shape[0], ref.shape[1]
    return jnp.concatenate([ref[:, j].reshape(rows * BLK, BLK) for j in range(cols)], axis=1)


def split_tile(ref, matrix):
    rows, cols = ref.shape[0], ref.shape[1]
    for j in range(cols):
        ref[:, j] = matrix[:, j * BLK : (j + 1) * BLK].reshape(rows, BLK, BLK).astype(ref.dtype)


def normalize(values):
    row_mean = jnp.mean(values, -1, keepdims=True)
    centered = values - row_mean
    row_var = jnp.mean(centered * centered, -1, keepdims=True)
    inv_std = lax.rsqrt(row_var + norm_eps)
    return centered * inv_std, inv_std


def norm_back(gradient, unit_vals, inv_std):
    grad_mean = jnp.mean(gradient, -1, keepdims=True)
    cross_mean = jnp.mean(gradient * unit_vals, -1, keepdims=True)
    return inv_std * (gradient - grad_mean - unit_vals * cross_mean)


def place_body(first, table, near_ref, far_ref, *refs):
    out_ref, sem = refs[-2:]
    count = near_ref.shape[0]
    half = table.shape[0] // 2
    start = first + pl.program_id(0) * count
    for slot in range(count):
        pltpu.make_async_copy(near_ref.at[slot], out_ref.at[table[start + slot]], sem).start()
        far_place = table[half + start + slot]
        pltpu.make_async_copy(far_ref.at[slot], out_ref.at[far_place], sem).start()
    done = out_ref.at[pl.ds(0, 2 * count)]
    pltpu.make_async_copy(done, done, sem).wait()


def place_blocks(table, first, near, far, kept):
    smem = pl.BlockSpec(memory_space=pltpu.SMEM)
    hbm = pl.BlockSpec(memory_space=pltpu.HBM)
    steps = 4
    part = pl.BlockSpec((near.shape[0] // steps, BLK, BLK), lambda i: (i, 0, 0))
    kept = () if kept is None else (kept,)
    return pl.pallas_call(
        functools.partial(place_body, first),
        grid=(steps,),
        out_shape=jax.ShapeDtypeStruct((table.shape[0], BLK, BLK), BF),
        in_specs=[smem, part, part] + [hbm] * len(kept),
        out_specs=hbm,
        scratch_shapes=[pltpu.SemaphoreType.DMA],
        input_output_aliases={3: 0} if kept else {},
        compiler_params=params(),
        cost_estimate=cost(0, 4 * near.size * 2),
        name="place_weights",
    )(table, near, far, *kept)


def qkv_body(own_ref, other_ref, gains_ref, w_ref, own_out, other_out, normed):
    step = pl.program_id(0)
    span = own_ref.shape[0]

    @pl.when(step == 0)
    def _():
        gain = gains_ref[0:1]
        normed[:span] = (normalize(own_ref[...].astype(F32))[0] * gain).astype(BF)
        normed[span:] = (normalize(other_ref[...].astype(F32))[0] * gain).astype(BF)

    weight = join_tile(w_ref)
    own_out[...] = mul_nn(normed[:span], weight).astype(BF)

    @pl.when(step >= D // COLS)
    def _():
        other_out[...] = mul_nn(normed[span:], weight).astype(BF)


def project(own, other, gains, weights):
    span = own.shape[0]
    skip = D // COLS
    whole = lambda j: (0, 0)
    return pl.pallas_call(
        qkv_body,
        grid=(3 * D // COLS,),
        in_specs=[
            pl.BlockSpec((span, D), whole),
            pl.BlockSpec((span, D), whole),
            pl.BlockSpec((2, D), whole),
            pl.BlockSpec((D // BLK, COLS // BLK, BLK, BLK), lambda j: (0, j, 0, 0)),
        ],
        out_specs=[
            pl.BlockSpec((span, COLS), lambda j: (0, j)),
            pl.BlockSpec((span, COLS), lambda j: (0, jnp.maximum(j - skip, 0))),
        ],
        out_shape=[
            jax.ShapeDtypeStruct((span, 3 * D), BF),
            jax.ShapeDtypeStruct((span, 2 * D), BF),
        ],
        scratch_shapes=[pltpu.VMEM((2 * span, D), BF)],
        compiler_params=params(),
        cost_estimate=cost(10 * span * D * D, 12 * MIB),
        name="qkv_projection",
    )(own, other, gains, weights.reshape(-1, 3 * D // BLK, BLK, BLK))


def lane_masks(head):
    lane = lax.broadcasted_iota(jnp.int32, (1, BLK), 1)
    first = HD * (1 - head)
    keep = (lane // HD == head).astype(F32)
    dead_lane = (lane == first).astype(F32)
    terms = [(lane == first + 1 + i).astype(F32) for i in range(3)]
    return keep, dead_lane, terms


def three_terms(values):
    high = values.astype(BF).astype(F32)
    rest = values - high
    middle = rest.astype(BF).astype(F32)
    return high, middle, rest - middle


def key_bias(span, live_count):
    row = lax.broadcasted_iota(jnp.int32, (span, 1), 0)
    return jnp.where(row < live_count, 0.0, masked_score).astype(F32)


def attend_body(live_ref, q_ref, ko_ref, vo_ref, kx_ref, vx_ref, out_ref, aug_ref):
    span = q_ref.shape[0]
    bias_own = key_bias(span, live_ref[0])
    bias_other = key_bias(span, live_ref[1])
    queries = q_ref[...].astype(F32) * score_scale
    k_own, k_other = ko_ref[...].astype(F32), kx_ref[...].astype(F32)
    results = []
    for head in range(2):
        keep, dead_lane, terms = lane_masks(head)
        q_head = (queries * keep + dead_lane).astype(BF)
        s_own = mul_nt(q_head, (k_own * keep + bias_own * dead_lane).astype(BF))
        s_other = mul_nt(q_head, (k_other * keep + bias_other * dead_lane).astype(BF))
        top = jnp.maximum(
            jnp.max(s_own, -1, keepdims=True), jnp.max(s_other, -1, keepdims=True)
        )
        p_own = jnp.exp(s_own - top)
        p_other = jnp.exp(s_other - top)
        total = jnp.sum(p_own, -1, keepdims=True) + jnp.sum(p_other, -1, keepdims=True)
        mixed = mul_nn(p_own.astype(BF), vo_ref[...]) + mul_nn(p_other.astype(BF), vx_ref[...])
        results.append(mixed / total * keep)
        parts = three_terms(-(top + jnp.log(total)))
        stats = sum(part * lane for part, lane in zip(parts, terms))
        aug_ref[:, head * BLK : (head + 1) * BLK] = (q_head.astype(F32) + stats).astype(BF)
    out_ref[...] = (results[0] + results[1]).astype(BF)


def attend(live, own, other):
    span = own.shape[0]
    pairs = D // BLK
    col = lambda shift: pl.BlockSpec((span, BLK), lambda p: (0, p + shift))
    return pl.pallas_call(
        attend_body,
        grid=(pairs,),
        in_specs=[
            pl.BlockSpec(memory_space=pltpu.SMEM),
            col(0),
            col(pairs),
            col(2 * pairs),
            col(0),
            col(pairs),
        ],
        out_specs=[col(0), pl.BlockSpec((span, 2 * BLK), lambda p: (0, p))],
        out_shape=[
            jax.ShapeDtypeStruct((span, D), BF),
            jax.ShapeDtypeStruct((span, 2 * D), BF),
        ],
        compiler_params=params(),
        cost_estimate=cost(40 * span * span * D, 8 * MIB),
        name="attention",
    )(live, own, own, own, other, other)


def attend_back_body(
    starts, live_ref, aug_ref, ko_ref, vo_ref, kx_ref, vx_ref, at_ref, g_ref, table, *refs
):
    sources = refs[: len(starts)]
    dq_ref, own_ref, other_ref, buffer, sem = refs[len(starts) :]
    span = at_ref.shape[0]
    step = pl.program_id(0)
    for start, src in zip(starts, sources):
        share = src.shape[0]
        for i in range(share):
            dest = table[start + step * share + i]
            pltpu.make_async_copy(src.at[i], buffer.at[dest], sem).start()
    grads = g_ref[...].astype(F32)
    product = grads * at_ref[...].astype(F32)
    keeps, g_augs, q_augs = [], [], []
    for head in range(2):
        keep, dead_lane, terms = lane_masks(head)
        delta = jnp.sum(product * keep, -1, keepdims=True)
        parts = three_terms(-delta)
        stats = sum(part * lane for part, lane in zip(parts, terms))
        g_augs.append((grads * keep + stats).astype(BF))
        q_augs.append(aug_ref[:, head * BLK : (head + 1) * BLK])
    d_query = [None, None]
    for k_ref, v_ref, out_ref, live in (
        (ko_ref, vo_ref, own_ref, live_ref[0]),
        (kx_ref, vx_ref, other_ref, live_ref[1]),
    ):
        bias = key_bias(span, live)
        keys = k_ref[...]
        keys_f, values_f = keys.astype(F32), v_ref[...].astype(F32)
        d_keys = d_values = None
        for head in range(2):
            keep, dead_lane, terms = lane_masks(head)
            ones = terms[0] + terms[1] + terms[2]
            k_aug = (keys_f * keep + (bias * dead_lane + ones)).astype(BF)
            v_aug = (values_f * keep + ones).astype(BF)
            probs = jnp.exp(mul_nt(k_aug, q_augs[head]))
            d_scores = (probs * mul_nt(v_aug, g_augs[head])).astype(BF)
            value_part = mul_nn(probs.astype(BF), g_augs[head]) * keep
            key_part = mul_nn(d_scores, q_augs[head]) * keep
            query_part = mul_tn(d_scores, keys) * (keep * score_scale)
            d_query[head] = query_part if d_query[head] is None else d_query[head] + query_part
            d_values = value_part if d_values is None else d_values + value_part
            d_keys = key_part if d_keys is None else d_keys + key_part
        out_ref[0] = d_keys.astype(out_ref.dtype)
        out_ref[1] = d_values.astype(out_ref.dtype)
    dq_ref[...] = (d_query[0] + d_query[1]).astype(BF)
    for src in sources:
        pltpu.make_async_copy(src, src, sem).wait()


def attend_back(live, aug, own, other, attended, grads, table, starts, sources):
    span = own.shape[0]
    hbm = pl.BlockSpec(memory_space=pltpu.HBM)
    pairs = D // BLK
    col = lambda shift: pl.BlockSpec((span, BLK), lambda p: (0, p + shift))
    pair_out = pl.BlockSpec((2, span, BLK), lambda p: (0, 0, p))
    return pl.pallas_call(
        functools.partial(attend_back_body, starts),
        grid=(pairs,),
        in_specs=[
            pl.BlockSpec(memory_space=pltpu.SMEM),
            pl.BlockSpec((span, 2 * BLK), lambda p: (0, p)),
            col(pairs),
            col(2 * pairs),
            col(0),
            col(pairs),
            col(0),
            col(0),
            pl.BlockSpec(memory_space=pltpu.SMEM),
        ]
        + [
            pl.BlockSpec((src.shape[0] // pairs, BLK, BLK), lambda p: (p, 0, 0))
            for src in sources
        ],
        out_specs=[col(0), pair_out, pair_out, hbm],
        out_shape=[
            jax.ShapeDtypeStruct((span, D), BF),
            jax.ShapeDtypeStruct((2, span, D), F32),
            jax.ShapeDtypeStruct((2, span, D), BF),
            jax.ShapeDtypeStruct((table.shape[0], BLK, BLK), BF),
        ],
        scratch_shapes=[pltpu.SemaphoreType.DMA],
        compiler_params=params(),
        cost_estimate=cost(60 * span * span * D, 50 * MIB),
        name="attention_backward",
    )(live, aug, own, own, other, other, attended, grads, table, *sources)


def feed_body(
    live_ref,
    tokens_ref,
    attended_ref,
    cot_ref,
    gains_ref,
    wo_ref,
    wu_ref,
    wd_ref,
    layer_ref,
    gu_ref,
    gd_ref,
    go_ref,
    gm_ref,
    ga_ref,
    gain_ref,
    unit,
    inv,
    normed,
    top,
    acc_out,
    acc_back,
):
    step = pl.program_id(0)
    span = tokens_ref.shape[0]

    @pl.when(step == 0)
    def _():
        weight = join_tile(wo_ref)
        middle = tokens_ref[...].astype(F32) + mul_nn(attended_ref[...], weight)
        unit_vals, inv_std = normalize(middle)
        unit[...] = unit_vals
        inv[...] = inv_std
        normed[...] = (unit_vals * gains_ref[1:2]).astype(BF)
        row = lax.broadcasted_iota(jnp.int32, (span, 1), 0)
        top[...] = jnp.where(row < live_ref[2], cot_ref[...].astype(F32), 0.0).astype(BF)
        acc_out[...] = middle
        acc_back[...] = jnp.zeros_like(acc_back)

    w_up = join_tile(wu_ref)
    w_down = join_tile(wd_ref)
    hidden = mul_nn(normed[...], w_up)
    grad_act = mul_nt(top[...], w_down)
    erf_part = 0.5 * (1.0 + lax.erf(hidden * 0.7071067811865476))
    activated = (hidden * erf_part).astype(BF)
    slope = erf_part + hidden * jnp.exp(-0.5 * hidden * hidden) * 0.3989422804014327
    grad_hidden = (grad_act * slope).astype(BF)
    acc_out[...] += mul_nn(activated, w_down)
    acc_back[...] += mul_nt(grad_hidden, w_up)
    split_tile(gd_ref, mul_tn(activated, top[...]))
    split_tile(gu_ref, mul_tn(normed[...], grad_hidden))

    @pl.when(step == pl.num_programs(0) - 1)
    def _():
        layer_ref[...] = acc_out[...].astype(BF)
        unit_vals = unit[...]
        back = acc_back[...]
        gain_ref[...] = jnp.sum(back * unit_vals, 0, keepdims=True)
        grad_middle = top[...].astype(F32) + norm_back(back * gains_ref[1:2], unit_vals, inv[...])
        gm_ref[...] = grad_middle
        back_middle = grad_middle.astype(BF)
        split_tile(go_ref, mul_tn(attended_ref[...], back_middle))
        ga_ref[...] = mul_nt(back_middle, join_tile(wo_ref)).astype(BF)


def feed(live, tokens, attended, cotangent, gains, weights):
    span = tokens.shape[0]
    side, width = D // BLK, COLS // BLK
    whole = lambda j: (0, 0)
    act = pl.BlockSpec((span, D), whole)
    per_row = weights.reshape(-1, side, BLK, BLK)
    per_up = weights.reshape(-1, FF // BLK, BLK, BLK)
    out_row = (3 * side * side) // side // side
    up_row = 4 * side * side // (FF // BLK) // side
    down_row = (4 * side * side + side * FF // BLK) // side // width
    return pl.pallas_call(
        feed_body,
        grid=(FF // COLS,),
        in_specs=[
            pl.BlockSpec(memory_space=pltpu.SMEM),
            act,
            act,
            act,
            pl.BlockSpec((2, D), whole),
            pl.BlockSpec((side, side, BLK, BLK), lambda j: (out_row, 0, 0, 0)),
            pl.BlockSpec((side, width, BLK, BLK), lambda j: (up_row, j, 0, 0)),
            pl.BlockSpec((width, side, BLK, BLK), lambda j: (down_row + j, 0, 0, 0)),
        ],
        out_specs=[
            act,
            pl.BlockSpec((side, width, BLK, BLK), lambda j: (0, j, 0, 0)),
            pl.BlockSpec((width, side, BLK, BLK), lambda j: (j, 0, 0, 0)),
            pl.BlockSpec((side, side, BLK, BLK), lambda j: (0, 0, 0, 0)),
            act,
            act,
            pl.BlockSpec((1, D), whole),
        ],
        out_shape=[
            jax.ShapeDtypeStruct((span, D), BF),
            jax.ShapeDtypeStruct((side, FF // BLK, BLK, BLK), BF),
            jax.ShapeDtypeStruct((FF // BLK, side, BLK, BLK), BF),
            jax.ShapeDtypeStruct((side, side, BLK, BLK), BF),
            jax.ShapeDtypeStruct((span, D), F32),
            jax.ShapeDtypeStruct((span, D), BF),
            jax.ShapeDtypeStruct((1, D), F32),
        ],
        scratch_shapes=[
            pltpu.VMEM((span, D), F32),
            pltpu.VMEM((span, 1), F32),
            pltpu.VMEM((span, D), BF),
            pltpu.VMEM((span, D), BF),
            pltpu.VMEM((span, D), F32),
            pltpu.VMEM((span, D), F32),
        ],
        compiler_params=params(),
        cost_estimate=cost(14 * span * D * FF, 50 * MIB),
        name="feed_forward",
    )(live, tokens, attended, cotangent, gains, per_row, per_up, per_row)


def input_body(
    tokens_ref, gains_ref, dq_ref, own_ref, recv_ref, gm_ref, w_ref, table, kept_ref,
    buffer, out_ref, gain_ref, unit, inv, normed, acc, tile, stage, sems
):
    step = pl.program_id(0)
    last = pl.num_programs(0) - 1
    place = step % 2

    def drain(which):
        pltpu.make_async_copy(stage.at[which], stage.at[which], sems.at[which]).wait()

    @pl.when(step == 0)
    def _():
        unit_vals, inv_std = normalize(tokens_ref[...].astype(F32))
        unit[...] = unit_vals
        inv[...] = inv_std
        normed[...] = (unit_vals * gains_ref[0:1]).astype(BF)
        acc[...] = jnp.zeros_like(acc)

    @pl.when(step < D // COLS)
    def _():
        tile[...] = dq_ref[...]

    @pl.when(step >= D // COLS)
    def _():
        tile[...] = (own_ref[0] + recv_ref[0].astype(F32)).astype(BF)

    grad = tile[...]
    acc[...] += mul_nt(grad, join_tile(w_ref))

    @pl.when(step >= 2)
    def _():
        drain(place)

    split_tile(stage.at[place], mul_tn(normed[...], grad))
    rows, cols = stage.shape[1], stage.shape[2]
    for i in range(rows):
        for j in range(cols):
            dest = table[i * (3 * D // BLK) + step * cols + j]
            pltpu.make_async_copy(stage.at[place, i, j], buffer.at[dest], sems.at[place]).start()

    @pl.when(step == last)
    def _():
        drain(1 - place)
        drain(place)
        unit_vals = unit[...]
        back = acc[...]
        gain_ref[...] = jnp.sum(back * unit_vals, 0, keepdims=True)
        out_ref[...] = (
            gm_ref[...] + norm_back(back * gains_ref[0:1], unit_vals, inv[...])
        ).astype(BF)


def input_back(tokens, gains, d_query, own, received, grad_middle, weights, table, kept):
    span = tokens.shape[0]
    hbm = pl.BlockSpec(memory_space=pltpu.HBM)
    side, width = D // BLK, COLS // BLK
    per = D // COLS
    whole = lambda j: (0, 0)
    act = pl.BlockSpec((span, D), whole)
    later = lambda j: (jnp.maximum(j - per, 0) // per, 0, jnp.maximum(j - per, 0) % per)
    tile = pl.BlockSpec((side, width, BLK, BLK), lambda j: (0, j, 0, 0))
    return pl.pallas_call(
        input_body,
        grid=(3 * per,),
        in_specs=[
            act,
            pl.BlockSpec((2, D), whole),
            pl.BlockSpec((span, COLS), lambda j: (0, jnp.minimum(j, per - 1))),
            pl.BlockSpec((1, span, COLS), later),
            pl.BlockSpec((1, span, COLS), later),
            act,
            tile,
            pl.BlockSpec(memory_space=pltpu.SMEM),
            hbm,
        ],
        out_specs=[hbm, act, pl.BlockSpec((1, D), whole)],
        input_output_aliases={8: 0},
        out_shape=[
            jax.ShapeDtypeStruct(kept.shape, BF),
            jax.ShapeDtypeStruct((span, D), BF),
            jax.ShapeDtypeStruct((1, D), F32),
        ],
        scratch_shapes=[
            pltpu.VMEM((span, D), F32),
            pltpu.VMEM((span, 1), F32),
            pltpu.VMEM((span, D), BF),
            pltpu.VMEM((span, D), F32),
            pltpu.VMEM((span, COLS), BF),
            pltpu.VMEM((2, side, width, BLK, BLK), BF),
            pltpu.SemaphoreType.DMA((2,)),
        ],
        compiler_params=params(),
        cost_estimate=cost(14 * span * D * D, 25 * MIB),
        name="qkv_backward",
    )(
        tokens, gains, d_query, own, received, grad_middle,
        weights.reshape(-1, 3 * side, BLK, BLK), table, kept,
    )


def two_terms(values):
    high = values.astype(BF)
    return high, (values - high.astype(F32)).astype(BF)


def update_body(g_ref, m_ref, sl_ref, sr_ref, rl_ref, rr_ref, sl_out, sr_out, m_out):
    def long_left(terms, axis):
        return jnp.concatenate([terms[0], terms[0], terms[1]], axis)

    def long_right(terms, axis):
        return jnp.concatenate([terms[0], terms[1], terms[0]], axis)

    for i in range(g_ref.shape[0]):
        grad = two_terms(g_ref[i])
        sl_out[i] = sl_ref[i] + mul_nt(long_left(grad, 1), long_right(grad, 1))
        tall = long_right(grad, 0)
        sr_out[i] = sr_ref[i] + mul_tn(long_left(grad, 0), tall)
        inner = mul_nn(long_left(two_terms(rl_ref[i]), 1), tall)
        direction = mul_nn(
            long_left(two_terms(inner), 1), long_right(two_terms(rr_ref[i]), 0)
        )
        master = m_ref[i]
        scale = jnp.sqrt(jnp.mean(master * master, keepdims=True) + 1e-06)
        scale = scale * lax.rsqrt(jnp.mean(direction * direction, keepdims=True) + 1e-06)
        m_out[i] = master - 0.3 * scale * direction


def update(grads, master, stat_left, stat_right, root_left, root_right):
    count = grads.shape[0]
    group = 3 if count % 3 == 0 else 1
    block = pl.BlockSpec((group, BLK, BLK), lambda i: (i, 0, 0))
    shape = jax.ShapeDtypeStruct(grads.shape, F32)
    return pl.pallas_call(
        update_body,
        grid=(count // group,),
        in_specs=[block] * 6,
        out_specs=[block] * 3,
        out_shape=[shape] * 3,
        compiler_params=params(),
        cost_estimate=cost(48 * count * BLK**3, 15 * MIB),
        name="block_update",
    )(grads, master, stat_left, stat_right, root_left, root_right)


def pair_moves():
    moves_same, moves_cross = [], []
    for z in range(4):
        for c in range(2):
            for moves, bit in ((moves_same, z % 2), (moves_cross, 1 - z % 2)):
                moves.append((z * 2 + c, (2 * c + bit) * 2 + z // 2))
    return moves_same, moves_cross


def spread_rows(values, parity):
    moves_same, moves_cross = pair_moves()
    kept = lax.dynamic_index_in_dim(values, parity, 0, False)
    crossed = lax.dynamic_index_in_dim(values, 1 - parity, 0, False)
    kept = lax.ppermute(kept, ("seq", "core"), moves_same)
    crossed = lax.ppermute(crossed, ("seq", "core"), moves_cross)
    low_part = jnp.where(parity == 0, kept, crossed)
    high_part = jnp.where(parity == 0, crossed, kept)
    return jnp.concatenate([low_part, high_part], 0)


def gather_rows(values, parity):
    moves_same, moves_cross = pair_moves()
    parts = values.reshape(2, values.shape[0] // 2, values.shape[1])
    kept = lax.dynamic_index_in_dim(parts, parity, 0, False)
    crossed = lax.dynamic_index_in_dim(parts, 1 - parity, 0, False)
    kept = lax.ppermute(kept, ("seq", "core"), [(b, a) for a, b in moves_same])
    crossed = lax.ppermute(crossed, ("seq", "core"), [(b, a) for a, b in moves_cross])
    return jnp.stack([jnp.where(parity == 0, kept, crossed), jnp.where(parity == 0, crossed, kept)], 0)


def swap_cores(values):
    return lax.ppermute(values, "core", [(0, 1), (1, 0)])


def chip_orders(chips):
    bits = [1 << i for i in range(chips.bit_length() - 1)]
    return bits, bits[::-1]


def offsets(order):
    result = [0]
    for bit in order:
        result = result + [o ^ bit for o in result]
    return result


def place_lists(chips, owned, planes):
    shape = (2, planes, chips, owned)
    by_core = np.array([offsets(order) for order in chip_orders(chips)], np.int32)
    grid = np.indices(shape).astype(np.int32).reshape(4, 2, -1)
    offset = np.broadcast_to(by_core[:, None, :, None], shape).reshape(2, -1)
    return grid[1, 0], offset, grid[3, 0]


def swap_chips(values, bits):
    chips = lax.axis_size("chip")
    moves = [(i * 2 + c, (i ^ bits[c]) * 2 + c) for i in range(chips) for c in range(2)]
    return lax.ppermute(values, ("chip", "core"), moves)


def move_planes(values, shift):
    planes = lax.axis_size("seq")
    return lax.ppermute(values, "seq", [(i, (i + shift) % planes) for i in range(planes)])


def after(value, *deps):
    return lax.optimization_barrier((value, *deps))[0]


def gather_plane(part, deps, later_deps):
    part = after(part, *deps)
    first = None
    for bits in zip(*chip_orders(lax.axis_size("chip"))):
        came = swap_chips(part, bits)
        part = jnp.concatenate([part, came], 0)
        if first is None:
            first = came
            part = after(part, *later_deps)
    return part, (first,)


def add_halves(kept, came):
    return (kept.astype(F32) + came.astype(F32)).astype(BF)


def scatter_plane(part, deps):
    part = after(part, *deps)
    first = None
    for bits in zip(*(order[::-1] for order in chip_orders(lax.axis_size("chip")))):
        count = part.shape[0] // 2
        came = swap_chips(part[count:], bits)
        first = came if first is None else first
        part = add_halves(part[:count], came)
    return part, (first,)


def local(
    tokens,
    cotangent,
    lengths,
    owner_perm,
    master,
    norm_gains,
    stat_left,
    stat_right,
    root_left,
    root_right,
    moment_first,
    moment_second,
):
    core = lax.axis_index("core")
    place_z = lax.axis_index("seq")
    parity = place_z % 2
    block_count = owner_perm.shape[0]
    owned = master.shape[0]
    half = block_count // 2

    chips, planes = lax.axis_size("chip"), lax.axis_size("seq")
    me = lax.axis_index("chip")

    pair_lengths = jnp.stack([lengths, swap_cores(lengths)])
    pair_lengths = jnp.where(core == 0, pair_lengths, pair_lengths[::-1]).reshape(-1)
    length = lax.dynamic_index_in_dim(pair_lengths, place_z, 0, False)
    span = tokens.shape[0] * tokens.shape[1]
    live = jnp.stack([length - core * span, length - (1 - core) * span, length - core * span])

    distance, offset, slot = place_lists(chips, owned, planes)
    offset = jnp.where(core == 0, offset, offset[::-1])
    device = ((place_z - distance) % planes * chips + (me ^ offset)) * 2
    device = device + jnp.stack([core, 1 - core])[:, None]
    table = owner_perm[(device * owned + slot).reshape(-1)]
    inverse = jnp.zeros((block_count,), jnp.int32).at[table].set(
        jnp.arange(block_count, dtype=jnp.int32)
    )

    shard = master.astype(BF)
    shards = [shard]
    for k in range(1, planes):
        shards.append(move_planes(shards[-1], 1))
    own_tokens = spread_rows(after(tokens, shards[-1]), parity)
    other_tokens = swap_cores(own_tokens)
    per_plane = chips * owned
    weights, deps, later = None, (), (shards[1],)
    placed = [(), (live, table, inverse), ()]
    for k in range(planes):
        near, deps = gather_plane(shards[k], (*deps, *placed[k]), later)
        later = ()
        if k == planes - 1:
            near = after(near, weights, own_tokens, other_tokens)
        weights = place_blocks(table, k * per_plane, near, swap_cores(near), weights)
        placed.append((weights,) if k == 0 else ())
    own_cot = spread_rows(after(cotangent, weights), parity)

    own_qkv, other_kv = project(own_tokens, other_tokens, norm_gains, weights)
    attended, q_aug = attend(live, own_qkv, other_kv)
    layer, g_up, g_down, g_out, grad_middle, grad_attended, gain_second = feed(
        live, own_tokens, attended, own_cot, norm_gains, weights
    )
    layer_out = gather_rows(layer, parity)
    side = D // BLK
    flat = lambda g: g.reshape(-1, BLK, BLK)
    first_rest = 3 * side * side
    starts = (first_rest, first_rest + side * side, first_rest + side * side + side * FF // BLK)
    d_query, d_own, d_other, sends = attend_back(
        live, q_aug, own_qkv, other_kv, attended, grad_attended,
        inverse, starts, (flat(g_out), flat(g_up), flat(g_down)),
    )
    received = swap_cores(after(d_other, layer_out))
    sends, grad_in, gain_first = input_back(
        own_tokens, norm_gains, d_query, d_own, received, grad_middle, weights, inverse, sends
    )
    input_grad = gather_rows(grad_in, parity).astype(F32)
    gain_grad = jnp.concatenate([gain_first, gain_second], 0)
    gain_grad = jnp.sum(lax.all_gather(gain_grad, ("seq", "chip", "core")), 0)
    passed, deps, swapped = None, (), ()
    for k in reversed(range(planes)):
        sends = after(sends, *swapped)
        mine = sends[k * per_plane : (k + 1) * per_plane]
        other = swap_cores(sends[half + k * per_plane : half + (k + 1) * per_plane])
        chip_sum = add_halves(mine, other)
        swapped = (chip_sum,)
        if k == planes - 3:
            deps = (*deps, input_grad)
        if k == 0:
            deps = (*deps, gain_grad)
        part, deps = scatter_plane(chip_sum, deps)
        if k == 0:
            grad_blocks = part.astype(F32) + passed.astype(F32)
        else:
            part = part if passed is None else add_halves(part, passed)
            passed = move_planes(part, -1)
    stat_left_new, stat_right_new, master_new = update(
        grad_blocks, master, stat_left, stat_right, root_left, root_right
    )
    first_new = 0.9 * moment_first + 0.1 * gain_grad
    second_new = 0.999 * moment_second + 0.001 * gain_grad * gain_grad
    first_hat = first_new / (1.0 - 0.9**STEP)
    second_hat = second_new / (1.0 - 0.999**STEP)
    gains_new = norm_gains - 0.5 * first_hat / (jnp.sqrt(second_hat) + 1e-08)
    return (
        layer_out,
        input_grad,
        grad_blocks,
        stat_left_new,
        stat_right_new,
        master_new,
        first_new,
        second_new,
        gains_new,
    )


def solution(mesh):
    seq_size, rows_size = mesh.shape["seq"], mesh.shape["rows"]
    mesh = Mesh(mesh.devices.reshape(seq_size, rows_size // 2, 2), ("seq", "chip", "core"))
    activation = P(("chip", "core"), "seq", None)
    blocks = P(("seq", "chip", "core"), None, None)
    return jax.shard_map(
        local,
        mesh=mesh,
        in_specs=(
            activation, activation, P(("chip", "core")), P(), blocks, P(),
            blocks, blocks, blocks, blocks, P(), P(),
        ),
        out_specs=(activation, activation, blocks, blocks, blocks, blocks, P(), P(), P()),
        check_vma=False,
    )
```

```python
import functools
import jax
import jax.numpy as jnp
import numpy as np
from jax import lax
from jax.experimental import pallas as pl
from jax.experimental.pallas import tpu as pltpu
from jax.sharding import Mesh
from jax.sharding import PartitionSpec as P

D = 1024
HD = 64
FF = 4096
BLK = 128
STEP = 10
COLS = 512
BF = jnp.bfloat16
F32 = jnp.float32
MIB = 1024 * 1024

norm_eps = 1e-05
score_scale = 0.125
masked_score = -1e30


def params():
    return pltpu.CompilerParams(vmem_limit_bytes=56 * MIB)


def cost(flops, nbytes):
    return pl.CostEstimate(flops=int(flops), bytes_accessed=int(nbytes), transcendentals=0)


def mul_nn(left, right):
    return jnp.dot(left, right, preferred_element_type=F32)


def mul_nt(left, right):
    return lax.dot_general(left, right, (((1,), (1,)), ((), ())), preferred_element_type=F32)


def mul_tn(left, right):
    return lax.dot_general(left, right, (((0,), (0,)), ((), ())), preferred_element_type=F32)


def join_tile(ref):
    rows, cols = ref.shape[0], ref.shape[1]
    return jnp.concatenate([ref[:, j].reshape(rows * BLK, BLK) for j in range(cols)], axis=1)


def split_tile(ref, matrix):
    rows, cols = ref.shape[0], ref.shape[1]
    for j in range(cols):
        ref[:, j] = matrix[:, j * BLK : (j + 1) * BLK].reshape(rows, BLK, BLK).astype(ref.dtype)


def normalize(values):
    row_mean = jnp.mean(values, -1, keepdims=True)
    centered = values - row_mean
    row_var = jnp.mean(centered * centered, -1, keepdims=True)
    inv_std = lax.rsqrt(row_var + norm_eps)
    return centered * inv_std, inv_std


def norm_back(gradient, unit_vals, inv_std):
    grad_mean = jnp.mean(gradient, -1, keepdims=True)
    cross_mean = jnp.mean(gradient * unit_vals, -1, keepdims=True)
    return inv_std * (gradient - grad_mean - unit_vals * cross_mean)


def place_body(first, table, near_ref, far_ref, *refs):
    out_ref, sem = refs[-2:]
    count = near_ref.shape[0]
    half = table.shape[0] // 2
    start = first + pl.program_id(0) * count
    for slot in range(count):
        pltpu.make_async_copy(near_ref.at[slot], out_ref.at[table[start + slot]], sem).start()
        far_place = table[half + start + slot]
        pltpu.make_async_copy(far_ref.at[slot], out_ref.at[far_place], sem).start()
    done = out_ref.at[pl.ds(0, 2 * count)]
    pltpu.make_async_copy(done, done, sem).wait()


def place_blocks(table, first, near, far, kept):
    smem = pl.BlockSpec(memory_space=pltpu.SMEM)
    hbm = pl.BlockSpec(memory_space=pltpu.HBM)
    steps = max(near.shape[0] // 24, 1)
    part = pl.BlockSpec((near.shape[0] // steps, BLK, BLK), lambda i: (i, 0, 0))
    kept = () if kept is None else (kept,)
    return pl.pallas_call(
        functools.partial(place_body, first),
        grid=(steps,),
        out_shape=jax.ShapeDtypeStruct((table.shape[0], BLK, BLK), BF),
        in_specs=[smem, part, part] + [hbm] * len(kept),
        out_specs=hbm,
        scratch_shapes=[pltpu.SemaphoreType.DMA],
        input_output_aliases={3: 0} if kept else {},
        compiler_params=params(),
        cost_estimate=cost(0, 4 * near.size * 2),
        name="place_weights",
    )(table, near, far, *kept)


def qkv_body(own_ref, other_ref, gains_ref, w_ref, own_out, other_out, normed):
    step = pl.program_id(0)
    span = own_ref.shape[0]

    @pl.when(step == 0)
    def _():
        gain = gains_ref[0:1]
        normed[:span] = (normalize(own_ref[...].astype(F32))[0] * gain).astype(BF)
        normed[span:] = (normalize(other_ref[...].astype(F32))[0] * gain).astype(BF)

    weight = join_tile(w_ref)
    own_out[...] = mul_nn(normed[:span], weight).astype(BF)

    @pl.when(step >= D // COLS)
    def _():
        other_out[...] = mul_nn(normed[span:], weight).astype(BF)


def project(own, other, gains, weights):
    span = own.shape[0]
    skip = D // COLS
    whole = lambda j: (0, 0)
    return pl.pallas_call(
        qkv_body,
        grid=(3 * D // COLS,),
        in_specs=[
            pl.BlockSpec((span, D), whole),
            pl.BlockSpec((span, D), whole),
            pl.BlockSpec((2, D), whole),
            pl.BlockSpec((D // BLK, COLS // BLK, BLK, BLK), lambda j: (0, j, 0, 0)),
        ],
        out_specs=[
            pl.BlockSpec((span, COLS), lambda j: (0, j)),
            pl.BlockSpec((span, COLS), lambda j: (0, jnp.maximum(j - skip, 0))),
        ],
        out_shape=[
            jax.ShapeDtypeStruct((span, 3 * D), BF),
            jax.ShapeDtypeStruct((span, 2 * D), BF),
        ],
        scratch_shapes=[pltpu.VMEM((2 * span, D), BF)],
        compiler_params=params(),
        cost_estimate=cost(10 * span * D * D, 12 * MIB),
        name="qkv_projection",
    )(own, other, gains, weights.reshape(-1, 3 * D // BLK, BLK, BLK))


def lane_masks(head):
    lane = lax.broadcasted_iota(jnp.int32, (1, BLK), 1)
    first = HD * (1 - head)
    keep = (lane // HD == head).astype(F32)
    dead_lane = (lane == first).astype(F32)
    terms = [(lane == first + 1 + i).astype(F32) for i in range(3)]
    return keep, dead_lane, terms


def three_terms(values):
    high = values.astype(BF).astype(F32)
    rest = values - high
    middle = rest.astype(BF).astype(F32)
    return high, middle, rest - middle


def key_bias(span, live_count):
    row = lax.broadcasted_iota(jnp.int32, (span, 1), 0)
    return jnp.where(row < live_count, 0.0, masked_score).astype(F32)


def attend_body(live_ref, q_ref, ko_ref, vo_ref, kx_ref, vx_ref, out_ref, aug_ref):
    span = q_ref.shape[0]
    bias_own = key_bias(span, live_ref[0])
    bias_other = key_bias(span, live_ref[1])
    queries = q_ref[...].astype(F32) * score_scale
    k_own, k_other = ko_ref[...].astype(F32), kx_ref[...].astype(F32)
    results = []
    for head in range(2):
        keep, dead_lane, terms = lane_masks(head)
        q_head = (queries * keep + dead_lane).astype(BF)
        s_own = mul_nt(q_head, (k_own * keep + bias_own * dead_lane).astype(BF))
        s_other = mul_nt(q_head, (k_other * keep + bias_other * dead_lane).astype(BF))
        top = jnp.maximum(
            jnp.max(s_own, -1, keepdims=True), jnp.max(s_other, -1, keepdims=True)
        )
        p_own = jnp.exp(s_own - top)
        p_other = jnp.exp(s_other - top)
        total = jnp.sum(p_own, -1, keepdims=True) + jnp.sum(p_other, -1, keepdims=True)
        mixed = mul_nn(p_own.astype(BF), vo_ref[...]) + mul_nn(p_other.astype(BF), vx_ref[...])
        results.append(mixed / total * keep)
        parts = three_terms(-(top + jnp.log(total)))
        stats = sum(part * lane for part, lane in zip(parts, terms))
        aug_ref[:, head * BLK : (head + 1) * BLK] = (q_head.astype(F32) + stats).astype(BF)
    out_ref[...] = (results[0] + results[1]).astype(BF)


def attend(live, own, other):
    span = own.shape[0]
    pairs = D // BLK
    col = lambda shift: pl.BlockSpec((span, BLK), lambda p: (0, p + shift))
    return pl.pallas_call(
        attend_body,
        grid=(pairs,),
        in_specs=[
            pl.BlockSpec(memory_space=pltpu.SMEM),
            col(0),
            col(pairs),
            col(2 * pairs),
            col(0),
            col(pairs),
        ],
        out_specs=[col(0), pl.BlockSpec((span, 2 * BLK), lambda p: (0, p))],
        out_shape=[
            jax.ShapeDtypeStruct((span, D), BF),
            jax.ShapeDtypeStruct((span, 2 * D), BF),
        ],
        compiler_params=params(),
        cost_estimate=cost(40 * span * span * D, 8 * MIB),
        name="attention",
    )(live, own, own, own, other, other)


def attend_back_body(
    starts, live_ref, aug_ref, ko_ref, vo_ref, kx_ref, vx_ref, at_ref, g_ref, table, *refs
):
    sources = refs[: len(starts)]
    dq_ref, own_ref, other_ref, buffer, sem = refs[len(starts) :]
    span = at_ref.shape[0]
    step = pl.program_id(0)
    for start, src in zip(starts, sources):
        share = src.shape[0]
        for i in range(share):
            dest = table[start + step * share + i]
            pltpu.make_async_copy(src.at[i], buffer.at[dest], sem).start()
    grads = g_ref[...].astype(F32)
    product = grads * at_ref[...].astype(F32)
    keeps, g_augs, q_augs = [], [], []
    for head in range(2):
        keep, dead_lane, terms = lane_masks(head)
        delta = jnp.sum(product * keep, -1, keepdims=True)
        parts = three_terms(-delta)
        stats = sum(part * lane for part, lane in zip(parts, terms))
        g_augs.append((grads * keep + stats).astype(BF))
        q_augs.append(aug_ref[:, head * BLK : (head + 1) * BLK])
    d_query = [None, None]
    for k_ref, v_ref, out_ref, live in (
        (ko_ref, vo_ref, own_ref, live_ref[0]),
        (kx_ref, vx_ref, other_ref, live_ref[1]),
    ):
        bias = key_bias(span, live)
        keys = k_ref[...]
        keys_f, values_f = keys.astype(F32), v_ref[...].astype(F32)
        d_keys = d_values = None
        for head in range(2):
            keep, dead_lane, terms = lane_masks(head)
            ones = terms[0] + terms[1] + terms[2]
            k_aug = (keys_f * keep + (bias * dead_lane + ones)).astype(BF)
            v_aug = (values_f * keep + ones).astype(BF)
            probs = jnp.exp(mul_nt(k_aug, q_augs[head]))
            d_scores = (probs * mul_nt(v_aug, g_augs[head])).astype(BF)
            value_part = mul_nn(probs.astype(BF), g_augs[head]) * keep
            key_part = mul_nn(d_scores, q_augs[head]) * keep
            query_part = mul_tn(d_scores, keys) * (keep * score_scale)
            d_query[head] = query_part if d_query[head] is None else d_query[head] + query_part
            d_values = value_part if d_values is None else d_values + value_part
            d_keys = key_part if d_keys is None else d_keys + key_part
        out_ref[0] = d_keys.astype(out_ref.dtype)
        out_ref[1] = d_values.astype(out_ref.dtype)
    dq_ref[...] = (d_query[0] + d_query[1]).astype(BF)
    for src in sources:
        pltpu.make_async_copy(src, src, sem).wait()


def attend_back(live, aug, own, other, attended, grads, table, starts, sources):
    span = own.shape[0]
    hbm = pl.BlockSpec(memory_space=pltpu.HBM)
    pairs = D // BLK
    col = lambda shift: pl.BlockSpec((span, BLK), lambda p: (0, p + shift))
    pair_out = pl.BlockSpec((2, span, BLK), lambda p: (0, 0, p))
    return pl.pallas_call(
        functools.partial(attend_back_body, starts),
        grid=(pairs,),
        in_specs=[
            pl.BlockSpec(memory_space=pltpu.SMEM),
            pl.BlockSpec((span, 2 * BLK), lambda p: (0, p)),
            col(pairs),
            col(2 * pairs),
            col(0),
            col(pairs),
            col(0),
            col(0),
            pl.BlockSpec(memory_space=pltpu.SMEM),
        ]
        + [
            pl.BlockSpec((src.shape[0] // pairs, BLK, BLK), lambda p: (p, 0, 0))
            for src in sources
        ],
        out_specs=[col(0), pair_out, pair_out, hbm],
        out_shape=[
            jax.ShapeDtypeStruct((span, D), BF),
            jax.ShapeDtypeStruct((2, span, D), F32),
            jax.ShapeDtypeStruct((2, span, D), BF),
            jax.ShapeDtypeStruct((table.shape[0], BLK, BLK), BF),
        ],
        scratch_shapes=[pltpu.SemaphoreType.DMA],
        compiler_params=params(),
        cost_estimate=cost(60 * span * span * D, 50 * MIB),
        name="attention_backward",
    )(live, aug, own, own, other, other, attended, grads, table, *sources)


def feed_body(
    live_ref,
    tokens_ref,
    attended_ref,
    cot_ref,
    gains_ref,
    wo_ref,
    wu_ref,
    wd_ref,
    layer_ref,
    gu_ref,
    gd_ref,
    go_ref,
    gm_ref,
    ga_ref,
    gain_ref,
    unit,
    inv,
    normed,
    top,
    acc_out,
    acc_back,
):
    step = pl.program_id(0)
    span = tokens_ref.shape[0]

    @pl.when(step == 0)
    def _():
        weight = join_tile(wo_ref)
        middle = tokens_ref[...].astype(F32) + mul_nn(attended_ref[...], weight)
        unit_vals, inv_std = normalize(middle)
        unit[...] = unit_vals
        inv[...] = inv_std
        normed[...] = (unit_vals * gains_ref[1:2]).astype(BF)
        row = lax.broadcasted_iota(jnp.int32, (span, 1), 0)
        top[...] = jnp.where(row < live_ref[2], cot_ref[...].astype(F32), 0.0).astype(BF)
        acc_out[...] = middle
        acc_back[...] = jnp.zeros_like(acc_back)

    w_up = join_tile(wu_ref)
    w_down = join_tile(wd_ref)
    hidden = mul_nn(normed[...], w_up)
    grad_act = mul_nt(top[...], w_down)
    erf_part = 0.5 * (1.0 + lax.erf(hidden * 0.7071067811865476))
    activated = (hidden * erf_part).astype(BF)
    slope = erf_part + hidden * jnp.exp(-0.5 * hidden * hidden) * 0.3989422804014327
    grad_hidden = (grad_act * slope).astype(BF)
    acc_out[...] += mul_nn(activated, w_down)
    acc_back[...] += mul_nt(grad_hidden, w_up)
    split_tile(gd_ref, mul_tn(activated, top[...]))
    split_tile(gu_ref, mul_tn(normed[...], grad_hidden))

    @pl.when(step == pl.num_programs(0) - 1)
    def _():
        layer_ref[...] = acc_out[...].astype(BF)
        unit_vals = unit[...]
        back = acc_back[...]
        gain_ref[...] = jnp.sum(back * unit_vals, 0, keepdims=True)
        grad_middle = top[...].astype(F32) + norm_back(back * gains_ref[1:2], unit_vals, inv[...])
        gm_ref[...] = grad_middle
        back_middle = grad_middle.astype(BF)
        split_tile(go_ref, mul_tn(attended_ref[...], back_middle))
        ga_ref[...] = mul_nt(back_middle, join_tile(wo_ref)).astype(BF)


def feed(live, tokens, attended, cotangent, gains, weights):
    span = tokens.shape[0]
    side, width = D // BLK, COLS // BLK
    whole = lambda j: (0, 0)
    act = pl.BlockSpec((span, D), whole)
    per_row = weights.reshape(-1, side, BLK, BLK)
    per_up = weights.reshape(-1, FF // BLK, BLK, BLK)
    out_row = (3 * side * side) // side // side
    up_row = 4 * side * side // (FF // BLK) // side
    down_row = (4 * side * side + side * FF // BLK) // side // width
    return pl.pallas_call(
        feed_body,
        grid=(FF // COLS,),
        in_specs=[
            pl.BlockSpec(memory_space=pltpu.SMEM),
            act,
            act,
            act,
            pl.BlockSpec((2, D), whole),
            pl.BlockSpec((side, side, BLK, BLK), lambda j: (out_row, 0, 0, 0)),
            pl.BlockSpec((side, width, BLK, BLK), lambda j: (up_row, j, 0, 0)),
            pl.BlockSpec((width, side, BLK, BLK), lambda j: (down_row + j, 0, 0, 0)),
        ],
        out_specs=[
            act,
            pl.BlockSpec((side, width, BLK, BLK), lambda j: (0, j, 0, 0)),
            pl.BlockSpec((width, side, BLK, BLK), lambda j: (j, 0, 0, 0)),
            pl.BlockSpec((side, side, BLK, BLK), lambda j: (0, 0, 0, 0)),
            act,
            act,
            pl.BlockSpec((1, D), whole),
        ],
        out_shape=[
            jax.ShapeDtypeStruct((span, D), BF),
            jax.ShapeDtypeStruct((side, FF // BLK, BLK, BLK), BF),
            jax.ShapeDtypeStruct((FF // BLK, side, BLK, BLK), BF),
            jax.ShapeDtypeStruct((side, side, BLK, BLK), BF),
            jax.ShapeDtypeStruct((span, D), F32),
            jax.ShapeDtypeStruct((span, D), BF),
            jax.ShapeDtypeStruct((1, D), F32),
        ],
        scratch_shapes=[
            pltpu.VMEM((span, D), F32),
            pltpu.VMEM((span, 1), F32),
            pltpu.VMEM((span, D), BF),
            pltpu.VMEM((span, D), BF),
            pltpu.VMEM((span, D), F32),
            pltpu.VMEM((span, D), F32),
        ],
        compiler_params=params(),
        cost_estimate=cost(14 * span * D * FF, 50 * MIB),
        name="feed_forward",
    )(live, tokens, attended, cotangent, gains, per_row, per_up, per_row)


def input_body(
    tokens_ref, gains_ref, dq_ref, own_ref, recv_ref, gm_ref, w_ref, table, kept_ref,
    buffer, out_ref, gain_ref, unit, inv, normed, acc, tile, stage, sems
):
    step = pl.program_id(0)
    last = pl.num_programs(0) - 1
    place = step % 2

    def drain(which):
        pltpu.make_async_copy(stage.at[which], stage.at[which], sems.at[which]).wait()

    @pl.when(step == 0)
    def _():
        unit_vals, inv_std = normalize(tokens_ref[...].astype(F32))
        unit[...] = unit_vals
        inv[...] = inv_std
        normed[...] = (unit_vals * gains_ref[0:1]).astype(BF)
        acc[...] = jnp.zeros_like(acc)

    @pl.when(step < D // COLS)
    def _():
        tile[...] = dq_ref[...]

    @pl.when(step >= D // COLS)
    def _():
        tile[...] = (own_ref[0] + recv_ref[0].astype(F32)).astype(BF)

    grad = tile[...]
    acc[...] += mul_nt(grad, join_tile(w_ref))

    @pl.when(step >= 2)
    def _():
        drain(place)

    split_tile(stage.at[place], mul_tn(normed[...], grad))
    rows, cols = stage.shape[1], stage.shape[2]
    for i in range(rows):
        for j in range(cols):
            dest = table[i * (3 * D // BLK) + step * cols + j]
            pltpu.make_async_copy(stage.at[place, i, j], buffer.at[dest], sems.at[place]).start()

    @pl.when(step == last)
    def _():
        drain(1 - place)
        drain(place)
        unit_vals = unit[...]
        back = acc[...]
        gain_ref[...] = jnp.sum(back * unit_vals, 0, keepdims=True)
        out_ref[...] = (
            gm_ref[...] + norm_back(back * gains_ref[0:1], unit_vals, inv[...])
        ).astype(BF)


def input_back(tokens, gains, d_query, own, received, grad_middle, weights, table, kept):
    span = tokens.shape[0]
    hbm = pl.BlockSpec(memory_space=pltpu.HBM)
    side, width = D // BLK, COLS // BLK
    per = D // COLS
    whole = lambda j: (0, 0)
    act = pl.BlockSpec((span, D), whole)
    later = lambda j: (jnp.maximum(j - per, 0) // per, 0, jnp.maximum(j - per, 0) % per)
    tile = pl.BlockSpec((side, width, BLK, BLK), lambda j: (0, j, 0, 0))
    return pl.pallas_call(
        input_body,
        grid=(3 * per,),
        in_specs=[
            act,
            pl.BlockSpec((2, D), whole),
            pl.BlockSpec((span, COLS), lambda j: (0, jnp.minimum(j, per - 1))),
            pl.BlockSpec((1, span, COLS), later),
            pl.BlockSpec((1, span, COLS), later),
            act,
            tile,
            pl.BlockSpec(memory_space=pltpu.SMEM),
            hbm,
        ],
        out_specs=[hbm, act, pl.BlockSpec((1, D), whole)],
        input_output_aliases={8: 0},
        out_shape=[
            jax.ShapeDtypeStruct(kept.shape, BF),
            jax.ShapeDtypeStruct((span, D), BF),
            jax.ShapeDtypeStruct((1, D), F32),
        ],
        scratch_shapes=[
            pltpu.VMEM((span, D), F32),
            pltpu.VMEM((span, 1), F32),
            pltpu.VMEM((span, D), BF),
            pltpu.VMEM((span, D), F32),
            pltpu.VMEM((span, COLS), BF),
            pltpu.VMEM((2, side, width, BLK, BLK), BF),
            pltpu.SemaphoreType.DMA((2,)),
        ],
        compiler_params=params(),
        cost_estimate=cost(14 * span * D * D, 25 * MIB),
        name="qkv_backward",
    )(
        tokens, gains, d_query, own, received, grad_middle,
        weights.reshape(-1, 3 * side, BLK, BLK), table, kept,
    )


def two_terms(values):
    high = values.astype(BF)
    return high, (values - high.astype(F32)).astype(BF)


def update_body(g_ref, m_ref, sl_ref, sr_ref, rl_ref, rr_ref, sl_out, sr_out, m_out):
    def long_left(terms, axis):
        return jnp.concatenate([terms[0], terms[0], terms[1]], axis)

    def long_right(terms, axis):
        return jnp.concatenate([terms[0], terms[1], terms[0]], axis)

    for i in range(g_ref.shape[0]):
        grad = two_terms(g_ref[i])
        sl_out[i] = sl_ref[i] + mul_nt(long_left(grad, 1), long_right(grad, 1))
        tall = long_right(grad, 0)
        sr_out[i] = sr_ref[i] + mul_tn(long_left(grad, 0), tall)
        inner = mul_nn(long_left(two_terms(rl_ref[i]), 1), tall)
        direction = mul_nn(
            long_left(two_terms(inner), 1), long_right(two_terms(rr_ref[i]), 0)
        )
        master = m_ref[i]
        scale = jnp.sqrt(jnp.mean(master * master, keepdims=True) + 1e-06)
        scale = scale * lax.rsqrt(jnp.mean(direction * direction, keepdims=True) + 1e-06)
        m_out[i] = master - 0.3 * scale * direction


def update(grads, master, stat_left, stat_right, root_left, root_right):
    count = grads.shape[0]
    group = 3 if count % 3 == 0 else 1
    block = pl.BlockSpec((group, BLK, BLK), lambda i: (i, 0, 0))
    shape = jax.ShapeDtypeStruct(grads.shape, F32)
    return pl.pallas_call(
        update_body,
        grid=(count // group,),
        in_specs=[block] * 6,
        out_specs=[block] * 3,
        out_shape=[shape] * 3,
        compiler_params=params(),
        cost_estimate=cost(48 * count * BLK**3, 15 * MIB),
        name="block_update",
    )(grads, master, stat_left, stat_right, root_left, root_right)


def pair_moves():
    moves_same, moves_cross = [], []
    for z in range(4):
        for c in range(2):
            for moves, bit in ((moves_same, z % 2), (moves_cross, 1 - z % 2)):
                moves.append((z * 2 + c, (2 * c + bit) * 2 + z // 2))
    return moves_same, moves_cross


def spread_rows(values, parity):
    moves_same, moves_cross = pair_moves()
    kept = lax.dynamic_index_in_dim(values, parity, 0, False)
    crossed = lax.dynamic_index_in_dim(values, 1 - parity, 0, False)
    kept = lax.ppermute(kept, ("seq", "core"), moves_same)
    crossed = lax.ppermute(crossed, ("seq", "core"), moves_cross)
    low_part = jnp.where(parity == 0, kept, crossed)
    high_part = jnp.where(parity == 0, crossed, kept)
    return jnp.concatenate([low_part, high_part], 0)


def gather_rows(values, parity):
    moves_same, moves_cross = pair_moves()
    parts = values.reshape(2, values.shape[0] // 2, values.shape[1])
    kept = lax.dynamic_index_in_dim(parts, parity, 0, False)
    crossed = lax.dynamic_index_in_dim(parts, 1 - parity, 0, False)
    kept = lax.ppermute(kept, ("seq", "core"), [(b, a) for a, b in moves_same])
    crossed = lax.ppermute(crossed, ("seq", "core"), [(b, a) for a, b in moves_cross])
    return jnp.stack([jnp.where(parity == 0, kept, crossed), jnp.where(parity == 0, crossed, kept)], 0)


def swap_cores(values):
    return lax.ppermute(values, "core", [(0, 1), (1, 0)])


def chip_orders(chips):
    bits = [1 << i for i in range(chips.bit_length() - 1)]
    return bits, bits[::-1]


def offsets(order):
    result = [0]
    for bit in order:
        result = result + [o ^ bit for o in result]
    return result


def place_lists(chips, owned, planes):
    shape = (2, planes, chips, owned)
    by_core = np.array([offsets(order) for order in chip_orders(chips)], np.int32)
    grid = np.indices(shape).astype(np.int32).reshape(4, 2, -1)
    offset = np.broadcast_to(by_core[:, None, :, None], shape).reshape(2, -1)
    return grid[1, 0], offset, grid[3, 0]


def swap_chips(values, bits):
    chips = lax.axis_size("chip")
    moves = [(i * 2 + c, (i ^ bits[c]) * 2 + c) for i in range(chips) for c in range(2)]
    return lax.ppermute(values, ("chip", "core"), moves)


def move_planes(values, shift):
    planes = lax.axis_size("seq")
    return lax.ppermute(values, "seq", [(i, (i + shift) % planes) for i in range(planes)])


def after(value, *deps):
    return lax.optimization_barrier((value, *deps))[0]


def gather_plane(own, deps, later):
    steps = list(zip(*chip_orders(lax.axis_size("chip"))))
    own = after(own, *deps)
    came = swap_chips(own, steps[0])
    crossed = swap_chips(own, steps[1])
    pieces = [own, came, crossed, swap_chips(after(came, *later), steps[1])]
    for bits in steps[2:]:
        joined = jnp.concatenate(pieces, 0)
        pieces = [joined, swap_chips(joined, bits)]
    return pieces, (came, crossed)


def add_halves(kept, came):
    return (kept.astype(F32) + came.astype(F32)).astype(BF)


def pack_terms(values):
    high = lax.optimization_barrier(values.astype(BF))
    low = (values - high.astype(F32)).astype(BF)
    terms = jnp.stack([high, low]).reshape(-1, BLK)
    return jnp.pad(terms, ((0, BLK - terms.shape[0]), (0, 0)))[None]


def unpack_terms(blocks, shape):
    terms = blocks.reshape(-1, BLK, BLK)[:, : 2 * shape[0] * shape[1] // BLK]
    terms = terms.reshape(-1, 2, *shape).astype(F32)
    return terms[:, 0] + terms[:, 1]


def scatter_plane(part_low, part_high, deps, riders):
    first, part, send = None, part_low, after(part_high, *deps)
    for bits in zip(*(order[::-1] for order in chip_orders(lax.axis_size("chip")))):
        if first is not None:
            count = part.shape[0] // 2
            part, send = part[:count], part[count:]
        if riders is not None:
            send = jnp.concatenate([send, riders], 0)
        came = swap_chips(send, bits)
        first = came if first is None else first
        if riders is not None:
            riders = jnp.concatenate([riders, came[part.shape[0] :]], 0)
        part = add_halves(part, came[: part.shape[0]])
    return part, (first,), riders


def by_chip(riders, me, core):
    chips = lax.axis_size("chip")
    ranks = np.array([np.argsort(offsets(order[::-1])) for order in chip_orders(chips)], np.int32)
    rank = jnp.asarray(ranks)[core][me ^ jnp.arange(chips, dtype=jnp.int32)]
    return riders.reshape(chips, -1, BLK, BLK)[rank]


def local(
    tokens,
    cotangent,
    lengths,
    owner_perm,
    master,
    norm_gains,
    stat_left,
    stat_right,
    root_left,
    root_right,
    moment_first,
    moment_second,
):
    core = lax.axis_index("core")
    place_z = lax.axis_index("seq")
    parity = place_z % 2
    block_count = owner_perm.shape[0]
    owned = master.shape[0]
    half = block_count // 2

    chips, planes = lax.axis_size("chip"), lax.axis_size("seq")
    me = lax.axis_index("chip")

    pair_lengths = jnp.stack([lengths, swap_cores(lengths)])
    pair_lengths = jnp.where(core == 0, pair_lengths, pair_lengths[::-1]).reshape(-1)
    length = lax.dynamic_index_in_dim(pair_lengths, place_z, 0, False)
    span = tokens.shape[0] * tokens.shape[1]
    live = jnp.stack([length - core * span, length - (1 - core) * span, length - core * span])

    distance, offset, slot = place_lists(chips, owned, planes)
    offset = jnp.where(core == 0, offset, offset[::-1])
    device = ((place_z - distance) % planes * chips + (me ^ offset)) * 2
    device = device + jnp.stack([core, 1 - core])[:, None]
    table = owner_perm[(device * owned + slot).reshape(-1)]
    inverse = jnp.zeros((block_count,), jnp.int32).at[table].set(
        jnp.arange(block_count, dtype=jnp.int32)
    )

    shard = master.astype(BF)
    shards = [shard]
    for k in range(1, planes):
        shards.append(move_planes(shards[-1], 1))
    own_tokens = spread_rows(after(tokens, shards[-1]), parity)
    other_tokens = swap_cores(own_tokens)
    per_plane = chips * owned
    weights, deps = None, ()
    for k in range(planes):
        if k == 1:
            deps = (*deps, live, table, inverse)
        later = (shards[k + 1],) if k < planes - 1 else ()
        pieces, deps = gather_plane(shards[k], deps, later)
        if k < planes - 1:
            pieces = [jnp.concatenate(pieces, 0)]
        else:
            pieces[-1] = after(pieces[-1], weights, own_tokens, other_tokens)
        first = k * per_plane
        for piece in pieces:
            weights = place_blocks(table, first, piece, swap_cores(piece), weights)
            first += piece.shape[0]
    own_cot = spread_rows(after(cotangent, weights), parity)

    own_qkv, other_kv = project(own_tokens, other_tokens, norm_gains, weights)
    attended, q_aug = attend(live, own_qkv, other_kv)
    layer, g_up, g_down, g_out, grad_middle, grad_attended, gain_second = feed(
        live, own_tokens, attended, own_cot, norm_gains, weights
    )
    layer_out = gather_rows(layer, parity)
    side = D // BLK
    flat = lambda g: g.reshape(-1, BLK, BLK)
    first_rest = 3 * side * side
    starts = (first_rest, first_rest + side * side, first_rest + side * side + side * FF // BLK)
    d_query, d_own, d_other, sends = attend_back(
        live, q_aug, own_qkv, other_kv, attended, grad_attended,
        inverse, starts, (flat(g_out), flat(g_up), flat(g_down)),
    )
    received = swap_cores(after(d_other, layer_out))
    sends, grad_in, gain_first = input_back(
        own_tokens, norm_gains, d_query, d_own, received, grad_middle, weights, inverse, sends
    )
    input_grad = gather_rows(grad_in, parity).astype(F32)
    gain_part = jnp.concatenate([gain_first, gain_second], 0)
    passed, deps, planes_gain = None, (), []
    middle = per_plane // 2
    for k in reversed(range(planes)):
        low = k * per_plane
        first_turn = k == planes - 1
        sums, riders, held = [], None, deps
        for start in (low + middle, low):
            buffer = after(sends, *held)
            other = buffer[half + start : half + start + middle]
            if first_turn and start != low:
                mine = pack_terms(gain_part)
                other = swap_cores(jnp.concatenate([other, mine], 0))
                theirs = other[middle:]
                riders = jnp.where(
                    core == 0,
                    jnp.concatenate([mine, theirs], 0),
                    jnp.concatenate([theirs, mine], 0),
                )
                other = other[:middle]
            else:
                other = swap_cores(other)
            sums.append(add_halves(buffer[start : start + middle], other))
            held = (sums[-1],)
        if k == planes - 3:
            deps = (*deps, input_grad)
        part, deps, riders = scatter_plane(sums[1], sums[0], deps, riders)
        if first_turn:
            plane_gain = jnp.sum(unpack_terms(by_chip(riders, me, core), gain_part.shape), 0)
            rider = pack_terms(plane_gain)
        if passed is not None:
            rider = passed[owned:]
            passed = passed[:owned]
        planes_gain.append(unpack_terms(rider, gain_part.shape)[0])
        if k == 0:
            grad_blocks = part.astype(F32) + passed.astype(F32)
        else:
            part = part if passed is None else add_halves(part, passed)
            passed = move_planes(jnp.concatenate([part, rider], 0), -1)
    turned = (jnp.arange(planes, dtype=jnp.int32) - place_z) % planes
    gain_grad = jnp.sum(jnp.stack(planes_gain)[turned], 0)
    stat_left_new, stat_right_new, master_new = update(
        grad_blocks, master, stat_left, stat_right, root_left, root_right
    )
    first_new = 0.9 * moment_first + 0.1 * gain_grad
    second_new = 0.999 * moment_second + 0.001 * gain_grad * gain_grad
    first_hat = first_new / (1.0 - 0.9**STEP)
    second_hat = second_new / (1.0 - 0.999**STEP)
    gains_new = norm_gains - 0.5 * first_hat / (jnp.sqrt(second_hat) + 1e-08)
    return (
        layer_out,
        input_grad,
        grad_blocks,
        stat_left_new,
        stat_right_new,
        master_new,
        first_new,
        second_new,
        gains_new,
    )


def solution(mesh):
    seq_size, rows_size = mesh.shape["seq"], mesh.shape["rows"]
    mesh = Mesh(mesh.devices.reshape(seq_size, rows_size // 2, 2), ("seq", "chip", "core"))
    activation = P(("chip", "core"), "seq", None)
    blocks = P(("seq", "chip", "core"), None, None)
    return jax.shard_map(
        local,
        mesh=mesh,
        in_specs=(
            activation, activation, P(("chip", "core")), P(), blocks, P(),
            blocks, blocks, blocks, blocks, P(), P(),
        ),
        out_specs=(activation, activation, blocks, blocks, blocks, blocks, P(), P(), P()),
        check_vma=False,
    )
```

```python
import functools
import jax
import jax.numpy as jnp
import numpy as np
from jax import lax
from jax.experimental import pallas as pl
from jax.experimental.pallas import tpu as pltpu
from jax.sharding import Mesh
from jax.sharding import PartitionSpec as P

D = 1024
HD = 64
FF = 4096
BLK = 128
STEP = 10
COLS = 512
BF = jnp.bfloat16
F32 = jnp.float32
MIB = 1024 * 1024

norm_eps = 1e-05
score_scale = 0.125
masked_score = -1e30


def params():
    return pltpu.CompilerParams(vmem_limit_bytes=56 * MIB)


def cost(flops, nbytes):
    return pl.CostEstimate(flops=int(flops), bytes_accessed=int(nbytes), transcendentals=0)


def mul_nn(left, right):
    return jnp.dot(left, right, preferred_element_type=F32)


def mul_nt(left, right):
    return lax.dot_general(left, right, (((1,), (1,)), ((), ())), preferred_element_type=F32)


def mul_tn(left, right):
    return lax.dot_general(left, right, (((0,), (0,)), ((), ())), preferred_element_type=F32)


def join_tile(ref):
    rows, cols = ref.shape[0], ref.shape[1]
    return jnp.concatenate([ref[:, j].reshape(rows * BLK, BLK) for j in range(cols)], axis=1)


def split_tile(ref, matrix):
    rows, cols = ref.shape[0], ref.shape[1]
    for j in range(cols):
        ref[:, j] = matrix[:, j * BLK : (j + 1) * BLK].reshape(rows, BLK, BLK).astype(ref.dtype)


def split_flat(ref, matrix):
    cols = matrix.shape[1] // BLK
    for i in range(matrix.shape[0] // BLK):
        for j in range(cols):
            block = matrix[i * BLK : (i + 1) * BLK, j * BLK : (j + 1) * BLK]
            ref[i * cols + j] = block.astype(ref.dtype)


def normalize(values):
    row_mean = jnp.mean(values, -1, keepdims=True)
    centered = values - row_mean
    row_var = jnp.mean(centered * centered, -1, keepdims=True)
    inv_std = lax.rsqrt(row_var + norm_eps)
    return centered * inv_std, inv_std


def norm_back(gradient, unit_vals, inv_std):
    grad_mean = jnp.mean(gradient, -1, keepdims=True)
    cross_mean = jnp.mean(gradient * unit_vals, -1, keepdims=True)
    return inv_std * (gradient - grad_mean - unit_vals * cross_mean)


def place_body(first, table, near_ref, far_ref, *refs):
    out_ref, sem = refs[-2:]
    count = near_ref.shape[0]
    half = table.shape[0] // 2
    start = first + pl.program_id(0) * count
    for slot in range(count):
        pltpu.make_async_copy(near_ref.at[slot], out_ref.at[table[start + slot]], sem).start()
        far_place = table[half + start + slot]
        pltpu.make_async_copy(far_ref.at[slot], out_ref.at[far_place], sem).start()
    done = out_ref.at[pl.ds(0, 2 * count)]
    pltpu.make_async_copy(done, done, sem).wait()


def place_blocks(table, first, near, far, kept):
    smem = pl.BlockSpec(memory_space=pltpu.SMEM)
    hbm = pl.BlockSpec(memory_space=pltpu.HBM)
    steps = max(near.shape[0] // 24, 1)
    part = pl.BlockSpec((near.shape[0] // steps, BLK, BLK), lambda i: (i, 0, 0))
    kept = () if kept is None else (kept,)
    return pl.pallas_call(
        functools.partial(place_body, first),
        grid=(steps,),
        out_shape=jax.ShapeDtypeStruct((table.shape[0], BLK, BLK), BF),
        in_specs=[smem, part, part] + [hbm] * len(kept),
        out_specs=hbm,
        scratch_shapes=[pltpu.SemaphoreType.DMA],
        input_output_aliases={3: 0} if kept else {},
        compiler_params=params(),
        cost_estimate=cost(0, 4 * near.size * 2),
        name="place_weights",
    )(table, near, far, *kept)


def qkv_body(own_ref, other_ref, gains_ref, w_ref, own_out, other_out, normed):
    step = pl.program_id(0)
    span = own_ref.shape[0]

    @pl.when(step == 0)
    def _():
        gain = gains_ref[0:1]
        normed[:span] = (normalize(own_ref[...].astype(F32))[0] * gain).astype(BF)
        normed[span:] = (normalize(other_ref[...].astype(F32))[0] * gain).astype(BF)

    weight = join_tile(w_ref)
    own_out[...] = mul_nn(normed[:span], weight).astype(BF)

    @pl.when(step >= D // COLS)
    def _():
        other_out[...] = mul_nn(normed[span:], weight).astype(BF)


def project(own, other, gains, weights):
    span = own.shape[0]
    skip = D // COLS
    whole = lambda j: (0, 0)
    return pl.pallas_call(
        qkv_body,
        grid=(3 * D // COLS,),
        in_specs=[
            pl.BlockSpec((span, D), whole),
            pl.BlockSpec((span, D), whole),
            pl.BlockSpec((2, D), whole),
            pl.BlockSpec((D // BLK, COLS // BLK, BLK, BLK), lambda j: (0, j, 0, 0)),
        ],
        out_specs=[
            pl.BlockSpec((span, COLS), lambda j: (0, j)),
            pl.BlockSpec((span, COLS), lambda j: (0, jnp.maximum(j - skip, 0))),
        ],
        out_shape=[
            jax.ShapeDtypeStruct((span, 3 * D), BF),
            jax.ShapeDtypeStruct((span, 2 * D), BF),
        ],
        scratch_shapes=[pltpu.VMEM((2 * span, D), BF)],
        compiler_params=params(),
        cost_estimate=cost(10 * span * D * D, 12 * MIB),
        name="qkv_projection",
    )(own, other, gains, weights.reshape(-1, 3 * D // BLK, BLK, BLK))


def lane_masks(head):
    lane = lax.broadcasted_iota(jnp.int32, (1, BLK), 1)
    first = HD * (1 - head)
    keep = (lane // HD == head).astype(F32)
    dead_lane = (lane == first).astype(F32)
    terms = [(lane == first + 1 + i).astype(F32) for i in range(3)]
    return keep, dead_lane, terms


def three_terms(values):
    high = values.astype(BF).astype(F32)
    rest = values - high
    middle = rest.astype(BF).astype(F32)
    return high, middle, rest - middle


def key_bias(span, live_count):
    row = lax.broadcasted_iota(jnp.int32, (span, 1), 0)
    return jnp.where(row < live_count, 0.0, masked_score).astype(F32)


def attend_body(live_ref, q_ref, ko_ref, vo_ref, kx_ref, vx_ref, out_ref, aug_ref):
    span = q_ref.shape[0]
    bias_own = key_bias(span, live_ref[0])
    bias_other = key_bias(span, live_ref[1])
    queries = q_ref[...].astype(F32) * score_scale
    k_own, k_other = ko_ref[...].astype(F32), kx_ref[...].astype(F32)
    results = []
    for head in range(2):
        keep, dead_lane, terms = lane_masks(head)
        q_head = (queries * keep + dead_lane).astype(BF)
        s_own = mul_nt(q_head, (k_own * keep + bias_own * dead_lane).astype(BF))
        s_other = mul_nt(q_head, (k_other * keep + bias_other * dead_lane).astype(BF))
        top = jnp.maximum(
            jnp.max(s_own, -1, keepdims=True), jnp.max(s_other, -1, keepdims=True)
        )
        p_own = jnp.exp(s_own - top)
        p_other = jnp.exp(s_other - top)
        total = jnp.sum(p_own, -1, keepdims=True) + jnp.sum(p_other, -1, keepdims=True)
        mixed = mul_nn(p_own.astype(BF), vo_ref[...]) + mul_nn(p_other.astype(BF), vx_ref[...])
        results.append(mixed / total * keep)
        parts = three_terms(-(top + jnp.log(total)))
        stats = sum(part * lane for part, lane in zip(parts, terms))
        aug_ref[:, head * BLK : (head + 1) * BLK] = (q_head.astype(F32) + stats).astype(BF)
    out_ref[...] = (results[0] + results[1]).astype(BF)


def attend(live, own, other):
    span = own.shape[0]
    pairs = D // BLK
    col = lambda shift: pl.BlockSpec((span, BLK), lambda p: (0, p + shift))
    return pl.pallas_call(
        attend_body,
        grid=(pairs,),
        in_specs=[
            pl.BlockSpec(memory_space=pltpu.SMEM),
            col(0),
            col(pairs),
            col(2 * pairs),
            col(0),
            col(pairs),
        ],
        out_specs=[col(0), pl.BlockSpec((span, 2 * BLK), lambda p: (0, p))],
        out_shape=[
            jax.ShapeDtypeStruct((span, D), BF),
            jax.ShapeDtypeStruct((span, 2 * D), BF),
        ],
        compiler_params=params(),
        cost_estimate=cost(40 * span * span * D, 8 * MIB),
        name="attention",
    )(live, own, own, own, other, other)


def attend_back_body(
    live_ref, aug_ref, ko_ref, vo_ref, kx_ref, vx_ref, at_ref, g_ref, dq_ref, own_ref, other_ref
):
    span = at_ref.shape[0]
    grads = g_ref[...].astype(F32)
    product = grads * at_ref[...].astype(F32)
    keeps, g_augs, q_augs = [], [], []
    for head in range(2):
        keep, dead_lane, terms = lane_masks(head)
        delta = jnp.sum(product * keep, -1, keepdims=True)
        parts = three_terms(-delta)
        stats = sum(part * lane for part, lane in zip(parts, terms))
        g_augs.append((grads * keep + stats).astype(BF))
        q_augs.append(aug_ref[:, head * BLK : (head + 1) * BLK])
    d_query = [None, None]
    for k_ref, v_ref, out_ref, live in (
        (ko_ref, vo_ref, own_ref, live_ref[0]),
        (kx_ref, vx_ref, other_ref, live_ref[1]),
    ):
        bias = key_bias(span, live)
        keys = k_ref[...]
        keys_f, values_f = keys.astype(F32), v_ref[...].astype(F32)
        d_keys = d_values = None
        for head in range(2):
            keep, dead_lane, terms = lane_masks(head)
            ones = terms[0] + terms[1] + terms[2]
            k_aug = (keys_f * keep + (bias * dead_lane + ones)).astype(BF)
            v_aug = (values_f * keep + ones).astype(BF)
            probs = jnp.exp(mul_nt(k_aug, q_augs[head]))
            d_scores = (probs * mul_nt(v_aug, g_augs[head])).astype(BF)
            value_part = mul_nn(probs.astype(BF), g_augs[head]) * keep
            key_part = mul_nn(d_scores, q_augs[head]) * keep
            query_part = mul_tn(d_scores, keys) * (keep * score_scale)
            d_query[head] = query_part if d_query[head] is None else d_query[head] + query_part
            d_values = value_part if d_values is None else d_values + value_part
            d_keys = key_part if d_keys is None else d_keys + key_part
        out_ref[0] = d_keys.astype(out_ref.dtype)
        out_ref[1] = d_values.astype(out_ref.dtype)
    dq_ref[...] = (d_query[0] + d_query[1]).astype(BF)


def attend_back(live, aug, own, other, attended, grads):
    span = own.shape[0]
    pairs = D // BLK
    col = lambda shift: pl.BlockSpec((span, BLK), lambda p: (0, p + shift))
    pair_out = pl.BlockSpec((2, span, BLK), lambda p: (0, 0, p))
    return pl.pallas_call(
        attend_back_body,
        grid=(pairs,),
        in_specs=[
            pl.BlockSpec(memory_space=pltpu.SMEM),
            pl.BlockSpec((span, 2 * BLK), lambda p: (0, p)),
            col(pairs),
            col(2 * pairs),
            col(0),
            col(pairs),
            col(0),
            col(0),
        ],
        out_specs=[col(0), pair_out, pair_out],
        out_shape=[
            jax.ShapeDtypeStruct((span, D), BF),
            jax.ShapeDtypeStruct((2, span, D), F32),
            jax.ShapeDtypeStruct((2, span, D), BF),
        ],
        compiler_params=params(),
        cost_estimate=cost(60 * span * span * D, 12 * MIB),
        name="attention_backward",
    )(live, aug, own, own, other, other, attended, grads)


def feed_body(
    live_ref,
    tokens_ref,
    attended_ref,
    cot_ref,
    gains_ref,
    wo_ref,
    wu_ref,
    wd_ref,
    layer_ref,
    rest_ref,
    gm_ref,
    ga_ref,
    gain_ref,
    unit,
    inv,
    normed,
    top,
    acc_out,
    acc_back,
    up_stage,
    down_stage,
    out_stage,
    sems,
    out_sem,
):
    step = pl.program_id(0)
    place = step % 2
    side, width = up_stage.shape[1], up_stage.shape[2]
    per_tile = side * width
    up_first = side * side
    down_first = up_first + side * FF // BLK

    def drain(which):
        pltpu.make_async_copy(up_stage.at[which], up_stage.at[which], sems.at[0, which]).wait()
        pltpu.make_async_copy(down_stage.at[which], down_stage.at[which], sems.at[1, which]).wait()
    span = tokens_ref.shape[0]

    @pl.when(step == 0)
    def _():
        weight = join_tile(wo_ref)
        middle = tokens_ref[...].astype(F32) + mul_nn(attended_ref[...], weight)
        unit_vals, inv_std = normalize(middle)
        unit[...] = unit_vals
        inv[...] = inv_std
        normed[...] = (unit_vals * gains_ref[1:2]).astype(BF)
        row = lax.broadcasted_iota(jnp.int32, (span, 1), 0)
        top[...] = jnp.where(row < live_ref[2], cot_ref[...].astype(F32), 0.0).astype(BF)
        acc_out[...] = middle
        acc_back[...] = jnp.zeros_like(acc_back)

    w_up = join_tile(wu_ref)
    w_down = join_tile(wd_ref)
    hidden = mul_nn(normed[...], w_up)
    grad_act = mul_nt(top[...], w_down)
    erf_part = 0.5 * (1.0 + lax.erf(hidden * 0.7071067811865476))
    activated = (hidden * erf_part).astype(BF)
    slope = erf_part + hidden * jnp.exp(-0.5 * hidden * hidden) * 0.3989422804014327
    grad_hidden = (grad_act * slope).astype(BF)
    acc_out[...] += mul_nn(activated, w_down)
    acc_back[...] += mul_nt(grad_hidden, w_up)

    @pl.when(step >= 2)
    def _():
        drain(place)

    split_flat(down_stage.at[place], mul_tn(activated, top[...]))
    dest = rest_ref.at[pl.ds(down_first + step * per_tile, per_tile)]
    pltpu.make_async_copy(down_stage.at[place], dest, sems.at[1, place]).start()
    split_tile(up_stage.at[place], mul_tn(normed[...], grad_hidden))
    for i in range(side):
        dest = rest_ref.at[pl.ds(up_first + i * (FF // BLK) + step * width, width)]
        pltpu.make_async_copy(up_stage.at[place, i], dest, sems.at[0, place]).start()

    @pl.when(step == pl.num_programs(0) - 1)
    def _():
        layer_ref[...] = acc_out[...].astype(BF)
        unit_vals = unit[...]
        back = acc_back[...]
        gain_ref[...] = jnp.sum(back * unit_vals, 0, keepdims=True)
        grad_middle = top[...].astype(F32) + norm_back(back * gains_ref[1:2], unit_vals, inv[...])
        gm_ref[...] = grad_middle
        back_middle = grad_middle.astype(BF)
        split_flat(out_stage, mul_tn(attended_ref[...], back_middle))
        out_copy = pltpu.make_async_copy(out_stage, rest_ref.at[pl.ds(0, up_first)], out_sem)
        out_copy.start()
        ga_ref[...] = mul_nt(back_middle, join_tile(wo_ref)).astype(BF)
        drain(1 - place)
        drain(place)
        out_copy.wait()


def feed(live, tokens, attended, cotangent, gains, weights):
    span = tokens.shape[0]
    side, width = D // BLK, COLS // BLK
    whole = lambda j: (0, 0)
    act = pl.BlockSpec((span, D), whole)
    per_row = weights.reshape(-1, side, BLK, BLK)
    per_up = weights.reshape(-1, FF // BLK, BLK, BLK)
    out_row = (3 * side * side) // side // side
    up_row = 4 * side * side // (FF // BLK) // side
    down_row = (4 * side * side + side * FF // BLK) // side // width
    return pl.pallas_call(
        feed_body,
        grid=(FF // COLS,),
        in_specs=[
            pl.BlockSpec(memory_space=pltpu.SMEM),
            act,
            act,
            act,
            pl.BlockSpec((2, D), whole),
            pl.BlockSpec((side, side, BLK, BLK), lambda j: (out_row, 0, 0, 0)),
            pl.BlockSpec((side, width, BLK, BLK), lambda j: (up_row, j, 0, 0)),
            pl.BlockSpec((width, side, BLK, BLK), lambda j: (down_row + j, 0, 0, 0)),
        ],
        out_specs=[
            act,
            pl.BlockSpec(memory_space=pltpu.HBM),
            act,
            act,
            pl.BlockSpec((1, D), whole),
        ],
        out_shape=[
            jax.ShapeDtypeStruct((span, D), BF),
            jax.ShapeDtypeStruct((side * side + 2 * side * (FF // BLK), BLK, BLK), BF),
            jax.ShapeDtypeStruct((span, D), F32),
            jax.ShapeDtypeStruct((span, D), BF),
            jax.ShapeDtypeStruct((1, D), F32),
        ],
        scratch_shapes=[
            pltpu.VMEM((span, D), F32),
            pltpu.VMEM((span, 1), F32),
            pltpu.VMEM((span, D), BF),
            pltpu.VMEM((span, D), BF),
            pltpu.VMEM((span, D), F32),
            pltpu.VMEM((span, D), F32),
            pltpu.VMEM((2, side, width, BLK, BLK), BF),
            pltpu.VMEM((2, side * width, BLK, BLK), BF),
            pltpu.VMEM((side * side, BLK, BLK), BF),
            pltpu.SemaphoreType.DMA((2, 2)),
            pltpu.SemaphoreType.DMA,
        ],
        compiler_params=params(),
        cost_estimate=cost(14 * span * D * FF, 50 * MIB),
        name="feed_forward",
    )(live, tokens, attended, cotangent, gains, per_row, per_up, per_row)


def query_body(tokens_ref, gains_ref, dq_ref, w_ref, grad_ref, acc_ref, normed):
    step = pl.program_id(0)

    @pl.when(step == 0)
    def _():
        unit_vals, _ = normalize(tokens_ref[...].astype(F32))
        normed[...] = (unit_vals * gains_ref[0:1]).astype(BF)
        acc_ref[...] = jnp.zeros_like(acc_ref)

    grad = dq_ref[...]
    acc_ref[...] += mul_nt(grad, join_tile(w_ref))
    split_tile(grad_ref, mul_tn(normed[...], grad))


def query_back(tokens, gains, d_query, weights):
    span = tokens.shape[0]
    side, width = D // BLK, COLS // BLK
    whole = lambda j: (0, 0)
    act = pl.BlockSpec((span, D), whole)
    tile = pl.BlockSpec((side, width, BLK, BLK), lambda j: (0, j, 0, 0))
    return pl.pallas_call(
        query_body,
        grid=(D // COLS,),
        in_specs=[
            act,
            pl.BlockSpec((2, D), whole),
            pl.BlockSpec((span, COLS), lambda j: (0, j)),
            tile,
        ],
        out_specs=[tile, act],
        out_shape=[
            jax.ShapeDtypeStruct((side, side, BLK, BLK), BF),
            jax.ShapeDtypeStruct((span, D), F32),
        ],
        scratch_shapes=[pltpu.VMEM((span, D), BF)],
        compiler_params=params(),
        cost_estimate=cost(4 * span * D * D, 8 * MIB),
        name="query_backward",
    )(tokens, gains, d_query, weights.reshape(-1, 3 * side, BLK, BLK))


def input_body(
    tokens_ref, gains_ref, own_ref, recv_ref, acc_ref, gm_ref, w_ref, grad_ref, out_ref, gain_ref,
    unit, inv, normed, acc
):
    step = pl.program_id(0)

    @pl.when(step == 0)
    def _():
        unit_vals, inv_std = normalize(tokens_ref[...].astype(F32))
        unit[...] = unit_vals
        inv[...] = inv_std
        normed[...] = (unit_vals * gains_ref[0:1]).astype(BF)
        acc[...] = acc_ref[...]

    grad = (own_ref[0] + recv_ref[0].astype(F32)).astype(BF)
    acc[...] += mul_nt(grad, join_tile(w_ref))
    split_tile(grad_ref, mul_tn(normed[...], grad))

    @pl.when(step == pl.num_programs(0) - 1)
    def _():
        unit_vals = unit[...]
        back = acc[...]
        gain_ref[...] = jnp.sum(back * unit_vals, 0, keepdims=True)
        out_ref[...] = (
            gm_ref[...] + norm_back(back * gains_ref[0:1], unit_vals, inv[...])
        ).astype(BF)


def input_back(tokens, gains, own, received, partial, grad_middle, weights):
    span = tokens.shape[0]
    side, width = D // BLK, COLS // BLK
    per = D // COLS
    whole = lambda j: (0, 0)
    act = pl.BlockSpec((span, D), whole)
    part = pl.BlockSpec((1, span, COLS), lambda j: (j // per, 0, j % per))
    return pl.pallas_call(
        input_body,
        grid=(2 * per,),
        in_specs=[
            act,
            pl.BlockSpec((2, D), whole),
            part,
            part,
            act,
            act,
            pl.BlockSpec((side, width, BLK, BLK), lambda j: (0, j + per, 0, 0)),
        ],
        out_specs=[
            pl.BlockSpec((side, width, BLK, BLK), lambda j: (0, j, 0, 0)),
            act,
            pl.BlockSpec((1, D), whole),
        ],
        out_shape=[
            jax.ShapeDtypeStruct((side, 2 * side, BLK, BLK), BF),
            jax.ShapeDtypeStruct((span, D), BF),
            jax.ShapeDtypeStruct((1, D), F32),
        ],
        scratch_shapes=[
            pltpu.VMEM((span, D), F32),
            pltpu.VMEM((span, 1), F32),
            pltpu.VMEM((span, D), BF),
            pltpu.VMEM((span, D), F32),
        ],
        compiler_params=params(),
        cost_estimate=cost(8 * span * D * D, 20 * MIB),
        name="input_backward",
    )(
        tokens, gains, own, received, partial, grad_middle,
        weights.reshape(-1, 3 * side, BLK, BLK),
    )


def source_numbers():
    side = D // BLK
    numbers = np.arange(3 * side * side + side * side + 2 * side * (FF // BLK), dtype=np.int32)
    row, col = np.divmod(numbers[: 3 * side * side], 3 * side)
    numbers[: 3 * side * side] = np.where(
        col < side, row * side + col, side * side + row * 2 * side + col - side
    )
    return numbers


def gather_body(first, bounds, table, *refs):
    sources = refs[:6]
    low_ref, high_ref, stage, sems = refs[6:]
    step, steps = pl.program_id(0), pl.num_programs(0)
    count = stage.shape[1] // 2
    turn = steps // 2

    def fetch(which, slot):
        start = first + (which + turn) % steps * count
        for i in range(count):
            number = table[start + i]
            for low, high, own, other in zip(bounds, bounds[1:], sources[:3], sources[3:]):

                @pl.when((number >= low) & (number < high))
                def _():
                    for src, at in ((own, i), (other, count + i)):
                        pltpu.make_async_copy(
                            src.at[number - low], stage.at[slot, at], sems.at[slot]
                        ).start()

    @pl.when(step == 0)
    def _():
        fetch(0, 0)

    @pl.when(step + 1 < steps)
    def _():
        fetch(step + 1, (step + 1) % 2)

    slot = step % 2
    pltpu.make_async_copy(stage.at[slot], stage.at[slot], sems.at[slot]).wait()
    total = stage[slot, :count].astype(F32) + stage[slot, count:].astype(F32)

    @pl.when(step < turn)
    def _():
        high_ref[...] = total.astype(BF)

    @pl.when(step >= turn)
    def _():
        low_ref[...] = total.astype(BF)


def gather_sums(table, first, count, own, other):
    hbm = pl.BlockSpec(memory_space=pltpu.HBM)
    steps = 4
    part = count // steps
    turn = steps // 2
    bounds = np.cumsum([0] + [src.shape[0] for src in own]).tolist()
    shape = jax.ShapeDtypeStruct((count // 2, BLK, BLK), BF)
    return pl.pallas_call(
        functools.partial(gather_body, first, bounds),
        grid=(steps,),
        in_specs=[pl.BlockSpec(memory_space=pltpu.SMEM)] + [hbm] * 6,
        out_specs=[
            pl.BlockSpec((part, BLK, BLK), lambda i: (jnp.maximum(i - turn, 0), 0, 0)),
            pl.BlockSpec((part, BLK, BLK), lambda i: (jnp.minimum(i, turn - 1), 0, 0)),
        ],
        out_shape=[shape, shape],
        scratch_shapes=[
            pltpu.VMEM((2, 2 * part, BLK, BLK), BF),
            pltpu.SemaphoreType.DMA((2,)),
        ],
        compiler_params=params(),
        cost_estimate=cost(0, 6 * count * BLK * BLK),
        name="gradient_sums",
    )(table, *own, *other)


def two_terms(values):
    high = values.astype(BF)
    return high, (values - high.astype(F32)).astype(BF)


def update_body(g_ref, m_ref, sl_ref, sr_ref, rl_ref, rr_ref, sl_out, sr_out, m_out):
    def long_left(terms, axis):
        return jnp.concatenate([terms[0], terms[0], terms[1]], axis)

    def long_right(terms, axis):
        return jnp.concatenate([terms[0], terms[1], terms[0]], axis)

    for i in range(g_ref.shape[0]):
        grad = two_terms(g_ref[i])
        sl_out[i] = sl_ref[i] + mul_nt(long_left(grad, 1), long_right(grad, 1))
        tall = long_right(grad, 0)
        sr_out[i] = sr_ref[i] + mul_tn(long_left(grad, 0), tall)
        inner = mul_nn(long_left(two_terms(rl_ref[i]), 1), tall)
        direction = mul_nn(
            long_left(two_terms(inner), 1), long_right(two_terms(rr_ref[i]), 0)
        )
        master = m_ref[i]
        scale = jnp.sqrt(jnp.mean(master * master, keepdims=True) + 1e-06)
        scale = scale * lax.rsqrt(jnp.mean(direction * direction, keepdims=True) + 1e-06)
        m_out[i] = master - 0.3 * scale * direction


def update(grads, master, stat_left, stat_right, root_left, root_right):
    count = grads.shape[0]
    group = 3 if count % 3 == 0 else 1
    block = pl.BlockSpec((group, BLK, BLK), lambda i: (i, 0, 0))
    shape = jax.ShapeDtypeStruct(grads.shape, F32)
    return pl.pallas_call(
        update_body,
        grid=(count // group,),
        in_specs=[block] * 6,
        out_specs=[block] * 3,
        out_shape=[shape] * 3,
        compiler_params=params(),
        cost_estimate=cost(48 * count * BLK**3, 15 * MIB),
        name="block_update",
    )(grads, master, stat_left, stat_right, root_left, root_right)


def pair_moves():
    moves_same, moves_cross = [], []
    for z in range(4):
        for c in range(2):
            for moves, bit in ((moves_same, z % 2), (moves_cross, 1 - z % 2)):
                moves.append((z * 2 + c, (2 * c + bit) * 2 + z // 2))
    return moves_same, moves_cross


def spread_rows(values, parity):
    moves_same, moves_cross = pair_moves()
    kept = lax.dynamic_index_in_dim(values, parity, 0, False)
    crossed = lax.dynamic_index_in_dim(values, 1 - parity, 0, False)
    kept = lax.ppermute(kept, ("seq", "core"), moves_same)
    crossed = lax.ppermute(crossed, ("seq", "core"), moves_cross)
    low_part = jnp.where(parity == 0, kept, crossed)
    high_part = jnp.where(parity == 0, crossed, kept)
    return jnp.concatenate([low_part, high_part], 0)


def gather_rows(values, parity):
    moves_same, moves_cross = pair_moves()
    parts = values.reshape(2, values.shape[0] // 2, values.shape[1])
    kept = lax.dynamic_index_in_dim(parts, parity, 0, False)
    crossed = lax.dynamic_index_in_dim(parts, 1 - parity, 0, False)
    kept = lax.ppermute(kept, ("seq", "core"), [(b, a) for a, b in moves_same])
    crossed = lax.ppermute(crossed, ("seq", "core"), [(b, a) for a, b in moves_cross])
    return jnp.stack([jnp.where(parity == 0, kept, crossed), jnp.where(parity == 0, crossed, kept)], 0)


def swap_cores(values):
    return lax.ppermute(values, "core", [(0, 1), (1, 0)])


def chip_orders(chips):
    bits = [1 << i for i in range(chips.bit_length() - 1)]
    return bits, bits[::-1]


def offsets(order):
    result = [0]
    for bit in order:
        result = result + [o ^ bit for o in result]
    return result


def place_lists(chips, owned, planes):
    shape = (2, planes, chips, owned)
    by_core = np.array([offsets(order) for order in chip_orders(chips)], np.int32)
    grid = np.indices(shape).astype(np.int32).reshape(4, 2, -1)
    offset = np.broadcast_to(by_core[:, None, :, None], shape).reshape(2, -1)
    return grid[1, 0], offset, grid[3, 0]


def swap_chips(values, bits):
    chips = lax.axis_size("chip")
    moves = [(i * 2 + c, (i ^ bits[c]) * 2 + c) for i in range(chips) for c in range(2)]
    return lax.ppermute(values, ("chip", "core"), moves)


def move_planes(values, shift):
    planes = lax.axis_size("seq")
    return lax.ppermute(values, "seq", [(i, (i + shift) % planes) for i in range(planes)])


def after(value, *deps):
    return lax.optimization_barrier((value, *deps))[0]


def gather_plane(own, deps, later):
    steps = list(zip(*chip_orders(lax.axis_size("chip"))))
    own = after(own, *deps)
    came = swap_chips(own, steps[0])
    crossed = swap_chips(own, steps[1])
    pieces = [own, came, crossed, swap_chips(after(came, *later), steps[1])]
    for bits in steps[2:]:
        joined = jnp.concatenate(pieces, 0)
        pieces = [joined, swap_chips(joined, bits)]
    return pieces, (came, crossed)


def add_halves(kept, came):
    return (kept.astype(F32) + came.astype(F32)).astype(BF)


def pack_terms(values):
    high = lax.optimization_barrier(values.astype(BF))
    low = (values - high.astype(F32)).astype(BF)
    terms = jnp.stack([high, low]).reshape(-1, BLK)
    return jnp.pad(terms, ((0, BLK - terms.shape[0]), (0, 0)))[None]


def unpack_terms(blocks, shape):
    terms = blocks.reshape(-1, BLK, BLK)[:, : 2 * shape[0] * shape[1] // BLK]
    terms = terms.reshape(-1, 2, *shape).astype(F32)
    return terms[:, 0] + terms[:, 1]


def scatter_plane(low, high, deps, riders):
    first, keep, send = None, low, after(high, *deps)
    for bits in zip(*(order[::-1] for order in chip_orders(lax.axis_size("chip")))):
        if first is not None:
            count = keep.shape[0] // 2
            send = add_halves(keep[count:], came[count : 2 * count])
            keep = add_halves(keep[:count], came[:count])
        if riders is not None:
            send = jnp.concatenate([send, riders], 0)
        came = swap_chips(send, bits)
        first = came if first is None else first
        if riders is not None:
            riders = jnp.concatenate([riders, came[keep.shape[0] :]], 0)
    return add_halves(keep, came[: keep.shape[0]]), (first,), riders


def by_chip(riders, me, core):
    chips = lax.axis_size("chip")
    ranks = np.array([np.argsort(offsets(order[::-1])) for order in chip_orders(chips)], np.int32)
    rank = jnp.asarray(ranks)[core][me ^ jnp.arange(chips, dtype=jnp.int32)]
    return riders.reshape(chips, -1, BLK, BLK)[rank]


def local(
    tokens,
    cotangent,
    lengths,
    owner_perm,
    master,
    norm_gains,
    stat_left,
    stat_right,
    root_left,
    root_right,
    moment_first,
    moment_second,
):
    core = lax.axis_index("core")
    place_z = lax.axis_index("seq")
    parity = place_z % 2
    block_count = owner_perm.shape[0]
    owned = master.shape[0]
    half = block_count // 2

    chips, planes = lax.axis_size("chip"), lax.axis_size("seq")
    me = lax.axis_index("chip")

    pair_lengths = jnp.stack([lengths, swap_cores(lengths)])
    pair_lengths = jnp.where(core == 0, pair_lengths, pair_lengths[::-1]).reshape(-1)
    length = lax.dynamic_index_in_dim(pair_lengths, place_z, 0, False)
    span = tokens.shape[0] * tokens.shape[1]
    live = jnp.stack([length - core * span, length - (1 - core) * span, length - core * span])

    distance, offset, slot = place_lists(chips, owned, planes)
    offset = jnp.where(core == 0, offset, offset[::-1])
    device = ((place_z - distance) % planes * chips + (me ^ offset)) * 2
    device = device + jnp.stack([core, 1 - core])[:, None]
    table = owner_perm[(device * owned + slot).reshape(-1)]
    sums_table = jnp.asarray(source_numbers())[table[:half]]

    shard = master.astype(BF)
    shards = [shard]
    for k in range(1, planes):
        shards.append(move_planes(shards[-1], 1))
    own_tokens = spread_rows(after(tokens, shards[-2]), parity)
    other_tokens = swap_cores(own_tokens)
    per_plane = chips * owned
    weights, deps, placed = None, (), []
    for k in range(planes):
        later = (shards[k + 1],) if k < planes - 1 else (placed[1],)
        if k == 1:
            deps = (*deps, live, table, sums_table)
        if k == planes - 1:
            deps = (*deps, own_tokens, placed[0])
        pieces, deps = gather_plane(shards[k], deps, later)
        if k < planes - 1:
            pieces = [jnp.concatenate(pieces, 0)]
        else:
            pieces[-1] = after(pieces[-1], weights, other_tokens)
        first = k * per_plane
        for piece in pieces:
            weights = place_blocks(table, first, piece, swap_cores(piece), weights)
            first += piece.shape[0]
        placed.append(weights)
    own_cot = spread_rows(after(cotangent, weights), parity)

    own_qkv, other_kv = project(own_tokens, other_tokens, norm_gains, weights)
    attended, q_aug = attend(live, own_qkv, other_kv)
    layer, g_rest, grad_middle, grad_attended, gain_second = feed(
        live, own_tokens, attended, own_cot, norm_gains, weights
    )
    other_rest = swap_cores(g_rest)
    layer_out = gather_rows(layer, parity)
    d_query, d_own, d_other = attend_back(live, q_aug, own_qkv, other_kv, attended, grad_attended)
    received = swap_cores(after(d_other, layer_out))
    flat = lambda g: g.reshape(-1, BLK, BLK)
    g_query, partial = query_back(own_tokens, norm_gains, d_query, weights)
    g_query = flat(g_query)
    other_query = swap_cores(g_query)
    g_kv, grad_in, gain_first = input_back(
        own_tokens, norm_gains, d_own, received, partial, grad_middle, weights
    )
    g_kv = flat(g_kv)
    gain_part = jnp.concatenate([gain_first, gain_second], 0)
    mine = pack_terms(gain_part)
    swapped = swap_cores(jnp.concatenate([g_kv, mine], 0))
    other_kv_grad, theirs = swapped[: g_kv.shape[0]], swapped[g_kv.shape[0] :]
    input_grad = gather_rows(grad_in, parity).astype(F32)
    passed, deps, planes_gain = None, (), []
    pair = jnp.concatenate([mine, theirs], 0)
    riders = jnp.where(core == 0, pair, pair[::-1])
    for k in reversed(range(planes)):
        low, high = gather_sums(
            sums_table,
            k * per_plane,
            per_plane,
            (after(g_query, *deps), g_kv, g_rest),
            (other_query, other_kv_grad, other_rest),
        )
        if k == planes - 3:
            deps = (*deps, input_grad)
        part, deps, riders = scatter_plane(low, high, deps, riders)
        if k == planes - 1:
            plane_gain = jnp.sum(unpack_terms(by_chip(riders, me, core), gain_part.shape), 0)
            rider = pack_terms(plane_gain)
            riders = None
        if passed is not None:
            rider = passed[owned:]
            passed = passed[:owned]
        planes_gain.append(unpack_terms(rider, gain_part.shape)[0])
        if k == 0:
            grad_blocks = part.astype(F32) + passed.astype(F32)
        else:
            part = part if passed is None else add_halves(part, passed)
            passed = move_planes(jnp.concatenate([part, rider], 0), -1)
    turned = (jnp.arange(planes, dtype=jnp.int32) - place_z) % planes
    gain_grad = jnp.sum(jnp.stack(planes_gain)[turned], 0)
    stat_left_new, stat_right_new, master_new = update(
        grad_blocks, master, stat_left, stat_right, root_left, root_right
    )
    first_new = 0.9 * moment_first + 0.1 * gain_grad
    second_new = 0.999 * moment_second + 0.001 * gain_grad * gain_grad
    first_hat = first_new / (1.0 - 0.9**STEP)
    second_hat = second_new / (1.0 - 0.999**STEP)
    gains_new = norm_gains - 0.5 * first_hat / (jnp.sqrt(second_hat) + 1e-08)
    return (
        layer_out,
        input_grad,
        grad_blocks,
        stat_left_new,
        stat_right_new,
        master_new,
        first_new,
        second_new,
        gains_new,
    )


def solution(mesh):
    seq_size, rows_size = mesh.shape["seq"], mesh.shape["rows"]
    mesh = Mesh(mesh.devices.reshape(seq_size, rows_size // 2, 2), ("seq", "chip", "core"))
    activation = P(("chip", "core"), "seq", None)
    blocks = P(("seq", "chip", "core"), None, None)
    return jax.shard_map(
        local,
        mesh=mesh,
        in_specs=(
            activation, activation, P(("chip", "core")), P(), blocks, P(),
            blocks, blocks, blocks, blocks, P(), P(),
        ),
        out_specs=(activation, activation, blocks, blocks, blocks, blocks, P(), P(), P()),
        check_vma=False,
    )
```

```python
import functools
import jax
import jax.numpy as jnp
import numpy as np
from jax import lax
from jax.experimental import pallas as pl
from jax.experimental.pallas import tpu as pltpu
from jax.sharding import Mesh
from jax.sharding import PartitionSpec as P

D = 1024
HD = 64
FF = 4096
BLK = 128
STEP = 10
COLS = 512
BF = jnp.bfloat16
F32 = jnp.float32
MIB = 1024 * 1024

norm_eps = 1e-05
score_scale = 0.125
masked_score = -1e30


def params():
    return pltpu.CompilerParams(vmem_limit_bytes=56 * MIB)


def cost(flops, nbytes):
    return pl.CostEstimate(flops=int(flops), bytes_accessed=int(nbytes), transcendentals=0)


def mul_nn(left, right):
    return jnp.dot(left, right, preferred_element_type=F32)


def mul_nt(left, right):
    return lax.dot_general(left, right, (((1,), (1,)), ((), ())), preferred_element_type=F32)


def mul_tn(left, right):
    return lax.dot_general(left, right, (((0,), (0,)), ((), ())), preferred_element_type=F32)


def join_tile(ref):
    rows, cols = ref.shape[0], ref.shape[1]
    return jnp.concatenate([ref[:, j].reshape(rows * BLK, BLK) for j in range(cols)], axis=1)


def split_tile(ref, matrix):
    rows, cols = ref.shape[0], ref.shape[1]
    for j in range(cols):
        ref[:, j] = matrix[:, j * BLK : (j + 1) * BLK].reshape(rows, BLK, BLK).astype(ref.dtype)


def split_flat(ref, matrix):
    cols = matrix.shape[1] // BLK
    for i in range(matrix.shape[0] // BLK):
        for j in range(cols):
            block = matrix[i * BLK : (i + 1) * BLK, j * BLK : (j + 1) * BLK]
            ref[i * cols + j] = block.astype(ref.dtype)


def normalize(values):
    row_mean = jnp.mean(values, -1, keepdims=True)
    centered = values - row_mean
    row_var = jnp.mean(centered * centered, -1, keepdims=True)
    inv_std = lax.rsqrt(row_var + norm_eps)
    return centered * inv_std, inv_std


def norm_back(gradient, unit_vals, inv_std):
    grad_mean = jnp.mean(gradient, -1, keepdims=True)
    cross_mean = jnp.mean(gradient * unit_vals, -1, keepdims=True)
    return inv_std * (gradient - grad_mean - unit_vals * cross_mean)


def place_body(first, table, near_ref, far_ref, *refs):
    out_ref, sem = refs[-2:]
    count = near_ref.shape[0]
    half = table.shape[0] // 2
    start = first + pl.program_id(0) * count
    for slot in range(count):
        pltpu.make_async_copy(near_ref.at[slot], out_ref.at[table[start + slot]], sem).start()
        far_place = table[half + start + slot]
        pltpu.make_async_copy(far_ref.at[slot], out_ref.at[far_place], sem).start()
    done = out_ref.at[pl.ds(0, 2 * count)]
    pltpu.make_async_copy(done, done, sem).wait()


def place_blocks(table, first, near, far, kept):
    smem = pl.BlockSpec(memory_space=pltpu.SMEM)
    hbm = pl.BlockSpec(memory_space=pltpu.HBM)
    steps = max(near.shape[0] // 24, 1)
    part = pl.BlockSpec((near.shape[0] // steps, BLK, BLK), lambda i: (i, 0, 0))
    kept = () if kept is None else (kept,)
    return pl.pallas_call(
        functools.partial(place_body, first),
        grid=(steps,),
        out_shape=jax.ShapeDtypeStruct((table.shape[0], BLK, BLK), BF),
        in_specs=[smem, part, part] + [hbm] * len(kept),
        out_specs=hbm,
        scratch_shapes=[pltpu.SemaphoreType.DMA],
        input_output_aliases={3: 0} if kept else {},
        compiler_params=params(),
        cost_estimate=cost(0, 4 * near.size * 2),
        name="place_weights",
    )(table, near, far, *kept)


def qkv_body(own_ref, other_ref, gains_ref, w_ref, own_out, other_out, normed):
    step = pl.program_id(0)
    span = own_ref.shape[0]

    @pl.when(step == 0)
    def _():
        gain = gains_ref[0:1]
        normed[:span] = (normalize(own_ref[...].astype(F32))[0] * gain).astype(BF)
        normed[span:] = (normalize(other_ref[...].astype(F32))[0] * gain).astype(BF)

    weight = join_tile(w_ref)
    own_out[...] = mul_nn(normed[:span], weight).astype(BF)

    @pl.when(step >= D // COLS)
    def _():
        other_out[...] = mul_nn(normed[span:], weight).astype(BF)


def project(own, other, gains, weights):
    span = own.shape[0]
    skip = D // COLS
    whole = lambda j: (0, 0)
    return pl.pallas_call(
        qkv_body,
        grid=(3 * D // COLS,),
        in_specs=[
            pl.BlockSpec((span, D), whole),
            pl.BlockSpec((span, D), whole),
            pl.BlockSpec((2, D), whole),
            pl.BlockSpec((D // BLK, COLS // BLK, BLK, BLK), lambda j: (0, j, 0, 0)),
        ],
        out_specs=[
            pl.BlockSpec((span, COLS), lambda j: (0, j)),
            pl.BlockSpec((span, COLS), lambda j: (0, jnp.maximum(j - skip, 0))),
        ],
        out_shape=[
            jax.ShapeDtypeStruct((span, 3 * D), BF),
            jax.ShapeDtypeStruct((span, 2 * D), BF),
        ],
        scratch_shapes=[pltpu.VMEM((2 * span, D), BF)],
        compiler_params=params(),
        cost_estimate=cost(10 * span * D * D, 12 * MIB),
        name="qkv_projection",
    )(own, other, gains, weights.reshape(-1, 3 * D // BLK, BLK, BLK))


def lane_masks(head):
    lane = lax.broadcasted_iota(jnp.int32, (1, BLK), 1)
    first = HD * (1 - head)
    keep = (lane // HD == head).astype(F32)
    dead_lane = (lane == first).astype(F32)
    terms = [(lane == first + 1 + i).astype(F32) for i in range(3)]
    return keep, dead_lane, terms


def three_terms(values):
    high = values.astype(BF).astype(F32)
    rest = values - high
    middle = rest.astype(BF).astype(F32)
    return high, middle, rest - middle


def key_bias(span, live_count):
    row = lax.broadcasted_iota(jnp.int32, (span, 1), 0)
    return jnp.where(row < live_count, 0.0, masked_score).astype(F32)


def attend_body(live_ref, q_ref, ko_ref, vo_ref, kx_ref, vx_ref, out_ref, aug_ref):
    span = q_ref.shape[0]
    bias_own = key_bias(span, live_ref[0])
    bias_other = key_bias(span, live_ref[1])
    queries = q_ref[...].astype(F32) * score_scale
    k_own, k_other = ko_ref[...].astype(F32), kx_ref[...].astype(F32)
    results = []
    for head in range(2):
        keep, dead_lane, terms = lane_masks(head)
        q_head = (queries * keep + dead_lane).astype(BF)
        s_own = mul_nt(q_head, (k_own * keep + bias_own * dead_lane).astype(BF))
        s_other = mul_nt(q_head, (k_other * keep + bias_other * dead_lane).astype(BF))
        top = jnp.maximum(
            jnp.max(s_own, -1, keepdims=True), jnp.max(s_other, -1, keepdims=True)
        )
        p_own = jnp.exp(s_own - top)
        p_other = jnp.exp(s_other - top)
        total = jnp.sum(p_own, -1, keepdims=True) + jnp.sum(p_other, -1, keepdims=True)
        mixed = mul_nn(p_own.astype(BF), vo_ref[...]) + mul_nn(p_other.astype(BF), vx_ref[...])
        results.append(mixed / total * keep)
        parts = three_terms(-(top + jnp.log(total)))
        stats = sum(part * lane for part, lane in zip(parts, terms))
        aug_ref[:, head * BLK : (head + 1) * BLK] = (q_head.astype(F32) + stats).astype(BF)
    out_ref[...] = (results[0] + results[1]).astype(BF)


def attend(live, own, other):
    span = own.shape[0]
    pairs = D // BLK
    col = lambda shift: pl.BlockSpec((span, BLK), lambda p: (0, p + shift))
    return pl.pallas_call(
        attend_body,
        grid=(pairs,),
        in_specs=[
            pl.BlockSpec(memory_space=pltpu.SMEM),
            col(0),
            col(pairs),
            col(2 * pairs),
            col(0),
            col(pairs),
        ],
        out_specs=[col(0), pl.BlockSpec((span, 2 * BLK), lambda p: (0, p))],
        out_shape=[
            jax.ShapeDtypeStruct((span, D), BF),
            jax.ShapeDtypeStruct((span, 2 * D), BF),
        ],
        compiler_params=params(),
        cost_estimate=cost(40 * span * span * D, 8 * MIB),
        name="attention",
    )(live, own, own, own, other, other)


def attend_back_body(
    live_ref, aug_ref, ko_ref, vo_ref, kx_ref, vx_ref, at_ref, g_ref, dq_ref, own_ref, other_ref
):
    span = at_ref.shape[0]
    grads = g_ref[...].astype(F32)
    product = grads * at_ref[...].astype(F32)
    keeps, g_augs, q_augs = [], [], []
    for head in range(2):
        keep, dead_lane, terms = lane_masks(head)
        delta = jnp.sum(product * keep, -1, keepdims=True)
        parts = three_terms(-delta)
        stats = sum(part * lane for part, lane in zip(parts, terms))
        g_augs.append((grads * keep + stats).astype(BF))
        q_augs.append(aug_ref[:, head * BLK : (head + 1) * BLK])
    d_query = [None, None]
    for k_ref, v_ref, out_ref, live in (
        (ko_ref, vo_ref, own_ref, live_ref[0]),
        (kx_ref, vx_ref, other_ref, live_ref[1]),
    ):
        bias = key_bias(span, live)
        keys = k_ref[...]
        keys_f, values_f = keys.astype(F32), v_ref[...].astype(F32)
        d_keys = d_values = None
        for head in range(2):
            keep, dead_lane, terms = lane_masks(head)
            ones = terms[0] + terms[1] + terms[2]
            k_aug = (keys_f * keep + (bias * dead_lane + ones)).astype(BF)
            v_aug = (values_f * keep + ones).astype(BF)
            probs = jnp.exp(mul_nt(k_aug, q_augs[head]))
            d_scores = (probs * mul_nt(v_aug, g_augs[head])).astype(BF)
            value_part = mul_nn(probs.astype(BF), g_augs[head]) * keep
            key_part = mul_nn(d_scores, q_augs[head]) * keep
            query_part = mul_tn(d_scores, keys) * (keep * score_scale)
            d_query[head] = query_part if d_query[head] is None else d_query[head] + query_part
            d_values = value_part if d_values is None else d_values + value_part
            d_keys = key_part if d_keys is None else d_keys + key_part
        out_ref[0] = d_keys.astype(out_ref.dtype)
        out_ref[1] = d_values.astype(out_ref.dtype)
    dq_ref[...] = (d_query[0] + d_query[1]).astype(BF)


def attend_back(live, aug, own, other, attended, grads):
    span = own.shape[0]
    pairs = D // BLK
    col = lambda shift: pl.BlockSpec((span, BLK), lambda p: (0, p + shift))
    pair_out = pl.BlockSpec((2, span, BLK), lambda p: (0, 0, p))
    return pl.pallas_call(
        attend_back_body,
        grid=(pairs,),
        in_specs=[
            pl.BlockSpec(memory_space=pltpu.SMEM),
            pl.BlockSpec((span, 2 * BLK), lambda p: (0, p)),
            col(pairs),
            col(2 * pairs),
            col(0),
            col(pairs),
            col(0),
            col(0),
        ],
        out_specs=[col(0), pair_out, pair_out],
        out_shape=[
            jax.ShapeDtypeStruct((span, D), BF),
            jax.ShapeDtypeStruct((2, span, D), F32),
            jax.ShapeDtypeStruct((2, span, D), BF),
        ],
        compiler_params=params(),
        cost_estimate=cost(60 * span * span * D, 12 * MIB),
        name="attention_backward",
    )(live, aug, own, own, other, other, attended, grads)


def feed_body(
    live_ref,
    tokens_ref,
    attended_ref,
    cot_ref,
    gains_ref,
    wo_ref,
    wu_ref,
    wd_ref,
    layer_ref,
    rest_ref,
    gm_ref,
    ga_ref,
    gain_ref,
    unit,
    inv,
    normed,
    top,
    acc_out,
    acc_back,
    up_stage,
    down_stage,
    out_stage,
    sems,
    out_sem,
):
    step = pl.program_id(0)
    place = step % 2
    side, width = up_stage.shape[1], up_stage.shape[2]
    per_tile = side * width
    up_first = side * side
    down_first = up_first + side * FF // BLK

    def drain(which):
        pltpu.make_async_copy(up_stage.at[which], up_stage.at[which], sems.at[0, which]).wait()
        pltpu.make_async_copy(down_stage.at[which], down_stage.at[which], sems.at[1, which]).wait()
    span = tokens_ref.shape[0]

    @pl.when(step == 0)
    def _():
        weight = join_tile(wo_ref)
        middle = tokens_ref[...].astype(F32) + mul_nn(attended_ref[...], weight)
        unit_vals, inv_std = normalize(middle)
        unit[...] = unit_vals
        inv[...] = inv_std
        normed[...] = (unit_vals * gains_ref[1:2]).astype(BF)
        row = lax.broadcasted_iota(jnp.int32, (span, 1), 0)
        top[...] = jnp.where(row < live_ref[2], cot_ref[...].astype(F32), 0.0).astype(BF)
        acc_out[...] = middle
        acc_back[...] = jnp.zeros_like(acc_back)

    w_up = join_tile(wu_ref)
    w_down = join_tile(wd_ref)
    hidden = mul_nn(normed[...], w_up)
    grad_act = mul_nt(top[...], w_down)
    erf_part = 0.5 * (1.0 + lax.erf(hidden * 0.7071067811865476))
    activated = (hidden * erf_part).astype(BF)
    slope = erf_part + hidden * jnp.exp(-0.5 * hidden * hidden) * 0.3989422804014327
    grad_hidden = (grad_act * slope).astype(BF)
    acc_out[...] += mul_nn(activated, w_down)
    acc_back[...] += mul_nt(grad_hidden, w_up)

    @pl.when(step >= 2)
    def _():
        drain(place)

    split_flat(down_stage.at[place], mul_tn(activated, top[...]))
    dest = rest_ref.at[pl.ds(down_first + step * per_tile, per_tile)]
    pltpu.make_async_copy(down_stage.at[place], dest, sems.at[1, place]).start()
    split_tile(up_stage.at[place], mul_tn(normed[...], grad_hidden))
    for i in range(side):
        dest = rest_ref.at[pl.ds(up_first + i * (FF // BLK) + step * width, width)]
        pltpu.make_async_copy(up_stage.at[place, i], dest, sems.at[0, place]).start()

    @pl.when(step == pl.num_programs(0) - 1)
    def _():
        layer_ref[...] = acc_out[...].astype(BF)
        unit_vals = unit[...]
        back = acc_back[...]
        gain_ref[...] = jnp.sum(back * unit_vals, 0, keepdims=True)
        grad_middle = top[...].astype(F32) + norm_back(back * gains_ref[1:2], unit_vals, inv[...])
        gm_ref[...] = grad_middle
        back_middle = grad_middle.astype(BF)
        split_flat(out_stage, mul_tn(attended_ref[...], back_middle))
        out_copy = pltpu.make_async_copy(out_stage, rest_ref.at[pl.ds(0, up_first)], out_sem)
        out_copy.start()
        ga_ref[...] = mul_nt(back_middle, join_tile(wo_ref)).astype(BF)
        drain(1 - place)
        drain(place)
        out_copy.wait()


def feed(live, tokens, attended, cotangent, gains, weights):
    span = tokens.shape[0]
    side, width = D // BLK, COLS // BLK
    whole = lambda j: (0, 0)
    act = pl.BlockSpec((span, D), whole)
    per_row = weights.reshape(-1, side, BLK, BLK)
    per_up = weights.reshape(-1, FF // BLK, BLK, BLK)
    out_row = (3 * side * side) // side // side
    up_row = 4 * side * side // (FF // BLK) // side
    down_row = (4 * side * side + side * FF // BLK) // side // width
    return pl.pallas_call(
        feed_body,
        grid=(FF // COLS,),
        in_specs=[
            pl.BlockSpec(memory_space=pltpu.SMEM),
            act,
            act,
            act,
            pl.BlockSpec((2, D), whole),
            pl.BlockSpec((side, side, BLK, BLK), lambda j: (out_row, 0, 0, 0)),
            pl.BlockSpec((side, width, BLK, BLK), lambda j: (up_row, j, 0, 0)),
            pl.BlockSpec((width, side, BLK, BLK), lambda j: (down_row + j, 0, 0, 0)),
        ],
        out_specs=[
            act,
            pl.BlockSpec(memory_space=pltpu.HBM),
            act,
            act,
            pl.BlockSpec((1, D), whole),
        ],
        out_shape=[
            jax.ShapeDtypeStruct((span, D), BF),
            jax.ShapeDtypeStruct((side * side + 2 * side * (FF // BLK), BLK, BLK), BF),
            jax.ShapeDtypeStruct((span, D), F32),
            jax.ShapeDtypeStruct((span, D), BF),
            jax.ShapeDtypeStruct((1, D), F32),
        ],
        scratch_shapes=[
            pltpu.VMEM((span, D), F32),
            pltpu.VMEM((span, 1), F32),
            pltpu.VMEM((span, D), BF),
            pltpu.VMEM((span, D), BF),
            pltpu.VMEM((span, D), F32),
            pltpu.VMEM((span, D), F32),
            pltpu.VMEM((2, side, width, BLK, BLK), BF),
            pltpu.VMEM((2, side * width, BLK, BLK), BF),
            pltpu.VMEM((side * side, BLK, BLK), BF),
            pltpu.SemaphoreType.DMA((2, 2)),
            pltpu.SemaphoreType.DMA,
        ],
        compiler_params=params(),
        cost_estimate=cost(14 * span * D * FF, 50 * MIB),
        name="feed_forward",
    )(live, tokens, attended, cotangent, gains, per_row, per_up, per_row)


def query_body(tokens_ref, gains_ref, dq_ref, w_ref, grad_ref, acc_ref, normed):
    step = pl.program_id(0)

    @pl.when(step == 0)
    def _():
        unit_vals, _ = normalize(tokens_ref[...].astype(F32))
        normed[...] = (unit_vals * gains_ref[0:1]).astype(BF)
        acc_ref[...] = jnp.zeros_like(acc_ref)

    grad = dq_ref[...]
    acc_ref[...] += mul_nt(grad, join_tile(w_ref))
    split_tile(grad_ref, mul_tn(normed[...], grad))


def query_back(tokens, gains, d_query, weights):
    span = tokens.shape[0]
    side, width = D // BLK, COLS // BLK
    whole = lambda j: (0, 0)
    act = pl.BlockSpec((span, D), whole)
    tile = pl.BlockSpec((side, width, BLK, BLK), lambda j: (0, j, 0, 0))
    return pl.pallas_call(
        query_body,
        grid=(D // COLS,),
        in_specs=[
            act,
            pl.BlockSpec((2, D), whole),
            pl.BlockSpec((span, COLS), lambda j: (0, j)),
            tile,
        ],
        out_specs=[tile, act],
        out_shape=[
            jax.ShapeDtypeStruct((side, side, BLK, BLK), BF),
            jax.ShapeDtypeStruct((span, D), F32),
        ],
        scratch_shapes=[pltpu.VMEM((span, D), BF)],
        compiler_params=params(),
        cost_estimate=cost(4 * span * D * D, 8 * MIB),
        name="query_backward",
    )(tokens, gains, d_query, weights.reshape(-1, 3 * side, BLK, BLK))


def input_body(
    tokens_ref, gains_ref, own_ref, recv_ref, acc_ref, gm_ref, w_ref, grad_ref, out_ref, gain_ref,
    unit, inv, normed, acc
):
    step = pl.program_id(0)

    @pl.when(step == 0)
    def _():
        unit_vals, inv_std = normalize(tokens_ref[...].astype(F32))
        unit[...] = unit_vals
        inv[...] = inv_std
        normed[...] = (unit_vals * gains_ref[0:1]).astype(BF)
        acc[...] = acc_ref[...]

    grad = (own_ref[0] + recv_ref[0].astype(F32)).astype(BF)
    acc[...] += mul_nt(grad, join_tile(w_ref))
    split_tile(grad_ref, mul_tn(normed[...], grad))

    @pl.when(step == pl.num_programs(0) - 1)
    def _():
        unit_vals = unit[...]
        back = acc[...]
        gain_ref[...] = jnp.sum(back * unit_vals, 0, keepdims=True)
        out_ref[...] = (
            gm_ref[...] + norm_back(back * gains_ref[0:1], unit_vals, inv[...])
        ).astype(BF)


def input_back(tokens, gains, own, received, partial, grad_middle, weights):
    span = tokens.shape[0]
    side, width = D // BLK, COLS // BLK
    per = D // COLS
    whole = lambda j: (0, 0)
    act = pl.BlockSpec((span, D), whole)
    part = pl.BlockSpec((1, span, COLS), lambda j: (j // per, 0, j % per))
    return pl.pallas_call(
        input_body,
        grid=(2 * per,),
        in_specs=[
            act,
            pl.BlockSpec((2, D), whole),
            part,
            part,
            act,
            act,
            pl.BlockSpec((side, width, BLK, BLK), lambda j: (0, j + per, 0, 0)),
        ],
        out_specs=[
            pl.BlockSpec((side, width, BLK, BLK), lambda j: (0, j, 0, 0)),
            act,
            pl.BlockSpec((1, D), whole),
        ],
        out_shape=[
            jax.ShapeDtypeStruct((side, 2 * side, BLK, BLK), BF),
            jax.ShapeDtypeStruct((span, D), BF),
            jax.ShapeDtypeStruct((1, D), F32),
        ],
        scratch_shapes=[
            pltpu.VMEM((span, D), F32),
            pltpu.VMEM((span, 1), F32),
            pltpu.VMEM((span, D), BF),
            pltpu.VMEM((span, D), F32),
        ],
        compiler_params=params(),
        cost_estimate=cost(8 * span * D * D, 20 * MIB),
        name="input_backward",
    )(
        tokens, gains, own, received, partial, grad_middle,
        weights.reshape(-1, 3 * side, BLK, BLK),
    )


def source_numbers():
    side = D // BLK
    numbers = np.arange(3 * side * side + side * side + 2 * side * (FF // BLK), dtype=np.int32)
    row, col = np.divmod(numbers[: 3 * side * side], 3 * side)
    numbers[: 3 * side * side] = np.where(
        col < side, row * side + col, side * side + row * 2 * side + col - side
    )
    return numbers


def gather_body(first, bounds, table, *refs):
    sources = refs[:6]
    out_ref, stage, sems = refs[6:]
    step, steps = pl.program_id(0), pl.num_programs(0)
    count = stage.shape[1] // 2

    def fetch(which, slot):
        start = first + which * count
        for i in range(count):
            number = table[start + i]
            for low, high, own, other in zip(bounds, bounds[1:], sources[:3], sources[3:]):

                @pl.when((number >= low) & (number < high))
                def _():
                    for src, at in ((own, i), (other, count + i)):
                        pltpu.make_async_copy(
                            src.at[number - low], stage.at[slot, at], sems.at[slot]
                        ).start()

    @pl.when(step == 0)
    def _():
        fetch(0, 0)

    @pl.when(step + 1 < steps)
    def _():
        fetch(step + 1, (step + 1) % 2)

    slot = step % 2
    pltpu.make_async_copy(stage.at[slot], stage.at[slot], sems.at[slot]).wait()
    total = stage[slot, :count].astype(F32) + stage[slot, count:].astype(F32)
    out_ref[...] = total.astype(BF)


def gather_sums(table, first, count, own, other):
    hbm = pl.BlockSpec(memory_space=pltpu.HBM)
    steps = 4
    part = count // steps
    bounds = np.cumsum([0] + [src.shape[0] for src in own]).tolist()
    return pl.pallas_call(
        functools.partial(gather_body, first, bounds),
        grid=(steps,),
        in_specs=[pl.BlockSpec(memory_space=pltpu.SMEM)] + [hbm] * 6,
        out_specs=pl.BlockSpec((part, BLK, BLK), lambda i: (i, 0, 0)),
        out_shape=jax.ShapeDtypeStruct((count, BLK, BLK), BF),
        scratch_shapes=[
            pltpu.VMEM((2, 2 * part, BLK, BLK), BF),
            pltpu.SemaphoreType.DMA((2,)),
        ],
        compiler_params=params(),
        cost_estimate=cost(0, 6 * count * BLK * BLK),
        name="gradient_sums",
    )(table, *own, *other)


def two_terms(values):
    high = values.astype(BF)
    return high, (values - high.astype(F32)).astype(BF)


def update_body(count, *refs):
    parts = refs[:count]
    m_ref, sl_ref, sr_ref, rl_ref, rr_ref, g_out, sl_out, sr_out, m_out = refs[count:]

    def long_left(terms, axis):
        return jnp.concatenate([terms[0], terms[0], terms[1]], axis)

    def long_right(terms, axis):
        return jnp.concatenate([terms[0], terms[1], terms[0]], axis)

    for i in range(g_out.shape[0]):
        total = sum(part[i].astype(F32) for part in parts)
        g_out[i] = total
        grad = two_terms(total)
        sl_out[i] = sl_ref[i] + mul_nt(long_left(grad, 1), long_right(grad, 1))
        tall = long_right(grad, 0)
        sr_out[i] = sr_ref[i] + mul_tn(long_left(grad, 0), tall)
        inner = mul_nn(long_left(two_terms(rl_ref[i]), 1), tall)
        direction = mul_nn(
            long_left(two_terms(inner), 1), long_right(two_terms(rr_ref[i]), 0)
        )
        master = m_ref[i]
        scale = jnp.sqrt(jnp.mean(master * master, keepdims=True) + 1e-06)
        scale = scale * lax.rsqrt(jnp.mean(direction * direction, keepdims=True) + 1e-06)
        m_out[i] = master - 0.3 * scale * direction


def update(parts, master, stat_left, stat_right, root_left, root_right):
    count = master.shape[0]
    group = 3 if count % 3 == 0 else 1
    block = pl.BlockSpec((group, BLK, BLK), lambda i: (i, 0, 0))
    shape = jax.ShapeDtypeStruct(master.shape, F32)
    return pl.pallas_call(
        functools.partial(update_body, len(parts)),
        grid=(count // group,),
        in_specs=[block] * (len(parts) + 5),
        out_specs=[block] * 4,
        out_shape=[shape] * 4,
        compiler_params=params(),
        cost_estimate=cost(48 * count * BLK**3, 15 * MIB),
        name="block_update",
    )(*parts, master, stat_left, stat_right, root_left, root_right)


def pair_moves():
    moves_same, moves_cross = [], []
    for z in range(4):
        for c in range(2):
            for moves, bit in ((moves_same, z % 2), (moves_cross, 1 - z % 2)):
                moves.append((z * 2 + c, (2 * c + bit) * 2 + z // 2))
    return moves_same, moves_cross


def row_part(values, which):
    return lax.dynamic_index_in_dim(values, which, 0, False)


def move_rows(values, crossed, back=False):
    moves = pair_moves()[crossed]
    return lax.ppermute(values, ("seq", "core"), [(b, a) for a, b in moves] if back else moves)


def in_order(kept, crossed, parity):
    return jnp.where(parity == 0, kept, crossed), jnp.where(parity == 0, crossed, kept)


def spread_rows(values, parity):
    kept = move_rows(row_part(values, parity), False)
    crossed = move_rows(row_part(values, 1 - parity), True)
    return jnp.concatenate(in_order(kept, crossed, parity), 0)


def gather_rows(values, parity):
    parts = values.reshape(2, values.shape[0] // 2, values.shape[1])
    kept = move_rows(row_part(parts, parity), False, True)
    crossed = move_rows(row_part(parts, 1 - parity), True, True)
    return jnp.stack(in_order(kept, crossed, parity), 0)


def swap_cores(values):
    return lax.ppermute(values, "core", [(0, 1), (1, 0)])


def chip_orders(chips):
    bits = [1 << i for i in range(chips.bit_length() - 1)]
    return bits, bits[::-1]


def offsets(order):
    result = [0]
    for bit in order:
        result = result + [o ^ bit for o in result]
    return result


def place_lists(chips, owned, planes):
    shape = (2, planes, chips, owned)
    by_core = np.array([offsets(order) for order in chip_orders(chips)], np.int32)
    grid = np.indices(shape).astype(np.int32).reshape(4, 2, -1)
    offset = np.broadcast_to(by_core[:, None, :, None], shape).reshape(2, -1)
    return grid[1, 0], offset, grid[3, 0]


def swap_chips(values, bits):
    chips = lax.axis_size("chip")
    moves = [(i * 2 + c, (i ^ bits[c]) * 2 + c) for i in range(chips) for c in range(2)]
    return lax.ppermute(values, ("chip", "core"), moves)


def move_planes(values, shift):
    planes = lax.axis_size("seq")
    return lax.ppermute(values, "seq", [(i, (i + shift) % planes) for i in range(planes)])


def after(value, *deps):
    return lax.optimization_barrier((value, *deps))[0]


def together(*values):
    return lax.optimization_barrier(values)


def chip_steps():
    return list(zip(*chip_orders(lax.axis_size("chip"))))


def finish_pieces(pieces):
    for bits in chip_steps()[2:]:
        joined = jnp.concatenate(pieces, 0)
        pieces = [joined, swap_chips(joined, bits)]
    return pieces


def add_halves(kept, came):
    return (kept.astype(F32) + came.astype(F32)).astype(BF)


def pack_terms(values):
    high = lax.optimization_barrier(values.astype(BF))
    low = (values - high.astype(F32)).astype(BF)
    terms = jnp.stack([high, low]).reshape(-1, BLK)
    return jnp.pad(terms, ((0, BLK - terms.shape[0]), (0, 0)))[None]


def unpack_terms(blocks, shape):
    terms = blocks.reshape(-1, BLK, BLK)[:, : 2 * shape[0] * shape[1] // BLK]
    terms = terms.reshape(-1, 2, *shape).astype(F32)
    return terms[:, 0] + terms[:, 1]


def finish_sums(keep, send, riders):
    for bits in chip_steps()[::-1][1:-1]:
        count = keep.shape[0] // 2
        came = swap_chips(with_riders(send, riders), bits)
        riders = more_riders(riders, came, keep.shape[0])
        send = add_halves(keep[count:], came[count : 2 * count])
        keep = add_halves(keep[:count], came[:count])
    return keep, send, riders


def with_riders(send, riders):
    return send if riders is None else jnp.concatenate([send, riders], 0)


def more_riders(riders, came, count):
    return riders if riders is None else jnp.concatenate([riders, came[count:]], 0)


def by_chip(riders, me, core):
    chips = lax.axis_size("chip")
    ranks = np.array([np.argsort(offsets(order[::-1])) for order in chip_orders(chips)], np.int32)
    rank = jnp.asarray(ranks)[core][me ^ jnp.arange(chips, dtype=jnp.int32)]
    return riders.reshape(chips, -1, BLK, BLK)[rank]


def local(
    tokens,
    cotangent,
    lengths,
    owner_perm,
    master,
    norm_gains,
    stat_left,
    stat_right,
    root_left,
    root_right,
    moment_first,
    moment_second,
):
    core = lax.axis_index("core")
    place_z = lax.axis_index("seq")
    parity = place_z % 2
    block_count = owner_perm.shape[0]
    owned = master.shape[0]
    half = block_count // 2

    chips, planes = lax.axis_size("chip"), lax.axis_size("seq")
    me = lax.axis_index("chip")

    pair_lengths = jnp.stack([lengths, swap_cores(lengths)])
    pair_lengths = jnp.where(core == 0, pair_lengths, pair_lengths[::-1]).reshape(-1)
    length = lax.dynamic_index_in_dim(pair_lengths, place_z, 0, False)
    span = tokens.shape[0] * tokens.shape[1]
    live = jnp.stack([length - core * span, length - (1 - core) * span, length - core * span])

    distance, offset, slot = place_lists(chips, owned, planes)
    offset = jnp.where(core == 0, offset, offset[::-1])
    device = ((place_z - distance) % planes * chips + (me ^ offset)) * 2
    device = device + jnp.stack([core, 1 - core])[:, None]
    table = owner_perm[(device * owned + slot).reshape(-1)]
    sums_table = jnp.asarray(source_numbers())[table[:half]]

    shard = master.astype(BF)
    first_bits, second_bits = chip_steps()[:2]
    per_plane = chips * owned
    rows = (row_part(tokens, parity), row_part(tokens, 1 - parity))
    moved_rows, cross, far, weights = [], [], [], None
    came, turned = swap_chips(shard, first_bits), swap_chips(shard, second_bits)
    next_shard = move_planes(shard, 1)
    pieces = [[shard, came, turned]]
    for k in range(1, planes):
        ready = ()
        if k == 1:
            ready = (live, table, sums_table)
        if k == planes - 1:
            ready = (far[0],)
        this_shard, came, turned, row, *done = together(
            next_shard, came, turned, rows[min(k, 2) - 1], *cross[-1:], *moved_rows[-1:], *ready
        )
        if k > 1:
            pieces[k - 2].append(done[0])
        cross.append(swap_chips(came, second_bits))
        came, turned = swap_chips(this_shard, first_bits), swap_chips(this_shard, second_bits)
        pieces.append([this_shard, came, turned])
        if k < planes - 1:
            next_shard = move_planes(this_shard, 1)
            moved_rows.append(move_rows(row, len(moved_rows) == 1))
        if k > 1:
            near = jnp.concatenate(finish_pieces(pieces[k - 2]), 0)
            far.append(swap_cores(near))
            weights = place_blocks(table, (k - 2) * per_plane, near, far[-1], weights)
    own_tokens = jnp.concatenate(in_order(*moved_rows, parity), 0)
    came, _, done, *_ = together(came, turned, cross[-1], far[-1], weights)
    pieces[-2].append(done)
    pieces[-1].append(swap_chips(came, second_bits))
    near = jnp.concatenate(finish_pieces(pieces[-2]), 0)
    far.append(swap_cores(near))
    weights = place_blocks(table, (planes - 2) * per_plane, near, far[-1], weights)
    other_tokens = swap_cores(own_tokens)
    first = (planes - 1) * per_plane
    last_pieces = finish_pieces(pieces[-1])
    last_pieces[-1], *_ = together(last_pieces[-1], weights, other_tokens)
    for piece in last_pieces:
        weights = place_blocks(table, first, piece, swap_cores(piece), weights)
        first += piece.shape[0]
    own_cot = spread_rows(after(cotangent, weights), parity)

    own_qkv, other_kv = project(own_tokens, other_tokens, norm_gains, weights)
    attended, q_aug = attend(live, own_qkv, other_kv)
    layer, g_rest, grad_middle, grad_attended, gain_second = feed(
        live, own_tokens, attended, own_cot, norm_gains, weights
    )
    other_rest = swap_cores(g_rest)
    layer_out = gather_rows(layer, parity)
    d_query, d_own, d_other = attend_back(live, q_aug, own_qkv, other_kv, attended, grad_attended)
    received = swap_cores(after(d_other, layer_out))
    flat = lambda g: g.reshape(-1, BLK, BLK)
    g_query, partial = query_back(own_tokens, norm_gains, d_query, weights)
    g_query = flat(g_query)
    other_query = swap_cores(g_query)
    g_kv, grad_in, gain_first = input_back(
        own_tokens, norm_gains, d_own, received, partial, grad_middle, weights
    )
    g_kv = flat(g_kv)
    gain_part = jnp.concatenate([gain_first, gain_second], 0)
    mine = pack_terms(gain_part)
    other_kv_grad = swap_cores(after(g_kv, other_query))
    theirs = swap_cores(mine)
    pair = jnp.concatenate([mine, theirs], 0)
    riders = jnp.where(core == 0, pair, pair[::-1])
    own_grads = (g_query, g_kv, g_rest)
    other_grads = (other_query, other_kv_grad, other_rest)
    half_plane = per_plane // 2
    last_bits, before_bits = chip_steps()[-1], chip_steps()[0]
    halves = grad_in.reshape(2, span // 2, D)
    rows = [row_part(halves, parity), row_part(halves, 1 - parity)]
    moved_rows, lows, sent, passed, riders_z = [], [], None, None, []

    def sums(k, part, held):
        first = k * per_plane + part * half_plane
        return gather_sums(held, first, half_plane, own_grads, other_grads)

    order = list(range(planes))[::-1]
    high = sums(order[0], 1, sums_table)
    held = sums_table
    for turn in range(planes + 2):
        group, moves = [], []
        if turn < planes:
            group.append(with_riders(high, riders if turn == 0 else None))
            moves.append(lambda v: swap_chips(v, last_bits))
        if 1 <= turn <= planes:
            group.append(with_riders(sent, riders if turn == 1 else None))
            moves.append(lambda v: swap_chips(v, before_bits))
        if 2 <= turn <= planes:
            group.append(part)
            moves.append(lambda v: move_planes(v, -1))
        if turn < 2:
            group.append(rows[turn])
            moves.append(lambda v: move_rows(v, len(moved_rows) == 1, True))
        if turn == 3:
            group += [rider] * (planes - 1)
            moves += [functools.partial(move_planes, shift=-k) for k in range(1, planes)]
        if turn == planes + 1:
            break
        came = [move(value) for move, value in zip(moves, together(*group))]
        if turn < 2:
            moved_rows.append(came.pop())
        if turn == 3:
            riders_z, came = came[-(planes - 1) :], came[: -(planes - 1)]
        if turn >= 2:
            passed = came.pop()
        if turn < planes:
            low = sums(order[turn], 0, after(held, high))
            if turn + 1 < planes:
                high = sums(order[turn + 1], 1, after(held, low))
            held = after(sums_table, *came)
        if turn >= 1:
            last = came[-1]
            kept = keep_before
            if turn == 1:
                riders = more_riders(riders, last, kept.shape[0])
                plane_gain = by_chip(riders, me, core)
                plane_gain = jnp.sum(unpack_terms(plane_gain, gain_part.shape), 0)
                rider = pack_terms(plane_gain)
            total = kept.astype(F32) + last[: kept.shape[0]].astype(F32)
            if turn < planes:
                part = total if passed is None else total + passed.astype(F32)
                part = part.astype(BF)
            else:
                parts = [total.astype(BF), passed]
        if turn < planes:
            first_came, count = came[0], half_plane // 2
            if turn == 0:
                riders = more_riders(riders, first_came, half_plane)
            sent = add_halves(low[count:], first_came[count:half_plane])
            keep = add_halves(low[:count], first_came[:count])
            keep_before, sent, grown = finish_sums(keep, sent, riders if turn == 0 else None)
            riders = grown if turn == 0 else riders
    input_grad = jnp.stack(in_order(*moved_rows, parity), 0).astype(F32)
    planes_gain = [unpack_terms(each, gain_part.shape)[0] for each in (rider, *riders_z)]
    turned = (jnp.arange(planes, dtype=jnp.int32) - place_z) % planes
    gain_grad = jnp.sum(jnp.stack(planes_gain)[turned], 0)
    grad_blocks, stat_left_new, stat_right_new, master_new = update(
        parts, master, stat_left, stat_right, root_left, root_right
    )
    first_new = 0.9 * moment_first + 0.1 * gain_grad
    second_new = 0.999 * moment_second + 0.001 * gain_grad * gain_grad
    first_hat = first_new / (1.0 - 0.9**STEP)
    second_hat = second_new / (1.0 - 0.999**STEP)
    gains_new = norm_gains - 0.5 * first_hat / (jnp.sqrt(second_hat) + 1e-08)
    return (
        layer_out,
        input_grad,
        grad_blocks,
        stat_left_new,
        stat_right_new,
        master_new,
        first_new,
        second_new,
        gains_new,
    )


def solution(mesh):
    seq_size, rows_size = mesh.shape["seq"], mesh.shape["rows"]
    mesh = Mesh(mesh.devices.reshape(seq_size, rows_size // 2, 2), ("seq", "chip", "core"))
    activation = P(("chip", "core"), "seq", None)
    blocks = P(("seq", "chip", "core"), None, None)
    return jax.shard_map(
        local,
        mesh=mesh,
        in_specs=(
            activation, activation, P(("chip", "core")), P(), blocks, P(),
            blocks, blocks, blocks, blocks, P(), P(),
        ),
        out_specs=(activation, activation, blocks, blocks, blocks, blocks, P(), P(), P()),
        check_vma=False,
    )
```

```python
import functools
import jax
import jax.numpy as jnp
import numpy as np
from jax import lax
from jax.experimental import pallas as pl
from jax.experimental.pallas import tpu as pltpu
from jax.sharding import Mesh
from jax.sharding import PartitionSpec as P

D = 1024
HD = 64
FF = 4096
BLK = 128
STEP = 10
COLS = 512
BF = jnp.bfloat16
F32 = jnp.float32
MIB = 1024 * 1024

norm_eps = 1e-05
score_scale = 0.125
masked_score = -1e30


def params(limit=56):
    return pltpu.CompilerParams(vmem_limit_bytes=limit * MIB)


def cost(flops, nbytes):
    return pl.CostEstimate(flops=int(flops), bytes_accessed=int(nbytes), transcendentals=0)


def mul_nn(left, right):
    return jnp.dot(left, right, preferred_element_type=F32)


def mul_nt(left, right):
    return lax.dot_general(left, right, (((1,), (1,)), ((), ())), preferred_element_type=F32)


def mul_tn(left, right):
    return lax.dot_general(left, right, (((0,), (0,)), ((), ())), preferred_element_type=F32)


def join_tile(ref):
    rows, cols = ref.shape[0], ref.shape[1]
    return jnp.concatenate([ref[:, j].reshape(rows * BLK, BLK) for j in range(cols)], axis=1)


def split_tile(ref, matrix):
    rows, cols = ref.shape[0], ref.shape[1]
    for j in range(cols):
        ref[:, j] = matrix[:, j * BLK : (j + 1) * BLK].reshape(rows, BLK, BLK).astype(ref.dtype)


def split_flat(ref, matrix):
    cols = matrix.shape[1] // BLK
    for i in range(matrix.shape[0] // BLK):
        for j in range(cols):
            block = matrix[i * BLK : (i + 1) * BLK, j * BLK : (j + 1) * BLK]
            ref[i * cols + j] = block.astype(ref.dtype)


def normalize(values):
    row_mean = jnp.mean(values, -1, keepdims=True)
    centered = values - row_mean
    row_var = jnp.mean(centered * centered, -1, keepdims=True)
    inv_std = lax.rsqrt(row_var + norm_eps)
    return centered * inv_std, inv_std


def norm_back(gradient, unit_vals, inv_std):
    grad_mean = jnp.mean(gradient, -1, keepdims=True)
    cross_mean = jnp.mean(gradient * unit_vals, -1, keepdims=True)
    return inv_std * (gradient - grad_mean - unit_vals * cross_mean)


def place_body(first, table, near_ref, far_ref, *refs):
    out_ref, sem = refs[-2:]
    count = near_ref.shape[0]
    half = table.shape[0] // 2
    for start, src in ((first, near_ref), (half + first, far_ref)):
        for slot in range(count):
            pltpu.make_async_copy(src.at[slot], out_ref.at[table[start + slot]], sem).start()
    done = out_ref.at[pl.ds(0, 2 * count)]
    pltpu.make_async_copy(done, done, sem).wait()


def place_blocks(table, first, near, far, kept):
    smem = pl.BlockSpec(memory_space=pltpu.SMEM)
    hbm = pl.BlockSpec(memory_space=pltpu.HBM)
    vmem = pl.BlockSpec(memory_space=pltpu.VMEM)
    kept = () if kept is None else (kept,)
    return pl.pallas_call(
        functools.partial(place_body, first),
        out_shape=jax.ShapeDtypeStruct((table.shape[0], BLK, BLK), BF),
        in_specs=[smem, vmem, vmem] + [hbm] * len(kept),
        out_specs=hbm,
        scratch_shapes=[pltpu.SemaphoreType.DMA],
        input_output_aliases={3: 0} if kept else {},
        compiler_params=params(44),
        cost_estimate=cost(0, 4 * near.size * 2),
        name="place_weights",
    )(table, near, far, *kept)


def qkv_body(own_ref, other_ref, gains_ref, w_ref, own_out, other_out, normed):
    step = pl.program_id(0)
    span = own_ref.shape[0]

    @pl.when(step == 0)
    def _():
        gain = gains_ref[0:1]
        normed[:span] = (normalize(own_ref[...].astype(F32))[0] * gain).astype(BF)
        normed[span:] = (normalize(other_ref[...].astype(F32))[0] * gain).astype(BF)

    weight = join_tile(w_ref)
    own_out[...] = mul_nn(normed[:span], weight).astype(BF)

    @pl.when(step >= D // COLS)
    def _():
        other_out[...] = mul_nn(normed[span:], weight).astype(BF)


def project(own, other, gains, weights):
    span = own.shape[0]
    skip = D // COLS
    whole = lambda j: (0, 0)
    return pl.pallas_call(
        qkv_body,
        grid=(3 * D // COLS,),
        in_specs=[
            pl.BlockSpec((span, D), whole),
            pl.BlockSpec((span, D), whole),
            pl.BlockSpec((2, D), whole),
            pl.BlockSpec((D // BLK, COLS // BLK, BLK, BLK), lambda j: (0, j, 0, 0)),
        ],
        out_specs=[
            pl.BlockSpec((span, COLS), lambda j: (0, j)),
            pl.BlockSpec((span, COLS), lambda j: (0, jnp.maximum(j - skip, 0))),
        ],
        out_shape=[
            jax.ShapeDtypeStruct((span, 3 * D), BF),
            jax.ShapeDtypeStruct((span, 2 * D), BF),
        ],
        scratch_shapes=[pltpu.VMEM((2 * span, D), BF)],
        compiler_params=params(),
        cost_estimate=cost(10 * span * D * D, 12 * MIB),
        name="qkv_projection",
    )(own, other, gains, weights.reshape(-1, 3 * D // BLK, BLK, BLK))


def lane_masks(head):
    lane = lax.broadcasted_iota(jnp.int32, (1, BLK), 1)
    first = HD * (1 - head)
    keep = (lane // HD == head).astype(F32)
    dead_lane = (lane == first).astype(F32)
    terms = [(lane == first + 1 + i).astype(F32) for i in range(3)]
    return keep, dead_lane, terms


def three_terms(values):
    high = values.astype(BF).astype(F32)
    rest = values - high
    middle = rest.astype(BF).astype(F32)
    return high, middle, rest - middle


def key_bias(span, live_count):
    row = lax.broadcasted_iota(jnp.int32, (span, 1), 0)
    return jnp.where(row < live_count, 0.0, masked_score).astype(F32)


def attend_body(live_ref, q_ref, ko_ref, vo_ref, kx_ref, vx_ref, out_ref, aug_ref):
    span = q_ref.shape[0]
    bias_own = key_bias(span, live_ref[0])
    bias_other = key_bias(span, live_ref[1])
    queries = q_ref[...].astype(F32) * score_scale
    k_own, k_other = ko_ref[...].astype(F32), kx_ref[...].astype(F32)
    results = []
    for head in range(2):
        keep, dead_lane, terms = lane_masks(head)
        q_head = (queries * keep + dead_lane).astype(BF)
        s_own = mul_nt(q_head, (k_own * keep + bias_own * dead_lane).astype(BF))
        s_other = mul_nt(q_head, (k_other * keep + bias_other * dead_lane).astype(BF))
        top = jnp.maximum(
            jnp.max(s_own, -1, keepdims=True), jnp.max(s_other, -1, keepdims=True)
        )
        p_own = jnp.exp(s_own - top)
        p_other = jnp.exp(s_other - top)
        total = jnp.sum(p_own, -1, keepdims=True) + jnp.sum(p_other, -1, keepdims=True)
        mixed = mul_nn(p_own.astype(BF), vo_ref[...]) + mul_nn(p_other.astype(BF), vx_ref[...])
        results.append(mixed / total * keep)
        parts = three_terms(-(top + jnp.log(total)))
        stats = sum(part * lane for part, lane in zip(parts, terms))
        aug_ref[:, head * BLK : (head + 1) * BLK] = (q_head.astype(F32) + stats).astype(BF)
    out_ref[...] = (results[0] + results[1]).astype(BF)


def attend(live, own, other):
    span = own.shape[0]
    pairs = D // BLK
    col = lambda shift: pl.BlockSpec((span, BLK), lambda p: (0, p + shift))
    return pl.pallas_call(
        attend_body,
        grid=(pairs,),
        in_specs=[
            pl.BlockSpec(memory_space=pltpu.SMEM),
            col(0),
            col(pairs),
            col(2 * pairs),
            col(0),
            col(pairs),
        ],
        out_specs=[col(0), pl.BlockSpec((span, 2 * BLK), lambda p: (0, p))],
        out_shape=[
            jax.ShapeDtypeStruct((span, D), BF),
            jax.ShapeDtypeStruct((span, 2 * D), BF),
        ],
        compiler_params=params(),
        cost_estimate=cost(40 * span * span * D, 8 * MIB),
        name="attention",
    )(live, own, own, own, other, other)


def attend_back_body(
    live_ref, aug_ref, ko_ref, vo_ref, kx_ref, vx_ref, at_ref, g_ref, dq_ref, own_ref, other_ref
):
    span = at_ref.shape[0]
    grads = g_ref[...].astype(F32)
    product = grads * at_ref[...].astype(F32)
    keeps, g_augs, q_augs = [], [], []
    for head in range(2):
        keep, dead_lane, terms = lane_masks(head)
        delta = jnp.sum(product * keep, -1, keepdims=True)
        parts = three_terms(-delta)
        stats = sum(part * lane for part, lane in zip(parts, terms))
        g_augs.append((grads * keep + stats).astype(BF))
        q_augs.append(aug_ref[:, head * BLK : (head + 1) * BLK])
    d_query = [None, None]
    for k_ref, v_ref, out_ref, live in (
        (ko_ref, vo_ref, own_ref, live_ref[0]),
        (kx_ref, vx_ref, other_ref, live_ref[1]),
    ):
        bias = key_bias(span, live)
        keys = k_ref[...]
        keys_f, values_f = keys.astype(F32), v_ref[...].astype(F32)
        d_keys = d_values = None
        for head in range(2):
            keep, dead_lane, terms = lane_masks(head)
            ones = terms[0] + terms[1] + terms[2]
            k_aug = (keys_f * keep + (bias * dead_lane + ones)).astype(BF)
            v_aug = (values_f * keep + ones).astype(BF)
            probs = jnp.exp(mul_nt(k_aug, q_augs[head]))
            d_scores = (probs * mul_nt(v_aug, g_augs[head])).astype(BF)
            value_part = mul_nn(probs.astype(BF), g_augs[head]) * keep
            key_part = mul_nn(d_scores, q_augs[head]) * keep
            query_part = mul_tn(d_scores, keys) * (keep * score_scale)
            d_query[head] = query_part if d_query[head] is None else d_query[head] + query_part
            d_values = value_part if d_values is None else d_values + value_part
            d_keys = key_part if d_keys is None else d_keys + key_part
        out_ref[0] = d_keys.astype(out_ref.dtype)
        out_ref[1] = d_values.astype(out_ref.dtype)
    dq_ref[...] = (d_query[0] + d_query[1]).astype(BF)


def attend_back(live, aug, own, other, attended, grads):
    span = own.shape[0]
    pairs = D // BLK
    col = lambda shift: pl.BlockSpec((span, BLK), lambda p: (0, p + shift))
    pair_out = pl.BlockSpec((2, span, BLK), lambda p: (0, 0, p))
    return pl.pallas_call(
        attend_back_body,
        grid=(pairs,),
        in_specs=[
            pl.BlockSpec(memory_space=pltpu.SMEM),
            pl.BlockSpec((span, 2 * BLK), lambda p: (0, p)),
            col(pairs),
            col(2 * pairs),
            col(0),
            col(pairs),
            col(0),
            col(0),
        ],
        out_specs=[col(0), pair_out, pair_out],
        out_shape=[
            jax.ShapeDtypeStruct((span, D), BF),
            jax.ShapeDtypeStruct((2, span, D), F32),
            jax.ShapeDtypeStruct((2, span, D), BF),
        ],
        compiler_params=params(),
        cost_estimate=cost(60 * span * span * D, 12 * MIB),
        name="attention_backward",
    )(live, aug, own, own, other, other, attended, grads)


def feed_body(
    live_ref,
    tokens_ref,
    attended_ref,
    cot_ref,
    gains_ref,
    wo_ref,
    wu_ref,
    wd_ref,
    layer_ref,
    rest_ref,
    gm_ref,
    ga_ref,
    gain_ref,
    unit,
    inv,
    normed,
    top,
    acc_out,
    acc_back,
    up_stage,
    down_stage,
    out_stage,
    sems,
    out_sem,
):
    step = pl.program_id(0)
    place = step % 2
    side, width = up_stage.shape[1], up_stage.shape[2]
    per_tile = side * width
    up_first = side * side
    down_first = up_first + side * FF // BLK

    def drain(which):
        pltpu.make_async_copy(up_stage.at[which], up_stage.at[which], sems.at[0, which]).wait()
        pltpu.make_async_copy(down_stage.at[which], down_stage.at[which], sems.at[1, which]).wait()
    span = tokens_ref.shape[0]

    @pl.when(step == 0)
    def _():
        weight = join_tile(wo_ref)
        middle = tokens_ref[...].astype(F32) + mul_nn(attended_ref[...], weight)
        unit_vals, inv_std = normalize(middle)
        unit[...] = unit_vals
        inv[...] = inv_std
        normed[...] = (unit_vals * gains_ref[1:2]).astype(BF)
        row = lax.broadcasted_iota(jnp.int32, (span, 1), 0)
        top[...] = jnp.where(row < live_ref[2], cot_ref[...].astype(F32), 0.0).astype(BF)
        acc_out[...] = middle
        acc_back[...] = jnp.zeros_like(acc_back)

    w_up = join_tile(wu_ref)
    w_down = join_tile(wd_ref)
    hidden = mul_nn(normed[...], w_up)
    grad_act = mul_nt(top[...], w_down)
    erf_part = 0.5 * (1.0 + lax.erf(hidden * 0.7071067811865476))
    activated = (hidden * erf_part).astype(BF)
    slope = erf_part + hidden * jnp.exp(-0.5 * hidden * hidden) * 0.3989422804014327
    grad_hidden = (grad_act * slope).astype(BF)
    acc_out[...] += mul_nn(activated, w_down)
    acc_back[...] += mul_nt(grad_hidden, w_up)

    @pl.when(step >= 2)
    def _():
        drain(place)

    split_flat(down_stage.at[place], mul_tn(activated, top[...]))
    dest = rest_ref.at[pl.ds(down_first + step * per_tile, per_tile)]
    pltpu.make_async_copy(down_stage.at[place], dest, sems.at[1, place]).start()
    split_tile(up_stage.at[place], mul_tn(normed[...], grad_hidden))
    for i in range(side):
        dest = rest_ref.at[pl.ds(up_first + i * (FF // BLK) + step * width, width)]
        pltpu.make_async_copy(up_stage.at[place, i], dest, sems.at[0, place]).start()

    @pl.when(step == pl.num_programs(0) - 1)
    def _():
        layer_ref[...] = acc_out[...].astype(BF)
        unit_vals = unit[...]
        back = acc_back[...]
        gain_ref[...] = jnp.sum(back * unit_vals, 0, keepdims=True)
        grad_middle = top[...].astype(F32) + norm_back(back * gains_ref[1:2], unit_vals, inv[...])
        gm_ref[...] = grad_middle
        back_middle = grad_middle.astype(BF)
        split_flat(out_stage, mul_tn(attended_ref[...], back_middle))
        out_copy = pltpu.make_async_copy(out_stage, rest_ref.at[pl.ds(0, up_first)], out_sem)
        out_copy.start()
        ga_ref[...] = mul_nt(back_middle, join_tile(wo_ref)).astype(BF)
        drain(1 - place)
        drain(place)
        out_copy.wait()


def feed(live, tokens, attended, cotangent, gains, weights):
    span = tokens.shape[0]
    side, width = D // BLK, COLS // BLK
    whole = lambda j: (0, 0)
    act = pl.BlockSpec((span, D), whole)
    per_row = weights.reshape(-1, side, BLK, BLK)
    per_up = weights.reshape(-1, FF // BLK, BLK, BLK)
    out_row = (3 * side * side) // side // side
    up_row = 4 * side * side // (FF // BLK) // side
    down_row = (4 * side * side + side * FF // BLK) // side // width
    return pl.pallas_call(
        feed_body,
        grid=(FF // COLS,),
        in_specs=[
            pl.BlockSpec(memory_space=pltpu.SMEM),
            act,
            act,
            act,
            pl.BlockSpec((2, D), whole),
            pl.BlockSpec((side, side, BLK, BLK), lambda j: (out_row, 0, 0, 0)),
            pl.BlockSpec((side, width, BLK, BLK), lambda j: (up_row, j, 0, 0)),
            pl.BlockSpec((width, side, BLK, BLK), lambda j: (down_row + j, 0, 0, 0)),
        ],
        out_specs=[
            act,
            pl.BlockSpec(memory_space=pltpu.HBM),
            act,
            act,
            pl.BlockSpec((1, D), whole),
        ],
        out_shape=[
            jax.ShapeDtypeStruct((span, D), BF),
            jax.ShapeDtypeStruct((side * side + 2 * side * (FF // BLK), BLK, BLK), BF),
            jax.ShapeDtypeStruct((span, D), F32),
            jax.ShapeDtypeStruct((span, D), BF),
            jax.ShapeDtypeStruct((1, D), F32),
        ],
        scratch_shapes=[
            pltpu.VMEM((span, D), F32),
            pltpu.VMEM((span, 1), F32),
            pltpu.VMEM((span, D), BF),
            pltpu.VMEM((span, D), BF),
            pltpu.VMEM((span, D), F32),
            pltpu.VMEM((span, D), F32),
            pltpu.VMEM((2, side, width, BLK, BLK), BF),
            pltpu.VMEM((2, side * width, BLK, BLK), BF),
            pltpu.VMEM((side * side, BLK, BLK), BF),
            pltpu.SemaphoreType.DMA((2, 2)),
            pltpu.SemaphoreType.DMA,
        ],
        compiler_params=params(),
        cost_estimate=cost(14 * span * D * FF, 50 * MIB),
        name="feed_forward",
    )(live, tokens, attended, cotangent, gains, per_row, per_up, per_row)


def query_body(tokens_ref, gains_ref, dq_ref, w_ref, grad_ref, acc_ref, normed):
    step = pl.program_id(0)

    @pl.when(step == 0)
    def _():
        unit_vals, _ = normalize(tokens_ref[...].astype(F32))
        normed[...] = (unit_vals * gains_ref[0:1]).astype(BF)
        acc_ref[...] = jnp.zeros_like(acc_ref)

    grad = dq_ref[...]
    acc_ref[...] += mul_nt(grad, join_tile(w_ref))
    split_tile(grad_ref, mul_tn(normed[...], grad))


def query_back(tokens, gains, d_query, weights):
    span = tokens.shape[0]
    side, width = D // BLK, COLS // BLK
    whole = lambda j: (0, 0)
    act = pl.BlockSpec((span, D), whole)
    tile = pl.BlockSpec((side, width, BLK, BLK), lambda j: (0, j, 0, 0))
    return pl.pallas_call(
        query_body,
        grid=(D // COLS,),
        in_specs=[
            act,
            pl.BlockSpec((2, D), whole),
            pl.BlockSpec((span, COLS), lambda j: (0, j)),
            tile,
        ],
        out_specs=[tile, act],
        out_shape=[
            jax.ShapeDtypeStruct((side, side, BLK, BLK), BF),
            jax.ShapeDtypeStruct((span, D), F32),
        ],
        scratch_shapes=[pltpu.VMEM((span, D), BF)],
        compiler_params=params(),
        cost_estimate=cost(4 * span * D * D, 8 * MIB),
        name="query_backward",
    )(tokens, gains, d_query, weights.reshape(-1, 3 * side, BLK, BLK))


def input_body(
    tokens_ref, gains_ref, own_ref, recv_ref, acc_ref, gm_ref, w_ref, grad_ref, out_ref, gain_ref,
    unit, inv, normed, acc
):
    step = pl.program_id(0)

    @pl.when(step == 0)
    def _():
        unit_vals, inv_std = normalize(tokens_ref[...].astype(F32))
        unit[...] = unit_vals
        inv[...] = inv_std
        normed[...] = (unit_vals * gains_ref[0:1]).astype(BF)
        acc[...] = acc_ref[...]

    grad = (own_ref[0] + recv_ref[0].astype(F32)).astype(BF)
    acc[...] += mul_nt(grad, join_tile(w_ref))
    split_tile(grad_ref, mul_tn(normed[...], grad))

    @pl.when(step == pl.num_programs(0) - 1)
    def _():
        unit_vals = unit[...]
        back = acc[...]
        gain_ref[...] = jnp.sum(back * unit_vals, 0, keepdims=True)
        out_ref[...] = (
            gm_ref[...] + norm_back(back * gains_ref[0:1], unit_vals, inv[...])
        ).astype(BF)


def input_back(tokens, gains, own, received, partial, grad_middle, weights):
    span = tokens.shape[0]
    side, width = D // BLK, COLS // BLK
    per = D // COLS
    whole = lambda j: (0, 0)
    act = pl.BlockSpec((span, D), whole)
    part = pl.BlockSpec((1, span, COLS), lambda j: (j // per, 0, j % per))
    return pl.pallas_call(
        input_body,
        grid=(2 * per,),
        in_specs=[
            act,
            pl.BlockSpec((2, D), whole),
            part,
            part,
            act,
            act,
            pl.BlockSpec((side, width, BLK, BLK), lambda j: (0, j + per, 0, 0)),
        ],
        out_specs=[
            pl.BlockSpec((side, width, BLK, BLK), lambda j: (0, j, 0, 0)),
            act,
            pl.BlockSpec((1, D), whole),
        ],
        out_shape=[
            jax.ShapeDtypeStruct((side, 2 * side, BLK, BLK), BF),
            jax.ShapeDtypeStruct((span, D), BF),
            jax.ShapeDtypeStruct((1, D), F32),
        ],
        scratch_shapes=[
            pltpu.VMEM((span, D), F32),
            pltpu.VMEM((span, 1), F32),
            pltpu.VMEM((span, D), BF),
            pltpu.VMEM((span, D), F32),
        ],
        compiler_params=params(),
        cost_estimate=cost(8 * span * D * D, 20 * MIB),
        name="input_backward",
    )(
        tokens, gains, own, received, partial, grad_middle,
        weights.reshape(-1, 3 * side, BLK, BLK),
    )


def source_numbers():
    side = D // BLK
    numbers = np.arange(3 * side * side + side * side + 2 * side * (FF // BLK), dtype=np.int32)
    row, col = np.divmod(numbers[: 3 * side * side], 3 * side)
    numbers[: 3 * side * side] = np.where(
        col < side, row * side + col, side * side + row * 2 * side + col - side
    )
    return numbers


def gather_body(first, bounds, table, *refs):
    sources = refs[:6]
    out_ref, stage, sems = refs[6:]
    step, steps = pl.program_id(0), pl.num_programs(0)
    count = stage.shape[1] // 2

    def fetch(which, slot):
        start = first + which * count
        for i in range(count):
            number = table[start + i]
            for low, high, own, other in zip(bounds, bounds[1:], sources[:3], sources[3:]):

                @pl.when((number >= low) & (number < high))
                def _():
                    for src, at in ((own, i), (other, count + i)):
                        pltpu.make_async_copy(
                            src.at[number - low], stage.at[slot, at], sems.at[slot]
                        ).start()

    @pl.when(step == 0)
    def _():
        fetch(0, 0)

    @pl.when(step + 1 < steps)
    def _():
        fetch(step + 1, (step + 1) % 2)

    slot = step % 2
    pltpu.make_async_copy(stage.at[slot], stage.at[slot], sems.at[slot]).wait()
    total = stage[slot, :count].astype(F32) + stage[slot, count:].astype(F32)
    out_ref[...] = total.astype(BF)


def gather_sums(table, first, count, own, other):
    hbm = pl.BlockSpec(memory_space=pltpu.HBM)
    steps = 4
    part = count // steps
    bounds = np.cumsum([0] + [src.shape[0] for src in own]).tolist()
    return pl.pallas_call(
        functools.partial(gather_body, first, bounds),
        grid=(steps,),
        in_specs=[pl.BlockSpec(memory_space=pltpu.SMEM)] + [hbm] * 6,
        out_specs=pl.BlockSpec((part, BLK, BLK), lambda i: (i, 0, 0)),
        out_shape=jax.ShapeDtypeStruct((count, BLK, BLK), BF),
        scratch_shapes=[
            pltpu.VMEM((2, 2 * part, BLK, BLK), BF),
            pltpu.SemaphoreType.DMA((2,)),
        ],
        compiler_params=params(),
        cost_estimate=cost(0, 6 * count * BLK * BLK),
        name="gradient_sums",
    )(table, *own, *other)


def merge_body(first, second, passed, *refs):
    refs = list(refs)

    def total(count):
        return sum(refs.pop(0)[...].astype(F32) for _ in range(count))

    sums = [total(2), total(2)] if first else []
    if second:
        sums.append(total(3 if passed else 2))
    for ref, value in zip(refs, sums):
        ref[...] = value.astype(BF)


def merge_sums(low, came, kept, last, passed):
    steps = 3
    args, specs, shapes, outs = [], [], [], []

    def part(array, count, start):
        args.append(array)
        size = count // steps
        specs.append(pl.BlockSpec((size, BLK, BLK), lambda i: (i + start * steps, 0, 0)))

    def out(count):
        shapes.append(jax.ShapeDtypeStruct((count, BLK, BLK), BF))
        outs.append(pl.BlockSpec((count // steps, BLK, BLK), lambda i: (i, 0, 0)))

    if low is not None:
        count = low.shape[0] // 2
        for start in range(2):
            part(low, count, start)
            part(came, count, start)
            out(count)
    if kept is not None:
        for array in (kept, last) if passed is None else (kept, last, passed):
            part(array, kept.shape[0], 0)
        out(kept.shape[0])
    body = functools.partial(merge_body, low is not None, kept is not None, passed is not None)
    return pl.pallas_call(
        body,
        grid=(steps,),
        in_specs=specs,
        out_specs=outs,
        out_shape=shapes,
        compiler_params=params(44),
        cost_estimate=cost(0, 6 * MIB),
        name="merge_sums",
    )(*args)


def two_terms(values):
    high = values.astype(BF)
    return high, (values - high.astype(F32)).astype(BF)


def update_body(count, *refs):
    parts = refs[:count]
    m_ref, sl_ref, sr_ref, rl_ref, rr_ref, g_out, sl_out, sr_out, m_out = refs[count:]

    def long_left(terms, axis):
        return jnp.concatenate([terms[0], terms[0], terms[1]], axis)

    def long_right(terms, axis):
        return jnp.concatenate([terms[0], terms[1], terms[0]], axis)

    for i in range(g_out.shape[0]):
        total = sum(part[i].astype(F32) for part in parts)
        g_out[i] = total
        grad = two_terms(total)
        sl_out[i] = sl_ref[i] + mul_nt(long_left(grad, 1), long_right(grad, 1))
        tall = long_right(grad, 0)
        sr_out[i] = sr_ref[i] + mul_tn(long_left(grad, 0), tall)
        inner = mul_nn(long_left(two_terms(rl_ref[i]), 1), tall)
        direction = mul_nn(
            long_left(two_terms(inner), 1), long_right(two_terms(rr_ref[i]), 0)
        )
        master = m_ref[i]
        scale = jnp.sqrt(jnp.mean(master * master, keepdims=True) + 1e-06)
        scale = scale * lax.rsqrt(jnp.mean(direction * direction, keepdims=True) + 1e-06)
        m_out[i] = master - 0.3 * scale * direction


def update(parts, master, stat_left, stat_right, root_left, root_right):
    count = master.shape[0]
    group = 3 if count % 3 == 0 else 1
    block = pl.BlockSpec((group, BLK, BLK), lambda i: (i, 0, 0))
    shape = jax.ShapeDtypeStruct(master.shape, F32)
    return pl.pallas_call(
        functools.partial(update_body, len(parts)),
        grid=(count // group,),
        in_specs=[block] * (len(parts) + 5),
        out_specs=[block] * 4,
        out_shape=[shape] * 4,
        compiler_params=params(),
        cost_estimate=cost(48 * count * BLK**3, 15 * MIB),
        name="block_update",
    )(*parts, master, stat_left, stat_right, root_left, root_right)


def pair_moves():
    moves_same, moves_cross = [], []
    for z in range(4):
        for c in range(2):
            for moves, bit in ((moves_same, z % 2), (moves_cross, 1 - z % 2)):
                moves.append((z * 2 + c, (2 * c + bit) * 2 + z // 2))
    return moves_same, moves_cross


def row_part(values, which):
    return lax.dynamic_index_in_dim(values, which, 0, False)


def move_rows(values, crossed, back=False):
    moves = pair_moves()[crossed]
    return lax.ppermute(values, ("seq", "core"), [(b, a) for a, b in moves] if back else moves)


def in_order(kept, crossed, parity):
    return jnp.where(parity == 0, kept, crossed), jnp.where(parity == 0, crossed, kept)


def spread_rows(values, parity):
    kept = move_rows(row_part(values, parity), False)
    crossed = move_rows(row_part(values, 1 - parity), True)
    return jnp.concatenate(in_order(kept, crossed, parity), 0)


def gather_rows(values, parity):
    parts = values.reshape(2, values.shape[0] // 2, values.shape[1])
    kept = move_rows(row_part(parts, parity), False, True)
    crossed = move_rows(row_part(parts, 1 - parity), True, True)
    return jnp.stack(in_order(kept, crossed, parity), 0)


def swap_cores(values):
    return lax.ppermute(values, "core", [(0, 1), (1, 0)])


def chip_orders(chips):
    bits = [1 << i for i in range(chips.bit_length() - 1)]
    return bits, bits[::-1]


def offsets(order):
    result = [0]
    for bit in order:
        result = result + [o ^ bit for o in result]
    return result


def place_lists(chips, owned, planes):
    shape = (2, planes, chips, owned)
    by_core = np.array([offsets(order) for order in chip_orders(chips)], np.int32)
    grid = np.indices(shape).astype(np.int32).reshape(4, 2, -1)
    offset = np.broadcast_to(by_core[:, None, :, None], shape).reshape(2, -1)
    return grid[1, 0], offset, grid[3, 0]


def swap_chips(values, bits):
    chips = lax.axis_size("chip")
    moves = [(i * 2 + c, (i ^ bits[c]) * 2 + c) for i in range(chips) for c in range(2)]
    return lax.ppermute(values, ("chip", "core"), moves)


def move_planes(values, shift):
    planes = lax.axis_size("seq")
    return lax.ppermute(values, "seq", [(i, (i + shift) % planes) for i in range(planes)])


def after(value, *deps):
    return lax.optimization_barrier((value, *deps))[0]


def together(*values):
    return lax.optimization_barrier(values)


def chip_steps():
    return list(zip(*chip_orders(lax.axis_size("chip"))))


def finish_pieces(pieces):
    for bits in chip_steps()[2:]:
        joined = jnp.concatenate(pieces, 0)
        pieces = [joined, swap_chips(joined, bits)]
    return pieces


def add_halves(kept, came):
    return (kept.astype(F32) + came.astype(F32)).astype(BF)


def pack_terms(values):
    high = lax.optimization_barrier(values.astype(BF))
    low = (values - high.astype(F32)).astype(BF)
    terms = jnp.stack([high, low]).reshape(-1, BLK)
    return jnp.pad(terms, ((0, BLK - terms.shape[0]), (0, 0)))[None]


def unpack_terms(blocks, shape):
    terms = blocks.reshape(-1, BLK, BLK)[:, : 2 * shape[0] * shape[1] // BLK]
    terms = terms.reshape(-1, 2, *shape).astype(F32)
    return terms[:, 0] + terms[:, 1]


def finish_sums(keep, send, riders):
    for bits in chip_steps()[::-1][1:-1]:
        count = keep.shape[0] // 2
        came = swap_chips(with_riders(send, riders), bits)
        riders = more_riders(riders, came, keep.shape[0])
        send = add_halves(keep[count:], came[count : 2 * count])
        keep = add_halves(keep[:count], came[:count])
    return keep, send, riders


def with_riders(send, riders):
    return send if riders is None else jnp.concatenate([send, riders], 0)


def more_riders(riders, came, count):
    return riders if riders is None else jnp.concatenate([riders, came[count:]], 0)


def by_chip(riders, me, core):
    chips = lax.axis_size("chip")
    ranks = np.array([np.argsort(offsets(order[::-1])) for order in chip_orders(chips)], np.int32)
    rank = jnp.asarray(ranks)[core][me ^ jnp.arange(chips, dtype=jnp.int32)]
    return riders.reshape(chips, -1, BLK, BLK)[rank]


def local(
    tokens,
    cotangent,
    lengths,
    owner_perm,
    master,
    norm_gains,
    stat_left,
    stat_right,
    root_left,
    root_right,
    moment_first,
    moment_second,
):
    core = lax.axis_index("core")
    place_z = lax.axis_index("seq")
    parity = place_z % 2
    block_count = owner_perm.shape[0]
    owned = master.shape[0]
    half = block_count // 2

    chips, planes = lax.axis_size("chip"), lax.axis_size("seq")
    me = lax.axis_index("chip")

    pair_lengths = jnp.stack([lengths, swap_cores(lengths)])
    pair_lengths = jnp.where(core == 0, pair_lengths, pair_lengths[::-1]).reshape(-1)
    length = lax.dynamic_index_in_dim(pair_lengths, place_z, 0, False)
    span = tokens.shape[0] * tokens.shape[1]
    live = jnp.stack([length - core * span, length - (1 - core) * span, length - core * span])

    distance, offset, slot = place_lists(chips, owned, planes)
    offset = jnp.where(core == 0, offset, offset[::-1])
    device = ((place_z - distance) % planes * chips + (me ^ offset)) * 2
    device = device + jnp.stack([core, 1 - core])[:, None]
    table = owner_perm[(device * owned + slot).reshape(-1)]
    sums_table = jnp.asarray(source_numbers())[table[:half]]

    shard = master.astype(BF)
    first_bits, second_bits = chip_steps()[:2]
    per_plane = chips * owned
    row_same, row_cross = row_part(tokens, parity), row_part(tokens, 1 - parity)
    cross, far, weights = [], [], None
    came, turned = swap_chips(shard, first_bits), swap_chips(shard, second_bits)
    next_shard = move_planes(shard, 1)
    row_same = move_rows(row_same, False)
    pieces = [[shard, came, turned]]
    for k in range(1, planes):
        if k == 1:
            ready = (live, table, sums_table, row_same)
        else:
            ready = (row_cross, *far[-1:])
        this_shard, came, turned, row, *done = together(
            next_shard, came, turned, row_cross, *cross[-1:], *ready
        )
        if k > 1:
            pieces[k - 2].append(done[0])
        cross.append(swap_chips(came, second_bits))
        came, turned = swap_chips(this_shard, first_bits), swap_chips(this_shard, second_bits)
        pieces.append([this_shard, came, turned])
        if k < planes - 1:
            next_shard = move_planes(this_shard, 1)
        if k == 1:
            row_cross = move_rows(row, True)
        else:
            near = jnp.concatenate(finish_pieces(pieces[k - 2]), 0)
            far.append(swap_cores(near))
            weights = place_blocks(table, (k - 2) * per_plane, near, far[-1], weights)
    own_tokens = jnp.concatenate(in_order(row_same, row_cross, parity), 0)
    first = (planes - 1) * per_plane

    def place_piece(piece, first, weights):
        return place_blocks(table, first, piece, swap_cores(piece), weights), first + piece.shape[0]

    split = len(chip_steps()) == 2
    if split:
        weights, first = place_piece(this_shard, first, weights)
    came, turned, done, *_ = together(came, turned, cross[-1], far[-1], weights)
    pieces[-2].append(done)
    pieces[-1].append(swap_chips(came, second_bits))
    near = jnp.concatenate(finish_pieces(pieces[-2]), 0)
    far.append(swap_cores(near))
    weights = place_blocks(table, (planes - 2) * per_plane, near, far[-1], weights)
    other_tokens = swap_cores(own_tokens)
    if split:
        weights, first = place_piece(came, first, weights)
        weights, first = place_piece(turned, first, weights)
        last, *_ = together(pieces[-1][-1], other_tokens)
        weights, _ = place_piece(last, first, weights)
    else:
        weights, _ = place_piece(jnp.concatenate(finish_pieces(pieces[-1]), 0), first, weights)
    own_cot = spread_rows(after(cotangent, weights), parity)

    own_qkv, other_kv = project(own_tokens, other_tokens, norm_gains, weights)
    attended, q_aug = attend(live, own_qkv, other_kv)
    layer, g_rest, grad_middle, grad_attended, gain_second = feed(
        live, own_tokens, attended, own_cot, norm_gains, weights
    )
    other_rest = swap_cores(g_rest)
    layer_out = gather_rows(layer, parity)
    d_query, d_own, d_other = attend_back(live, q_aug, own_qkv, other_kv, attended, grad_attended)
    received = swap_cores(after(d_other, layer_out))
    flat = lambda g: g.reshape(-1, BLK, BLK)
    g_query, partial = query_back(own_tokens, norm_gains, d_query, weights)
    g_query = flat(g_query)
    other_query = swap_cores(g_query)
    g_kv, grad_in, gain_first = input_back(
        own_tokens, norm_gains, d_own, received, partial, grad_middle, weights
    )
    g_kv = flat(g_kv)
    gain_part = jnp.concatenate([gain_first, gain_second], 0)
    mine = pack_terms(gain_part)
    other_kv_grad = swap_cores(after(g_kv, other_query))
    theirs = swap_cores(mine)
    pair = jnp.concatenate([mine, theirs], 0)
    riders = jnp.where(core == 0, pair, pair[::-1])
    own_grads = (g_query, g_kv, g_rest)
    other_grads = (other_query, other_kv_grad, other_rest)
    half_plane = per_plane // 2
    last_bits, before_bits = chip_steps()[-1], chip_steps()[0]
    halves = grad_in.reshape(2, span // 2, D)
    rows = [row_part(halves, parity), row_part(halves, 1 - parity)]
    moved_rows, lows, sent, passed, riders_z = [], [], None, None, []

    def sums(k, part, held):
        first = k * per_plane + part * half_plane
        return gather_sums(held, first, half_plane, own_grads, other_grads)

    order = list(range(planes))[::-1]
    high = sums(order[0], 1, sums_table)
    held = sums_table
    for turn in range(planes + 1):
        group, moves = [], []
        if turn < planes:
            group.append(with_riders(high, riders if turn == 0 else None))
            moves.append(lambda v: swap_chips(v, last_bits))
        if 1 <= turn <= planes:
            group.append(with_riders(sent, riders if turn == 1 else None))
            moves.append(lambda v: swap_chips(v, before_bits))
        if 2 <= turn <= planes:
            group.append(part)
            moves.append(lambda v: move_planes(v, -1))
        if turn < 2:
            group.append(rows[turn])
            moves.append(lambda v: move_rows(v, len(moved_rows) == 1, True))
        far_riders = [] if turn < planes - 1 else [1, 2] if turn == planes - 1 else range(3, planes)
        group += [rider for _ in far_riders]
        moves += [functools.partial(move_planes, shift=-k) for k in far_riders]
        came = [move(value) for move, value in zip(moves, together(*group, *moved_rows[-1:]))]
        if turn < 2:
            moved_rows.append(came.pop())
        count = len(came) - len(far_riders)
        riders_z, came = riders_z + came[count:], came[:count]
        if turn >= 2:
            passed = came.pop()
        if turn < planes:
            low = sums(order[turn], 0, after(held, high))
            if turn + 1 < planes:
                high = sums(order[turn + 1], 1, after(held, low))
            held = after(sums_table, *came)
        last = came[-1]
        if turn == 0:
            riders = more_riders(riders, came[0], half_plane)
        if turn == 1:
            riders = more_riders(riders, last, keep_before.shape[0])
            plane_gain = by_chip(riders, me, core)
            plane_gain = jnp.sum(unpack_terms(plane_gain, gain_part.shape), 0)
            rider = pack_terms(plane_gain)
        if turn == planes:
            parts = [keep_before, last, passed]
            continue
        second = (None, None, None) if turn == 0 else (keep_before, last, passed)
        keep, sent, *part = merge_sums(low, came[0], *second)
        part = part[0] if part else None
        keep_before, sent, grown = finish_sums(keep, sent, riders if turn == 0 else None)
        riders = grown if turn == 0 else riders
    input_grad = jnp.stack(in_order(*moved_rows, parity), 0).astype(F32)
    planes_gain = [unpack_terms(each, gain_part.shape)[0] for each in (rider, *riders_z)]
    turned = (jnp.arange(planes, dtype=jnp.int32) - place_z) % planes
    gain_grad = jnp.sum(jnp.stack(planes_gain)[turned], 0)
    grad_blocks, stat_left_new, stat_right_new, master_new = update(
        parts, master, stat_left, stat_right, root_left, root_right
    )
    first_new = 0.9 * moment_first + 0.1 * gain_grad
    second_new = 0.999 * moment_second + 0.001 * gain_grad * gain_grad
    first_hat = first_new / (1.0 - 0.9**STEP)
    second_hat = second_new / (1.0 - 0.999**STEP)
    gains_new = norm_gains - 0.5 * first_hat / (jnp.sqrt(second_hat) + 1e-08)
    return (
        layer_out,
        input_grad,
        grad_blocks,
        stat_left_new,
        stat_right_new,
        master_new,
        first_new,
        second_new,
        gains_new,
    )


def solution(mesh):
    seq_size, rows_size = mesh.shape["seq"], mesh.shape["rows"]
    mesh = Mesh(mesh.devices.reshape(seq_size, rows_size // 2, 2), ("seq", "chip", "core"))
    activation = P(("chip", "core"), "seq", None)
    blocks = P(("seq", "chip", "core"), None, None)
    return jax.shard_map(
        local,
        mesh=mesh,
        in_specs=(
            activation, activation, P(("chip", "core")), P(), blocks, P(),
            blocks, blocks, blocks, blocks, P(), P(),
        ),
        out_specs=(activation, activation, blocks, blocks, blocks, blocks, P(), P(), P()),
        check_vma=False,
    )
```

```python
import functools
import jax
import jax.numpy as jnp
import numpy as np
from jax import lax
from jax.experimental import pallas as pl
from jax.experimental.pallas import tpu as pltpu
from jax.sharding import Mesh
from jax.sharding import PartitionSpec as P

D = 1024
HD = 64
FF = 4096
BLK = 128
STEP = 10
COLS = 512
BF = jnp.bfloat16
F32 = jnp.float32
MIB = 1024 * 1024

norm_eps = 1e-05
score_scale = 0.125
masked_score = -1e30


def params(limit=56):
    return pltpu.CompilerParams(vmem_limit_bytes=limit * MIB)


def cost(flops, nbytes):
    return pl.CostEstimate(flops=int(flops), bytes_accessed=int(nbytes), transcendentals=0)


def mul_nn(left, right):
    return jnp.dot(left, right, preferred_element_type=F32)


def mul_nt(left, right):
    return lax.dot_general(left, right, (((1,), (1,)), ((), ())), preferred_element_type=F32)


def mul_tn(left, right):
    return lax.dot_general(left, right, (((0,), (0,)), ((), ())), preferred_element_type=F32)


def join_tile(ref):
    rows, cols = ref.shape[0], ref.shape[1]
    return jnp.concatenate([ref[:, j].reshape(rows * BLK, BLK) for j in range(cols)], axis=1)


def split_tile(ref, matrix):
    rows, cols = ref.shape[0], ref.shape[1]
    for j in range(cols):
        ref[:, j] = matrix[:, j * BLK : (j + 1) * BLK].reshape(rows, BLK, BLK).astype(ref.dtype)


def split_flat(ref, matrix):
    cols = matrix.shape[1] // BLK
    for i in range(matrix.shape[0] // BLK):
        for j in range(cols):
            block = matrix[i * BLK : (i + 1) * BLK, j * BLK : (j + 1) * BLK]
            ref[i * cols + j] = block.astype(ref.dtype)


def normalize(values):
    row_mean = jnp.mean(values, -1, keepdims=True)
    centered = values - row_mean
    row_var = jnp.mean(centered * centered, -1, keepdims=True)
    inv_std = lax.rsqrt(row_var + norm_eps)
    return centered * inv_std, inv_std


def norm_back(gradient, unit_vals, inv_std):
    grad_mean = jnp.mean(gradient, -1, keepdims=True)
    cross_mean = jnp.mean(gradient * unit_vals, -1, keepdims=True)
    return inv_std * (gradient - grad_mean - unit_vals * cross_mean)


def place_body(first, table, near_ref, far_ref, *refs):
    out_ref, sem = refs[-2:]
    count = near_ref.shape[0]
    half = table.shape[0] // 2
    for start, src in ((first, near_ref), (half + first, far_ref)):
        for slot in range(count):
            pltpu.make_async_copy(src.at[slot], out_ref.at[table[start + slot]], sem).start()
    done = out_ref.at[pl.ds(0, 2 * count)]
    pltpu.make_async_copy(done, done, sem).wait()


def place_blocks(table, first, near, far, kept):
    smem = pl.BlockSpec(memory_space=pltpu.SMEM)
    hbm = pl.BlockSpec(memory_space=pltpu.HBM)
    vmem = pl.BlockSpec(memory_space=pltpu.VMEM)
    kept = () if kept is None else (kept,)
    return pl.pallas_call(
        functools.partial(place_body, first),
        out_shape=jax.ShapeDtypeStruct((table.shape[0], BLK, BLK), BF),
        in_specs=[smem, vmem, vmem] + [hbm] * len(kept),
        out_specs=hbm,
        scratch_shapes=[pltpu.SemaphoreType.DMA],
        input_output_aliases={3: 0} if kept else {},
        compiler_params=params(44),
        cost_estimate=cost(0, 4 * near.size * 2),
        name="place_weights",
    )(table, near, far, *kept)


def qkv_body(own_ref, other_ref, gains_ref, w_ref, own_out, other_out, keep_out, normed):
    step = pl.program_id(0)
    span = own_ref.shape[0]

    @pl.when(step == 0)
    def _():
        gain = gains_ref[0:1]
        normed[:span] = (normalize(own_ref[...].astype(F32))[0] * gain).astype(BF)
        normed[span:] = (normalize(other_ref[...].astype(F32))[0] * gain).astype(BF)
        keep_out[...] = normed[:span]

    @pl.when(step < D // COLS)
    def _():
        own_out[...] = mul_nn(normed[:span], join_tile(w_ref)).astype(BF)

    @pl.when(step >= D // COLS)
    def _():
        both = mul_nn(normed[...], join_tile(w_ref)).astype(BF)
        own_out[...] = both[:span]
        other_out[...] = both[span:]


def project(own, other, gains, weights):
    span = own.shape[0]
    skip = D // COLS
    whole = lambda j: (0, 0)
    return pl.pallas_call(
        qkv_body,
        grid=(3 * D // COLS,),
        in_specs=[
            pl.BlockSpec((span, D), whole),
            pl.BlockSpec((span, D), whole),
            pl.BlockSpec((2, D), whole),
            pl.BlockSpec((D // BLK, COLS // BLK, BLK, BLK), lambda j: (0, j, 0, 0)),
        ],
        out_specs=[
            pl.BlockSpec((span, COLS), lambda j: (0, j)),
            pl.BlockSpec((span, COLS), lambda j: (0, jnp.maximum(j - skip, 0))),
            pl.BlockSpec((span, D), whole),
        ],
        out_shape=[
            jax.ShapeDtypeStruct((span, 3 * D), BF),
            jax.ShapeDtypeStruct((span, 2 * D), BF),
            jax.ShapeDtypeStruct((span, D), BF),
        ],
        scratch_shapes=[pltpu.VMEM((2 * span, D), BF)],
        compiler_params=params(),
        cost_estimate=cost(10 * span * D * D, 12 * MIB),
        name="qkv_projection",
    )(own, other, gains, weights.reshape(-1, 3 * D // BLK, BLK, BLK))


def lane_masks(head):
    lane = lax.broadcasted_iota(jnp.int32, (1, BLK), 1)
    first = HD * (1 - head)
    keep = (lane // HD == head).astype(F32)
    dead_lane = (lane == first).astype(F32)
    terms = [(lane == first + 1 + i).astype(F32) for i in range(3)]
    return keep, dead_lane, terms


def three_terms(values):
    high = values.astype(BF).astype(F32)
    rest = values - high
    middle = rest.astype(BF).astype(F32)
    return high, middle, rest - middle


def key_bias(span, live_count):
    row = lax.broadcasted_iota(jnp.int32, (span, 1), 0)
    return jnp.where(row < live_count, 0.0, masked_score).astype(F32)


def attend_body(live_ref, q_ref, ko_ref, vo_ref, kx_ref, vx_ref, out_ref, aug_ref):
    span = q_ref.shape[0]
    bias_own = key_bias(span, live_ref[0])
    bias_other = key_bias(span, live_ref[1])
    queries = q_ref[...].astype(F32) * score_scale
    k_own, k_other = ko_ref[...].astype(F32), kx_ref[...].astype(F32)
    v_own_f, v_other_f = vo_ref[...].astype(F32), vx_ref[...].astype(F32)
    results = []
    for head in range(2):
        keep, dead_lane, terms = lane_masks(head)
        q_head = (queries * keep + dead_lane).astype(BF)
        s_own = mul_nt(q_head, (k_own * keep + bias_own * dead_lane).astype(BF))
        s_other = mul_nt(q_head, (k_other * keep + bias_other * dead_lane).astype(BF))
        top = jnp.maximum(
            jnp.max(s_own, -1, keepdims=True), jnp.max(s_other, -1, keepdims=True)
        )
        p_own = jnp.exp(s_own - top)
        p_other = jnp.exp(s_other - top)
        v_own = (v_own_f * keep + (1.0 - keep)).astype(BF)
        v_other = (v_other_f * keep + (1.0 - keep)).astype(BF)
        mixed = mul_nn(p_own.astype(BF), v_own) + mul_nn(p_other.astype(BF), v_other)
        total = mixed[:, HD * (1 - head) : HD * (1 - head) + 1]
        results.append(mixed / total * keep)
        parts = three_terms(-(top + jnp.log(total)))
        stats = sum(part * lane for part, lane in zip(parts, terms))
        aug_ref[:, head * BLK : (head + 1) * BLK] = (q_head.astype(F32) + stats).astype(BF)
    out_ref[...] = (results[0] + results[1]).astype(BF)


def attend(live, own, other):
    span = own.shape[0]
    pairs = D // BLK
    col = lambda shift: pl.BlockSpec((span, BLK), lambda p: (0, p + shift))
    return pl.pallas_call(
        attend_body,
        grid=(pairs,),
        in_specs=[
            pl.BlockSpec(memory_space=pltpu.SMEM),
            col(0),
            col(pairs),
            col(2 * pairs),
            col(0),
            col(pairs),
        ],
        out_specs=[col(0), pl.BlockSpec((span, 2 * BLK), lambda p: (0, p))],
        out_shape=[
            jax.ShapeDtypeStruct((span, D), BF),
            jax.ShapeDtypeStruct((span, 2 * D), BF),
        ],
        compiler_params=params(),
        cost_estimate=cost(40 * span * span * D, 8 * MIB),
        name="attention",
    )(live, own, own, own, other, other)


def attend_back_body(
    live_ref, aug_ref, ko_ref, vo_ref, kx_ref, vx_ref, at_ref, g_ref, dq_ref, own_ref, other_ref
):
    span = at_ref.shape[0]
    grads = g_ref[...].astype(F32)
    product = grads * at_ref[...].astype(F32)
    keeps, g_augs, q_augs = [], [], []
    for head in range(2):
        keep, dead_lane, terms = lane_masks(head)
        delta = jnp.sum(product * keep, -1, keepdims=True)
        parts = three_terms(-delta)
        stats = sum(part * lane for part, lane in zip(parts, terms))
        g_augs.append((grads * keep + stats).astype(BF))
        q_augs.append(aug_ref[:, head * BLK : (head + 1) * BLK])
    d_query = [None, None]
    for k_ref, v_ref, out_ref, live in (
        (ko_ref, vo_ref, own_ref, live_ref[0]),
        (kx_ref, vx_ref, other_ref, live_ref[1]),
    ):
        bias = key_bias(span, live)
        keys = k_ref[...]
        keys_f, values_f = keys.astype(F32), v_ref[...].astype(F32)
        d_keys = d_values = None
        for head in range(2):
            keep, dead_lane, terms = lane_masks(head)
            ones = terms[0] + terms[1] + terms[2]
            k_aug = (keys_f * keep + (bias * dead_lane + ones)).astype(BF)
            v_aug = (values_f * keep + ones).astype(BF)
            probs = jnp.exp(mul_nt(k_aug, q_augs[head]))
            d_scores = (probs * mul_nt(v_aug, g_augs[head])).astype(BF)
            value_part = mul_nn(probs.astype(BF), g_augs[head]) * keep
            key_part = mul_nn(d_scores, q_augs[head]) * keep
            query_part = mul_tn(d_scores, keys) * (keep * score_scale)
            d_query[head] = query_part if d_query[head] is None else d_query[head] + query_part
            d_values = value_part if d_values is None else d_values + value_part
            d_keys = key_part if d_keys is None else d_keys + key_part
        out_ref[0] = d_keys.astype(out_ref.dtype)
        out_ref[1] = d_values.astype(out_ref.dtype)
    dq_ref[...] = (d_query[0] + d_query[1]).astype(BF)


def attend_back(live, aug, own, other, attended, grads):
    span = own.shape[0]
    pairs = D // BLK
    col = lambda shift: pl.BlockSpec((span, BLK), lambda p: (0, p + shift))
    pair_out = pl.BlockSpec((2, span, BLK), lambda p: (0, 0, p))
    return pl.pallas_call(
        attend_back_body,
        grid=(pairs,),
        in_specs=[
            pl.BlockSpec(memory_space=pltpu.SMEM),
            pl.BlockSpec((span, 2 * BLK), lambda p: (0, p)),
            col(pairs),
            col(2 * pairs),
            col(0),
            col(pairs),
            col(0),
            col(0),
        ],
        out_specs=[col(0), pair_out, pair_out],
        out_shape=[
            jax.ShapeDtypeStruct((span, D), BF),
            jax.ShapeDtypeStruct((2, span, D), F32),
            jax.ShapeDtypeStruct((2, span, D), BF),
        ],
        compiler_params=params(),
        cost_estimate=cost(60 * span * span * D, 12 * MIB),
        name="attention_backward",
    )(live, aug, own, own, other, other, attended, grads)


def feed_body(
    live_ref,
    tokens_ref,
    attended_ref,
    cot_ref,
    gains_ref,
    wo_ref,
    wu_ref,
    wd_ref,
    wu_old_ref,
    wd_old_ref,
    layer_ref,
    rest_ref,
    gm_ref,
    ga_ref,
    gain_ref,
    unit,
    inv,
    normed,
    top,
    acc_out,
    acc_back,
    hidden_keep,
    grad_keep,
    up_stage,
    down_stage,
    out_stage,
    sems,
    out_sem,
):
    step = pl.program_id(0)
    place = step % 2
    side, width = up_stage.shape[1], up_stage.shape[2]
    per_tile = side * width
    up_first = side * side
    down_first = up_first + side * FF // BLK

    def drain(which):
        pltpu.make_async_copy(up_stage.at[which], up_stage.at[which], sems.at[0, which]).wait()
        pltpu.make_async_copy(down_stage.at[which], down_stage.at[which], sems.at[1, which]).wait()
    span = tokens_ref.shape[0]

    @pl.when(step == 0)
    def _():
        weight = join_tile(wo_ref)
        middle = tokens_ref[...].astype(F32) + mul_nn(attended_ref[...], weight)
        unit_vals, inv_std = normalize(middle)
        unit[...] = unit_vals
        inv[...] = inv_std
        normed[...] = (unit_vals * gains_ref[1:2]).astype(BF)
        row = lax.broadcasted_iota(jnp.int32, (span, 1), 0)
        top[...] = jnp.where(row < live_ref[2], cot_ref[...].astype(F32), 0.0).astype(BF)
        acc_out[...] = middle
        acc_back[...] = jnp.zeros_like(acc_back)
        hidden_keep[1] = jnp.zeros_like(hidden_keep[1])
        grad_keep[1] = jnp.zeros_like(grad_keep[1])

    old_hidden, old_grad = hidden_keep[1 - place], grad_keep[1 - place]
    hidden_keep[place] = mul_nn(normed[...], join_tile(wu_ref))
    grad_keep[place] = mul_nt(top[...], join_tile(wd_ref))
    w_up = join_tile(wu_old_ref)
    w_down = join_tile(wd_old_ref)
    erf_part = 0.5 * (1.0 + lax.erf(old_hidden * 0.7071067811865476))
    activated = (old_hidden * erf_part).astype(BF)
    slope = erf_part + old_hidden * jnp.exp(-0.5 * old_hidden * old_hidden) * 0.3989422804014327
    grad_hidden = (old_grad * slope).astype(BF)
    acc_out[...] += mul_nn(activated, w_down)
    acc_back[...] += mul_nt(grad_hidden, w_up)
    down_grad = mul_tn(activated, top[...])
    up_grad = mul_tn(normed[...], grad_hidden)

    @pl.when(step >= 3)
    def _():
        drain(place)

    split_flat(down_stage.at[place], down_grad)
    split_tile(up_stage.at[place], up_grad)

    @pl.when(step >= 1)
    def _():
        dest = rest_ref.at[pl.ds(down_first + (step - 1) * per_tile, per_tile)]
        pltpu.make_async_copy(down_stage.at[place], dest, sems.at[1, place]).start()
        for i in range(side):
            start = up_first + i * (FF // BLK) + (step - 1) * width
            dest = rest_ref.at[pl.ds(start, width)]
            pltpu.make_async_copy(up_stage.at[place, i], dest, sems.at[0, place]).start()

    @pl.when(step == pl.num_programs(0) - 1)
    def _():
        layer_ref[...] = acc_out[...].astype(BF)
        unit_vals = unit[...]
        back = acc_back[...]
        gain_ref[...] = jnp.sum(back * unit_vals, 0, keepdims=True)
        grad_middle = top[...].astype(F32) + norm_back(back * gains_ref[1:2], unit_vals, inv[...])
        gm_ref[...] = grad_middle
        back_middle = grad_middle.astype(BF)
        split_flat(out_stage, mul_tn(attended_ref[...], back_middle))
        out_copy = pltpu.make_async_copy(out_stage, rest_ref.at[pl.ds(0, up_first)], out_sem)
        out_copy.start()
        ga_ref[...] = mul_nt(back_middle, join_tile(wo_ref)).astype(BF)
        drain(1 - place)
        drain(place)
        out_copy.wait()


def feed(live, tokens, attended, cotangent, gains, weights):
    span = tokens.shape[0]
    side, width = D // BLK, COLS // BLK
    whole = lambda j: (0, 0)
    act = pl.BlockSpec((span, D), whole)
    per_row = weights.reshape(-1, side, BLK, BLK)
    per_up = weights.reshape(-1, FF // BLK, BLK, BLK)
    tiles = FF // COLS
    new = lambda j: jnp.minimum(j, tiles - 1)
    old = lambda j: jnp.maximum(j - 1, 0)
    out_row = (3 * side * side) // side // side
    up_row = 4 * side * side // (FF // BLK) // side
    down_row = (4 * side * side + side * FF // BLK) // side // width
    return pl.pallas_call(
        feed_body,
        grid=(tiles + 1,),
        in_specs=[
            pl.BlockSpec(memory_space=pltpu.SMEM),
            act,
            act,
            act,
            pl.BlockSpec((2, D), whole),
            pl.BlockSpec((side, side, BLK, BLK), lambda j: (out_row, 0, 0, 0)),
            pl.BlockSpec((side, width, BLK, BLK), lambda j: (up_row, new(j), 0, 0)),
            pl.BlockSpec((width, side, BLK, BLK), lambda j: (down_row + new(j), 0, 0, 0)),
            pl.BlockSpec((side, width, BLK, BLK), lambda j: (up_row, old(j), 0, 0)),
            pl.BlockSpec((width, side, BLK, BLK), lambda j: (down_row + old(j), 0, 0, 0)),
        ],
        out_specs=[
            act,
            pl.BlockSpec(memory_space=pltpu.HBM),
            act,
            act,
            pl.BlockSpec((1, D), whole),
        ],
        out_shape=[
            jax.ShapeDtypeStruct((span, D), BF),
            jax.ShapeDtypeStruct((side * side + 2 * side * (FF // BLK), BLK, BLK), BF),
            jax.ShapeDtypeStruct((span, D), F32),
            jax.ShapeDtypeStruct((span, D), BF),
            jax.ShapeDtypeStruct((1, D), F32),
        ],
        scratch_shapes=[
            pltpu.VMEM((span, D), F32),
            pltpu.VMEM((span, 1), F32),
            pltpu.VMEM((span, D), BF),
            pltpu.VMEM((span, D), BF),
            pltpu.VMEM((span, D), F32),
            pltpu.VMEM((span, D), F32),
            pltpu.VMEM((2, span, COLS), F32),
            pltpu.VMEM((2, span, COLS), F32),
            pltpu.VMEM((2, side, width, BLK, BLK), BF),
            pltpu.VMEM((2, side * width, BLK, BLK), BF),
            pltpu.VMEM((side * side, BLK, BLK), BF),
            pltpu.SemaphoreType.DMA((2, 2)),
            pltpu.SemaphoreType.DMA,
        ],
        compiler_params=params(),
        cost_estimate=cost(14 * span * D * FF, 50 * MIB),
        name="feed_forward",
    )(
        live, tokens, attended, cotangent, gains, per_row, per_up, per_row, per_up, per_row
    )


def query_body(normed, dq_ref, w_ref, grad_ref, acc_ref):
    step = pl.program_id(0)

    @pl.when(step == 0)
    def _():
        acc_ref[...] = jnp.zeros_like(acc_ref)

    grad = dq_ref[...]
    acc_ref[...] += mul_nt(grad, join_tile(w_ref))
    split_tile(grad_ref, mul_tn(normed[...], grad))


def query_back(normed1, d_query, weights):
    span = normed1.shape[0]
    side, width = D // BLK, COLS // BLK
    whole = lambda j: (0, 0)
    act = pl.BlockSpec((span, D), whole)
    tile = pl.BlockSpec((side, width, BLK, BLK), lambda j: (0, j, 0, 0))
    return pl.pallas_call(
        query_body,
        grid=(D // COLS,),
        in_specs=[act, pl.BlockSpec((span, COLS), lambda j: (0, j)), tile],
        out_specs=[tile, act],
        out_shape=[
            jax.ShapeDtypeStruct((side, side, BLK, BLK), BF),
            jax.ShapeDtypeStruct((span, D), F32),
        ],
        compiler_params=params(),
        cost_estimate=cost(4 * span * D * D, 8 * MIB),
        name="query_backward",
    )(normed1, d_query, weights.reshape(-1, 3 * side, BLK, BLK))


def input_body(
    tokens_ref, gains_ref, normed, own_ref, recv_ref, acc_ref, gm_ref, w_ref, grad_ref, out_ref,
    gain_ref, acc
):
    step = pl.program_id(0)

    @pl.when(step == 0)
    def _():
        acc[...] = acc_ref[...]

    grad = (own_ref[0] + recv_ref[0].astype(F32)).astype(BF)
    acc[...] += mul_nt(grad, join_tile(w_ref))
    split_tile(grad_ref, mul_tn(normed[...], grad))

    @pl.when(step == pl.num_programs(0) - 1)
    def _():
        unit_vals, inv_std = normalize(tokens_ref[...].astype(F32))
        back = acc[...]
        gain_ref[...] = jnp.sum(back * unit_vals, 0, keepdims=True)
        out_ref[...] = (
            gm_ref[...] + norm_back(back * gains_ref[0:1], unit_vals, inv_std)
        ).astype(BF)


def input_back(tokens, gains, normed1, own, received, partial, grad_middle, weights):
    span = tokens.shape[0]
    side, width = D // BLK, COLS // BLK
    per = D // COLS
    whole = lambda j: (0, 0)
    act = pl.BlockSpec((span, D), whole)
    part = pl.BlockSpec((1, span, COLS), lambda j: (j // per, 0, j % per))
    return pl.pallas_call(
        input_body,
        grid=(2 * per,),
        in_specs=[
            act,
            pl.BlockSpec((2, D), whole),
            act,
            part,
            part,
            act,
            act,
            pl.BlockSpec((side, width, BLK, BLK), lambda j: (0, j + per, 0, 0)),
        ],
        out_specs=[
            pl.BlockSpec((side, width, BLK, BLK), lambda j: (0, j, 0, 0)),
            act,
            pl.BlockSpec((1, D), whole),
        ],
        out_shape=[
            jax.ShapeDtypeStruct((side, 2 * side, BLK, BLK), BF),
            jax.ShapeDtypeStruct((span, D), BF),
            jax.ShapeDtypeStruct((1, D), F32),
        ],
        scratch_shapes=[pltpu.VMEM((span, D), F32)],
        compiler_params=params(),
        cost_estimate=cost(8 * span * D * D, 20 * MIB),
        name="input_backward",
    )(
        tokens, gains, normed1, own, received, partial, grad_middle,
        weights.reshape(-1, 3 * side, BLK, BLK),
    )


def source_numbers():
    side = D // BLK
    numbers = np.arange(3 * side * side + side * side + 2 * side * (FF // BLK), dtype=np.int32)
    row, col = np.divmod(numbers[: 3 * side * side], 3 * side)
    numbers[: 3 * side * side] = np.where(
        col < side, row * side + col, side * side + row * 2 * side + col - side
    )
    return numbers


def gather_body(first, bounds, table, *refs):
    sources = refs[:6]
    out_ref, stage, sems = refs[6:]
    step, steps = pl.program_id(0), pl.num_programs(0)
    count = stage.shape[1] // 2

    def fetch(which, slot):
        start = first + which * count
        for i in range(count):
            number = table[start + i]
            for low, high, own, other in zip(bounds, bounds[1:], sources[:3], sources[3:]):

                @pl.when((number >= low) & (number < high))
                def _():
                    for src, at in ((own, i), (other, count + i)):
                        pltpu.make_async_copy(
                            src.at[number - low], stage.at[slot, at], sems.at[slot]
                        ).start()

    @pl.when(step == 0)
    def _():
        fetch(0, 0)

    @pl.when(step + 1 < steps)
    def _():
        fetch(step + 1, (step + 1) % 2)

    slot = step % 2
    pltpu.make_async_copy(stage.at[slot], stage.at[slot], sems.at[slot]).wait()
    total = stage[slot, :count].astype(F32) + stage[slot, count:].astype(F32)
    out_ref[...] = total.astype(BF)


def gather_sums(table, first, count, own, other):
    hbm = pl.BlockSpec(memory_space=pltpu.HBM)
    steps = 4
    part = count // steps
    bounds = np.cumsum([0] + [src.shape[0] for src in own]).tolist()
    return pl.pallas_call(
        functools.partial(gather_body, first, bounds),
        grid=(steps,),
        in_specs=[pl.BlockSpec(memory_space=pltpu.SMEM)] + [hbm] * 6,
        out_specs=pl.BlockSpec((part, BLK, BLK), lambda i: (i, 0, 0)),
        out_shape=jax.ShapeDtypeStruct((count, BLK, BLK), BF),
        scratch_shapes=[
            pltpu.VMEM((2, 2 * part, BLK, BLK), BF),
            pltpu.SemaphoreType.DMA((2,)),
        ],
        compiler_params=params(),
        cost_estimate=cost(0, 6 * count * BLK * BLK),
        name="gradient_sums",
    )(table, *own, *other)


def merge_body(first, second, passed, *refs):
    refs = list(refs)

    def total(count):
        return sum(refs.pop(0)[...].astype(F32) for _ in range(count))

    sums = [total(2), total(2)] if first else []
    if second:
        sums.append(total(3 if passed else 2))
    for ref, value in zip(refs, sums):
        ref[...] = value.astype(BF)


def merge_sums(low, came, kept, last, passed):
    steps = 3
    args, specs, shapes, outs = [], [], [], []

    def part(array, count, start):
        args.append(array)
        size = count // steps
        specs.append(pl.BlockSpec((size, BLK, BLK), lambda i: (i + start * steps, 0, 0)))

    def out(count):
        shapes.append(jax.ShapeDtypeStruct((count, BLK, BLK), BF))
        outs.append(pl.BlockSpec((count // steps, BLK, BLK), lambda i: (i, 0, 0)))

    if low is not None:
        count = low.shape[0] // 2
        for start in range(2):
            part(low, count, start)
            part(came, count, start)
            out(count)
    if kept is not None:
        for array in (kept, last) if passed is None else (kept, last, passed):
            part(array, kept.shape[0], 0)
        out(kept.shape[0])
    body = functools.partial(merge_body, low is not None, kept is not None, passed is not None)
    return pl.pallas_call(
        body,
        grid=(steps,),
        in_specs=specs,
        out_specs=outs,
        out_shape=shapes,
        compiler_params=params(44),
        cost_estimate=cost(0, 6 * MIB),
        name="merge_sums",
    )(*args)


def two_terms(values):
    high = values.astype(BF)
    return high, (values - high.astype(F32)).astype(BF)


def update_body(count, *refs):
    parts = refs[:count]
    m_ref, sl_ref, sr_ref, rl_ref, rr_ref, g_out, sl_out, sr_out, m_out = refs[count:]

    def long_left(terms, axis):
        return jnp.concatenate([terms[0], terms[0], terms[1]], axis)

    def long_right(terms, axis):
        return jnp.concatenate([terms[0], terms[1], terms[0]], axis)

    for i in range(g_out.shape[0]):
        total = sum(part[i].astype(F32) for part in parts)
        g_out[i] = total
        grad = two_terms(total)
        sl_out[i] = sl_ref[i] + mul_nt(long_left(grad, 1), long_right(grad, 1))
        tall = long_right(grad, 0)
        sr_out[i] = sr_ref[i] + mul_tn(long_left(grad, 0), tall)
        inner = mul_nn(long_left(two_terms(rl_ref[i]), 1), tall)
        direction = mul_nn(
            long_left(two_terms(inner), 1), long_right(two_terms(rr_ref[i]), 0)
        )
        master = m_ref[i]
        scale = jnp.sqrt(jnp.mean(master * master, keepdims=True) + 1e-06)
        scale = scale * lax.rsqrt(jnp.mean(direction * direction, keepdims=True) + 1e-06)
        m_out[i] = master - 0.3 * scale * direction


def update(parts, master, stat_left, stat_right, root_left, root_right):
    count = master.shape[0]
    group = 3 if count % 3 == 0 else 1
    block = pl.BlockSpec((group, BLK, BLK), lambda i: (i, 0, 0))
    shape = jax.ShapeDtypeStruct(master.shape, F32)
    return pl.pallas_call(
        functools.partial(update_body, len(parts)),
        grid=(count // group,),
        in_specs=[block] * (len(parts) + 5),
        out_specs=[block] * 4,
        out_shape=[shape] * 4,
        compiler_params=params(),
        cost_estimate=cost(48 * count * BLK**3, 15 * MIB),
        name="block_update",
    )(*parts, master, stat_left, stat_right, root_left, root_right)


def pair_moves():
    moves_same, moves_cross = [], []
    for z in range(4):
        for c in range(2):
            for moves, bit in ((moves_same, z % 2), (moves_cross, 1 - z % 2)):
                moves.append((z * 2 + c, (2 * c + bit) * 2 + z // 2))
    return moves_same, moves_cross


def row_part(values, which):
    return lax.dynamic_index_in_dim(values, which, 0, False)


def move_rows(values, crossed, back=False):
    moves = pair_moves()[crossed]
    return lax.ppermute(values, ("seq", "core"), [(b, a) for a, b in moves] if back else moves)


def in_order(kept, crossed, parity):
    return jnp.where(parity == 0, kept, crossed), jnp.where(parity == 0, crossed, kept)


def spread_rows(values, parity):
    kept = move_rows(row_part(values, parity), False)
    crossed = move_rows(row_part(values, 1 - parity), True)
    return jnp.concatenate(in_order(kept, crossed, parity), 0)


def gather_rows(values, parity):
    parts = values.reshape(2, values.shape[0] // 2, values.shape[1])
    kept = move_rows(row_part(parts, parity), False, True)
    crossed = move_rows(row_part(parts, 1 - parity), True, True)
    return jnp.stack(in_order(kept, crossed, parity), 0)


def swap_cores(values):
    return lax.ppermute(values, "core", [(0, 1), (1, 0)])


def chip_orders(chips):
    bits = [1 << i for i in range(chips.bit_length() - 1)]
    return bits, bits[::-1]


def offsets(order):
    result = [0]
    for bit in order:
        result = result + [o ^ bit for o in result]
    return result


def place_lists(chips, owned, planes):
    shape = (2, planes, chips, owned)
    by_core = np.array([offsets(order) for order in chip_orders(chips)], np.int32)
    grid = np.indices(shape).astype(np.int32).reshape(4, 2, -1)
    offset = np.broadcast_to(by_core[:, None, :, None], shape).reshape(2, -1)
    return grid[1, 0], offset, grid[3, 0]


def swap_chips(values, bits):
    chips = lax.axis_size("chip")
    moves = [(i * 2 + c, (i ^ bits[c]) * 2 + c) for i in range(chips) for c in range(2)]
    return lax.ppermute(values, ("chip", "core"), moves)


def move_planes(values, shift):
    planes = lax.axis_size("seq")
    return lax.ppermute(values, "seq", [(i, (i + shift) % planes) for i in range(planes)])


def after(value, *deps):
    return lax.optimization_barrier((value, *deps))[0]


def together(*values):
    return lax.optimization_barrier(values)


def chip_steps():
    return list(zip(*chip_orders(lax.axis_size("chip"))))


def finish_pieces(pieces):
    for bits in chip_steps()[2:]:
        joined = jnp.concatenate(pieces, 0)
        pieces = [joined, swap_chips(joined, bits)]
    return pieces


def add_halves(kept, came):
    return (kept.astype(F32) + came.astype(F32)).astype(BF)


def pack_terms(values):
    high = lax.optimization_barrier(values.astype(BF))
    low = (values - high.astype(F32)).astype(BF)
    terms = jnp.stack([high, low]).reshape(-1, BLK)
    return jnp.pad(terms, ((0, BLK - terms.shape[0]), (0, 0)))[None]


def unpack_terms(blocks, shape):
    terms = blocks.reshape(-1, BLK, BLK)[:, : 2 * shape[0] * shape[1] // BLK]
    terms = terms.reshape(-1, 2, *shape).astype(F32)
    return terms[:, 0] + terms[:, 1]


def finish_sums(keep, send, riders):
    for bits in chip_steps()[::-1][1:-1]:
        count = keep.shape[0] // 2
        came = swap_chips(with_riders(send, riders), bits)
        riders = more_riders(riders, came, keep.shape[0])
        send = add_halves(keep[count:], came[count : 2 * count])
        keep = add_halves(keep[:count], came[:count])
    return keep, send, riders


def with_riders(send, riders):
    return send if riders is None else jnp.concatenate([send, riders], 0)


def more_riders(riders, came, count):
    return riders if riders is None else jnp.concatenate([riders, came[count:]], 0)


def by_chip(riders, me, core):
    chips = lax.axis_size("chip")
    ranks = np.array([np.argsort(offsets(order[::-1])) for order in chip_orders(chips)], np.int32)
    rank = jnp.asarray(ranks)[core][me ^ jnp.arange(chips, dtype=jnp.int32)]
    return riders.reshape(chips, -1, BLK, BLK)[rank]


def local(
    tokens,
    cotangent,
    lengths,
    owner_perm,
    master,
    norm_gains,
    stat_left,
    stat_right,
    root_left,
    root_right,
    moment_first,
    moment_second,
):
    core = lax.axis_index("core")
    place_z = lax.axis_index("seq")
    parity = place_z % 2
    block_count = owner_perm.shape[0]
    owned = master.shape[0]
    half = block_count // 2

    chips, planes = lax.axis_size("chip"), lax.axis_size("seq")
    me = lax.axis_index("chip")

    pair_lengths = jnp.stack([lengths, swap_cores(lengths)])
    pair_lengths = jnp.where(core == 0, pair_lengths, pair_lengths[::-1]).reshape(-1)
    length = lax.dynamic_index_in_dim(pair_lengths, place_z, 0, False)
    span = tokens.shape[0] * tokens.shape[1]
    live = jnp.stack([length - core * span, length - (1 - core) * span, length - core * span])

    distance, offset, slot = place_lists(chips, owned, planes)
    offset = jnp.where(core == 0, offset, offset[::-1])
    device = ((place_z - distance) % planes * chips + (me ^ offset)) * 2
    device = device + jnp.stack([core, 1 - core])[:, None]
    table = owner_perm[(device * owned + slot).reshape(-1)]
    sums_table = jnp.asarray(source_numbers())[table[:half]]

    shard = master.astype(BF)
    first_bits, second_bits = chip_steps()[:2]
    per_plane = chips * owned
    cross, far, weights = [], [], None
    came, turned = swap_chips(shard, first_bits), swap_chips(shard, second_bits)
    next_shard = move_planes(shard, 1)
    pieces = [[shard, came, turned]]
    for k in range(1, planes):
        ready = (live, table, sums_table) if k == 1 else far[-1:]
        this_shard, came, turned, rows, *done = together(
            next_shard, came, turned, tokens, *cross[-1:], *ready
        )
        if k > 1:
            pieces[k - 2].append(done[0])
        cross.append(swap_chips(came, second_bits))
        came, turned = swap_chips(this_shard, first_bits), swap_chips(this_shard, second_bits)
        pieces.append([this_shard, came, turned])
        if k < planes - 1:
            next_shard = move_planes(this_shard, 1)
        else:
            row_same = move_rows(row_part(rows, parity), False)
            row_cross = row_part(after(rows, row_same), 1 - parity)
            row_cross = move_rows(row_cross, True)
        if k > 1:
            near = jnp.concatenate(finish_pieces(pieces[k - 2]), 0)
            far.append(swap_cores(near))
            weights = place_blocks(table, (k - 2) * per_plane, near, far[-1], weights)
    first = (planes - 1) * per_plane

    def place_piece(piece, first, weights):
        return place_blocks(table, first, piece, swap_cores(piece), weights), first + piece.shape[0]

    came, turned, done, row_same, row_cross, *_ = together(
        came, turned, cross[-1], row_same, row_cross, far[-1], weights
    )
    own_tokens = jnp.concatenate(in_order(row_same, row_cross, parity), 0)
    pieces[-2].append(done)
    pieces[-1][1:] = [came, turned, swap_chips(came, second_bits)]
    near = jnp.concatenate(finish_pieces(pieces[-2]), 0)
    far.append(swap_cores(near))
    weights = place_blocks(table, (planes - 2) * per_plane, near, far[-1], weights)
    other_tokens = swap_cores(own_tokens)
    if len(chip_steps()) == 2:
        for piece in pieces[-1][:3]:
            weights, first = place_piece(piece, first, weights)
        last, *_ = together(pieces[-1][-1], other_tokens)
        weights, _ = place_piece(last, first, weights)
    else:
        weights, _ = place_piece(jnp.concatenate(finish_pieces(pieces[-1]), 0), first, weights)
    own_cot = spread_rows(after(cotangent, weights), parity)

    own_qkv, other_kv, normed1 = project(own_tokens, other_tokens, norm_gains, weights)
    attended, q_aug = attend(live, own_qkv, other_kv)
    layer, g_rest, grad_middle, grad_attended, gain_second = feed(
        live, own_tokens, attended, own_cot, norm_gains, weights
    )
    other_rest = swap_cores(g_rest)
    layer_out = gather_rows(layer, parity)
    d_query, d_own, d_other = attend_back(live, q_aug, own_qkv, other_kv, attended, grad_attended)
    received = swap_cores(after(d_other, layer_out))
    flat = lambda g: g.reshape(-1, BLK, BLK)
    g_query, partial = query_back(normed1, d_query, weights)
    g_query = flat(g_query)
    other_query = swap_cores(g_query)
    g_kv, grad_in, gain_first = input_back(
        own_tokens, norm_gains, normed1, d_own, received, partial, grad_middle, weights
    )
    g_kv = flat(g_kv)
    gain_part = jnp.concatenate([gain_first, gain_second], 0)
    mine = pack_terms(gain_part)
    other_kv_grad = swap_cores(after(g_kv, other_query))
    theirs = swap_cores(mine)
    pair = jnp.concatenate([mine, theirs], 0)
    riders = jnp.where(core == 0, pair, pair[::-1])
    own_grads = (g_query, g_kv, g_rest)
    other_grads = (other_query, other_kv_grad, other_rest)
    half_plane = per_plane // 2
    last_bits, before_bits = chip_steps()[-1], chip_steps()[0]
    halves = grad_in.reshape(2, span // 2, D)
    rows = [row_part(halves, parity), row_part(halves, 1 - parity)]
    moved_rows, lows, sent, passed, riders_z = [], [], None, None, []

    def sums(k, part, held):
        first = k * per_plane + part * half_plane
        return gather_sums(held, first, half_plane, own_grads, other_grads)

    order = list(range(planes))[::-1]
    high = sums(order[0], 1, sums_table)
    held = sums_table
    for turn in range(planes + 1):
        group, moves = [], []
        if turn < planes:
            group.append(with_riders(high, riders if turn == 0 else None))
            moves.append(lambda v: swap_chips(v, last_bits))
        if 1 <= turn <= planes:
            group.append(with_riders(sent, riders if turn == 1 else None))
            moves.append(lambda v: swap_chips(v, before_bits))
        if 2 <= turn <= planes:
            group.append(part)
            moves.append(lambda v: move_planes(v, -1))
        if turn == 1:
            group += rows
            moves += [lambda v: move_rows(v, False, True), lambda v: move_rows(v, True, True)]
        far_riders = [] if turn < planes - 1 else [1, 2] if turn == planes - 1 else range(3, planes)
        group += [rider for _ in far_riders]
        moves += [functools.partial(move_planes, shift=-k) for k in far_riders]
        came = [move(value) for move, value in zip(moves, together(*group, *moved_rows))]
        if turn == 1:
            came, moved_rows = came[:-2], came[-2:]
        count = len(came) - len(far_riders)
        riders_z, came = riders_z + came[count:], came[:count]
        if turn >= 2:
            passed = came.pop()
        if turn < planes:
            low = sums(order[turn], 0, after(held, high))
            if turn + 1 < planes:
                high = sums(order[turn + 1], 1, after(held, low))
            held = after(sums_table, *came)
        last = came[-1]
        if turn == 0:
            riders = more_riders(riders, came[0], half_plane)
        if turn == 1:
            riders = more_riders(riders, last, keep_before.shape[0])
            plane_gain = by_chip(riders, me, core)
            plane_gain = jnp.sum(unpack_terms(plane_gain, gain_part.shape), 0)
            rider = pack_terms(plane_gain)
        if turn == planes:
            parts = [keep_before, last, passed]
            continue
        second = (None, None, None) if turn == 0 else (keep_before, last, passed)
        keep, sent, *part = merge_sums(low, came[0], *second)
        part = part[0] if part else None
        keep_before, sent, grown = finish_sums(keep, sent, riders if turn == 0 else None)
        riders = grown if turn == 0 else riders
    input_grad = jnp.stack(in_order(*moved_rows, parity), 0).astype(F32)
    planes_gain = [unpack_terms(each, gain_part.shape)[0] for each in (rider, *riders_z)]
    turned = (jnp.arange(planes, dtype=jnp.int32) - place_z) % planes
    gain_grad = jnp.sum(jnp.stack(planes_gain)[turned], 0)
    grad_blocks, stat_left_new, stat_right_new, master_new = update(
        parts, master, stat_left, stat_right, root_left, root_right
    )
    first_new = 0.9 * moment_first + 0.1 * gain_grad
    second_new = 0.999 * moment_second + 0.001 * gain_grad * gain_grad
    first_hat = first_new / (1.0 - 0.9**STEP)
    second_hat = second_new / (1.0 - 0.999**STEP)
    gains_new = norm_gains - 0.5 * first_hat / (jnp.sqrt(second_hat) + 1e-08)
    return (
        layer_out,
        input_grad,
        grad_blocks,
        stat_left_new,
        stat_right_new,
        master_new,
        first_new,
        second_new,
        gains_new,
    )


def solution(mesh):
    seq_size, rows_size = mesh.shape["seq"], mesh.shape["rows"]
    mesh = Mesh(mesh.devices.reshape(seq_size, rows_size // 2, 2), ("seq", "chip", "core"))
    activation = P(("chip", "core"), "seq", None)
    blocks = P(("seq", "chip", "core"), None, None)
    return jax.shard_map(
        local,
        mesh=mesh,
        in_specs=(
            activation, activation, P(("chip", "core")), P(), blocks, P(),
            blocks, blocks, blocks, blocks, P(), P(),
        ),
        out_specs=(activation, activation, blocks, blocks, blocks, blocks, P(), P(), P()),
        check_vma=False,
    )
```

```python
import functools
import jax
import jax.numpy as jnp
import numpy as np
from jax import lax
from jax.experimental import pallas as pl
from jax.experimental.pallas import tpu as pltpu
from jax.sharding import Mesh
from jax.sharding import PartitionSpec as P

D = 1024
HD = 64
FF = 4096
BLK = 128
STEP = 10
COLS = 1024
BF = jnp.bfloat16
F32 = jnp.float32
MIB = 1024 * 1024

norm_eps = 1e-05
score_scale = 0.125
masked_score = -1e30


def params(limit=56):
    return pltpu.CompilerParams(vmem_limit_bytes=limit * MIB)


def cost(flops, nbytes):
    return pl.CostEstimate(flops=int(flops), bytes_accessed=int(nbytes), transcendentals=0)


def mul_nn(left, right):
    return jnp.dot(left, right, preferred_element_type=F32)


def mul_nt(left, right):
    return lax.dot_general(left, right, (((1,), (1,)), ((), ())), preferred_element_type=F32)


def mul_tn(left, right):
    return lax.dot_general(left, right, (((0,), (0,)), ((), ())), preferred_element_type=F32)


def join_tile(ref):
    rows, cols = ref.shape[0], ref.shape[1]
    return jnp.concatenate([ref[:, j].reshape(rows * BLK, BLK) for j in range(cols)], axis=1)


def split_tile(ref, matrix):
    rows, cols = ref.shape[0], ref.shape[1]
    for j in range(cols):
        ref[:, j] = matrix[:, j * BLK : (j + 1) * BLK].reshape(rows, BLK, BLK).astype(ref.dtype)


def split_flat(ref, matrix):
    cols = matrix.shape[1] // BLK
    for i in range(matrix.shape[0] // BLK):
        for j in range(cols):
            block = matrix[i * BLK : (i + 1) * BLK, j * BLK : (j + 1) * BLK]
            ref[i * cols + j] = block.astype(ref.dtype)


def normalize(values):
    row_mean = jnp.mean(values, -1, keepdims=True)
    centered = values - row_mean
    row_var = jnp.mean(centered * centered, -1, keepdims=True)
    inv_std = lax.rsqrt(row_var + norm_eps)
    return centered * inv_std, inv_std


def norm_back(gradient, unit_vals, inv_std):
    grad_mean = jnp.mean(gradient, -1, keepdims=True)
    cross_mean = jnp.mean(gradient * unit_vals, -1, keepdims=True)
    return inv_std * (gradient - grad_mean - unit_vals * cross_mean)


def place_body(first, table, near_ref, far_ref, *refs):
    out_ref, sem = refs[-2:]
    count = near_ref.shape[0]
    half = table.shape[0] // 2
    for start, src in ((first, near_ref), (half + first, far_ref)):
        for slot in range(count):
            pltpu.make_async_copy(src.at[slot], out_ref.at[table[start + slot]], sem).start()
    done = out_ref.at[pl.ds(0, 2 * count)]
    pltpu.make_async_copy(done, done, sem).wait()


def place_blocks(table, first, near, far, kept):
    smem = pl.BlockSpec(memory_space=pltpu.SMEM)
    hbm = pl.BlockSpec(memory_space=pltpu.HBM)
    vmem = pl.BlockSpec(memory_space=pltpu.VMEM)
    kept = () if kept is None else (kept,)
    return pl.pallas_call(
        functools.partial(place_body, first),
        out_shape=jax.ShapeDtypeStruct((table.shape[0], BLK, BLK), BF),
        in_specs=[smem, vmem, vmem] + [hbm] * len(kept),
        out_specs=hbm,
        scratch_shapes=[pltpu.SemaphoreType.DMA],
        input_output_aliases={3: 0} if kept else {},
        compiler_params=params(44),
        cost_estimate=cost(0, 4 * near.size * 2),
        name="place_weights",
    )(table, near, far, *kept)


def qkv_body(own_ref, other_ref, gains_ref, w_ref, own_out, other_out, keep_out, normed):
    step = pl.program_id(0)
    span = own_ref.shape[0]

    @pl.when(step == 0)
    def _():
        gain = gains_ref[0:1]
        normed[:span] = (normalize(own_ref[...].astype(F32))[0] * gain).astype(BF)
        normed[span:] = (normalize(other_ref[...].astype(F32))[0] * gain).astype(BF)
        keep_out[...] = normed[:span]

    @pl.when(step < D // COLS)
    def _():
        own_out[...] = mul_nn(normed[:span], join_tile(w_ref)).astype(BF)

    @pl.when(step >= D // COLS)
    def _():
        both = mul_nn(normed[...], join_tile(w_ref)).astype(BF)
        own_out[...] = both[:span]
        other_out[...] = both[span:]


def project(own, other, gains, weights):
    span = own.shape[0]
    skip = D // COLS
    whole = lambda j: (0, 0)
    return pl.pallas_call(
        qkv_body,
        grid=(3 * D // COLS,),
        in_specs=[
            pl.BlockSpec((span, D), whole),
            pl.BlockSpec((span, D), whole),
            pl.BlockSpec((2, D), whole),
            pl.BlockSpec((D // BLK, COLS // BLK, BLK, BLK), lambda j: (0, j, 0, 0)),
        ],
        out_specs=[
            pl.BlockSpec((span, COLS), lambda j: (0, j)),
            pl.BlockSpec((span, COLS), lambda j: (0, jnp.maximum(j - skip, 0))),
            pl.BlockSpec((span, D), whole),
        ],
        out_shape=[
            jax.ShapeDtypeStruct((span, 3 * D), BF),
            jax.ShapeDtypeStruct((span, 2 * D), BF),
            jax.ShapeDtypeStruct((span, D), BF),
        ],
        scratch_shapes=[pltpu.VMEM((2 * span, D), BF)],
        compiler_params=params(),
        cost_estimate=cost(10 * span * D * D, 12 * MIB),
        name="qkv_projection",
    )(own, other, gains, weights.reshape(-1, 3 * D // BLK, BLK, BLK))


def lane_masks(head):
    lane = lax.broadcasted_iota(jnp.int32, (1, BLK), 1)
    first = HD * (1 - head)
    keep = (lane // HD == head).astype(F32)
    dead_lane = (lane == first).astype(F32)
    terms = [(lane == first + 1 + i).astype(F32) for i in range(3)]
    return keep, dead_lane, terms


def three_terms(values):
    high = values.astype(BF).astype(F32)
    rest = values - high
    middle = rest.astype(BF).astype(F32)
    return high, middle, rest - middle


def key_bias(span, live_count):
    row = lax.broadcasted_iota(jnp.int32, (span, 1), 0)
    return jnp.where(row < live_count, 0.0, masked_score).astype(F32)


def attend_body(live_ref, q_ref, ko_ref, vo_ref, kx_ref, vx_ref, out_ref, aug_ref):
    span = q_ref.shape[0]
    bias_own = key_bias(span, live_ref[0])
    bias_other = key_bias(span, live_ref[1])
    queries = q_ref[...].astype(F32) * score_scale
    k_own, k_other = ko_ref[...].astype(F32), kx_ref[...].astype(F32)
    v_own_f, v_other_f = vo_ref[...].astype(F32), vx_ref[...].astype(F32)
    results, scores = [], []
    for head in range(2):
        keep, dead_lane, _ = lane_masks(head)
        q_head = (queries * keep + dead_lane).astype(BF)
        s_own = mul_nt(q_head, (k_own * keep + bias_own * dead_lane).astype(BF))
        s_other = mul_nt(q_head, (k_other * keep + bias_other * dead_lane).astype(BF))
        scores.append((q_head, s_own, s_other))
    for head in range(2):
        keep, _, terms = lane_masks(head)
        q_head, s_own, s_other = scores[head]
        top = jnp.max(jnp.maximum(s_own, s_other), -1, keepdims=True)
        p_own = jnp.exp(s_own - top)
        p_other = jnp.exp(s_other - top)
        v_own = (v_own_f * keep + (1.0 - keep)).astype(BF)
        v_other = (v_other_f * keep + (1.0 - keep)).astype(BF)
        mixed = mul_nn(p_own.astype(BF), v_own) + mul_nn(p_other.astype(BF), v_other)
        total = mixed[:, HD * (1 - head) : HD * (1 - head) + 1]
        results.append(mixed / total * keep)
        parts = three_terms(-(top + jnp.log(total)))
        stats = sum(part * lane for part, lane in zip(parts, terms))
        aug_ref[:, head * BLK : (head + 1) * BLK] = (q_head.astype(F32) + stats).astype(BF)
    out_ref[...] = (results[0] + results[1]).astype(BF)


def attend(live, own, other):
    span = own.shape[0]
    pairs = D // BLK
    col = lambda shift: pl.BlockSpec((span, BLK), lambda p: (0, p + shift))
    return pl.pallas_call(
        attend_body,
        grid=(pairs,),
        in_specs=[
            pl.BlockSpec(memory_space=pltpu.SMEM),
            col(0),
            col(pairs),
            col(2 * pairs),
            col(0),
            col(pairs),
        ],
        out_specs=[col(0), pl.BlockSpec((span, 2 * BLK), lambda p: (0, p))],
        out_shape=[
            jax.ShapeDtypeStruct((span, D), BF),
            jax.ShapeDtypeStruct((span, 2 * D), BF),
        ],
        compiler_params=params(),
        cost_estimate=cost(40 * span * span * D, 8 * MIB),
        name="attention",
    )(live, own, own, own, other, other)


def attend_back_body(
    live_ref, aug_ref, ko_ref, vo_ref, kx_ref, vx_ref, at_ref, g_ref, dq_ref, own_ref, other_ref
):
    span = at_ref.shape[0]
    grads = g_ref[...].astype(F32)
    product = grads * at_ref[...].astype(F32)
    keeps, g_augs, q_augs = [], [], []
    for head in range(2):
        keep, dead_lane, terms = lane_masks(head)
        delta = jnp.sum(product * keep, -1, keepdims=True)
        parts = three_terms(-delta)
        stats = sum(part * lane for part, lane in zip(parts, terms))
        g_augs.append((grads * keep + stats).astype(BF))
        q_augs.append(aug_ref[:, head * BLK : (head + 1) * BLK])
    d_query = [None, None]
    for k_ref, v_ref, out_ref, live in (
        (ko_ref, vo_ref, own_ref, live_ref[0]),
        (kx_ref, vx_ref, other_ref, live_ref[1]),
    ):
        bias = key_bias(span, live)
        keys = k_ref[...]
        keys_f, values_f = keys.astype(F32), v_ref[...].astype(F32)
        d_keys = d_values = None
        for head in range(2):
            keep, dead_lane, terms = lane_masks(head)
            ones = terms[0] + terms[1] + terms[2]
            k_aug = (keys_f * keep + (bias * dead_lane + ones)).astype(BF)
            v_aug = (values_f * keep + ones).astype(BF)
            probs = jnp.exp(mul_nt(k_aug, q_augs[head]))
            d_scores = (probs * mul_nt(v_aug, g_augs[head])).astype(BF)
            value_part = mul_nn(probs.astype(BF), g_augs[head]) * keep
            key_part = mul_nn(d_scores, q_augs[head]) * keep
            query_part = mul_tn(d_scores, keys) * (keep * score_scale)
            d_query[head] = query_part if d_query[head] is None else d_query[head] + query_part
            d_values = value_part if d_values is None else d_values + value_part
            d_keys = key_part if d_keys is None else d_keys + key_part
        out_ref[0] = d_keys.astype(out_ref.dtype)
        out_ref[1] = d_values.astype(out_ref.dtype)
    dq_ref[...] = (d_query[0] + d_query[1]).astype(BF)


def attend_back(live, aug, own, other, attended, grads):
    span = own.shape[0]
    pairs = D // BLK
    col = lambda shift: pl.BlockSpec((span, BLK), lambda p: (0, p + shift))
    pair_out = pl.BlockSpec((2, span, BLK), lambda p: (0, 0, p))
    return pl.pallas_call(
        attend_back_body,
        grid=(pairs,),
        in_specs=[
            pl.BlockSpec(memory_space=pltpu.SMEM),
            pl.BlockSpec((span, 2 * BLK), lambda p: (0, p)),
            col(pairs),
            col(2 * pairs),
            col(0),
            col(pairs),
            col(0),
            col(0),
        ],
        out_specs=[col(0), pair_out, pair_out],
        out_shape=[
            jax.ShapeDtypeStruct((span, D), BF),
            jax.ShapeDtypeStruct((2, span, D), F32),
            jax.ShapeDtypeStruct((2, span, D), BF),
        ],
        compiler_params=params(),
        cost_estimate=cost(60 * span * span * D, 12 * MIB),
        name="attention_backward",
    )(live, aug, own, own, other, other, attended, grads)


def feed_body(
    live_ref,
    tokens_ref,
    attended_ref,
    cot_ref,
    gains_ref,
    wo_ref,
    wu_ref,
    wd_ref,
    layer_ref,
    rest_ref,
    gm_ref,
    ga_ref,
    gain_ref,
    unit,
    inv,
    normed,
    top,
    acc_out,
    acc_back,
    up_stage,
    down_stage,
    out_stage,
    sems,
    out_sem,
):
    step = pl.program_id(0)
    place = step % 2
    side, width = up_stage.shape[1], up_stage.shape[2]
    per_tile = side * width
    up_first = side * side
    down_first = up_first + side * FF // BLK

    def drain(which):
        pltpu.make_async_copy(up_stage.at[which], up_stage.at[which], sems.at[0, which]).wait()
        pltpu.make_async_copy(down_stage.at[which], down_stage.at[which], sems.at[1, which]).wait()
    span = tokens_ref.shape[0]

    @pl.when(step == 0)
    def _():
        weight = join_tile(wo_ref)
        middle = tokens_ref[...].astype(F32) + mul_nn(attended_ref[...], weight)
        unit_vals, inv_std = normalize(middle)
        unit[...] = unit_vals
        inv[...] = inv_std
        normed[...] = (unit_vals * gains_ref[1:2]).astype(BF)
        row = lax.broadcasted_iota(jnp.int32, (span, 1), 0)
        top[...] = jnp.where(row < live_ref[2], cot_ref[...].astype(F32), 0.0).astype(BF)
        acc_out[...] = middle
        acc_back[...] = jnp.zeros_like(acc_back)

    w_up = join_tile(wu_ref)
    w_down = join_tile(wd_ref)
    hidden = mul_nn(normed[...], w_up)
    grad_act = mul_nt(top[...], w_down)
    erf_part = 0.5 * (1.0 + lax.erf(hidden * 0.7071067811865476))
    activated = (hidden * erf_part).astype(BF)
    slope = erf_part + hidden * jnp.exp(-0.5 * hidden * hidden) * 0.3989422804014327
    grad_hidden = (grad_act * slope).astype(BF)
    acc_out[...] += mul_nn(activated, w_down)
    acc_back[...] += mul_nt(grad_hidden, w_up)

    @pl.when(step >= 2)
    def _():
        drain(place)

    split_flat(down_stage.at[place], mul_tn(activated, top[...]))
    dest = rest_ref.at[pl.ds(down_first + step * per_tile, per_tile)]
    pltpu.make_async_copy(down_stage.at[place], dest, sems.at[1, place]).start()
    split_tile(up_stage.at[place], mul_tn(normed[...], grad_hidden))
    for i in range(side):
        dest = rest_ref.at[pl.ds(up_first + i * (FF // BLK) + step * width, width)]
        pltpu.make_async_copy(up_stage.at[place, i], dest, sems.at[0, place]).start()

    @pl.when(step == pl.num_programs(0) - 1)
    def _():
        layer_ref[...] = acc_out[...].astype(BF)
        unit_vals = unit[...]
        back = acc_back[...]
        gain_ref[...] = jnp.sum(back * unit_vals, 0, keepdims=True)
        grad_middle = top[...].astype(F32) + norm_back(back * gains_ref[1:2], unit_vals, inv[...])
        gm_ref[...] = grad_middle
        back_middle = grad_middle.astype(BF)
        split_flat(out_stage, mul_tn(attended_ref[...], back_middle))
        out_copy = pltpu.make_async_copy(out_stage, rest_ref.at[pl.ds(0, up_first)], out_sem)
        out_copy.start()
        ga_ref[...] = mul_nt(back_middle, join_tile(wo_ref)).astype(BF)
        drain(1 - place)
        drain(place)
        out_copy.wait()


def feed(live, tokens, attended, cotangent, gains, weights):
    span = tokens.shape[0]
    side, width = D // BLK, COLS // BLK
    whole = lambda j: (0, 0)
    act = pl.BlockSpec((span, D), whole)
    once = pl.BlockSpec((span, D), whole, pipeline_mode=pl.Buffered(1))
    per_row = weights.reshape(-1, side, BLK, BLK)
    per_up = weights.reshape(-1, FF // BLK, BLK, BLK)
    out_row = (3 * side * side) // side // side
    up_row = 4 * side * side // (FF // BLK) // side
    down_row = (4 * side * side + side * FF // BLK) // side // width
    return pl.pallas_call(
        feed_body,
        grid=(FF // COLS,),
        in_specs=[
            pl.BlockSpec(memory_space=pltpu.SMEM),
            once,
            once,
            once,
            pl.BlockSpec((2, D), whole),
            pl.BlockSpec(
                (side, side, BLK, BLK),
                lambda j: (out_row, 0, 0, 0),
                pipeline_mode=pl.Buffered(1),
            ),
            pl.BlockSpec((side, width, BLK, BLK), lambda j: (up_row, j, 0, 0)),
            pl.BlockSpec((width, side, BLK, BLK), lambda j: (down_row + j, 0, 0, 0)),
        ],
        out_specs=[
            act,
            pl.BlockSpec(memory_space=pltpu.HBM),
            act,
            act,
            pl.BlockSpec((1, D), whole),
        ],
        out_shape=[
            jax.ShapeDtypeStruct((span, D), BF),
            jax.ShapeDtypeStruct((side * side + 2 * side * (FF // BLK), BLK, BLK), BF),
            jax.ShapeDtypeStruct((span, D), F32),
            jax.ShapeDtypeStruct((span, D), BF),
            jax.ShapeDtypeStruct((1, D), F32),
        ],
        scratch_shapes=[
            pltpu.VMEM((span, D), F32),
            pltpu.VMEM((span, 1), F32),
            pltpu.VMEM((span, D), BF),
            pltpu.VMEM((span, D), BF),
            pltpu.VMEM((span, D), F32),
            pltpu.VMEM((span, D), F32),
            pltpu.VMEM((2, side, width, BLK, BLK), BF),
            pltpu.VMEM((2, side * width, BLK, BLK), BF),
            pltpu.VMEM((side * side, BLK, BLK), BF),
            pltpu.SemaphoreType.DMA((2, 2)),
            pltpu.SemaphoreType.DMA,
        ],
        compiler_params=params(),
        cost_estimate=cost(14 * span * D * FF, 50 * MIB),
        name="feed_forward",
    )(live, tokens, attended, cotangent, gains, per_row, per_up, per_row)


def query_body(normed, dq_ref, w_ref, grad_ref, acc_ref):
    step = pl.program_id(0)

    @pl.when(step == 0)
    def _():
        acc_ref[...] = jnp.zeros_like(acc_ref)

    grad = dq_ref[...]
    acc_ref[...] += mul_nt(grad, join_tile(w_ref))
    split_tile(grad_ref, mul_tn(normed[...], grad))


def query_back(normed1, d_query, weights):
    span = normed1.shape[0]
    side, width = D // BLK, COLS // BLK
    whole = lambda j: (0, 0)
    act = pl.BlockSpec((span, D), whole)
    tile = pl.BlockSpec((side, width, BLK, BLK), lambda j: (0, j, 0, 0))
    return pl.pallas_call(
        query_body,
        grid=(D // COLS,),
        in_specs=[act, pl.BlockSpec((span, COLS), lambda j: (0, j)), tile],
        out_specs=[tile, act],
        out_shape=[
            jax.ShapeDtypeStruct((side, side, BLK, BLK), BF),
            jax.ShapeDtypeStruct((span, D), F32),
        ],
        compiler_params=params(),
        cost_estimate=cost(4 * span * D * D, 8 * MIB),
        name="query_backward",
    )(normed1, d_query, weights.reshape(-1, 3 * side, BLK, BLK))


def input_body(
    tokens_ref, gains_ref, normed, own_ref, recv_ref, acc_ref, gm_ref, w_ref, grad_ref, out_ref,
    gain_ref, acc
):
    step = pl.program_id(0)

    @pl.when(step == 0)
    def _():
        acc[...] = acc_ref[...]

    grad = (own_ref[0] + recv_ref[0].astype(F32)).astype(BF)
    acc[...] += mul_nt(grad, join_tile(w_ref))
    split_tile(grad_ref, mul_tn(normed[...], grad))

    @pl.when(step == pl.num_programs(0) - 1)
    def _():
        unit_vals, inv_std = normalize(tokens_ref[...].astype(F32))
        back = acc[...]
        gain_ref[...] = jnp.sum(back * unit_vals, 0, keepdims=True)
        out_ref[...] = (
            gm_ref[...] + norm_back(back * gains_ref[0:1], unit_vals, inv_std)
        ).astype(BF)


def input_back(tokens, gains, normed1, own, received, partial, grad_middle, weights):
    span = tokens.shape[0]
    side, width = D // BLK, COLS // BLK
    per = D // COLS
    whole = lambda j: (0, 0)
    act = pl.BlockSpec((span, D), whole)
    part = pl.BlockSpec((1, span, COLS), lambda j: (j // per, 0, j % per))
    return pl.pallas_call(
        input_body,
        grid=(2 * per,),
        in_specs=[
            act,
            pl.BlockSpec((2, D), whole),
            act,
            part,
            part,
            act,
            act,
            pl.BlockSpec((side, width, BLK, BLK), lambda j: (0, j + per, 0, 0)),
        ],
        out_specs=[
            pl.BlockSpec((side, width, BLK, BLK), lambda j: (0, j, 0, 0)),
            act,
            pl.BlockSpec((1, D), whole),
        ],
        out_shape=[
            jax.ShapeDtypeStruct((side, 2 * side, BLK, BLK), BF),
            jax.ShapeDtypeStruct((span, D), BF),
            jax.ShapeDtypeStruct((1, D), F32),
        ],
        scratch_shapes=[pltpu.VMEM((span, D), F32)],
        compiler_params=params(),
        cost_estimate=cost(8 * span * D * D, 20 * MIB),
        name="input_backward",
    )(
        tokens, gains, normed1, own, received, partial, grad_middle,
        weights.reshape(-1, 3 * side, BLK, BLK),
    )


def source_numbers():
    side = D // BLK
    numbers = np.arange(3 * side * side + side * side + 2 * side * (FF // BLK), dtype=np.int32)
    row, col = np.divmod(numbers[: 3 * side * side], 3 * side)
    numbers[: 3 * side * side] = np.where(
        col < side, row * side + col, side * side + row * 2 * side + col - side
    )
    return numbers


def gather_body(first, bounds, table, *refs):
    sources = refs[:6]
    out_ref, stage, sems = refs[6:]
    step, steps = pl.program_id(0), pl.num_programs(0)
    count = stage.shape[1] // 2

    def fetch(which, slot):
        start = first + which * count
        for i in range(count):
            number = table[start + i]
            for low, high, own, other in zip(bounds, bounds[1:], sources[:3], sources[3:]):

                @pl.when((number >= low) & (number < high))
                def _():
                    for src, at in ((own, i), (other, count + i)):
                        pltpu.make_async_copy(
                            src.at[number - low], stage.at[slot, at], sems.at[slot]
                        ).start()

    @pl.when(step == 0)
    def _():
        fetch(0, 0)

    @pl.when(step + 1 < steps)
    def _():
        fetch(step + 1, (step + 1) % 2)

    slot = step % 2
    pltpu.make_async_copy(stage.at[slot], stage.at[slot], sems.at[slot]).wait()
    total = stage[slot, :count].astype(F32) + stage[slot, count:].astype(F32)
    out_ref[...] = total.astype(BF)


def gather_sums(table, first, count, own, other):
    hbm = pl.BlockSpec(memory_space=pltpu.HBM)
    steps = 4
    part = count // steps
    bounds = np.cumsum([0] + [src.shape[0] for src in own]).tolist()
    return pl.pallas_call(
        functools.partial(gather_body, first, bounds),
        grid=(steps,),
        in_specs=[pl.BlockSpec(memory_space=pltpu.SMEM)] + [hbm] * 6,
        out_specs=pl.BlockSpec((part, BLK, BLK), lambda i: (i, 0, 0)),
        out_shape=jax.ShapeDtypeStruct((count, BLK, BLK), BF),
        scratch_shapes=[
            pltpu.VMEM((2, 2 * part, BLK, BLK), BF),
            pltpu.SemaphoreType.DMA((2,)),
        ],
        compiler_params=params(),
        cost_estimate=cost(0, 6 * count * BLK * BLK),
        name="gradient_sums",
    )(table, *own, *other)


def merge_body(first, second, passed, *refs):
    refs = list(refs)

    def total(count):
        return sum(refs.pop(0)[...].astype(F32) for _ in range(count))

    sums = [total(2), total(2)] if first else []
    if second:
        sums.append(total(3 if passed else 2))
    for ref, value in zip(refs, sums):
        ref[...] = value.astype(BF)


def merge_sums(low, came, kept, last, passed):
    steps = 3
    args, specs, shapes, outs = [], [], [], []

    def part(array, count, start):
        args.append(array)
        size = count // steps
        specs.append(pl.BlockSpec((size, BLK, BLK), lambda i: (i + start * steps, 0, 0)))

    def out(count):
        shapes.append(jax.ShapeDtypeStruct((count, BLK, BLK), BF))
        outs.append(pl.BlockSpec((count // steps, BLK, BLK), lambda i: (i, 0, 0)))

    if low is not None:
        count = low.shape[0] // 2
        for start in range(2):
            part(low, count, start)
            part(came, count, start)
            out(count)
    if kept is not None:
        for array in (kept, last) if passed is None else (kept, last, passed):
            part(array, kept.shape[0], 0)
        out(kept.shape[0])
    body = functools.partial(merge_body, low is not None, kept is not None, passed is not None)
    return pl.pallas_call(
        body,
        grid=(steps,),
        in_specs=specs,
        out_specs=outs,
        out_shape=shapes,
        compiler_params=params(44),
        cost_estimate=cost(0, 6 * MIB),
        name="merge_sums",
    )(*args)


def two_terms(values):
    high = values.astype(BF)
    return high, (values - high.astype(F32)).astype(BF)


def update_body(count, *refs):
    parts = refs[:count]
    m_ref, sl_ref, sr_ref, rl_ref, rr_ref, g_out, sl_out, sr_out, m_out = refs[count:]

    def long_left(terms, axis):
        return jnp.concatenate([terms[0], terms[0], terms[1]], axis)

    def long_right(terms, axis):
        return jnp.concatenate([terms[0], terms[1], terms[0]], axis)

    for i in range(g_out.shape[0]):
        total = sum(part[i].astype(F32) for part in parts)
        g_out[i] = total
        grad = two_terms(total)
        sl_out[i] = sl_ref[i] + mul_nt(long_left(grad, 1), long_right(grad, 1))
        tall = long_right(grad, 0)
        sr_out[i] = sr_ref[i] + mul_tn(long_left(grad, 0), tall)
        inner = mul_nn(long_left(two_terms(rl_ref[i]), 1), tall)
        direction = mul_nn(
            long_left(two_terms(inner), 1), long_right(two_terms(rr_ref[i]), 0)
        )
        master = m_ref[i]
        scale = jnp.sqrt(jnp.mean(master * master, keepdims=True) + 1e-06)
        scale = scale * lax.rsqrt(jnp.mean(direction * direction, keepdims=True) + 1e-06)
        m_out[i] = master - 0.3 * scale * direction


def update(parts, master, stat_left, stat_right, root_left, root_right):
    count = master.shape[0]
    group = 3 if count % 3 == 0 else 1
    block = pl.BlockSpec((group, BLK, BLK), lambda i: (i, 0, 0))
    shape = jax.ShapeDtypeStruct(master.shape, F32)
    return pl.pallas_call(
        functools.partial(update_body, len(parts)),
        grid=(count // group,),
        in_specs=[block] * (len(parts) + 5),
        out_specs=[block] * 4,
        out_shape=[shape] * 4,
        compiler_params=params(),
        cost_estimate=cost(48 * count * BLK**3, 15 * MIB),
        name="block_update",
    )(*parts, master, stat_left, stat_right, root_left, root_right)


def pair_moves():
    moves_same, moves_cross = [], []
    for z in range(4):
        for c in range(2):
            for moves, bit in ((moves_same, z % 2), (moves_cross, 1 - z % 2)):
                moves.append((z * 2 + c, (2 * c + bit) * 2 + z // 2))
    return moves_same, moves_cross


def row_part(values, which):
    return lax.dynamic_index_in_dim(values, which, 0, False)


def move_rows(values, crossed, back=False):
    moves = pair_moves()[crossed]
    return lax.ppermute(values, ("seq", "core"), [(b, a) for a, b in moves] if back else moves)


def in_order(kept, crossed, parity):
    return jnp.where(parity == 0, kept, crossed), jnp.where(parity == 0, crossed, kept)


def spread_rows(values, parity):
    kept = move_rows(row_part(values, parity), False)
    crossed = move_rows(row_part(values, 1 - parity), True)
    return jnp.concatenate(in_order(kept, crossed, parity), 0)


def gather_rows(values, parity):
    parts = values.reshape(2, values.shape[0] // 2, values.shape[1])
    kept = move_rows(row_part(parts, parity), False, True)
    crossed = move_rows(row_part(parts, 1 - parity), True, True)
    return jnp.stack(in_order(kept, crossed, parity), 0)


def swap_cores(values):
    return lax.ppermute(values, "core", [(0, 1), (1, 0)])


def chip_orders(chips):
    bits = [1 << i for i in range(chips.bit_length() - 1)]
    return bits, bits[::-1]


def offsets(order):
    result = [0]
    for bit in order:
        result = result + [o ^ bit for o in result]
    return result


def place_lists(chips, owned, planes):
    shape = (2, planes, chips, owned)
    by_core = np.array([offsets(order) for order in chip_orders(chips)], np.int32)
    grid = np.indices(shape).astype(np.int32).reshape(4, 2, -1)
    offset = np.broadcast_to(by_core[:, None, :, None], shape).reshape(2, -1)
    return grid[1, 0], offset, grid[3, 0]


def swap_chips(values, bits):
    chips = lax.axis_size("chip")
    moves = [(i * 2 + c, (i ^ bits[c]) * 2 + c) for i in range(chips) for c in range(2)]
    return lax.ppermute(values, ("chip", "core"), moves)


def move_planes(values, shift):
    planes = lax.axis_size("seq")
    return lax.ppermute(values, "seq", [(i, (i + shift) % planes) for i in range(planes)])


def after(value, *deps):
    return lax.optimization_barrier((value, *deps))[0]


def together(*values):
    return lax.optimization_barrier(values)


def chip_steps():
    return list(zip(*chip_orders(lax.axis_size("chip"))))


def finish_pieces(pieces):
    for bits in chip_steps()[2:]:
        joined = jnp.concatenate(pieces, 0)
        pieces = [joined, swap_chips(joined, bits)]
    return pieces


def add_halves(kept, came):
    return (kept.astype(F32) + came.astype(F32)).astype(BF)


def pack_terms(values):
    high = lax.optimization_barrier(values.astype(BF))
    low = (values - high.astype(F32)).astype(BF)
    terms = jnp.stack([high, low]).reshape(-1, BLK)
    return jnp.pad(terms, ((0, BLK - terms.shape[0]), (0, 0)))[None]


def unpack_terms(blocks, shape):
    terms = blocks.reshape(-1, BLK, BLK)[:, : 2 * shape[0] * shape[1] // BLK]
    terms = terms.reshape(-1, 2, *shape).astype(F32)
    return terms[:, 0] + terms[:, 1]


def finish_sums(keep, send, riders):
    for bits in chip_steps()[::-1][1:-1]:
        count = keep.shape[0] // 2
        came = swap_chips(with_riders(send, riders), bits)
        riders = more_riders(riders, came, keep.shape[0])
        send = add_halves(keep[count:], came[count : 2 * count])
        keep = add_halves(keep[:count], came[:count])
    return keep, send, riders


def with_riders(send, riders):
    return send if riders is None else jnp.concatenate([send, riders], 0)


def more_riders(riders, came, count):
    return riders if riders is None else jnp.concatenate([riders, came[count:]], 0)


def by_chip(riders, me, core):
    chips = lax.axis_size("chip")
    ranks = np.array([np.argsort(offsets(order[::-1])) for order in chip_orders(chips)], np.int32)
    rank = jnp.asarray(ranks)[core][me ^ jnp.arange(chips, dtype=jnp.int32)]
    return riders.reshape(chips, -1, BLK, BLK)[rank]


def local(
    tokens,
    cotangent,
    lengths,
    owner_perm,
    master,
    norm_gains,
    stat_left,
    stat_right,
    root_left,
    root_right,
    moment_first,
    moment_second,
):
    core = lax.axis_index("core")
    place_z = lax.axis_index("seq")
    parity = place_z % 2
    block_count = owner_perm.shape[0]
    owned = master.shape[0]
    half = block_count // 2

    chips, planes = lax.axis_size("chip"), lax.axis_size("seq")
    me = lax.axis_index("chip")

    pair_lengths = jnp.stack([lengths, swap_cores(lengths)])
    pair_lengths = jnp.where(core == 0, pair_lengths, pair_lengths[::-1]).reshape(-1)
    length = lax.dynamic_index_in_dim(pair_lengths, place_z, 0, False)
    span = tokens.shape[0] * tokens.shape[1]
    live = jnp.stack([length - core * span, length - (1 - core) * span, length - core * span])

    distance, offset, slot = place_lists(chips, owned, planes)
    offset = jnp.where(core == 0, offset, offset[::-1])
    device = ((place_z - distance) % planes * chips + (me ^ offset)) * 2
    device = device + jnp.stack([core, 1 - core])[:, None]
    table = owner_perm[(device * owned + slot).reshape(-1)]
    sums_table = jnp.asarray(source_numbers())[table[:half]]

    shard = master.astype(BF)
    first_bits, second_bits = chip_steps()[:2]
    per_plane = chips * owned
    cross, far, weights = [], [], None
    came, turned = swap_chips(shard, first_bits), swap_chips(shard, second_bits)
    next_shard = move_planes(shard, 1)
    pieces = [[shard, came, turned]]
    for k in range(1, planes):
        ready = (live, table, sums_table) if k == 1 else far[-1:]
        this_shard, came, turned, rows, *done = together(
            next_shard, came, turned, tokens, *cross[-1:], *ready
        )
        if k > 1:
            pieces[k - 2].append(done[0])
        cross.append(swap_chips(came, second_bits))
        came, turned = swap_chips(this_shard, first_bits), swap_chips(this_shard, second_bits)
        pieces.append([this_shard, came, turned])
        if k < planes - 1:
            next_shard = move_planes(this_shard, 1)
        else:
            row_same = move_rows(row_part(rows, parity), False)
            row_cross = row_part(after(rows, row_same), 1 - parity)
            row_cross = move_rows(row_cross, True)
        if k > 1:
            near = jnp.concatenate(finish_pieces(pieces[k - 2]), 0)
            far.append(swap_cores(near))
            weights = place_blocks(table, (k - 2) * per_plane, near, far[-1], weights)
    first = (planes - 1) * per_plane

    def place_piece(piece, first, weights):
        return place_blocks(table, first, piece, swap_cores(piece), weights), first + piece.shape[0]

    came, turned, done, row_same, row_cross, *_ = together(
        came, turned, cross[-1], row_same, row_cross, far[-1], weights
    )
    own_tokens = jnp.concatenate(in_order(row_same, row_cross, parity), 0)
    pieces[-2].append(done)
    pieces[-1][1:] = [came, turned, swap_chips(came, second_bits)]
    near = jnp.concatenate(finish_pieces(pieces[-2]), 0)
    far.append(swap_cores(near))
    weights = place_blocks(table, (planes - 2) * per_plane, near, far[-1], weights)
    other_tokens = swap_cores(own_tokens)
    if len(chip_steps()) == 2:
        for piece in pieces[-1][:3]:
            weights, first = place_piece(piece, first, weights)
        last, *_ = together(pieces[-1][-1], other_tokens, weights)
        weights, _ = place_piece(last, first, weights)
    else:
        weights, _ = place_piece(jnp.concatenate(finish_pieces(pieces[-1]), 0), first, weights)
    own_cot = spread_rows(after(cotangent, weights), parity)

    own_qkv, other_kv, normed1 = project(own_tokens, other_tokens, norm_gains, weights)
    attended, q_aug = attend(live, own_qkv, other_kv)
    layer, g_rest, grad_middle, grad_attended, gain_second = feed(
        live, own_tokens, attended, own_cot, norm_gains, weights
    )
    other_rest = swap_cores(g_rest)
    layer_out = gather_rows(layer, parity)
    d_query, d_own, d_other = attend_back(live, q_aug, own_qkv, other_kv, attended, grad_attended)
    received = swap_cores(after(d_other, layer_out))
    flat = lambda g: g.reshape(-1, BLK, BLK)
    g_query, partial = query_back(normed1, d_query, weights)
    g_query = flat(g_query)
    other_query = swap_cores(g_query)
    g_kv, grad_in, gain_first = input_back(
        own_tokens, norm_gains, normed1, d_own, received, partial, grad_middle, weights
    )
    g_kv = flat(g_kv)
    gain_part = jnp.concatenate([gain_first, gain_second], 0)
    mine = pack_terms(gain_part)
    other_kv_grad = swap_cores(after(g_kv, other_query))
    theirs = swap_cores(mine)
    pair = jnp.concatenate([mine, theirs], 0)
    riders = jnp.where(core == 0, pair, pair[::-1])
    own_grads = (g_query, g_kv, g_rest)
    other_grads = (other_query, other_kv_grad, other_rest)
    half_plane = per_plane // 2
    last_bits, before_bits = chip_steps()[-1], chip_steps()[0]
    halves = grad_in.reshape(2, span // 2, D)
    rows = [row_part(halves, parity), row_part(halves, 1 - parity)]
    moved_rows, lows, sent, passed, riders_z = [], [], None, None, []

    def sums(k, part, held):
        first = k * per_plane + part * half_plane
        return gather_sums(held, first, half_plane, own_grads, other_grads)

    order = list(range(planes))[::-1]
    high = sums(order[0], 1, sums_table)
    held = sums_table
    for turn in range(planes + 1):
        group, moves = [], []
        if turn < planes:
            group.append(with_riders(high, riders if turn == 0 else None))
            moves.append(lambda v: swap_chips(v, last_bits))
        if 1 <= turn <= planes:
            group.append(with_riders(sent, riders if turn == 1 else None))
            moves.append(lambda v: swap_chips(v, before_bits))
        if 2 <= turn <= planes:
            group.append(part)
            moves.append(lambda v: move_planes(v, -1))
        if turn == 1:
            group += rows
            moves += [lambda v: move_rows(v, False, True), lambda v: move_rows(v, True, True)]
        far_riders = [] if turn < planes - 1 else [1, 2] if turn == planes - 1 else range(3, planes)
        group += [rider for _ in far_riders]
        moves += [functools.partial(move_planes, shift=-k) for k in far_riders]
        came = [move(value) for move, value in zip(moves, together(*group, *moved_rows))]
        if turn == 1:
            came, moved_rows = came[:-2], came[-2:]
        count = len(came) - len(far_riders)
        riders_z, came = riders_z + came[count:], came[:count]
        if turn >= 2:
            passed = came.pop()
        if turn < planes:
            low = sums(order[turn], 0, after(held, high))
            if turn + 1 < planes:
                high = sums(order[turn + 1], 1, after(held, low))
            held = after(sums_table, *came)
        last = came[-1]
        if turn == 0:
            riders = more_riders(riders, came[0], half_plane)
        if turn == 1:
            riders = more_riders(riders, last, keep_before.shape[0])
            plane_gain = by_chip(riders, me, core)
            plane_gain = jnp.sum(unpack_terms(plane_gain, gain_part.shape), 0)
            rider = pack_terms(plane_gain)
        if turn == planes:
            parts = [keep_before, last, passed]
            continue
        second = (None, None, None) if turn == 0 else (keep_before, last, passed)
        keep, sent, *part = merge_sums(low, came[0], *second)
        part = part[0] if part else None
        keep_before, sent, grown = finish_sums(keep, sent, riders if turn == 0 else None)
        riders = grown if turn == 0 else riders
    input_grad = jnp.stack(in_order(*moved_rows, parity), 0).astype(F32)
    planes_gain = [unpack_terms(each, gain_part.shape)[0] for each in (rider, *riders_z)]
    turned = (jnp.arange(planes, dtype=jnp.int32) - place_z) % planes
    gain_grad = jnp.sum(jnp.stack(planes_gain)[turned], 0)
    grad_blocks, stat_left_new, stat_right_new, master_new = update(
        parts, master, stat_left, stat_right, root_left, root_right
    )
    first_new = 0.9 * moment_first + 0.1 * gain_grad
    second_new = 0.999 * moment_second + 0.001 * gain_grad * gain_grad
    first_hat = first_new / (1.0 - 0.9**STEP)
    second_hat = second_new / (1.0 - 0.999**STEP)
    gains_new = norm_gains - 0.5 * first_hat / (jnp.sqrt(second_hat) + 1e-08)
    return (
        layer_out,
        input_grad,
        grad_blocks,
        stat_left_new,
        stat_right_new,
        master_new,
        first_new,
        second_new,
        gains_new,
    )


def solution(mesh):
    seq_size, rows_size = mesh.shape["seq"], mesh.shape["rows"]
    mesh = Mesh(mesh.devices.reshape(seq_size, rows_size // 2, 2), ("seq", "chip", "core"))
    activation = P(("chip", "core"), "seq", None)
    blocks = P(("seq", "chip", "core"), None, None)
    return jax.shard_map(
        local,
        mesh=mesh,
        in_specs=(
            activation, activation, P(("chip", "core")), P(), blocks, P(),
            blocks, blocks, blocks, blocks, P(), P(),
        ),
        out_specs=(activation, activation, blocks, blocks, blocks, blocks, P(), P(), P()),
        check_vma=False,
    )
```

```python
import functools
import jax
import jax.numpy as jnp
import numpy as np
from jax import lax
from jax.experimental import pallas as pl
from jax.experimental.pallas import tpu as pltpu
from jax.sharding import Mesh
from jax.sharding import PartitionSpec as P

D = 1024
HD = 64
FF = 4096
BLK = 128
STEP = 10
COLS = 1024
BF = jnp.bfloat16
F32 = jnp.float32
MIB = 1024 * 1024

norm_eps = 1e-05
score_scale = 0.125
masked_score = -1e30


def params(limit=56):
    return pltpu.CompilerParams(vmem_limit_bytes=limit * MIB)


def cost(flops, nbytes):
    return pl.CostEstimate(flops=int(flops), bytes_accessed=int(nbytes), transcendentals=0)


def mul_nn(left, right):
    return jnp.dot(left, right, preferred_element_type=F32)


def mul_nt(left, right):
    return lax.dot_general(left, right, (((1,), (1,)), ((), ())), preferred_element_type=F32)


def mul_tn(left, right):
    return lax.dot_general(left, right, (((0,), (0,)), ((), ())), preferred_element_type=F32)


def join_tile(ref):
    rows, cols = ref.shape[0], ref.shape[1]
    return jnp.concatenate([ref[:, j].reshape(rows * BLK, BLK) for j in range(cols)], axis=1)


def split_tile(ref, matrix):
    rows, cols = ref.shape[0], ref.shape[1]
    for j in range(cols):
        ref[:, j] = matrix[:, j * BLK : (j + 1) * BLK].reshape(rows, BLK, BLK).astype(ref.dtype)


def split_flat(ref, matrix):
    cols = matrix.shape[1] // BLK
    for i in range(matrix.shape[0] // BLK):
        for j in range(cols):
            block = matrix[i * BLK : (i + 1) * BLK, j * BLK : (j + 1) * BLK]
            ref[i * cols + j] = block.astype(ref.dtype)


def normalize(values):
    row_mean = jnp.mean(values, -1, keepdims=True)
    centered = values - row_mean
    row_var = jnp.mean(centered * centered, -1, keepdims=True)
    inv_std = lax.rsqrt(row_var + norm_eps)
    return centered * inv_std, inv_std


def gelu_parts(hidden):
    bell = jnp.exp(hidden * hidden * -0.5)
    t = 1.0 / (1.0 + jnp.abs(hidden) * (0.3275911 * 0.7071067811865476))
    poly = 1.061405429 * t - 1.453152027
    for term in (1.421413741, -0.284496736, 0.254829592):
        poly = poly * t + term
    tail = poly * t * 0.5 * bell
    return jnp.where(hidden < 0.0, tail, 1.0 - tail), hidden * bell * 0.3989422804014327


def norm_back(gradient, unit_vals, inv_std):
    grad_mean = jnp.mean(gradient, -1, keepdims=True)
    cross_mean = jnp.mean(gradient * unit_vals, -1, keepdims=True)
    return inv_std * (gradient - grad_mean - unit_vals * cross_mean)


def place_body(first, table, near_ref, far_ref, *refs):
    out_ref, sem = refs[-2:]
    count = near_ref.shape[0]
    half = table.shape[0] // 2
    for start, src in ((first, near_ref), (half + first, far_ref)):
        for slot in range(count):
            pltpu.make_async_copy(src.at[slot], out_ref.at[table[start + slot]], sem).start()
    done = out_ref.at[pl.ds(0, 2 * count)]
    pltpu.make_async_copy(done, done, sem).wait()


def place_blocks(table, first, near, far, kept):
    smem = pl.BlockSpec(memory_space=pltpu.SMEM)
    hbm = pl.BlockSpec(memory_space=pltpu.HBM)
    vmem = pl.BlockSpec(memory_space=pltpu.VMEM)
    kept = () if kept is None else (kept,)
    return pl.pallas_call(
        functools.partial(place_body, first),
        out_shape=jax.ShapeDtypeStruct((table.shape[0], BLK, BLK), BF),
        in_specs=[smem, vmem, vmem] + [hbm] * len(kept),
        out_specs=hbm,
        scratch_shapes=[pltpu.SemaphoreType.DMA],
        input_output_aliases={3: 0} if kept else {},
        compiler_params=params(44),
        cost_estimate=cost(0, 4 * near.size * 2),
        name="place_weights",
    )(table, near, far, *kept)


def norm_body(tokens_ref, gains_ref, out_ref):
    out_ref[...] = (normalize(tokens_ref[...].astype(F32))[0] * gains_ref[0:1]).astype(BF)


def norm_tokens(tokens, gains):
    span = tokens.shape[0]
    steps = 4
    part = pl.BlockSpec((span // steps, D), lambda i: (i, 0))
    return pl.pallas_call(
        norm_body,
        grid=(steps,),
        in_specs=[part, pl.BlockSpec((2, D), lambda i: (0, 0))],
        out_specs=part,
        out_shape=jax.ShapeDtypeStruct((span, D), BF),
        compiler_params=params(44),
        cost_estimate=cost(0, 2 * MIB),
        name="norm_tokens",
    )(tokens, gains)


def qkv_body(own_ref, other_ref, w_ref, own_out, other_out):
    step = pl.program_id(0)
    weight = join_tile(w_ref)
    own_out[...] = mul_nn(own_ref[...], weight).astype(BF)

    @pl.when(step >= D // COLS)
    def _():
        other_out[...] = mul_nn(other_ref[...], weight).astype(BF)


def project(own, other, weights):
    span = own.shape[0]
    skip = D // COLS
    once = pl.BlockSpec((span, D), lambda j: (0, 0))
    return pl.pallas_call(
        qkv_body,
        grid=(3 * D // COLS,),
        in_specs=[
            once,
            once,
            pl.BlockSpec((D // BLK, COLS // BLK, BLK, BLK), lambda j: (0, j, 0, 0)),
        ],
        out_specs=[
            pl.BlockSpec((span, COLS), lambda j: (0, j)),
            pl.BlockSpec((span, COLS), lambda j: (0, jnp.maximum(j - skip, 0))),
        ],
        out_shape=[
            jax.ShapeDtypeStruct((span, 3 * D), BF),
            jax.ShapeDtypeStruct((span, 2 * D), BF),
        ],
        compiler_params=params(),
        cost_estimate=cost(10 * span * D * D, 12 * MIB),
        name="qkv_projection",
    )(own, other, weights.reshape(-1, 3 * D // BLK, BLK, BLK))


def lane_masks(head):
    lane = lax.broadcasted_iota(jnp.int32, (1, BLK), 1)
    first = HD * (1 - head)
    keep = (lane // HD == head).astype(F32)
    dead_lane = (lane == first).astype(F32)
    terms = [(lane == first + 1 + i).astype(F32) for i in range(3)]
    return keep, dead_lane, terms


def three_terms(values):
    high = values.astype(BF).astype(F32)
    rest = values - high
    middle = rest.astype(BF).astype(F32)
    return high, middle, rest - middle


def key_bias(span, live_count):
    row = lax.broadcasted_iota(jnp.int32, (span, 1), 0)
    return jnp.where(row < live_count, 0.0, masked_score).astype(F32)


def attend_body(live_ref, q_ref, ko_ref, vo_ref, kx_ref, vx_ref, out_ref, aug_ref):
    span = q_ref.shape[0]
    bias_own = key_bias(span, live_ref[0])
    bias_other = key_bias(span, live_ref[1])
    queries = q_ref[...].astype(F32) * score_scale
    k_own, k_other = ko_ref[...].astype(F32), kx_ref[...].astype(F32)
    v_own_f, v_other_f = vo_ref[...].astype(F32), vx_ref[...].astype(F32)
    results, scores = [], []
    for head in range(2):
        keep, dead_lane, _ = lane_masks(head)
        q_head = (queries * keep + dead_lane).astype(BF)
        s_own = mul_nt(q_head, (k_own * keep + bias_own * dead_lane).astype(BF))
        s_other = mul_nt(q_head, (k_other * keep + bias_other * dead_lane).astype(BF))
        scores.append((q_head, s_own, s_other))
    for head in range(2):
        keep, _, terms = lane_masks(head)
        q_head, s_own, s_other = scores[head]
        top = jnp.max(jnp.maximum(s_own, s_other), -1, keepdims=True)
        p_own = jnp.exp(s_own - top)
        p_other = jnp.exp(s_other - top)
        v_own = (v_own_f * keep + (1.0 - keep)).astype(BF)
        v_other = (v_other_f * keep + (1.0 - keep)).astype(BF)
        mixed = mul_nn(p_own.astype(BF), v_own) + mul_nn(p_other.astype(BF), v_other)
        total = mixed[:, HD * (1 - head) : HD * (1 - head) + 1]
        results.append(mixed / total * keep)
        parts = three_terms(-(top + jnp.log(total)))
        stats = sum(part * lane for part, lane in zip(parts, terms))
        aug_ref[:, head * BLK : (head + 1) * BLK] = (q_head.astype(F32) + stats).astype(BF)
    out_ref[...] = (results[0] + results[1]).astype(BF)


def attend(live, own, other):
    span = own.shape[0]
    pairs = D // BLK
    col = lambda shift: pl.BlockSpec((span, BLK), lambda p: (0, p + shift))
    return pl.pallas_call(
        attend_body,
        grid=(pairs,),
        in_specs=[
            pl.BlockSpec(memory_space=pltpu.SMEM),
            col(0),
            col(pairs),
            col(2 * pairs),
            col(0),
            col(pairs),
        ],
        out_specs=[col(0), pl.BlockSpec((span, 2 * BLK), lambda p: (0, p))],
        out_shape=[
            jax.ShapeDtypeStruct((span, D), BF),
            jax.ShapeDtypeStruct((span, 2 * D), BF),
        ],
        compiler_params=params(),
        cost_estimate=cost(40 * span * span * D, 8 * MIB),
        name="attention",
    )(live, own, own, own, other, other)


def attend_back_body(
    live_ref, aug_ref, ko_ref, vo_ref, kx_ref, vx_ref, at_ref, g_ref, dq_ref, own_ref, other_ref
):
    span = at_ref.shape[0]
    grads = g_ref[...].astype(F32)
    product = grads * at_ref[...].astype(F32)
    keeps, g_augs, q_augs = [], [], []
    for head in range(2):
        keep, dead_lane, terms = lane_masks(head)
        delta = jnp.sum(product * keep, -1, keepdims=True)
        parts = three_terms(-delta)
        stats = sum(part * lane for part, lane in zip(parts, terms))
        g_augs.append((grads * keep + stats).astype(BF))
        q_augs.append(aug_ref[:, head * BLK : (head + 1) * BLK])
    d_query = [None, None]
    for k_ref, v_ref, out_ref, live in (
        (ko_ref, vo_ref, own_ref, live_ref[0]),
        (kx_ref, vx_ref, other_ref, live_ref[1]),
    ):
        bias = key_bias(span, live)
        keys = k_ref[...]
        keys_f, values_f = keys.astype(F32), v_ref[...].astype(F32)
        d_keys = d_values = None
        for head in range(2):
            keep, dead_lane, terms = lane_masks(head)
            ones = terms[0] + terms[1] + terms[2]
            k_aug = (keys_f * keep + (bias * dead_lane + ones)).astype(BF)
            v_aug = (values_f * keep + ones).astype(BF)
            probs = jnp.exp(mul_nt(k_aug, q_augs[head]))
            d_scores = (probs * mul_nt(v_aug, g_augs[head])).astype(BF)
            value_part = mul_nn(probs.astype(BF), g_augs[head]) * keep
            key_part = mul_nn(d_scores, q_augs[head]) * keep
            query_part = mul_tn(d_scores, keys) * (keep * score_scale)
            d_query[head] = query_part if d_query[head] is None else d_query[head] + query_part
            d_values = value_part if d_values is None else d_values + value_part
            d_keys = key_part if d_keys is None else d_keys + key_part
        out_ref[0] = d_keys.astype(out_ref.dtype)
        out_ref[1] = d_values.astype(out_ref.dtype)
    dq_ref[...] = (d_query[0] + d_query[1]).astype(BF)


def attend_back(live, aug, own, other, attended, grads):
    span = own.shape[0]
    pairs = D // BLK
    col = lambda shift: pl.BlockSpec((span, BLK), lambda p: (0, p + shift))
    pair_out = pl.BlockSpec((2, span, BLK), lambda p: (0, 0, p))
    return pl.pallas_call(
        attend_back_body,
        grid=(pairs,),
        in_specs=[
            pl.BlockSpec(memory_space=pltpu.SMEM),
            pl.BlockSpec((span, 2 * BLK), lambda p: (0, p)),
            col(pairs),
            col(2 * pairs),
            col(0),
            col(pairs),
            col(0),
            col(0),
        ],
        out_specs=[col(0), pair_out, pair_out],
        out_shape=[
            jax.ShapeDtypeStruct((span, D), BF),
            jax.ShapeDtypeStruct((2, span, D), BF),
            jax.ShapeDtypeStruct((2, span, D), BF),
        ],
        compiler_params=params(),
        cost_estimate=cost(60 * span * span * D, 12 * MIB),
        name="attention_backward",
    )(live, aug, own, own, other, other, attended, grads)


def feed_body(
    live_ref,
    tokens_ref,
    attended_ref,
    cot_ref,
    gains_ref,
    wo_ref,
    wu_ref,
    wd_ref,
    layer_ref,
    rest_ref,
    gm_ref,
    ga_ref,
    gain_ref,
    unit,
    inv,
    normed,
    top,
    acc_out,
    acc_back,
    up_stage,
    down_stage,
    out_stage,
    sems,
    out_sem,
):
    step = pl.program_id(0)
    place = step % 2
    side, width = up_stage.shape[1], up_stage.shape[2]
    per_tile = side * width
    up_first = side * side
    down_first = up_first + side * FF // BLK

    def drain(which):
        pltpu.make_async_copy(up_stage.at[which], up_stage.at[which], sems.at[0, which]).wait()
        pltpu.make_async_copy(down_stage.at[which], down_stage.at[which], sems.at[1, which]).wait()
    span = tokens_ref.shape[0]

    @pl.when(step == 0)
    def _():
        weight = join_tile(wo_ref)
        middle = tokens_ref[...].astype(F32) + mul_nn(attended_ref[...], weight)
        unit_vals, inv_std = normalize(middle)
        unit[...] = unit_vals
        inv[...] = inv_std
        normed[...] = (unit_vals * gains_ref[1:2]).astype(BF)
        row = lax.broadcasted_iota(jnp.int32, (span, 1), 0)
        top[...] = jnp.where(row < live_ref[2], cot_ref[...].astype(F32), 0.0).astype(BF)
        acc_out[...] = middle
        acc_back[...] = jnp.zeros_like(acc_back)

    w_up = join_tile(wu_ref)
    w_down = join_tile(wd_ref)
    hidden = mul_nn(normed[...], w_up)
    grad_act = mul_nt(top[...], w_down)
    share, slope_rest = gelu_parts(hidden)
    activated = (hidden * share).astype(BF)
    grad_hidden = (grad_act * (share + slope_rest)).astype(BF)
    acc_out[...] += mul_nn(activated, w_down)
    acc_back[...] += mul_nt(grad_hidden, w_up)

    @pl.when(step >= 2)
    def _():
        drain(place)

    split_flat(down_stage.at[place], mul_tn(activated, top[...]))
    dest = rest_ref.at[pl.ds(down_first + step * per_tile, per_tile)]
    pltpu.make_async_copy(down_stage.at[place], dest, sems.at[1, place]).start()
    split_tile(up_stage.at[place], mul_tn(normed[...], grad_hidden))
    for i in range(side):
        dest = rest_ref.at[pl.ds(up_first + i * (FF // BLK) + step * width, width)]
        pltpu.make_async_copy(up_stage.at[place, i], dest, sems.at[0, place]).start()

    @pl.when(step == pl.num_programs(0) - 1)
    def _():
        layer_ref[...] = acc_out[...].astype(BF)
        unit_vals = unit[...]
        back = acc_back[...]
        gain_ref[...] = jnp.sum(back * unit_vals, 0, keepdims=True)
        grad_middle = top[...].astype(F32) + norm_back(back * gains_ref[1:2], unit_vals, inv[...])
        gm_ref[...] = grad_middle
        back_middle = grad_middle.astype(BF)
        split_flat(out_stage, mul_tn(attended_ref[...], back_middle))
        out_copy = pltpu.make_async_copy(out_stage, rest_ref.at[pl.ds(0, up_first)], out_sem)
        out_copy.start()
        ga_ref[...] = mul_nt(back_middle, join_tile(wo_ref)).astype(BF)
        drain(1 - place)
        drain(place)
        out_copy.wait()


def feed(live, tokens, attended, cotangent, gains, weights):
    span = tokens.shape[0]
    side, width = D // BLK, COLS // BLK
    whole = lambda j: (0, 0)
    act = pl.BlockSpec((span, D), whole)
    once = pl.BlockSpec((span, D), whole, pipeline_mode=pl.Buffered(1))
    per_row = weights.reshape(-1, side, BLK, BLK)
    per_up = weights.reshape(-1, FF // BLK, BLK, BLK)
    out_row = (3 * side * side) // side // side
    up_row = 4 * side * side // (FF // BLK) // side
    down_row = (4 * side * side + side * FF // BLK) // side // width
    return pl.pallas_call(
        feed_body,
        grid=(FF // COLS,),
        in_specs=[
            pl.BlockSpec(memory_space=pltpu.SMEM),
            once,
            once,
            once,
            pl.BlockSpec((2, D), whole),
            pl.BlockSpec(
                (side, side, BLK, BLK),
                lambda j: (out_row, 0, 0, 0),
                pipeline_mode=pl.Buffered(1),
            ),
            pl.BlockSpec((side, width, BLK, BLK), lambda j: (up_row, j, 0, 0)),
            pl.BlockSpec((width, side, BLK, BLK), lambda j: (down_row + j, 0, 0, 0)),
        ],
        out_specs=[
            act,
            pl.BlockSpec(memory_space=pltpu.HBM),
            act,
            act,
            pl.BlockSpec((1, D), whole),
        ],
        out_shape=[
            jax.ShapeDtypeStruct((span, D), BF),
            jax.ShapeDtypeStruct((side * side + 2 * side * (FF // BLK), BLK, BLK), BF),
            jax.ShapeDtypeStruct((span, D), F32),
            jax.ShapeDtypeStruct((span, D), BF),
            jax.ShapeDtypeStruct((1, D), F32),
        ],
        scratch_shapes=[
            pltpu.VMEM((span, D), F32),
            pltpu.VMEM((span, 1), F32),
            pltpu.VMEM((span, D), BF),
            pltpu.VMEM((span, D), BF),
            pltpu.VMEM((span, D), F32),
            pltpu.VMEM((span, D), F32),
            pltpu.VMEM((2, side, width, BLK, BLK), BF),
            pltpu.VMEM((2, side * width, BLK, BLK), BF),
            pltpu.VMEM((side * side, BLK, BLK), BF),
            pltpu.SemaphoreType.DMA((2, 2)),
            pltpu.SemaphoreType.DMA,
        ],
        compiler_params=params(),
        cost_estimate=cost(14 * span * D * FF, 50 * MIB),
        name="feed_forward",
    )(live, tokens, attended, cotangent, gains, per_row, per_up, per_row)


def query_body(normed, dq_ref, w_ref, grad_ref, acc_ref):
    step = pl.program_id(0)

    @pl.when(step == 0)
    def _():
        acc_ref[...] = jnp.zeros_like(acc_ref)

    grad = dq_ref[...]
    acc_ref[...] += mul_nt(grad, join_tile(w_ref))
    split_tile(grad_ref, mul_tn(normed[...], grad))


def query_back(normed1, d_query, weights):
    span = normed1.shape[0]
    side, width = D // BLK, COLS // BLK
    whole = lambda j: (0, 0)
    act = pl.BlockSpec((span, D), whole)
    tile = pl.BlockSpec((side, width, BLK, BLK), lambda j: (0, j, 0, 0))
    return pl.pallas_call(
        query_body,
        grid=(D // COLS,),
        in_specs=[act, pl.BlockSpec((span, COLS), lambda j: (0, j)), tile],
        out_specs=[tile, act],
        out_shape=[
            jax.ShapeDtypeStruct((side, side, BLK, BLK), BF),
            jax.ShapeDtypeStruct((span, D), F32),
        ],
        compiler_params=params(),
        cost_estimate=cost(4 * span * D * D, 8 * MIB),
        name="query_backward",
    )(normed1, d_query, weights.reshape(-1, 3 * side, BLK, BLK))


def input_body(
    tokens_ref, gains_ref, normed, own_ref, recv_ref, acc_ref, gm_ref, w_ref, grad_ref, out_ref,
    gain_ref, acc
):
    step = pl.program_id(0)

    @pl.when(step == 0)
    def _():
        acc[...] = acc_ref[...]

    grad = (own_ref[0].astype(F32) + recv_ref[0].astype(F32)).astype(BF)
    acc[...] += mul_nt(grad, join_tile(w_ref))
    split_tile(grad_ref, mul_tn(normed[...], grad))

    @pl.when(step == pl.num_programs(0) - 1)
    def _():
        unit_vals, inv_std = normalize(tokens_ref[...].astype(F32))
        back = acc[...]
        gain_ref[...] = jnp.sum(back * unit_vals, 0, keepdims=True)
        out_ref[...] = (
            gm_ref[...] + norm_back(back * gains_ref[0:1], unit_vals, inv_std)
        ).astype(BF)


def input_back(tokens, gains, normed1, own, received, partial, grad_middle, weights):
    span = tokens.shape[0]
    side, width = D // BLK, COLS // BLK
    per = D // COLS
    whole = lambda j: (0, 0)
    act = pl.BlockSpec((span, D), whole)
    part = pl.BlockSpec((1, span, COLS), lambda j: (j // per, 0, j % per))
    return pl.pallas_call(
        input_body,
        grid=(2 * per,),
        in_specs=[
            act,
            pl.BlockSpec((2, D), whole),
            act,
            part,
            part,
            act,
            act,
            pl.BlockSpec((side, width, BLK, BLK), lambda j: (0, j + per, 0, 0)),
        ],
        out_specs=[
            pl.BlockSpec((side, width, BLK, BLK), lambda j: (0, j, 0, 0)),
            act,
            pl.BlockSpec((1, D), whole),
        ],
        out_shape=[
            jax.ShapeDtypeStruct((side, 2 * side, BLK, BLK), BF),
            jax.ShapeDtypeStruct((span, D), BF),
            jax.ShapeDtypeStruct((1, D), F32),
        ],
        scratch_shapes=[pltpu.VMEM((span, D), F32)],
        compiler_params=params(),
        cost_estimate=cost(8 * span * D * D, 20 * MIB),
        name="input_backward",
    )(
        tokens, gains, normed1, own, received, partial, grad_middle,
        weights.reshape(-1, 3 * side, BLK, BLK),
    )


def source_numbers():
    side = D // BLK
    numbers = np.arange(3 * side * side + side * side + 2 * side * (FF // BLK), dtype=np.int32)
    row, col = np.divmod(numbers[: 3 * side * side], 3 * side)
    numbers[: 3 * side * side] = np.where(
        col < side, row * side + col, side * side + row * 2 * side + col - side
    )
    return numbers


def gather_body(first, bounds, table, *refs):
    sources = refs[:6]
    out_ref, stage, sems = refs[6:]
    step, steps = pl.program_id(0), pl.num_programs(0)
    count = stage.shape[1] // 2

    def fetch(which, slot):
        start = first + which * count
        for i in range(count):
            number = table[start + i]
            for low, high, own, other in zip(bounds, bounds[1:], sources[:3], sources[3:]):

                @pl.when((number >= low) & (number < high))
                def _():
                    for src, at in ((own, i), (other, count + i)):
                        pltpu.make_async_copy(
                            src.at[number - low], stage.at[slot, at], sems.at[slot]
                        ).start()

    @pl.when(step == 0)
    def _():
        fetch(0, 0)

    @pl.when(step + 1 < steps)
    def _():
        fetch(step + 1, (step + 1) % 2)

    slot = step % 2
    pltpu.make_async_copy(stage.at[slot], stage.at[slot], sems.at[slot]).wait()
    total = stage[slot, :count].astype(F32) + stage[slot, count:].astype(F32)
    out_ref[...] = total.astype(BF)


def gather_sums(table, first, count, own, other):
    hbm = pl.BlockSpec(memory_space=pltpu.HBM)
    steps = 4
    part = count // steps
    bounds = np.cumsum([0] + [src.shape[0] for src in own]).tolist()
    return pl.pallas_call(
        functools.partial(gather_body, first, bounds),
        grid=(steps,),
        in_specs=[pl.BlockSpec(memory_space=pltpu.SMEM)] + [hbm] * 6,
        out_specs=pl.BlockSpec((part, BLK, BLK), lambda i: (i, 0, 0)),
        out_shape=jax.ShapeDtypeStruct((count, BLK, BLK), BF),
        scratch_shapes=[
            pltpu.VMEM((2, 2 * part, BLK, BLK), BF),
            pltpu.SemaphoreType.DMA((2,)),
        ],
        compiler_params=params(),
        cost_estimate=cost(0, 6 * count * BLK * BLK),
        name="gradient_sums",
    )(table, *own, *other)


def merge_body(first, second, passed, *refs):
    refs = list(refs)

    def total(count):
        return sum(refs.pop(0)[...].astype(F32) for _ in range(count))

    sums = [total(2), total(2)] if first else []
    if second:
        sums.append(total(3 if passed else 2))
    for ref, value in zip(refs, sums):
        ref[...] = value.astype(BF)


def merge_sums(low, came, kept, last, passed):
    steps = 3
    args, specs, shapes, outs = [], [], [], []

    def part(array, count, start):
        args.append(array)
        size = count // steps
        specs.append(pl.BlockSpec((size, BLK, BLK), lambda i: (i + start * steps, 0, 0)))

    def out(count):
        shapes.append(jax.ShapeDtypeStruct((count, BLK, BLK), BF))
        outs.append(pl.BlockSpec((count // steps, BLK, BLK), lambda i: (i, 0, 0)))

    if low is not None:
        count = low.shape[0] // 2
        for start in range(2):
            part(low, count, start)
            part(came, count, start)
            out(count)
    if kept is not None:
        for array in (kept, last) if passed is None else (kept, last, passed):
            part(array, kept.shape[0], 0)
        out(kept.shape[0])
    body = functools.partial(merge_body, low is not None, kept is not None, passed is not None)
    return pl.pallas_call(
        body,
        grid=(steps,),
        in_specs=specs,
        out_specs=outs,
        out_shape=shapes,
        compiler_params=params(44),
        cost_estimate=cost(0, 6 * MIB),
        name="merge_sums",
    )(*args)


def two_terms(values):
    high = values.astype(BF)
    return high, (values - high.astype(F32)).astype(BF)


def update_body(count, *refs):
    parts = refs[:count]
    m_ref, sl_ref, sr_ref, rl_ref, rr_ref, g_out, sl_out, sr_out, m_out = refs[count:]

    def long_left(terms, axis):
        return jnp.concatenate([terms[0], terms[0], terms[1]], axis)

    def long_right(terms, axis):
        return jnp.concatenate([terms[0], terms[1], terms[0]], axis)

    for i in range(g_out.shape[0]):
        total = sum(part[i].astype(F32) for part in parts)
        g_out[i] = total
        grad = two_terms(total)
        sl_out[i] = sl_ref[i] + mul_nt(long_left(grad, 1), long_right(grad, 1))
        tall = long_right(grad, 0)
        sr_out[i] = sr_ref[i] + mul_tn(long_left(grad, 0), tall)
        inner = mul_nn(long_left(two_terms(rl_ref[i]), 1), tall)
        direction = mul_nn(
            long_left(two_terms(inner), 1), long_right(two_terms(rr_ref[i]), 0)
        )
        master = m_ref[i]
        scale = jnp.sqrt(jnp.mean(master * master, keepdims=True) + 1e-06)
        scale = scale * lax.rsqrt(jnp.mean(direction * direction, keepdims=True) + 1e-06)
        m_out[i] = master - 0.3 * scale * direction


def update(parts, master, stat_left, stat_right, root_left, root_right):
    count = master.shape[0]
    group = 6 if count % 6 == 0 else 1
    block = pl.BlockSpec((group, BLK, BLK), lambda i: (i, 0, 0))
    shape = jax.ShapeDtypeStruct(master.shape, F32)
    return pl.pallas_call(
        functools.partial(update_body, len(parts)),
        grid=(count // group,),
        in_specs=[block] * (len(parts) + 5),
        out_specs=[block] * 4,
        out_shape=[shape] * 4,
        compiler_params=params(),
        cost_estimate=cost(48 * count * BLK**3, 15 * MIB),
        name="block_update",
    )(*parts, master, stat_left, stat_right, root_left, root_right)


def pair_moves():
    moves_same, moves_cross = [], []
    for z in range(4):
        for c in range(2):
            for moves, bit in ((moves_same, z % 2), (moves_cross, 1 - z % 2)):
                moves.append((z * 2 + c, (2 * c + bit) * 2 + z // 2))
    return moves_same, moves_cross


def row_part(values, which):
    return lax.dynamic_index_in_dim(values, which, 0, False)


def move_rows(values, crossed, back=False):
    moves = pair_moves()[crossed]
    return lax.ppermute(values, ("seq", "core"), [(b, a) for a, b in moves] if back else moves)


def in_order(kept, crossed, parity):
    return jnp.where(parity == 0, kept, crossed), jnp.where(parity == 0, crossed, kept)


def spread_rows(values, parity):
    kept = move_rows(row_part(values, parity), False)
    crossed = move_rows(row_part(values, 1 - parity), True)
    return jnp.concatenate(in_order(kept, crossed, parity), 0)


def gather_rows(values, parity):
    parts = values.reshape(2, values.shape[0] // 2, values.shape[1])
    kept = move_rows(row_part(parts, parity), False, True)
    crossed = move_rows(row_part(parts, 1 - parity), True, True)
    return jnp.stack(in_order(kept, crossed, parity), 0)


def swap_cores(values):
    return lax.ppermute(values, "core", [(0, 1), (1, 0)])


def chip_orders(chips):
    bits = [1 << i for i in range(chips.bit_length() - 1)]
    return bits, bits[::-1]


def offsets(order):
    result = [0]
    for bit in order:
        result = result + [o ^ bit for o in result]
    return result


def place_lists(chips, owned, planes):
    shape = (2, planes, chips, owned)
    by_core = np.array([offsets(order) for order in chip_orders(chips)], np.int32)
    grid = np.indices(shape).astype(np.int32).reshape(4, 2, -1)
    offset = np.broadcast_to(by_core[:, None, :, None], shape).reshape(2, -1)
    return grid[1, 0], offset, grid[3, 0]


def swap_chips(values, bits):
    chips = lax.axis_size("chip")
    moves = [(i * 2 + c, (i ^ bits[c]) * 2 + c) for i in range(chips) for c in range(2)]
    return lax.ppermute(values, ("chip", "core"), moves)


def move_planes(values, shift):
    planes = lax.axis_size("seq")
    return lax.ppermute(values, "seq", [(i, (i + shift) % planes) for i in range(planes)])


def after(value, *deps):
    return lax.optimization_barrier((value, *deps))[0]


def together(*values):
    return lax.optimization_barrier(values)


def chip_steps():
    return list(zip(*chip_orders(lax.axis_size("chip"))))


def finish_pieces(pieces):
    for bits in chip_steps()[2:]:
        joined = jnp.concatenate(pieces, 0)
        pieces = [joined, swap_chips(joined, bits)]
    return pieces


def add_halves(kept, came):
    return (kept.astype(F32) + came.astype(F32)).astype(BF)


def pack_terms(values):
    high = lax.optimization_barrier(values.astype(BF))
    low = (values - high.astype(F32)).astype(BF)
    terms = jnp.stack([high, low]).reshape(-1, BLK)
    return jnp.pad(terms, ((0, BLK - terms.shape[0]), (0, 0)))[None]


def unpack_terms(blocks, shape):
    terms = blocks.reshape(-1, BLK, BLK)[:, : 2 * shape[0] * shape[1] // BLK]
    terms = terms.reshape(-1, 2, *shape).astype(F32)
    return terms[:, 0] + terms[:, 1]


def finish_sums(keep, send, riders):
    for bits in chip_steps()[::-1][1:-1]:
        count = keep.shape[0] // 2
        came = swap_chips(with_riders(send, riders), bits)
        riders = more_riders(riders, came, keep.shape[0])
        send = add_halves(keep[count:], came[count : 2 * count])
        keep = add_halves(keep[:count], came[:count])
    return keep, send, riders


def with_riders(send, riders):
    return send if riders is None else jnp.concatenate([send, riders], 0)


def more_riders(riders, came, count):
    return riders if riders is None else jnp.concatenate([riders, came[count:]], 0)


def by_chip(riders, me, core):
    chips = lax.axis_size("chip")
    ranks = np.array([np.argsort(offsets(order[::-1])) for order in chip_orders(chips)], np.int32)
    rank = jnp.asarray(ranks)[core][me ^ jnp.arange(chips, dtype=jnp.int32)]
    return riders.reshape(chips, -1, BLK, BLK)[rank]


def local(
    tokens,
    cotangent,
    lengths,
    owner_perm,
    master,
    norm_gains,
    stat_left,
    stat_right,
    root_left,
    root_right,
    moment_first,
    moment_second,
):
    core = lax.axis_index("core")
    place_z = lax.axis_index("seq")
    parity = place_z % 2
    block_count = owner_perm.shape[0]
    owned = master.shape[0]
    half = block_count // 2

    chips, planes = lax.axis_size("chip"), lax.axis_size("seq")
    me = lax.axis_index("chip")

    pair_lengths = jnp.stack([lengths, swap_cores(lengths)])
    pair_lengths = jnp.where(core == 0, pair_lengths, pair_lengths[::-1]).reshape(-1)
    length = lax.dynamic_index_in_dim(pair_lengths, place_z, 0, False)
    span = tokens.shape[0] * tokens.shape[1]
    live = jnp.stack([length - core * span, length - (1 - core) * span, length - core * span])

    distance, offset, slot = place_lists(chips, owned, planes)
    offset = jnp.where(core == 0, offset, offset[::-1])
    device = ((place_z - distance) % planes * chips + (me ^ offset)) * 2
    device = device + jnp.stack([core, 1 - core])[:, None]
    table = owner_perm[(device * owned + slot).reshape(-1)]
    sums_table = jnp.asarray(source_numbers())[table[:half]]

    shard = master.astype(BF)
    first_bits, second_bits = chip_steps()[:2]
    per_plane = chips * owned
    cross, far, weights = [], [], None
    came, turned = swap_chips(shard, first_bits), swap_chips(shard, second_bits)
    next_shard = move_planes(shard, 1)
    pieces = [[shard, came, turned]]
    for k in range(1, planes):
        ready = (live, table, sums_table) if k == 1 else far[-1:]
        this_shard, came, turned, rows, *done = together(
            next_shard, came, turned, tokens, *cross[-1:], *ready
        )
        if k > 1:
            pieces[k - 2].append(done[0])
        cross.append(swap_chips(came, second_bits))
        came, turned = swap_chips(this_shard, first_bits), swap_chips(this_shard, second_bits)
        pieces.append([this_shard, came, turned])
        if k < planes - 1:
            next_shard = move_planes(this_shard, 1)
        else:
            row_same = move_rows(row_part(rows, parity), False)
            row_cross = row_part(after(rows, row_same), 1 - parity)
            row_cross = move_rows(row_cross, True)
        if k > 1:
            near = jnp.concatenate(finish_pieces(pieces[k - 2]), 0)
            far.append(swap_cores(near))
            weights = place_blocks(table, (k - 2) * per_plane, near, far[-1], weights)
    first = (planes - 1) * per_plane

    def place_piece(piece, first, weights):
        return place_blocks(table, first, piece, swap_cores(piece), weights), first + piece.shape[0]

    came, turned, done, row_same, row_cross, *_ = together(
        came, turned, cross[-1], row_same, row_cross, far[-1], weights
    )
    own_tokens = jnp.concatenate(in_order(row_same, row_cross, parity), 0)
    pieces[-2].append(done)
    pieces[-1][1:] = [came, turned, swap_chips(came, second_bits)]
    near = jnp.concatenate(finish_pieces(pieces[-2]), 0)
    far.append(swap_cores(near))
    weights = place_blocks(table, (planes - 2) * per_plane, near, far[-1], weights)
    normed1 = norm_tokens(own_tokens, norm_gains)
    if len(chip_steps()) == 2:
        for piece in pieces[-1][:3]:
            weights, first = place_piece(piece, first, weights)
        last, normed1, *_ = together(pieces[-1][-1], normed1, weights)
        other_normed = swap_cores(normed1)
        weights, _ = place_piece(last, first, weights)
    else:
        other_normed = swap_cores(normed1)
        weights, _ = place_piece(jnp.concatenate(finish_pieces(pieces[-1]), 0), first, weights)
    own_cot = spread_rows(after(cotangent, weights), parity)

    own_qkv, other_kv = project(normed1, other_normed, weights)
    attended, q_aug = attend(live, own_qkv, other_kv)
    layer, g_rest, grad_middle, grad_attended, gain_second = feed(
        live, own_tokens, attended, own_cot, norm_gains, weights
    )
    other_rest = swap_cores(g_rest)
    layer_out = gather_rows(layer, parity)
    d_query, d_own, d_other = attend_back(live, q_aug, own_qkv, other_kv, attended, grad_attended)
    received = swap_cores(after(d_other, layer_out))
    flat = lambda g: g.reshape(-1, BLK, BLK)
    g_query, partial = query_back(normed1, d_query, weights)
    g_query = flat(g_query)
    other_query = swap_cores(g_query)
    g_kv, grad_in, gain_first = input_back(
        own_tokens, norm_gains, normed1, d_own, received, partial, grad_middle, weights
    )
    g_kv = flat(g_kv)
    gain_part = jnp.concatenate([gain_first, gain_second], 0)
    mine = pack_terms(gain_part)
    other_kv_grad = swap_cores(after(g_kv, other_query))
    theirs = swap_cores(mine)
    pair = jnp.concatenate([mine, theirs], 0)
    riders = jnp.where(core == 0, pair, pair[::-1])
    own_grads = (g_query, g_kv, g_rest)
    other_grads = (other_query, other_kv_grad, other_rest)
    half_plane = per_plane // 2
    last_bits, before_bits = chip_steps()[-1], chip_steps()[0]
    halves = grad_in.reshape(2, span // 2, D)
    rows = [row_part(halves, parity), row_part(halves, 1 - parity)]
    moved_rows, lows, sent, passed, riders_z = [], [], None, None, []

    def sums(k, part, held):
        first = k * per_plane + part * half_plane
        return gather_sums(held, first, half_plane, own_grads, other_grads)

    order = list(range(planes))[::-1]
    high = sums(order[0], 1, sums_table)
    held = sums_table
    for turn in range(planes + 1):
        group, moves = [], []
        if turn < planes:
            group.append(with_riders(high, riders if turn == 0 else None))
            moves.append(lambda v: swap_chips(v, last_bits))
        if 1 <= turn <= planes:
            group.append(with_riders(sent, riders if turn == 1 else None))
            moves.append(lambda v: swap_chips(v, before_bits))
        if 2 <= turn <= planes:
            group.append(part)
            moves.append(lambda v: move_planes(v, -1))
        if turn == 1:
            group += rows
            moves += [lambda v: move_rows(v, False, True), lambda v: move_rows(v, True, True)]
        far_riders = [] if turn < planes - 1 else [1, 2] if turn == planes - 1 else range(3, planes)
        group += [rider for _ in far_riders]
        moves += [functools.partial(move_planes, shift=-k) for k in far_riders]
        came = [move(value) for move, value in zip(moves, together(*group, *moved_rows))]
        if turn == 1:
            came, moved_rows = came[:-2], came[-2:]
        count = len(came) - len(far_riders)
        riders_z, came = riders_z + came[count:], came[:count]
        if turn >= 2:
            passed = came.pop()
        if turn < planes:
            low = sums(order[turn], 0, after(held, high))
            if turn + 1 < planes:
                high = sums(order[turn + 1], 1, after(held, low))
            held = after(sums_table, *came)
        last = came[-1]
        if turn == 0:
            riders = more_riders(riders, came[0], half_plane)
        if turn == 1:
            riders = more_riders(riders, last, keep_before.shape[0])
            plane_gain = by_chip(riders, me, core)
            plane_gain = jnp.sum(unpack_terms(plane_gain, gain_part.shape), 0)
            rider = pack_terms(plane_gain)
        if turn == planes:
            parts = [keep_before, last, passed]
            continue
        second = (None, None, None) if turn == 0 else (keep_before, last, passed)
        keep, sent, *part = merge_sums(low, came[0], *second)
        part = part[0] if part else None
        keep_before, sent, grown = finish_sums(keep, sent, riders if turn == 0 else None)
        riders = grown if turn == 0 else riders
    input_grad = jnp.stack(in_order(*moved_rows, parity), 0).astype(F32)
    planes_gain = [unpack_terms(each, gain_part.shape)[0] for each in (rider, *riders_z)]
    turned = (jnp.arange(planes, dtype=jnp.int32) - place_z) % planes
    gain_grad = jnp.sum(jnp.stack(planes_gain)[turned], 0)
    grad_blocks, stat_left_new, stat_right_new, master_new = update(
        parts, master, stat_left, stat_right, root_left, root_right
    )
    first_new = 0.9 * moment_first + 0.1 * gain_grad
    second_new = 0.999 * moment_second + 0.001 * gain_grad * gain_grad
    first_hat = first_new / (1.0 - 0.9**STEP)
    second_hat = second_new / (1.0 - 0.999**STEP)
    gains_new = norm_gains - 0.5 * first_hat / (jnp.sqrt(second_hat) + 1e-08)
    return (
        layer_out,
        input_grad,
        grad_blocks,
        stat_left_new,
        stat_right_new,
        master_new,
        first_new,
        second_new,
        gains_new,
    )


def solution(mesh):
    seq_size, rows_size = mesh.shape["seq"], mesh.shape["rows"]
    mesh = Mesh(mesh.devices.reshape(seq_size, rows_size // 2, 2), ("seq", "chip", "core"))
    activation = P(("chip", "core"), "seq", None)
    blocks = P(("seq", "chip", "core"), None, None)
    return jax.shard_map(
        local,
        mesh=mesh,
        in_specs=(
            activation, activation, P(("chip", "core")), P(), blocks, P(),
            blocks, blocks, blocks, blocks, P(), P(),
        ),
        out_specs=(activation, activation, blocks, blocks, blocks, blocks, P(), P(), P()),
        check_vma=False,
    )
```

```python
import functools
import jax
import jax.numpy as jnp
import numpy as np
from jax import lax
from jax.experimental import pallas as pl
from jax.experimental.pallas import tpu as pltpu
from jax.sharding import Mesh
from jax.sharding import PartitionSpec as P

D = 1024
HD = 64
FF = 4096
BLK = 128
STEP = 10
COLS = 1024
BF = jnp.bfloat16
F32 = jnp.float32
MIB = 1024 * 1024

norm_eps = 1e-05
score_scale = 0.125
masked_score = -1e30


def params(limit=56):
    return pltpu.CompilerParams(vmem_limit_bytes=limit * MIB)


def cost(flops, nbytes):
    return pl.CostEstimate(flops=int(flops), bytes_accessed=int(nbytes), transcendentals=0)


def mul_nn(left, right):
    return jnp.dot(left, right, preferred_element_type=F32)


def mul_nt(left, right):
    return lax.dot_general(left, right, (((1,), (1,)), ((), ())), preferred_element_type=F32)


def mul_tn(left, right):
    return lax.dot_general(left, right, (((0,), (0,)), ((), ())), preferred_element_type=F32)


def join_tile(ref):
    rows, cols = ref.shape[0], ref.shape[1]
    return jnp.concatenate([ref[:, j].reshape(rows * BLK, BLK) for j in range(cols)], axis=1)


def split_tile(ref, matrix):
    rows, cols = ref.shape[0], ref.shape[1]
    for j in range(cols):
        ref[:, j] = matrix[:, j * BLK : (j + 1) * BLK].reshape(rows, BLK, BLK).astype(ref.dtype)


def split_flat(ref, matrix):
    cols = matrix.shape[1] // BLK
    for i in range(matrix.shape[0] // BLK):
        for j in range(cols):
            block = matrix[i * BLK : (i + 1) * BLK, j * BLK : (j + 1) * BLK]
            ref[i * cols + j] = block.astype(ref.dtype)


def normalize(values):
    row_mean = jnp.mean(values, -1, keepdims=True)
    centered = values - row_mean
    row_var = jnp.mean(centered * centered, -1, keepdims=True)
    inv_std = lax.rsqrt(row_var + norm_eps)
    return centered * inv_std, inv_std


def gelu_parts(hidden):
    bell = jnp.exp(hidden * hidden * -0.5)
    t = 1.0 / (1.0 + jnp.abs(hidden) * (0.3275911 * 0.7071067811865476))
    poly = 1.061405429 * t - 1.453152027
    for term in (1.421413741, -0.284496736, 0.254829592):
        poly = poly * t + term
    tail = poly * t * 0.5 * bell
    return jnp.where(hidden < 0.0, tail, 1.0 - tail), hidden * bell * 0.3989422804014327


def norm_back(gradient, unit_vals, inv_std):
    grad_mean = jnp.mean(gradient, -1, keepdims=True)
    cross_mean = jnp.mean(gradient * unit_vals, -1, keepdims=True)
    return inv_std * (gradient - grad_mean - unit_vals * cross_mean)


def place_body(first, pieces, table, *refs):
    near, far = refs[:pieces], refs[pieces : 2 * pieces]
    out_ref, sem = refs[-2:]
    total = 0
    for start, sources in ((first, near), (table.shape[0] // 2 + first, far)):
        for src in sources:
            for slot in range(src.shape[0]):
                pltpu.make_async_copy(src.at[slot], out_ref.at[table[start + slot]], sem).start()
            start += src.shape[0]
            total += src.shape[0]
    done = out_ref.at[pl.ds(0, total)]
    pltpu.make_async_copy(done, done, sem).wait()


def place_blocks(table, first, near, far, kept):
    smem = pl.BlockSpec(memory_space=pltpu.SMEM)
    hbm = pl.BlockSpec(memory_space=pltpu.HBM)
    vmem = pl.BlockSpec(memory_space=pltpu.VMEM)
    kept = () if kept is None else (kept,)
    count = 2 * len(near)
    return pl.pallas_call(
        functools.partial(place_body, first, len(near)),
        out_shape=jax.ShapeDtypeStruct((table.shape[0], BLK, BLK), BF),
        in_specs=[smem] + [vmem] * count + [hbm] * len(kept),
        out_specs=hbm,
        scratch_shapes=[pltpu.SemaphoreType.DMA],
        input_output_aliases={1 + count: 0} if kept else {},
        compiler_params=params(44),
        cost_estimate=cost(0, 6 * MIB),
        name="place_weights",
    )(table, *near, *far, *kept)


def norm_body(tokens_ref, gains_ref, out_ref, turned_ref):
    normed = normalize(tokens_ref[...].astype(F32))[0] * gains_ref[0:1]
    out_ref[...] = normed.astype(BF)
    turned_ref[...] = normed.T.astype(BF)


def norm_tokens(tokens, gains):
    span = tokens.shape[0]
    steps = 4
    part = pl.BlockSpec((span // steps, D), lambda i: (i, 0))
    return pl.pallas_call(
        norm_body,
        grid=(steps,),
        in_specs=[part, pl.BlockSpec((2, D), lambda i: (0, 0))],
        out_specs=[part, pl.BlockSpec((D, span // steps), lambda i: (0, i))],
        out_shape=[jax.ShapeDtypeStruct((span, D), BF), jax.ShapeDtypeStruct((D, span), BF)],
        compiler_params=params(44),
        cost_estimate=cost(0, 3 * MIB),
        name="norm_tokens",
    )(tokens, gains)


def qkv_body(own_ref, other_ref, w_ref, own_out, other_out):
    step = pl.program_id(0)
    weight = join_tile(w_ref)
    own_out[...] = mul_nn(own_ref[...], weight).astype(BF)

    @pl.when(step >= D // COLS)
    def _():
        other_out[...] = mul_nn(other_ref[...], weight).astype(BF)


def project(own, other, weights):
    span = own.shape[0]
    skip = D // COLS
    once = pl.BlockSpec((span, D), lambda j: (0, 0))
    return pl.pallas_call(
        qkv_body,
        grid=(3 * D // COLS,),
        in_specs=[
            once,
            once,
            pl.BlockSpec((D // BLK, COLS // BLK, BLK, BLK), lambda j: (0, j, 0, 0)),
        ],
        out_specs=[
            pl.BlockSpec((span, COLS), lambda j: (0, j)),
            pl.BlockSpec((span, COLS), lambda j: (0, jnp.maximum(j - skip, 0))),
        ],
        out_shape=[
            jax.ShapeDtypeStruct((span, 3 * D), BF),
            jax.ShapeDtypeStruct((span, 2 * D), BF),
        ],
        compiler_params=params(),
        cost_estimate=cost(10 * span * D * D, 12 * MIB),
        name="qkv_projection",
    )(own, other, weights.reshape(-1, 3 * D // BLK, BLK, BLK))


def lane_masks(head):
    lane = lax.broadcasted_iota(jnp.int32, (1, BLK), 1)
    first = HD * (1 - head)
    keep = (lane // HD == head).astype(F32)
    dead_lane = (lane == first).astype(F32)
    terms = [(lane == first + 1 + i).astype(F32) for i in range(3)]
    return keep, dead_lane, terms


def three_terms(values):
    high = values.astype(BF).astype(F32)
    rest = values - high
    middle = rest.astype(BF).astype(F32)
    return high, middle, rest - middle


def key_bias(span, live_count):
    row = lax.broadcasted_iota(jnp.int32, (span, 1), 0)
    return jnp.where(row < live_count, 0.0, masked_score).astype(F32)


def attend_body(live_ref, q_ref, ko_ref, vo_ref, kx_ref, vx_ref, out_ref, aug_ref):
    span = q_ref.shape[0]
    bias_own = key_bias(span, live_ref[0])
    bias_other = key_bias(span, live_ref[1])
    queries = q_ref[...].astype(F32) * score_scale
    k_own, k_other = ko_ref[...].astype(F32), kx_ref[...].astype(F32)
    v_own_f, v_other_f = vo_ref[...].astype(F32), vx_ref[...].astype(F32)
    results, scores = [], []
    for head in range(2):
        keep, dead_lane, _ = lane_masks(head)
        q_head = (queries * keep + dead_lane).astype(BF)
        s_own = mul_nt(q_head, (k_own * keep + bias_own * dead_lane).astype(BF))
        s_other = mul_nt(q_head, (k_other * keep + bias_other * dead_lane).astype(BF))
        scores.append((q_head, s_own, s_other))
    for head in range(2):
        keep, _, terms = lane_masks(head)
        q_head, s_own, s_other = scores[head]
        top = jnp.max(jnp.maximum(s_own, s_other), -1, keepdims=True)
        p_own = jnp.exp(s_own - top)
        p_other = jnp.exp(s_other - top)
        v_own = (v_own_f * keep + (1.0 - keep)).astype(BF)
        v_other = (v_other_f * keep + (1.0 - keep)).astype(BF)
        mixed = mul_nn(p_own.astype(BF), v_own) + mul_nn(p_other.astype(BF), v_other)
        total = mixed[:, HD * (1 - head) : HD * (1 - head) + 1]
        results.append(mixed / total * keep)
        parts = three_terms(-(top + jnp.log(total)))
        stats = sum(part * lane for part, lane in zip(parts, terms))
        aug_ref[:, head * BLK : (head + 1) * BLK] = (q_head.astype(F32) + stats).astype(BF)
    out_ref[...] = (results[0] + results[1]).astype(BF)


def attend(live, own, other):
    span = own.shape[0]
    pairs = D // BLK
    col = lambda shift: pl.BlockSpec((span, BLK), lambda p: (0, p + shift))
    return pl.pallas_call(
        attend_body,
        grid=(pairs,),
        in_specs=[
            pl.BlockSpec(memory_space=pltpu.SMEM),
            col(0),
            col(pairs),
            col(2 * pairs),
            col(0),
            col(pairs),
        ],
        out_specs=[col(0), pl.BlockSpec((span, 2 * BLK), lambda p: (0, p))],
        out_shape=[
            jax.ShapeDtypeStruct((span, D), BF),
            jax.ShapeDtypeStruct((span, 2 * D), BF),
        ],
        compiler_params=params(),
        cost_estimate=cost(40 * span * span * D, 8 * MIB),
        name="attention",
    )(live, own, own, own, other, other)


def attend_back_body(
    live_ref, aug_ref, ko_ref, vo_ref, kx_ref, vx_ref, at_ref, g_ref, dq_ref, own_ref, other_ref
):
    span = at_ref.shape[0]
    grads = g_ref[...].astype(F32)
    product = grads * at_ref[...].astype(F32)
    keeps, g_augs, q_augs = [], [], []
    for head in range(2):
        keep, dead_lane, terms = lane_masks(head)
        delta = jnp.sum(product * keep, -1, keepdims=True)
        parts = three_terms(-delta)
        stats = sum(part * lane for part, lane in zip(parts, terms))
        g_augs.append((grads * keep + stats).astype(BF))
        q_augs.append(aug_ref[:, head * BLK : (head + 1) * BLK])
    d_query = [None, None]
    for k_ref, v_ref, out_ref, live in (
        (ko_ref, vo_ref, own_ref, live_ref[0]),
        (kx_ref, vx_ref, other_ref, live_ref[1]),
    ):
        bias = key_bias(span, live)
        keys = k_ref[...]
        keys_f, values_f = keys.astype(F32), v_ref[...].astype(F32)
        d_keys = d_values = None
        for head in range(2):
            keep, dead_lane, terms = lane_masks(head)
            ones = terms[0] + terms[1] + terms[2]
            k_aug = (keys_f * keep + (bias * dead_lane + ones)).astype(BF)
            v_aug = (values_f * keep + ones).astype(BF)
            probs = jnp.exp(mul_nt(k_aug, q_augs[head]))
            d_scores = (probs * mul_nt(v_aug, g_augs[head])).astype(BF)
            value_part = mul_nn(probs.astype(BF), g_augs[head]) * keep
            key_part = mul_nn(d_scores, q_augs[head]) * keep
            query_part = mul_tn(d_scores, keys) * (keep * score_scale)
            d_query[head] = query_part if d_query[head] is None else d_query[head] + query_part
            d_values = value_part if d_values is None else d_values + value_part
            d_keys = key_part if d_keys is None else d_keys + key_part
        out_ref[0] = d_keys.astype(out_ref.dtype)
        out_ref[1] = d_values.astype(out_ref.dtype)
    dq_ref[...] = (d_query[0] + d_query[1]).astype(BF)


def attend_back(live, aug, own, other, attended, grads):
    span = own.shape[0]
    pairs = D // BLK
    col = lambda shift: pl.BlockSpec((span, BLK), lambda p: (0, p + shift))
    pair_out = pl.BlockSpec((2, span, BLK), lambda p: (0, 0, p))
    return pl.pallas_call(
        attend_back_body,
        grid=(pairs,),
        in_specs=[
            pl.BlockSpec(memory_space=pltpu.SMEM),
            pl.BlockSpec((span, 2 * BLK), lambda p: (0, p)),
            col(pairs),
            col(2 * pairs),
            col(0),
            col(pairs),
            col(0),
            col(0),
        ],
        out_specs=[col(0), pair_out, pair_out],
        out_shape=[
            jax.ShapeDtypeStruct((span, D), BF),
            jax.ShapeDtypeStruct((2, span, D), BF),
            jax.ShapeDtypeStruct((2, span, D), BF),
        ],
        compiler_params=params(),
        cost_estimate=cost(60 * span * span * D, 12 * MIB),
        name="attention_backward",
    )(live, aug, own, own, other, other, attended, grads)


def feed_body(
    live_ref,
    tokens_ref,
    attended_ref,
    cot_ref,
    gains_ref,
    wo_ref,
    wu_ref,
    wd_ref,
    layer_ref,
    rest_ref,
    gm_ref,
    ga_ref,
    gain_ref,
    unit,
    inv,
    normed,
    normed_t,
    top,
    acc_out,
    acc_back,
    up_stage,
    down_stage,
    out_stage,
    sems,
    out_sem,
):
    step = pl.program_id(0)
    place = step % 2
    side, width = up_stage.shape[1], up_stage.shape[2]
    per_tile = side * width
    up_first = side * side
    down_first = up_first + side * FF // BLK

    def drain(which):
        pltpu.make_async_copy(up_stage.at[which], up_stage.at[which], sems.at[0, which]).wait()
        pltpu.make_async_copy(down_stage.at[which], down_stage.at[which], sems.at[1, which]).wait()
    span = tokens_ref.shape[0]

    @pl.when(step == 0)
    def _():
        weight = join_tile(wo_ref)
        middle = tokens_ref[...].astype(F32) + mul_nn(attended_ref[...], weight)
        unit_vals, inv_std = normalize(middle)
        unit[...] = unit_vals
        inv[...] = inv_std
        normed_vals = unit_vals * gains_ref[1:2]
        normed[...] = normed_vals.astype(BF)
        normed_t[...] = normed_vals.T.astype(BF)
        row = lax.broadcasted_iota(jnp.int32, (span, 1), 0)
        top[...] = jnp.where(row < live_ref[2], cot_ref[...].astype(F32), 0.0).astype(BF)
        acc_out[...] = middle
        acc_back[...] = jnp.zeros_like(acc_back)

    w_up = join_tile(wu_ref)
    w_down = join_tile(wd_ref)
    hidden = mul_nn(normed[...], w_up)
    grad_act = mul_nt(top[...], w_down)
    share, slope_rest = gelu_parts(hidden)
    activated = (hidden * share).astype(BF)
    grad_hidden = (grad_act * (share + slope_rest)).astype(BF)
    acc_out[...] += mul_nn(activated, w_down)
    acc_back[...] += mul_nt(grad_hidden, w_up)

    @pl.when(step >= 2)
    def _():
        drain(place)

    split_flat(down_stage.at[place], mul_tn(activated, top[...]))
    dest = rest_ref.at[pl.ds(down_first + step * per_tile, per_tile)]
    pltpu.make_async_copy(down_stage.at[place], dest, sems.at[1, place]).start()
    split_tile(up_stage.at[place], mul_nn(normed_t[...], grad_hidden))
    for i in range(side):
        dest = rest_ref.at[pl.ds(up_first + i * (FF // BLK) + step * width, width)]
        pltpu.make_async_copy(up_stage.at[place, i], dest, sems.at[0, place]).start()

    @pl.when(step == pl.num_programs(0) - 1)
    def _():
        layer_ref[...] = acc_out[...].astype(BF)
        unit_vals = unit[...]
        back = acc_back[...]
        gain_ref[...] = jnp.sum(back * unit_vals, 0, keepdims=True)
        grad_middle = top[...].astype(F32) + norm_back(back * gains_ref[1:2], unit_vals, inv[...])
        gm_ref[...] = grad_middle
        back_middle = grad_middle.astype(BF)
        split_flat(out_stage, mul_tn(attended_ref[...], back_middle))
        out_copy = pltpu.make_async_copy(out_stage, rest_ref.at[pl.ds(0, up_first)], out_sem)
        out_copy.start()
        ga_ref[...] = mul_nt(back_middle, join_tile(wo_ref)).astype(BF)
        drain(1 - place)
        drain(place)
        out_copy.wait()


def feed(live, tokens, attended, cotangent, gains, weights):
    span = tokens.shape[0]
    side, width = D // BLK, COLS // BLK
    whole = lambda j: (0, 0)
    act = pl.BlockSpec((span, D), whole)
    once = pl.BlockSpec((span, D), whole, pipeline_mode=pl.Buffered(1))
    per_row = weights.reshape(-1, side, BLK, BLK)
    per_up = weights.reshape(-1, FF // BLK, BLK, BLK)
    out_row = (3 * side * side) // side // side
    up_row = 4 * side * side // (FF // BLK) // side
    down_row = (4 * side * side + side * FF // BLK) // side // width
    return pl.pallas_call(
        feed_body,
        grid=(FF // COLS,),
        in_specs=[
            pl.BlockSpec(memory_space=pltpu.SMEM),
            once,
            once,
            once,
            pl.BlockSpec((2, D), whole),
            pl.BlockSpec(
                (side, side, BLK, BLK),
                lambda j: (out_row, 0, 0, 0),
                pipeline_mode=pl.Buffered(1),
            ),
            pl.BlockSpec((side, width, BLK, BLK), lambda j: (up_row, j, 0, 0)),
            pl.BlockSpec((width, side, BLK, BLK), lambda j: (down_row + j, 0, 0, 0)),
        ],
        out_specs=[
            act,
            pl.BlockSpec(memory_space=pltpu.HBM),
            act,
            act,
            pl.BlockSpec((1, D), whole),
        ],
        out_shape=[
            jax.ShapeDtypeStruct((span, D), BF),
            jax.ShapeDtypeStruct((side * side + 2 * side * (FF // BLK), BLK, BLK), BF),
            jax.ShapeDtypeStruct((span, D), F32),
            jax.ShapeDtypeStruct((span, D), BF),
            jax.ShapeDtypeStruct((1, D), F32),
        ],
        scratch_shapes=[
            pltpu.VMEM((span, D), F32),
            pltpu.VMEM((span, 1), F32),
            pltpu.VMEM((span, D), BF),
            pltpu.VMEM((D, span), BF),
            pltpu.VMEM((span, D), BF),
            pltpu.VMEM((span, D), F32),
            pltpu.VMEM((span, D), F32),
            pltpu.VMEM((2, side, width, BLK, BLK), BF),
            pltpu.VMEM((2, side * width, BLK, BLK), BF),
            pltpu.VMEM((side * side, BLK, BLK), BF),
            pltpu.SemaphoreType.DMA((2, 2)),
            pltpu.SemaphoreType.DMA,
        ],
        compiler_params=params(),
        cost_estimate=cost(14 * span * D * FF, 50 * MIB),
        name="feed_forward",
    )(live, tokens, attended, cotangent, gains, per_row, per_up, per_row)


def query_body(normed_t, dq_ref, w_ref, grad_ref, acc_ref):
    step = pl.program_id(0)

    @pl.when(step == 0)
    def _():
        acc_ref[...] = jnp.zeros_like(acc_ref)

    grad = dq_ref[...]
    acc_ref[...] += mul_nt(grad, join_tile(w_ref))
    split_tile(grad_ref, mul_nn(normed_t[...], grad))


def query_back(normed1_t, d_query, weights):
    span = normed1_t.shape[1]
    side, width = D // BLK, COLS // BLK
    whole = lambda j: (0, 0)
    act = pl.BlockSpec((span, D), whole)
    tile = pl.BlockSpec((side, width, BLK, BLK), lambda j: (0, j, 0, 0))
    return pl.pallas_call(
        query_body,
        grid=(D // COLS,),
        in_specs=[
            pl.BlockSpec((D, span), whole),
            pl.BlockSpec((span, COLS), lambda j: (0, j)),
            tile,
        ],
        out_specs=[tile, act],
        out_shape=[
            jax.ShapeDtypeStruct((side, side, BLK, BLK), BF),
            jax.ShapeDtypeStruct((span, D), F32),
        ],
        compiler_params=params(),
        cost_estimate=cost(4 * span * D * D, 8 * MIB),
        name="query_backward",
    )(normed1_t, d_query, weights.reshape(-1, 3 * side, BLK, BLK))


def input_body(
    tokens_ref, gains_ref, normed_t, own_ref, recv_ref, acc_ref, gm_ref, w_ref, grad_ref, out_ref,
    gain_ref, acc
):
    step = pl.program_id(0)

    @pl.when(step == 0)
    def _():
        acc[...] = acc_ref[...]

    grad = (own_ref[0].astype(F32) + recv_ref[0].astype(F32)).astype(BF)
    acc[...] += mul_nt(grad, join_tile(w_ref))
    split_tile(grad_ref, mul_nn(normed_t[...], grad))

    @pl.when(step == pl.num_programs(0) - 1)
    def _():
        unit_vals, inv_std = normalize(tokens_ref[...].astype(F32))
        back = acc[...]
        gain_ref[...] = jnp.sum(back * unit_vals, 0, keepdims=True)
        out_ref[...] = (
            gm_ref[...] + norm_back(back * gains_ref[0:1], unit_vals, inv_std)
        ).astype(BF)


def input_back(tokens, gains, normed1_t, own, received, partial, grad_middle, weights):
    span = tokens.shape[0]
    side, width = D // BLK, COLS // BLK
    per = D // COLS
    whole = lambda j: (0, 0)
    act = pl.BlockSpec((span, D), whole)
    part = pl.BlockSpec((1, span, COLS), lambda j: (j // per, 0, j % per))
    return pl.pallas_call(
        input_body,
        grid=(2 * per,),
        in_specs=[
            act,
            pl.BlockSpec((2, D), whole),
            pl.BlockSpec((D, span), whole),
            part,
            part,
            act,
            act,
            pl.BlockSpec((side, width, BLK, BLK), lambda j: (0, j + per, 0, 0)),
        ],
        out_specs=[
            pl.BlockSpec((side, width, BLK, BLK), lambda j: (0, j, 0, 0)),
            act,
            pl.BlockSpec((1, D), whole),
        ],
        out_shape=[
            jax.ShapeDtypeStruct((side, 2 * side, BLK, BLK), BF),
            jax.ShapeDtypeStruct((span, D), BF),
            jax.ShapeDtypeStruct((1, D), F32),
        ],
        scratch_shapes=[pltpu.VMEM((span, D), F32)],
        compiler_params=params(),
        cost_estimate=cost(8 * span * D * D, 20 * MIB),
        name="input_backward",
    )(
        tokens, gains, normed1_t, own, received, partial, grad_middle,
        weights.reshape(-1, 3 * side, BLK, BLK),
    )


def source_numbers():
    side = D // BLK
    numbers = np.arange(3 * side * side + side * side + 2 * side * (FF // BLK), dtype=np.int32)
    row, col = np.divmod(numbers[: 3 * side * side], 3 * side)
    numbers[: 3 * side * side] = np.where(
        col < side, row * side + col, side * side + row * 2 * side + col - side
    )
    return numbers


def gather_body(first, bounds, table, *refs):
    sources = refs[:6]
    out_ref, stage, sems = refs[6:]
    step, steps = pl.program_id(0), pl.num_programs(0)
    count = stage.shape[1] // 2

    def fetch(which, slot):
        start = first + which * count
        for i in range(count):
            number = table[start + i]
            for low, high, own, other in zip(bounds, bounds[1:], sources[:3], sources[3:]):

                @pl.when((number >= low) & (number < high))
                def _():
                    for src, at in ((own, i), (other, count + i)):
                        pltpu.make_async_copy(
                            src.at[number - low], stage.at[slot, at], sems.at[slot]
                        ).start()

    @pl.when(step == 0)
    def _():
        fetch(0, 0)

    @pl.when(step + 1 < steps)
    def _():
        fetch(step + 1, (step + 1) % 2)

    slot = step % 2
    pltpu.make_async_copy(stage.at[slot], stage.at[slot], sems.at[slot]).wait()
    total = stage[slot, :count].astype(F32) + stage[slot, count:].astype(F32)
    out_ref[...] = total.astype(BF)


def gather_sums(table, first, count, own, other):
    hbm = pl.BlockSpec(memory_space=pltpu.HBM)
    steps = 4
    part = count // steps
    bounds = np.cumsum([0] + [src.shape[0] for src in own]).tolist()
    return pl.pallas_call(
        functools.partial(gather_body, first, bounds),
        grid=(steps,),
        in_specs=[pl.BlockSpec(memory_space=pltpu.SMEM)] + [hbm] * 6,
        out_specs=pl.BlockSpec((part, BLK, BLK), lambda i: (i, 0, 0)),
        out_shape=jax.ShapeDtypeStruct((count, BLK, BLK), BF),
        scratch_shapes=[
            pltpu.VMEM((2, 2 * part, BLK, BLK), BF),
            pltpu.SemaphoreType.DMA((2,)),
        ],
        compiler_params=params(),
        cost_estimate=cost(0, 6 * count * BLK * BLK),
        name="gradient_sums",
    )(table, *own, *other)


def merge_body(first, second, passed, *refs):
    refs = list(refs)

    def total(count):
        return sum(refs.pop(0)[...].astype(F32) for _ in range(count))

    sums = [total(2), total(2)] if first else []
    if second:
        sums.append(total(3 if passed else 2))
    for ref, value in zip(refs, sums):
        ref[...] = value.astype(BF)


def merge_sums(low, came, kept, last, passed):
    steps = 3
    args, specs, shapes, outs = [], [], [], []

    def part(array, count, start):
        args.append(array)
        size = count // steps
        specs.append(pl.BlockSpec((size, BLK, BLK), lambda i: (i + start * steps, 0, 0)))

    def out(count):
        shapes.append(jax.ShapeDtypeStruct((count, BLK, BLK), BF))
        outs.append(pl.BlockSpec((count // steps, BLK, BLK), lambda i: (i, 0, 0)))

    if low is not None:
        count = low.shape[0] // 2
        for start in range(2):
            part(low, count, start)
            part(came, count, start)
            out(count)
    if kept is not None:
        for array in (kept, last) if passed is None else (kept, last, passed):
            part(array, kept.shape[0], 0)
        out(kept.shape[0])
    body = functools.partial(merge_body, low is not None, kept is not None, passed is not None)
    return pl.pallas_call(
        body,
        grid=(steps,),
        in_specs=specs,
        out_specs=outs,
        out_shape=shapes,
        compiler_params=params(60),
        cost_estimate=cost(0, 6 * MIB),
        name="merge_sums",
    )(*args)


def two_terms(values):
    high = values.astype(BF)
    return high, (values - high.astype(F32)).astype(BF)


def update_body(count, *refs):
    parts = refs[:count]
    m_ref, sl_ref, sr_ref, rl_ref, rr_ref, g_out, sl_out, sr_out, m_out = refs[count:]

    def long_left(terms, axis):
        return jnp.concatenate([terms[0], terms[0], terms[1]], axis)

    def long_right(terms, axis):
        return jnp.concatenate([terms[0], terms[1], terms[0]], axis)

    for i in range(g_out.shape[0]):
        total = sum(part[i].astype(F32) for part in parts)
        g_out[i] = total
        grad = two_terms(total)
        sl_out[i] = sl_ref[i] + mul_nt(long_left(grad, 1), long_right(grad, 1))
        tall = long_right(grad, 0)
        sr_out[i] = sr_ref[i] + mul_tn(long_left(grad, 0), tall)
        inner = mul_nn(long_left(two_terms(rl_ref[i]), 1), tall)
        direction = mul_nn(
            long_left(two_terms(inner), 1), long_right(two_terms(rr_ref[i]), 0)
        )
        master = m_ref[i]
        scale = jnp.sqrt(jnp.mean(master * master, keepdims=True) + 1e-06)
        scale = scale * lax.rsqrt(jnp.mean(direction * direction, keepdims=True) + 1e-06)
        m_out[i] = master - 0.3 * scale * direction


def update(parts, master, stat_left, stat_right, root_left, root_right):
    count = master.shape[0]
    group = 6 if count % 6 == 0 else 1
    block = pl.BlockSpec((group, BLK, BLK), lambda i: (i, 0, 0))
    shape = jax.ShapeDtypeStruct(master.shape, F32)
    return pl.pallas_call(
        functools.partial(update_body, len(parts)),
        grid=(count // group,),
        in_specs=[block] * (len(parts) + 5),
        out_specs=[block] * 4,
        out_shape=[shape] * 4,
        compiler_params=params(),
        cost_estimate=cost(48 * count * BLK**3, 15 * MIB),
        name="block_update",
    )(*parts, master, stat_left, stat_right, root_left, root_right)


def pair_moves():
    moves_same, moves_cross = [], []
    for z in range(4):
        for c in range(2):
            for moves, bit in ((moves_same, z % 2), (moves_cross, 1 - z % 2)):
                moves.append((z * 2 + c, (2 * c + bit) * 2 + z // 2))
    return moves_same, moves_cross


def row_part(values, which):
    return lax.dynamic_index_in_dim(values, which, 0, False)


def move_rows(values, crossed, back=False):
    moves = pair_moves()[crossed]
    return lax.ppermute(values, ("seq", "core"), [(b, a) for a, b in moves] if back else moves)


def in_order(kept, crossed, parity):
    return jnp.where(parity == 0, kept, crossed), jnp.where(parity == 0, crossed, kept)


def spread_rows(values, parity):
    kept = move_rows(row_part(values, parity), False)
    crossed = move_rows(row_part(values, 1 - parity), True)
    return jnp.concatenate(in_order(kept, crossed, parity), 0)


def gather_rows(values, parity):
    parts = values.reshape(2, values.shape[0] // 2, values.shape[1])
    kept = move_rows(row_part(parts, parity), False, True)
    crossed = move_rows(row_part(parts, 1 - parity), True, True)
    return jnp.stack(in_order(kept, crossed, parity), 0)


def swap_cores(values):
    return lax.ppermute(values, "core", [(0, 1), (1, 0)])


def chip_orders(chips):
    bits = [1 << i for i in range(chips.bit_length() - 1)]
    return bits, bits[::-1]


def offsets(order):
    result = [0]
    for bit in order:
        result = result + [o ^ bit for o in result]
    return result


def place_lists(chips, owned, planes):
    shape = (2, planes, chips, owned)
    by_core = np.array([offsets(order) for order in chip_orders(chips)], np.int32)
    grid = np.indices(shape).astype(np.int32).reshape(4, 2, -1)
    offset = np.broadcast_to(by_core[:, None, :, None], shape).reshape(2, -1)
    return grid[1, 0], offset, grid[3, 0]


def arrival_order(chips, owned, planes):
    per_plane, quarter = chips * owned, owned
    if chips != 4:
        return np.arange(planes * per_plane)
    pieces = [(0, 0)]
    for k in range(1, planes + 1):
        pieces += [(k, 0)] if k < planes else []
        pieces += [(k - 1, 1), (k - 1, 2)]
        pieces += [(k - 2, 3)] if k > 1 else []
    pieces.append((planes - 1, 3))
    starts = [k * per_plane + r * quarter for k, r in pieces]
    return np.concatenate([np.arange(start, start + quarter) for start in starts])


def swap_chips(values, bits):
    chips = lax.axis_size("chip")
    moves = [(i * 2 + c, (i ^ bits[c]) * 2 + c) for i in range(chips) for c in range(2)]
    return lax.ppermute(values, ("chip", "core"), moves)


def move_planes(values, shift):
    planes = lax.axis_size("seq")
    return lax.ppermute(values, "seq", [(i, (i + shift) % planes) for i in range(planes)])


def after(value, *deps):
    return lax.optimization_barrier((value, *deps))[0]


def together(*values):
    return lax.optimization_barrier(values)


def chip_steps():
    return list(zip(*chip_orders(lax.axis_size("chip"))))


def finish_pieces(pieces):
    for bits in chip_steps()[2:]:
        joined = jnp.concatenate(pieces, 0)
        pieces = [joined, swap_chips(joined, bits)]
    return pieces


def add_halves(kept, came):
    return (kept.astype(F32) + came.astype(F32)).astype(BF)


def pack_terms(values):
    high = lax.optimization_barrier(values.astype(BF))
    low = (values - high.astype(F32)).astype(BF)
    terms = jnp.stack([high, low]).reshape(-1, BLK)
    return jnp.pad(terms, ((0, BLK - terms.shape[0]), (0, 0)))[None]


def unpack_terms(blocks, shape):
    terms = blocks.reshape(-1, BLK, BLK)[:, : 2 * shape[0] * shape[1] // BLK]
    terms = terms.reshape(-1, 2, *shape).astype(F32)
    return terms[:, 0] + terms[:, 1]


def finish_sums(keep, send, riders):
    for bits in chip_steps()[::-1][1:-1]:
        count = keep.shape[0] // 2
        came = swap_chips(with_riders(send, riders), bits)
        riders = more_riders(riders, came, keep.shape[0])
        send = add_halves(keep[count:], came[count : 2 * count])
        keep = add_halves(keep[:count], came[:count])
    return keep, send, riders


def with_riders(send, riders):
    return send if riders is None else jnp.concatenate([send, riders], 0)


def more_riders(riders, came, count):
    return riders if riders is None else jnp.concatenate([riders, came[count:]], 0)


def by_chip(riders, me, core):
    chips = lax.axis_size("chip")
    ranks = np.array([np.argsort(offsets(order[::-1])) for order in chip_orders(chips)], np.int32)
    rank = jnp.asarray(ranks)[core][me ^ jnp.arange(chips, dtype=jnp.int32)]
    return riders.reshape(chips, -1, BLK, BLK)[rank]


def local(
    tokens,
    cotangent,
    lengths,
    owner_perm,
    master,
    norm_gains,
    stat_left,
    stat_right,
    root_left,
    root_right,
    moment_first,
    moment_second,
):
    core = lax.axis_index("core")
    place_z = lax.axis_index("seq")
    parity = place_z % 2
    block_count = owner_perm.shape[0]
    owned = master.shape[0]
    half = block_count // 2

    chips, planes = lax.axis_size("chip"), lax.axis_size("seq")
    me = lax.axis_index("chip")

    pair_lengths = jnp.stack([lengths, swap_cores(lengths)])
    pair_lengths = jnp.where(core == 0, pair_lengths, pair_lengths[::-1]).reshape(-1)
    length = lax.dynamic_index_in_dim(pair_lengths, place_z, 0, False)
    span = tokens.shape[0] * tokens.shape[1]
    live = jnp.stack([length - core * span, length - (1 - core) * span, length - core * span])

    distance, offset, slot = place_lists(chips, owned, planes)
    offset = jnp.where(core == 0, offset, offset[::-1])
    device = ((place_z - distance) % planes * chips + (me ^ offset)) * 2
    device = device + jnp.stack([core, 1 - core])[:, None]
    table = owner_perm[(device * owned + slot).reshape(-1)]
    sums_table = jnp.asarray(source_numbers())[table[:half]]
    arrive = arrival_order(chips, owned, planes)
    near_slots, far_slots = device * owned + slot
    table = owner_perm[jnp.concatenate([near_slots[arrive], far_slots[arrive]])]

    shard = master.astype(BF)
    first_bits, second_bits = chip_steps()[:2]
    per_plane = chips * owned
    by_phase = chips == 4
    cross, held, weights, first = None, (), None, 0
    came, turned = swap_chips(shard, first_bits), swap_chips(shard, second_bits)
    next_shard = move_planes(shard, 1)
    pieces = [[shard, came, turned]]

    def place(parts, first, weights):
        others = [swap_cores(part) for part in parts]
        weights = place_blocks(table, first, parts, others, weights)
        return weights, first + sum(part.shape[0] for part in parts)

    for k in range(1, planes):
        ready = (live, table, sums_table) if k == 1 else (cross, *held)
        ready = ready if weights is None else (*ready, weights)
        this_shard, came, turned, rows, *done = together(next_shard, came, turned, tokens, *ready)
        if k > 1:
            pieces[k - 2].append(done[0])
        cross = swap_chips(came, second_bits)
        arrived = [this_shard, came, turned, *(pieces[0][:1] if k == 1 else done[:1])]
        arrived = arrived[3:] + arrived[:3] if k == 1 else arrived
        pieces[k - 1][1:] = [came, turned]
        came, turned = swap_chips(this_shard, first_bits), swap_chips(this_shard, second_bits)
        pieces.append([this_shard, came, turned])
        if k < planes - 1:
            next_shard = move_planes(this_shard, 1)
        else:
            row_same = move_rows(row_part(rows, parity), False)
            row_cross = row_part(after(rows, row_same), 1 - parity)
            row_cross = move_rows(row_cross, True)
        if by_phase:
            if k > 1:
                weights, first = place(done[1:2], first, weights)
            held = (jnp.concatenate(arrived, 0),)
    came, turned, done, row_same, row_cross, *held = together(
        came, turned, cross, row_same, row_cross, *held, *([] if weights is None else [weights])
    )
    own_tokens = jnp.concatenate(in_order(row_same, row_cross, parity), 0)
    pieces[-2].append(done)
    pieces[-1][1:] = [came, turned, swap_chips(came, second_bits)]
    normed1, normed1_t = norm_tokens(own_tokens, norm_gains)
    if by_phase:
        weights, first = place(held[:1], first, weights)
        weights, first = place([came, turned, done], first, weights)
        last, normed1, *_ = together(pieces[-1][-1], normed1, weights)
        other_normed = swap_cores(normed1)
        weights, _ = place([last], first, weights)
    else:
        for each in pieces:
            each = [jnp.concatenate(finish_pieces(each), 0)]
            weights, first = place(each, first, weights)
        other_normed = swap_cores(normed1)
    own_cot = spread_rows(after(cotangent, weights), parity)

    own_qkv, other_kv = project(normed1, other_normed, weights)
    attended, q_aug = attend(live, own_qkv, other_kv)
    layer, g_rest, grad_middle, grad_attended, gain_second = feed(
        live, own_tokens, attended, own_cot, norm_gains, weights
    )
    other_rest = swap_cores(g_rest)
    layer_out = gather_rows(layer, parity)
    d_query, d_own, d_other = attend_back(live, q_aug, own_qkv, other_kv, attended, grad_attended)
    received = swap_cores(after(d_other, layer_out))
    flat = lambda g: g.reshape(-1, BLK, BLK)
    g_query, partial = query_back(normed1_t, d_query, weights)
    g_query = flat(g_query)
    other_query = swap_cores(g_query)
    g_kv, grad_in, gain_first = input_back(
        own_tokens, norm_gains, normed1_t, d_own, received, partial, grad_middle, weights
    )
    g_kv = flat(g_kv)
    gain_part = jnp.concatenate([gain_first, gain_second], 0)
    mine = pack_terms(gain_part)
    other_kv_grad = swap_cores(after(g_kv, other_query))
    theirs = swap_cores(mine)
    pair = jnp.concatenate([mine, theirs], 0)
    riders = jnp.where(core == 0, pair, pair[::-1])
    own_grads = (g_query, g_kv, g_rest)
    other_grads = (other_query, other_kv_grad, other_rest)
    half_plane = per_plane // 2
    last_bits, before_bits = chip_steps()[-1], chip_steps()[0]
    halves = grad_in.reshape(2, span // 2, D)
    rows = [row_part(halves, parity), row_part(halves, 1 - parity)]
    moved_rows, lows, sent, passed, riders_z = [], [], None, None, []

    def sums(k, part, held):
        first = k * per_plane + part * half_plane
        return gather_sums(held, first, half_plane, own_grads, other_grads)

    order = list(range(planes))[::-1]
    high = sums(order[0], 1, sums_table)
    held = sums_table
    for turn in range(planes + 1):
        group, moves = [], []
        if turn < planes:
            group.append(with_riders(high, riders if turn == 0 else None))
            moves.append(lambda v: swap_chips(v, last_bits))
        if 1 <= turn <= planes:
            group.append(with_riders(sent, riders if turn == 1 else None))
            moves.append(lambda v: swap_chips(v, before_bits))
        if 2 <= turn <= planes:
            group.append(part)
            moves.append(lambda v: move_planes(v, -1))
        if turn == 1:
            group += rows
            moves += [lambda v: move_rows(v, False, True), lambda v: move_rows(v, True, True)]
        far_riders = [] if turn < planes - 1 else [1, 2] if turn == planes - 1 else range(3, planes)
        group += [rider for _ in far_riders]
        moves += [functools.partial(move_planes, shift=-k) for k in far_riders]
        came = [move(value) for move, value in zip(moves, together(*group, *moved_rows))]
        if turn == 1:
            came, moved_rows = came[:-2], came[-2:]
        count = len(came) - len(far_riders)
        riders_z, came = riders_z + came[count:], came[:count]
        if turn >= 2:
            passed = came.pop()
        if turn < planes:
            low = sums(order[turn], 0, after(held, high))
            if turn + 1 < planes:
                high = sums(order[turn + 1], 1, after(held, low))
            held = after(sums_table, *came)
        last = came[-1]
        if turn == 0:
            riders = more_riders(riders, came[0], half_plane)
        if turn == 1:
            riders = more_riders(riders, last, keep_before.shape[0])
            plane_gain = by_chip(riders, me, core)
            plane_gain = jnp.sum(unpack_terms(plane_gain, gain_part.shape), 0)
            rider = pack_terms(plane_gain)
        if turn == planes:
            parts = [keep_before, last, passed]
            continue
        second = (None, None, None) if turn == 0 else (keep_before, last, passed)
        keep, sent, *part = merge_sums(low, came[0], *second)
        part = part[0] if part else None
        keep_before, sent, grown = finish_sums(keep, sent, riders if turn == 0 else None)
        riders = grown if turn == 0 else riders
    input_grad = jnp.stack(in_order(*moved_rows, parity), 0).astype(F32)
    planes_gain = [unpack_terms(each, gain_part.shape)[0] for each in (rider, *riders_z)]
    turned = (jnp.arange(planes, dtype=jnp.int32) - place_z) % planes
    gain_grad = jnp.sum(jnp.stack(planes_gain)[turned], 0)
    grad_blocks, stat_left_new, stat_right_new, master_new = update(
        parts, master, stat_left, stat_right, root_left, root_right
    )
    first_new = 0.9 * moment_first + 0.1 * gain_grad
    second_new = 0.999 * moment_second + 0.001 * gain_grad * gain_grad
    first_hat = first_new / (1.0 - 0.9**STEP)
    second_hat = second_new / (1.0 - 0.999**STEP)
    gains_new = norm_gains - 0.5 * first_hat / (jnp.sqrt(second_hat) + 1e-08)
    return (
        layer_out,
        input_grad,
        grad_blocks,
        stat_left_new,
        stat_right_new,
        master_new,
        first_new,
        second_new,
        gains_new,
    )


def solution(mesh):
    seq_size, rows_size = mesh.shape["seq"], mesh.shape["rows"]
    mesh = Mesh(mesh.devices.reshape(seq_size, rows_size // 2, 2), ("seq", "chip", "core"))
    activation = P(("chip", "core"), "seq", None)
    blocks = P(("seq", "chip", "core"), None, None)
    return jax.shard_map(
        local,
        mesh=mesh,
        in_specs=(
            activation, activation, P(("chip", "core")), P(), blocks, P(),
            blocks, blocks, blocks, blocks, P(), P(),
        ),
        out_specs=(activation, activation, blocks, blocks, blocks, blocks, P(), P(), P()),
        check_vma=False,
    )
```

```python
import functools
import jax
import jax.numpy as jnp
import numpy as np
from jax import lax
from jax.experimental import pallas as pl
from jax.experimental.pallas import tpu as pltpu
from jax.sharding import Mesh
from jax.sharding import PartitionSpec as P

D = 1024
HD = 64
FF = 4096
BLK = 128
STEP = 10
COLS = 1024
BF = jnp.bfloat16
F32 = jnp.float32
MIB = 1024 * 1024

norm_eps = 1e-05
score_scale = 0.125
masked_score = -1e30


def params(limit=56):
    return pltpu.CompilerParams(vmem_limit_bytes=limit * MIB)


def cost(flops, nbytes):
    return pl.CostEstimate(flops=int(flops), bytes_accessed=int(nbytes), transcendentals=0)


def mul_nn(left, right):
    return jnp.dot(left, right, preferred_element_type=F32)


def mul_nt(left, right):
    return lax.dot_general(left, right, (((1,), (1,)), ((), ())), preferred_element_type=F32)


def mul_tn(left, right):
    return lax.dot_general(left, right, (((0,), (0,)), ((), ())), preferred_element_type=F32)


def join_tile(ref):
    rows, cols = ref.shape[0], ref.shape[1]
    return jnp.concatenate([ref[:, j].reshape(rows * BLK, BLK) for j in range(cols)], axis=1)


def split_tile(ref, matrix):
    rows, cols = ref.shape[0], ref.shape[1]
    for j in range(cols):
        ref[:, j] = matrix[:, j * BLK : (j + 1) * BLK].reshape(rows, BLK, BLK).astype(ref.dtype)


def split_flat(ref, matrix):
    cols = matrix.shape[1] // BLK
    for i in range(matrix.shape[0] // BLK):
        for j in range(cols):
            block = matrix[i * BLK : (i + 1) * BLK, j * BLK : (j + 1) * BLK]
            ref[i * cols + j] = block.astype(ref.dtype)


def normalize(values):
    row_mean = jnp.mean(values, -1, keepdims=True)
    centered = values - row_mean
    row_var = jnp.mean(centered * centered, -1, keepdims=True)
    inv_std = lax.rsqrt(row_var + norm_eps)
    return centered * inv_std, inv_std


def gelu_parts(hidden):
    bell = jnp.exp(hidden * hidden * -0.5)
    t = 1.0 / (1.0 + jnp.abs(hidden) * (0.3275911 * 0.7071067811865476))
    poly = 1.061405429 * t - 1.453152027
    for term in (1.421413741, -0.284496736, 0.254829592):
        poly = poly * t + term
    tail = poly * t * 0.5 * bell
    return jnp.where(hidden < 0.0, tail, 1.0 - tail), hidden * bell * 0.3989422804014327


def norm_back(gradient, unit_vals, inv_std):
    grad_mean = jnp.mean(gradient, -1, keepdims=True)
    cross_mean = jnp.mean(gradient * unit_vals, -1, keepdims=True)
    return inv_std * (gradient - grad_mean - unit_vals * cross_mean)


def place_body(first, pieces, table, *refs):
    near, far = refs[:pieces], refs[pieces : 2 * pieces]
    out_ref, sem = refs[-2:]
    total = 0
    for start, sources in ((first, near), (table.shape[0] // 2 + first, far)):
        for src in sources:
            for slot in range(src.shape[0]):
                pltpu.make_async_copy(src.at[slot], out_ref.at[table[start + slot]], sem).start()
            start += src.shape[0]
            total += src.shape[0]
    done = out_ref.at[pl.ds(0, total)]
    pltpu.make_async_copy(done, done, sem).wait()


def place_blocks(table, first, near, far, kept):
    smem = pl.BlockSpec(memory_space=pltpu.SMEM)
    hbm = pl.BlockSpec(memory_space=pltpu.HBM)
    vmem = pl.BlockSpec(memory_space=pltpu.VMEM)
    kept = () if kept is None else (kept,)
    count = 2 * len(near)
    return pl.pallas_call(
        functools.partial(place_body, first, len(near)),
        out_shape=jax.ShapeDtypeStruct((table.shape[0], BLK, BLK), BF),
        in_specs=[smem] + [vmem] * count + [hbm] * len(kept),
        out_specs=hbm,
        scratch_shapes=[pltpu.SemaphoreType.DMA],
        input_output_aliases={1 + count: 0} if kept else {},
        compiler_params=params(44),
        cost_estimate=cost(0, 6 * MIB),
        name="place_weights",
    )(table, *near, *far, *kept)


def norm_body(tokens_ref, gains_ref, out_ref, turned_ref):
    normed = normalize(tokens_ref[...].astype(F32))[0] * gains_ref[0:1]
    out_ref[...] = normed.astype(BF)
    turned_ref[...] = normed.T.astype(BF)


def norm_tokens(tokens, gains):
    span = tokens.shape[0]
    steps = 4
    part = pl.BlockSpec((span // steps, D), lambda i: (i, 0))
    return pl.pallas_call(
        norm_body,
        grid=(steps,),
        in_specs=[part, pl.BlockSpec((2, D), lambda i: (0, 0))],
        out_specs=[part, pl.BlockSpec((D, span // steps), lambda i: (0, i))],
        out_shape=[jax.ShapeDtypeStruct((span, D), BF), jax.ShapeDtypeStruct((D, span), BF)],
        compiler_params=params(44),
        cost_estimate=cost(0, 3 * MIB),
        name="norm_tokens",
    )(tokens, gains)


def qkv_body(own_ref, other_ref, w_ref, own_out, other_out):
    step = pl.program_id(0)
    weight = join_tile(w_ref)
    own_out[...] = mul_nn(own_ref[...], weight).astype(BF)

    @pl.when(step >= D // COLS)
    def _():
        other_out[...] = mul_nn(other_ref[...], weight).astype(BF)


def project(own, other, weights):
    span = own.shape[0]
    skip = D // COLS
    once = pl.BlockSpec((span, D), lambda j: (0, 0))
    return pl.pallas_call(
        qkv_body,
        grid=(3 * D // COLS,),
        in_specs=[
            once,
            once,
            pl.BlockSpec((D // BLK, COLS // BLK, BLK, BLK), lambda j: (0, j, 0, 0)),
        ],
        out_specs=[
            pl.BlockSpec((span, COLS), lambda j: (0, j)),
            pl.BlockSpec((span, COLS), lambda j: (0, jnp.maximum(j - skip, 0))),
        ],
        out_shape=[
            jax.ShapeDtypeStruct((span, 3 * D), BF),
            jax.ShapeDtypeStruct((span, 2 * D), BF),
        ],
        compiler_params=params(),
        cost_estimate=cost(10 * span * D * D, 12 * MIB),
        name="qkv_projection",
    )(own, other, weights.reshape(-1, 3 * D // BLK, BLK, BLK))


def lane_masks(head):
    lane = lax.broadcasted_iota(jnp.int32, (1, BLK), 1)
    first = HD * (1 - head)
    keep = (lane // HD == head).astype(F32)
    dead_lane = (lane == first).astype(F32)
    terms = [(lane == first + 1 + i).astype(F32) for i in range(3)]
    return keep, dead_lane, terms


def three_terms(values):
    high = values.astype(BF).astype(F32)
    rest = values - high
    middle = rest.astype(BF).astype(F32)
    return high, middle, rest - middle


def key_bias(span, live_count):
    row = lax.broadcasted_iota(jnp.int32, (span, 1), 0)
    return jnp.where(row < live_count, 0.0, masked_score).astype(F32)


def attend_body(live_ref, q_ref, ko_ref, vo_ref, kx_ref, vx_ref, out_ref, aug_ref):
    span = q_ref.shape[0]
    bias_own = key_bias(span, live_ref[0])
    bias_other = key_bias(span, live_ref[1])
    queries = q_ref[...].astype(F32) * score_scale
    k_own, k_other = ko_ref[...].astype(F32), kx_ref[...].astype(F32)
    v_own_f, v_other_f = vo_ref[...].astype(F32), vx_ref[...].astype(F32)
    results, scores = [], []
    for head in range(2):
        keep, dead_lane, _ = lane_masks(head)
        q_head = (queries * keep + dead_lane).astype(BF)
        s_own = mul_nt(q_head, (k_own * keep + bias_own * dead_lane).astype(BF))
        s_other = mul_nt(q_head, (k_other * keep + bias_other * dead_lane).astype(BF))
        scores.append((q_head, s_own, s_other))
    for head in range(2):
        keep, _, terms = lane_masks(head)
        q_head, s_own, s_other = scores[head]
        top = jnp.max(jnp.maximum(s_own, s_other), -1, keepdims=True)
        p_own = jnp.exp(s_own - top)
        p_other = jnp.exp(s_other - top)
        v_own = (v_own_f * keep + (1.0 - keep)).astype(BF)
        v_other = (v_other_f * keep + (1.0 - keep)).astype(BF)
        mixed = mul_nn(p_own.astype(BF), v_own) + mul_nn(p_other.astype(BF), v_other)
        total = mixed[:, HD * (1 - head) : HD * (1 - head) + 1]
        results.append(mixed / total * keep)
        parts = three_terms(-(top + jnp.log(total)))
        stats = sum(part * lane for part, lane in zip(parts, terms))
        aug_ref[:, head * BLK : (head + 1) * BLK] = (q_head.astype(F32) + stats).astype(BF)
    out_ref[...] = (results[0] + results[1]).astype(BF)


def attend(live, own, other):
    span = own.shape[0]
    pairs = D // BLK
    col = lambda shift: pl.BlockSpec((span, BLK), lambda p: (0, p + shift))
    return pl.pallas_call(
        attend_body,
        grid=(pairs,),
        in_specs=[
            pl.BlockSpec(memory_space=pltpu.SMEM),
            col(0),
            col(pairs),
            col(2 * pairs),
            col(0),
            col(pairs),
        ],
        out_specs=[col(0), pl.BlockSpec((span, 2 * BLK), lambda p: (0, p))],
        out_shape=[
            jax.ShapeDtypeStruct((span, D), BF),
            jax.ShapeDtypeStruct((span, 2 * D), BF),
        ],
        compiler_params=params(),
        cost_estimate=cost(40 * span * span * D, 8 * MIB),
        name="attention",
    )(live, own, own, own, other, other)


def attend_back_body(
    live_ref, aug_ref, ko_ref, vo_ref, kx_ref, vx_ref, at_ref, g_ref, dq_ref, own_ref, other_ref
):
    span = at_ref.shape[0]
    grads = g_ref[...].astype(F32)
    product = grads * at_ref[...].astype(F32)
    keeps, g_augs, q_augs = [], [], []
    for head in range(2):
        keep, dead_lane, terms = lane_masks(head)
        delta = jnp.sum(product * keep, -1, keepdims=True)
        parts = three_terms(-delta)
        stats = sum(part * lane for part, lane in zip(parts, terms))
        g_augs.append((grads * keep + stats).astype(BF))
        q_augs.append(aug_ref[:, head * BLK : (head + 1) * BLK])
    d_query = [None, None]
    for k_ref, v_ref, out_ref, live in (
        (ko_ref, vo_ref, own_ref, live_ref[0]),
        (kx_ref, vx_ref, other_ref, live_ref[1]),
    ):
        bias = key_bias(span, live)
        keys = k_ref[...]
        keys_f, values_f = keys.astype(F32), v_ref[...].astype(F32)
        d_keys = d_values = None
        for head in range(2):
            keep, dead_lane, terms = lane_masks(head)
            ones = terms[0] + terms[1] + terms[2]
            k_aug = (keys_f * keep + (bias * dead_lane + ones)).astype(BF)
            v_aug = (values_f * keep + ones).astype(BF)
            probs = jnp.exp(mul_nt(k_aug, q_augs[head]))
            d_scores = (probs * mul_nt(v_aug, g_augs[head])).astype(BF)
            value_part = mul_nn(probs.astype(BF), g_augs[head]) * keep
            key_part = mul_nn(d_scores, q_augs[head]) * keep
            query_part = mul_tn(d_scores, keys) * (keep * score_scale)
            d_query[head] = query_part if d_query[head] is None else d_query[head] + query_part
            d_values = value_part if d_values is None else d_values + value_part
            d_keys = key_part if d_keys is None else d_keys + key_part
        out_ref[0] = d_keys.astype(out_ref.dtype)
        out_ref[1] = d_values.astype(out_ref.dtype)
    dq_ref[...] = (d_query[0] + d_query[1]).astype(BF)


def attend_back(live, aug, own, other, attended, grads):
    span = own.shape[0]
    pairs = D // BLK
    col = lambda shift: pl.BlockSpec((span, BLK), lambda p: (0, p + shift))
    pair_out = pl.BlockSpec((2, span, BLK), lambda p: (0, 0, p))
    return pl.pallas_call(
        attend_back_body,
        grid=(pairs,),
        in_specs=[
            pl.BlockSpec(memory_space=pltpu.SMEM),
            pl.BlockSpec((span, 2 * BLK), lambda p: (0, p)),
            col(pairs),
            col(2 * pairs),
            col(0),
            col(pairs),
            col(0),
            col(0),
        ],
        out_specs=[col(0), pair_out, pair_out],
        out_shape=[
            jax.ShapeDtypeStruct((span, D), BF),
            jax.ShapeDtypeStruct((2, span, D), BF),
            jax.ShapeDtypeStruct((2, span, D), BF),
        ],
        compiler_params=params(),
        cost_estimate=cost(60 * span * span * D, 12 * MIB),
        name="attention_backward",
    )(live, aug, own, own, other, other, attended, grads)


def feed_body(
    live_ref,
    tokens_ref,
    attended_ref,
    cot_ref,
    gains_ref,
    wo_ref,
    wu_ref,
    wd_ref,
    layer_ref,
    rest_ref,
    gm_ref,
    ga_ref,
    gain_ref,
    unit,
    inv,
    normed,
    normed_t,
    top,
    acc_out,
    acc_back,
    up_stage,
    down_stage,
    out_stage,
    sems,
    out_sem,
):
    step = pl.program_id(0)
    place = step % 2
    side, width = up_stage.shape[1], up_stage.shape[2]
    per_tile = side * width
    up_first = side * side
    down_first = up_first + side * FF // BLK

    def drain(which):
        pltpu.make_async_copy(up_stage.at[which], up_stage.at[which], sems.at[0, which]).wait()
        pltpu.make_async_copy(down_stage.at[which], down_stage.at[which], sems.at[1, which]).wait()
    span = tokens_ref.shape[0]

    @pl.when(step == 0)
    def _():
        weight = join_tile(wo_ref)
        middle = tokens_ref[...].astype(F32) + mul_nn(attended_ref[...], weight)
        unit_vals, inv_std = normalize(middle)
        unit[...] = unit_vals
        inv[...] = inv_std
        normed_vals = unit_vals * gains_ref[1:2]
        normed[...] = normed_vals.astype(BF)
        normed_t[...] = normed_vals.T.astype(BF)
        row = lax.broadcasted_iota(jnp.int32, (span, 1), 0)
        top[...] = jnp.where(row < live_ref[2], cot_ref[...].astype(F32), 0.0).astype(BF)
        acc_out[...] = middle
        acc_back[...] = jnp.zeros_like(acc_back)

    w_up = join_tile(wu_ref)
    w_down = join_tile(wd_ref)
    hidden = mul_nn(normed[...], w_up)
    grad_act = mul_nt(top[...], w_down)
    share, slope_rest = gelu_parts(hidden)
    activated = (hidden * share).astype(BF)
    grad_hidden = (grad_act * (share + slope_rest)).astype(BF)
    acc_out[...] += mul_nn(activated, w_down)
    acc_back[...] += mul_nt(grad_hidden, w_up)

    @pl.when(step >= 2)
    def _():
        drain(place)

    split_flat(down_stage.at[place], mul_tn(activated, top[...]))
    dest = rest_ref.at[pl.ds(down_first + step * per_tile, per_tile)]
    pltpu.make_async_copy(down_stage.at[place], dest, sems.at[1, place]).start()
    split_tile(up_stage.at[place], mul_nn(normed_t[...], grad_hidden))
    for i in range(side):
        dest = rest_ref.at[pl.ds(up_first + i * (FF // BLK) + step * width, width)]
        pltpu.make_async_copy(up_stage.at[place, i], dest, sems.at[0, place]).start()

    @pl.when(step == pl.num_programs(0) - 1)
    def _():
        layer_ref[...] = acc_out[...].astype(BF)
        unit_vals = unit[...]
        back = acc_back[...]
        gain_ref[...] = jnp.sum(back * unit_vals, 0, keepdims=True)
        grad_middle = top[...].astype(F32) + norm_back(back * gains_ref[1:2], unit_vals, inv[...])
        gm_ref[...] = grad_middle
        back_middle = grad_middle.astype(BF)
        split_flat(out_stage, mul_tn(attended_ref[...], back_middle))
        out_copy = pltpu.make_async_copy(out_stage, rest_ref.at[pl.ds(0, up_first)], out_sem)
        out_copy.start()
        ga_ref[...] = mul_nt(back_middle, join_tile(wo_ref)).astype(BF)
        drain(1 - place)
        drain(place)
        out_copy.wait()


def feed(live, tokens, attended, cotangent, gains, weights):
    span = tokens.shape[0]
    side, width = D // BLK, COLS // BLK
    whole = lambda j: (0, 0)
    act = pl.BlockSpec((span, D), whole)
    once = pl.BlockSpec((span, D), whole, pipeline_mode=pl.Buffered(1))
    per_row = weights.reshape(-1, side, BLK, BLK)
    per_up = weights.reshape(-1, FF // BLK, BLK, BLK)
    out_row = (3 * side * side) // side // side
    up_row = 4 * side * side // (FF // BLK) // side
    down_row = (4 * side * side + side * FF // BLK) // side // width
    return pl.pallas_call(
        feed_body,
        grid=(FF // COLS,),
        in_specs=[
            pl.BlockSpec(memory_space=pltpu.SMEM),
            once,
            once,
            once,
            pl.BlockSpec((2, D), whole),
            pl.BlockSpec(
                (side, side, BLK, BLK),
                lambda j: (out_row, 0, 0, 0),
                pipeline_mode=pl.Buffered(1),
            ),
            pl.BlockSpec((side, width, BLK, BLK), lambda j: (up_row, j, 0, 0)),
            pl.BlockSpec((width, side, BLK, BLK), lambda j: (down_row + j, 0, 0, 0)),
        ],
        out_specs=[
            act,
            pl.BlockSpec(memory_space=pltpu.HBM),
            act,
            act,
            pl.BlockSpec((1, D), whole),
        ],
        out_shape=[
            jax.ShapeDtypeStruct((span, D), BF),
            jax.ShapeDtypeStruct((side * side + 2 * side * (FF // BLK), BLK, BLK), BF),
            jax.ShapeDtypeStruct((span, D), F32),
            jax.ShapeDtypeStruct((span, D), BF),
            jax.ShapeDtypeStruct((1, D), F32),
        ],
        scratch_shapes=[
            pltpu.VMEM((span, D), F32),
            pltpu.VMEM((span, 1), F32),
            pltpu.VMEM((span, D), BF),
            pltpu.VMEM((D, span), BF),
            pltpu.VMEM((span, D), BF),
            pltpu.VMEM((span, D), F32),
            pltpu.VMEM((span, D), F32),
            pltpu.VMEM((2, side, width, BLK, BLK), BF),
            pltpu.VMEM((2, side * width, BLK, BLK), BF),
            pltpu.VMEM((side * side, BLK, BLK), BF),
            pltpu.SemaphoreType.DMA((2, 2)),
            pltpu.SemaphoreType.DMA,
        ],
        compiler_params=params(),
        cost_estimate=cost(14 * span * D * FF, 50 * MIB),
        name="feed_forward",
    )(live, tokens, attended, cotangent, gains, per_row, per_up, per_row)


def query_body(normed_t, dq_ref, w_ref, grad_ref, acc_ref):
    step = pl.program_id(0)

    @pl.when(step == 0)
    def _():
        acc_ref[...] = jnp.zeros_like(acc_ref)

    grad = dq_ref[...]
    acc_ref[...] += mul_nt(grad, join_tile(w_ref))
    split_tile(grad_ref, mul_nn(normed_t[...], grad))


def query_back(normed1_t, d_query, weights):
    span = normed1_t.shape[1]
    side, width = D // BLK, COLS // BLK
    whole = lambda j: (0, 0)
    act = pl.BlockSpec((span, D), whole)
    tile = pl.BlockSpec((side, width, BLK, BLK), lambda j: (0, j, 0, 0))
    return pl.pallas_call(
        query_body,
        grid=(D // COLS,),
        in_specs=[
            pl.BlockSpec((D, span), whole),
            pl.BlockSpec((span, COLS), lambda j: (0, j)),
            tile,
        ],
        out_specs=[tile, act],
        out_shape=[
            jax.ShapeDtypeStruct((side, side, BLK, BLK), BF),
            jax.ShapeDtypeStruct((span, D), F32),
        ],
        compiler_params=params(),
        cost_estimate=cost(4 * span * D * D, 8 * MIB),
        name="query_backward",
    )(normed1_t, d_query, weights.reshape(-1, 3 * side, BLK, BLK))


def input_body(
    tokens_ref, gains_ref, normed_t, own_ref, recv_ref, acc_ref, gm_ref, w_ref, grad_ref, out_ref,
    gain_ref, acc
):
    step = pl.program_id(0)

    @pl.when(step == 0)
    def _():
        acc[...] = acc_ref[...]

    grad = (own_ref[0].astype(F32) + recv_ref[0].astype(F32)).astype(BF)
    acc[...] += mul_nt(grad, join_tile(w_ref))
    split_tile(grad_ref, mul_nn(normed_t[...], grad))

    @pl.when(step == pl.num_programs(0) - 1)
    def _():
        unit_vals, inv_std = normalize(tokens_ref[...].astype(F32))
        back = acc[...]
        gain_ref[...] = jnp.sum(back * unit_vals, 0, keepdims=True)
        out_ref[...] = (
            gm_ref[...] + norm_back(back * gains_ref[0:1], unit_vals, inv_std)
        ).astype(BF)


def input_back(tokens, gains, normed1_t, own, received, partial, grad_middle, weights):
    span = tokens.shape[0]
    side, width = D // BLK, COLS // BLK
    per = D // COLS
    whole = lambda j: (0, 0)
    act = pl.BlockSpec((span, D), whole)
    part = pl.BlockSpec((1, span, COLS), lambda j: (j // per, 0, j % per))
    return pl.pallas_call(
        input_body,
        grid=(2 * per,),
        in_specs=[
            act,
            pl.BlockSpec((2, D), whole),
            pl.BlockSpec((D, span), whole),
            part,
            part,
            act,
            act,
            pl.BlockSpec((side, width, BLK, BLK), lambda j: (0, j + per, 0, 0)),
        ],
        out_specs=[
            pl.BlockSpec((side, width, BLK, BLK), lambda j: (0, j, 0, 0)),
            act,
            pl.BlockSpec((1, D), whole),
        ],
        out_shape=[
            jax.ShapeDtypeStruct((side, 2 * side, BLK, BLK), BF),
            jax.ShapeDtypeStruct((span, D), BF),
            jax.ShapeDtypeStruct((1, D), F32),
        ],
        scratch_shapes=[pltpu.VMEM((span, D), F32)],
        compiler_params=params(),
        cost_estimate=cost(8 * span * D * D, 20 * MIB),
        name="input_backward",
    )(
        tokens, gains, normed1_t, own, received, partial, grad_middle,
        weights.reshape(-1, 3 * side, BLK, BLK),
    )


def source_numbers():
    side = D // BLK
    numbers = np.arange(3 * side * side + side * side + 2 * side * (FF // BLK), dtype=np.int32)
    row, col = np.divmod(numbers[: 3 * side * side], 3 * side)
    numbers[: 3 * side * side] = np.where(
        col < side, row * side + col, side * side + row * 2 * side + col - side
    )
    return numbers


def gather_body(first, bounds, table, *refs):
    sources = refs[:6]
    out_ref, stage, sems = refs[6:]
    step, steps = pl.program_id(0), pl.num_programs(0)
    count = stage.shape[1] // 2

    def fetch(which, slot):
        start = first + which * count
        for i in range(count):
            number = table[start + i]
            for low, high, own, other in zip(bounds, bounds[1:], sources[:3], sources[3:]):

                @pl.when((number >= low) & (number < high))
                def _():
                    for src, at in ((own, i), (other, count + i)):
                        pltpu.make_async_copy(
                            src.at[number - low], stage.at[slot, at], sems.at[slot]
                        ).start()

    @pl.when(step == 0)
    def _():
        fetch(0, 0)

    @pl.when(step + 1 < steps)
    def _():
        fetch(step + 1, (step + 1) % 2)

    slot = step % 2
    pltpu.make_async_copy(stage.at[slot], stage.at[slot], sems.at[slot]).wait()
    total = stage[slot, :count].astype(F32) + stage[slot, count:].astype(F32)
    out_ref[...] = total.astype(BF)


def gather_sums(table, first, count, own, other):
    hbm = pl.BlockSpec(memory_space=pltpu.HBM)
    steps = 4
    part = count // steps
    bounds = np.cumsum([0] + [src.shape[0] for src in own]).tolist()
    return pl.pallas_call(
        functools.partial(gather_body, first, bounds),
        grid=(steps,),
        in_specs=[pl.BlockSpec(memory_space=pltpu.SMEM)] + [hbm] * 6,
        out_specs=pl.BlockSpec((part, BLK, BLK), lambda i: (i, 0, 0)),
        out_shape=jax.ShapeDtypeStruct((count, BLK, BLK), BF),
        scratch_shapes=[
            pltpu.VMEM((2, 2 * part, BLK, BLK), BF),
            pltpu.SemaphoreType.DMA((2,)),
        ],
        compiler_params=params(),
        cost_estimate=cost(0, 6 * count * BLK * BLK),
        name="gradient_sums",
    )(table, *own, *other)


def merge_body(first, second, passed, *refs):
    refs = list(refs)

    def total(count):
        return sum(refs.pop(0)[...].astype(F32) for _ in range(count))

    sums = [total(2), total(2)] if first else []
    if second:
        sums.append(total(3 if passed else 2))
    for ref, value in zip(refs, sums):
        ref[...] = value.astype(BF)


def merge_sums(low, came, kept, last, passed):
    steps = 3
    args, specs, shapes, outs = [], [], [], []

    def part(array, count, start):
        args.append(array)
        size = count // steps
        specs.append(pl.BlockSpec((size, BLK, BLK), lambda i: (i + start * steps, 0, 0)))

    def out(count):
        shapes.append(jax.ShapeDtypeStruct((count, BLK, BLK), BF))
        outs.append(pl.BlockSpec((count // steps, BLK, BLK), lambda i: (i, 0, 0)))

    if low is not None:
        count = low.shape[0] // 2
        for start in range(2):
            part(low, count, start)
            part(came, count, start)
            out(count)
    if kept is not None:
        for array in (kept, last) if passed is None else (kept, last, passed):
            part(array, kept.shape[0], 0)
        out(kept.shape[0])
    body = functools.partial(merge_body, low is not None, kept is not None, passed is not None)
    return pl.pallas_call(
        body,
        grid=(steps,),
        in_specs=specs,
        out_specs=outs,
        out_shape=shapes,
        compiler_params=params(44),
        cost_estimate=cost(0, 6 * MIB),
        name="merge_sums",
    )(*args)


def two_terms(values):
    high = values.astype(BF)
    return high, (values - high.astype(F32)).astype(BF)


def update_body(count, *refs):
    parts = refs[:count]
    m_ref, sl_ref, sr_ref, rl_ref, rr_ref, g_out, sl_out, sr_out, m_out = refs[count:]

    def long_left(terms, axis):
        return jnp.concatenate([terms[0], terms[0], terms[1]], axis)

    def long_right(terms, axis):
        return jnp.concatenate([terms[0], terms[1], terms[0]], axis)

    for i in range(g_out.shape[0]):
        total = sum(part[i].astype(F32) for part in parts)
        g_out[i] = total
        grad = two_terms(total)
        sl_out[i] = sl_ref[i] + mul_nt(long_left(grad, 1), long_right(grad, 1))
        tall = long_right(grad, 0)
        sr_out[i] = sr_ref[i] + mul_tn(long_left(grad, 0), tall)
        inner = mul_nn(long_left(two_terms(rl_ref[i]), 1), tall)
        direction = mul_nn(
            long_left(two_terms(inner), 1), long_right(two_terms(rr_ref[i]), 0)
        )
        master = m_ref[i]
        scale = jnp.sqrt(jnp.mean(master * master, keepdims=True) + 1e-06)
        scale = scale * lax.rsqrt(jnp.mean(direction * direction, keepdims=True) + 1e-06)
        m_out[i] = master - 0.3 * scale * direction


def update(parts, master, stat_left, stat_right, root_left, root_right):
    count = master.shape[0]
    group = 6 if count % 6 == 0 else 1
    block = pl.BlockSpec((group, BLK, BLK), lambda i: (i, 0, 0))
    shape = jax.ShapeDtypeStruct(master.shape, F32)
    return pl.pallas_call(
        functools.partial(update_body, len(parts)),
        grid=(count // group,),
        in_specs=[block] * (len(parts) + 5),
        out_specs=[block] * 4,
        out_shape=[shape] * 4,
        compiler_params=params(),
        cost_estimate=cost(48 * count * BLK**3, 15 * MIB),
        name="block_update",
    )(*parts, master, stat_left, stat_right, root_left, root_right)


def pair_moves():
    moves_same, moves_cross = [], []
    for z in range(4):
        for c in range(2):
            for moves, bit in ((moves_same, z % 2), (moves_cross, 1 - z % 2)):
                moves.append((z * 2 + c, (2 * c + bit) * 2 + z // 2))
    return moves_same, moves_cross


def row_part(values, which):
    return lax.dynamic_index_in_dim(values, which, 0, False)


def move_rows(values, crossed, back=False):
    moves = pair_moves()[crossed]
    return lax.ppermute(values, ("seq", "core"), [(b, a) for a, b in moves] if back else moves)


def in_order(kept, crossed, parity):
    return jnp.where(parity == 0, kept, crossed), jnp.where(parity == 0, crossed, kept)


def spread_rows(values, parity):
    kept = move_rows(row_part(values, parity), False)
    crossed = move_rows(row_part(values, 1 - parity), True)
    return jnp.concatenate(in_order(kept, crossed, parity), 0)


def gather_rows(values, parity):
    parts = values.reshape(2, values.shape[0] // 2, values.shape[1])
    kept = move_rows(row_part(parts, parity), False, True)
    crossed = move_rows(row_part(parts, 1 - parity), True, True)
    return jnp.stack(in_order(kept, crossed, parity), 0)


def swap_cores(values):
    return lax.ppermute(values, "core", [(0, 1), (1, 0)])


def chip_orders(chips):
    bits = [1 << i for i in range(chips.bit_length() - 1)]
    return bits, bits[::-1]


def offsets(order):
    result = [0]
    for bit in order:
        result = result + [o ^ bit for o in result]
    return result


def place_lists(chips, owned, planes):
    shape = (2, planes, chips, owned)
    by_core = np.array([offsets(order) for order in chip_orders(chips)], np.int32)
    grid = np.indices(shape).astype(np.int32).reshape(4, 2, -1)
    offset = np.broadcast_to(by_core[:, None, :, None], shape).reshape(2, -1)
    return grid[1, 0], offset, grid[3, 0]


def arrival_order(chips, owned, planes):
    per_plane, quarter = chips * owned, owned
    if chips != 4:
        return np.arange(planes * per_plane)
    pieces = [(0, 0)]
    for k in range(1, planes + 1):
        pieces += [(k, 0)] if k < planes else []
        pieces += [(k - 1, 1), (k - 1, 2)]
        pieces += [(k - 2, 3)] if k > 1 else []
    pieces.append((planes - 1, 3))
    starts = [k * per_plane + r * quarter for k, r in pieces]
    return np.concatenate([np.arange(start, start + quarter) for start in starts])


def swap_chips(values, bits):
    chips = lax.axis_size("chip")
    moves = [(i * 2 + c, (i ^ bits[c]) * 2 + c) for i in range(chips) for c in range(2)]
    return lax.ppermute(values, ("chip", "core"), moves)


def move_planes(values, shift):
    planes = lax.axis_size("seq")
    return lax.ppermute(values, "seq", [(i, (i + shift) % planes) for i in range(planes)])


def after(value, *deps):
    return lax.optimization_barrier((value, *deps))[0]


def together(*values):
    return lax.optimization_barrier(values)


def chip_steps():
    return list(zip(*chip_orders(lax.axis_size("chip"))))


def finish_pieces(pieces):
    for bits in chip_steps()[2:]:
        joined = jnp.concatenate(pieces, 0)
        pieces = [joined, swap_chips(joined, bits)]
    return pieces


def add_halves(kept, came):
    return (kept.astype(F32) + came.astype(F32)).astype(BF)


def pack_terms(values):
    high = lax.optimization_barrier(values.astype(BF))
    low = (values - high.astype(F32)).astype(BF)
    terms = jnp.stack([high, low]).reshape(-1, BLK)
    return jnp.pad(terms, ((0, BLK - terms.shape[0]), (0, 0)))[None]


def unpack_terms(blocks, shape):
    terms = blocks.reshape(-1, BLK, BLK)[:, : 2 * shape[0] * shape[1] // BLK]
    terms = terms.reshape(-1, 2, *shape).astype(F32)
    return terms[:, 0] + terms[:, 1]


def finish_sums(keep, send, riders):
    for bits in chip_steps()[::-1][1:-1]:
        count = keep.shape[0] // 2
        came = swap_chips(with_riders(send, riders), bits)
        riders = more_riders(riders, came, keep.shape[0])
        send = add_halves(keep[count:], came[count : 2 * count])
        keep = add_halves(keep[:count], came[:count])
    return keep, send, riders


def with_riders(send, riders):
    return send if riders is None else jnp.concatenate([send, riders], 0)


def more_riders(riders, came, count):
    return riders if riders is None else jnp.concatenate([riders, came[count:]], 0)


def by_chip(riders, me, core):
    chips = lax.axis_size("chip")
    ranks = np.array([np.argsort(offsets(order[::-1])) for order in chip_orders(chips)], np.int32)
    rank = jnp.asarray(ranks)[core][me ^ jnp.arange(chips, dtype=jnp.int32)]
    return riders.reshape(chips, -1, BLK, BLK)[rank]


def local(
    tokens,
    cotangent,
    lengths,
    owner_perm,
    master,
    norm_gains,
    stat_left,
    stat_right,
    root_left,
    root_right,
    moment_first,
    moment_second,
):
    core = lax.axis_index("core")
    place_z = lax.axis_index("seq")
    parity = place_z % 2
    block_count = owner_perm.shape[0]
    owned = master.shape[0]
    half = block_count // 2

    chips, planes = lax.axis_size("chip"), lax.axis_size("seq")
    me = lax.axis_index("chip")

    pair_lengths = jnp.stack([lengths, swap_cores(lengths)])
    pair_lengths = jnp.where(core == 0, pair_lengths, pair_lengths[::-1]).reshape(-1)
    length = lax.dynamic_index_in_dim(pair_lengths, place_z, 0, False)
    span = tokens.shape[0] * tokens.shape[1]
    live = jnp.stack([length - core * span, length - (1 - core) * span, length - core * span])

    distance, offset, slot = place_lists(chips, owned, planes)
    offset = jnp.where(core == 0, offset, offset[::-1])
    device = ((place_z - distance) % planes * chips + (me ^ offset)) * 2
    device = device + jnp.stack([core, 1 - core])[:, None]
    table = owner_perm[(device * owned + slot).reshape(-1)]
    sums_table = jnp.asarray(source_numbers())[table[:half]]
    arrive = arrival_order(chips, owned, planes)
    near_slots, far_slots = device * owned + slot
    table = owner_perm[jnp.concatenate([near_slots[arrive], far_slots[arrive]])]

    shard = master.astype(BF)
    first_bits, second_bits = chip_steps()[:2]
    per_plane = chips * owned
    by_phase = chips == 4
    cross, held, weights, first = None, (), None, 0
    came, turned = swap_chips(shard, first_bits), swap_chips(shard, second_bits)
    next_shard = move_planes(shard, 1)
    pieces = [[shard, came, turned]]

    def place(parts, first, weights):
        others = [swap_cores(part) for part in parts]
        weights = place_blocks(table, first, parts, others, weights)
        return weights, first + sum(part.shape[0] for part in parts)

    for k in range(1, planes):
        ready = () if k == 1 else (cross, *held, live, table, sums_table)
        ready = ready if weights is None else (*ready, weights)
        this_shard, came, turned, rows, *done = together(next_shard, came, turned, tokens, *ready)
        if k > 1:
            pieces[k - 2].append(done[0])
        cross = swap_chips(came, second_bits)
        arrived = [this_shard, came, turned, *(pieces[0][:1] if k == 1 else done[:1])]
        arrived = arrived[3:] + arrived[:3] if k == 1 else arrived
        pieces[k - 1][1:] = [came, turned]
        came, turned = swap_chips(this_shard, first_bits), swap_chips(this_shard, second_bits)
        pieces.append([this_shard, came, turned])
        if k < planes - 1:
            next_shard = move_planes(this_shard, 1)
        else:
            row_same = move_rows(row_part(rows, parity), False)
            row_cross = row_part(after(rows, row_same), 1 - parity)
            row_cross = move_rows(row_cross, True)
        if by_phase:
            if k > 1:
                weights, first = place(done[1:2], first, weights)
            held = (jnp.concatenate(arrived, 0),)
    came, turned, done, row_same, row_cross, *held = together(
        came, turned, cross, row_same, row_cross, *held, *([] if weights is None else [weights])
    )
    own_tokens = jnp.concatenate(in_order(row_same, row_cross, parity), 0)
    pieces[-2].append(done)
    pieces[-1][1:] = [came, turned, swap_chips(came, second_bits)]
    normed1, normed1_t = norm_tokens(own_tokens, norm_gains)
    if by_phase:
        weights, first = place(held[:1], first, weights)
        weights, first = place([came, turned, done], first, weights)
        last, normed1, *_ = together(pieces[-1][-1], normed1, weights)
        other_normed = swap_cores(normed1)
        weights, _ = place([last], first, weights)
    else:
        for each in pieces:
            each = [jnp.concatenate(finish_pieces(each), 0)]
            weights, first = place(each, first, weights)
        other_normed = swap_cores(normed1)
    own_cot = spread_rows(after(cotangent, weights), parity)

    own_qkv, other_kv = project(normed1, other_normed, weights)
    attended, q_aug = attend(live, own_qkv, other_kv)
    layer, g_rest, grad_middle, grad_attended, gain_second = feed(
        live, own_tokens, attended, own_cot, norm_gains, weights
    )
    other_rest = swap_cores(g_rest)
    layer_out = gather_rows(layer, parity)
    d_query, d_own, d_other = attend_back(live, q_aug, own_qkv, other_kv, attended, grad_attended)
    received = swap_cores(after(d_other, layer_out))
    flat = lambda g: g.reshape(-1, BLK, BLK)
    g_query, partial = query_back(normed1_t, d_query, weights)
    g_query = flat(g_query)
    other_query = swap_cores(g_query)
    g_kv, grad_in, gain_first = input_back(
        own_tokens, norm_gains, normed1_t, d_own, received, partial, grad_middle, weights
    )
    g_kv = flat(g_kv)
    gain_part = jnp.concatenate([gain_first, gain_second], 0)
    mine = pack_terms(gain_part)
    other_kv_grad = swap_cores(after(g_kv, other_query))
    theirs = swap_cores(mine)
    pair = jnp.concatenate([mine, theirs], 0)
    riders = jnp.where(core == 0, pair, pair[::-1])
    own_grads = (g_query, g_kv, g_rest)
    other_grads = (other_query, other_kv_grad, other_rest)
    half_plane = per_plane // 2
    last_bits, before_bits = chip_steps()[-1], chip_steps()[0]
    halves = grad_in.reshape(2, span // 2, D)
    rows = [row_part(halves, parity), row_part(halves, 1 - parity)]
    moved_rows, lows, sent, passed, riders_z = [], [], None, None, []

    def sums(k, part, held):
        first = k * per_plane + part * half_plane
        return gather_sums(held, first, half_plane, own_grads, other_grads)

    order = list(range(planes))[::-1]
    high = sums(order[0], 1, sums_table)
    held = sums_table
    held_riders = []
    for turn in range(planes + 1):
        group, moves = [], []
        if turn < planes:
            group.append(high)
            moves.append(lambda v: swap_chips(v, last_bits))
        if 1 <= turn <= planes:
            group.append(sent)
            moves.append(lambda v: swap_chips(v, before_bits))
        if 2 <= turn <= planes:
            group.append(part)
            moves.append(lambda v: move_planes(v, -1))
        if turn < 2:
            group.append(riders)
            bits = last_bits if turn == 0 else before_bits
            moves.append(lambda v: swap_chips(v, bits))
        if turn in (1, 2):
            group.append(rows[turn - 1])
            crossed = turn == 2
            moves.append(lambda v: move_rows(v, crossed, True))
        far_riders = [] if turn < planes - 1 else [1, 2] if turn == planes - 1 else range(3, planes)
        group += [rider for _ in far_riders]
        moves += [functools.partial(move_planes, shift=-k) for k in far_riders]
        came = [move(value) for move, value in zip(moves, together(*group, *moved_rows, *held_riders))]
        if turn in (1, 2):
            moved_rows.append(came.pop())
        if turn < 2:
            riders = jnp.concatenate([riders, came.pop()], 0)
        count = len(came) - len(far_riders)
        riders_z, came = riders_z + came[count:], came[:count]
        if turn == planes:
            parts = [keep_before, *came]
            continue
        passed = came.pop() if turn >= 2 else None
        low = sums(order[turn], 0, after(held, high))
        if turn + 1 < planes:
            high = sums(order[turn + 1], 1, after(held, low))
        held = after(sums_table, *came)
        held_riders = [riders] if turn == 1 else []
        if turn == 1:
            plane_gain = by_chip(riders, me, core)
            plane_gain = jnp.sum(unpack_terms(plane_gain, gain_part.shape), 0)
            rider = pack_terms(plane_gain)
        second = (None, None, None) if turn == 0 else (keep_before, came[-1], passed)
        keep, sent, *part = merge_sums(low, came[0], *second)
        part = part[0] if part else None
        keep_before, sent, grown = finish_sums(keep, sent, riders if turn == 0 else None)
        riders = grown if turn == 0 else riders
    input_grad = jnp.stack(in_order(*moved_rows, parity), 0).astype(F32)
    planes_gain = [unpack_terms(each, gain_part.shape)[0] for each in (rider, *riders_z)]
    turned = (jnp.arange(planes, dtype=jnp.int32) - place_z) % planes
    gain_grad = jnp.sum(jnp.stack(planes_gain)[turned], 0)
    grad_blocks, stat_left_new, stat_right_new, master_new = update(
        parts, master, stat_left, stat_right, root_left, root_right
    )
    first_new = 0.9 * moment_first + 0.1 * gain_grad
    second_new = 0.999 * moment_second + 0.001 * gain_grad * gain_grad
    first_hat = first_new / (1.0 - 0.9**STEP)
    second_hat = second_new / (1.0 - 0.999**STEP)
    gains_new = norm_gains - 0.5 * first_hat / (jnp.sqrt(second_hat) + 1e-08)
    return (
        layer_out,
        input_grad,
        grad_blocks,
        stat_left_new,
        stat_right_new,
        master_new,
        first_new,
        second_new,
        gains_new,
    )


def solution(mesh):
    seq_size, rows_size = mesh.shape["seq"], mesh.shape["rows"]
    mesh = Mesh(mesh.devices.reshape(seq_size, rows_size // 2, 2), ("seq", "chip", "core"))
    activation = P(("chip", "core"), "seq", None)
    blocks = P(("seq", "chip", "core"), None, None)
    return jax.shard_map(
        local,
        mesh=mesh,
        in_specs=(
            activation, activation, P(("chip", "core")), P(), blocks, P(),
            blocks, blocks, blocks, blocks, P(), P(),
        ),
        out_specs=(activation, activation, blocks, blocks, blocks, blocks, P(), P(), P()),
        check_vma=False,
    )
```

```python
import functools
import jax
import jax.numpy as jnp
import numpy as np
from jax import lax
from jax.experimental import pallas as pl
from jax.experimental.pallas import tpu as pltpu
from jax.sharding import Mesh
from jax.sharding import PartitionSpec as P

D = 1024
HD = 64
FF = 4096
BLK = 128
STEP = 10
COLS = 1024
BF = jnp.bfloat16
F32 = jnp.float32
MIB = 1024 * 1024

norm_eps = 1e-05
score_scale = 0.125
masked_score = -1e30


def params(limit=56):
    return pltpu.CompilerParams(vmem_limit_bytes=limit * MIB)


def cost(flops, nbytes):
    return pl.CostEstimate(flops=int(flops), bytes_accessed=int(nbytes), transcendentals=0)


def mul_nn(left, right):
    return jnp.dot(left, right, preferred_element_type=F32)


def mul_nt(left, right):
    return lax.dot_general(left, right, (((1,), (1,)), ((), ())), preferred_element_type=F32)


def mul_tn(left, right):
    return lax.dot_general(left, right, (((0,), (0,)), ((), ())), preferred_element_type=F32)


def join_tile(ref):
    rows, cols = ref.shape[0], ref.shape[1]
    return jnp.concatenate([ref[:, j].reshape(rows * BLK, BLK) for j in range(cols)], axis=1)


def split_tile(ref, matrix):
    rows, cols = ref.shape[0], ref.shape[1]
    for j in range(cols):
        ref[:, j] = matrix[:, j * BLK : (j + 1) * BLK].reshape(rows, BLK, BLK).astype(ref.dtype)


def split_flat(ref, matrix):
    cols = matrix.shape[1] // BLK
    for i in range(matrix.shape[0] // BLK):
        for j in range(cols):
            block = matrix[i * BLK : (i + 1) * BLK, j * BLK : (j + 1) * BLK]
            ref[i * cols + j] = block.astype(ref.dtype)


def normalize(values):
    row_mean = jnp.mean(values, -1, keepdims=True)
    centered = values - row_mean
    row_var = jnp.mean(centered * centered, -1, keepdims=True)
    inv_std = lax.rsqrt(row_var + norm_eps)
    return centered * inv_std, inv_std


def gelu_parts(hidden):
    bell = jnp.exp(hidden * hidden * -0.5)
    t = 1.0 / (1.0 + jnp.abs(hidden) * (0.3275911 * 0.7071067811865476))
    poly = 1.061405429 * t - 1.453152027
    for term in (1.421413741, -0.284496736, 0.254829592):
        poly = poly * t + term
    tail = poly * t * 0.5 * bell
    return jnp.where(hidden < 0.0, tail, 1.0 - tail), hidden * bell * 0.3989422804014327


def norm_back(gradient, unit_vals, inv_std):
    grad_mean = jnp.mean(gradient, -1, keepdims=True)
    cross_mean = jnp.mean(gradient * unit_vals, -1, keepdims=True)
    return inv_std * (gradient - grad_mean - unit_vals * cross_mean)


def place_body(first, pieces, table, *refs):
    near, far = refs[:pieces], refs[pieces : 2 * pieces]
    out_ref, sem = refs[-2:]
    total = 0
    for start, sources in ((first, near), (table.shape[0] // 2 + first, far)):
        for src in sources:
            for slot in range(src.shape[0]):
                pltpu.make_async_copy(src.at[slot], out_ref.at[table[start + slot]], sem).start()
            start += src.shape[0]
            total += src.shape[0]
    done = out_ref.at[pl.ds(0, total)]
    pltpu.make_async_copy(done, done, sem).wait()


def place_blocks(table, first, near, far, kept):
    smem = pl.BlockSpec(memory_space=pltpu.SMEM)
    hbm = pl.BlockSpec(memory_space=pltpu.HBM)
    vmem = pl.BlockSpec(memory_space=pltpu.VMEM)
    kept = () if kept is None else (kept,)
    count = 2 * len(near)
    return pl.pallas_call(
        functools.partial(place_body, first, len(near)),
        out_shape=jax.ShapeDtypeStruct((table.shape[0], BLK, BLK), BF),
        in_specs=[smem] + [vmem] * count + [hbm] * len(kept),
        out_specs=hbm,
        scratch_shapes=[pltpu.SemaphoreType.DMA],
        input_output_aliases={1 + count: 0} if kept else {},
        compiler_params=params(46),
        cost_estimate=cost(0, 6 * MIB),
        name="place_weights",
    )(table, *near, *far, *kept)


def norm_body(tokens_ref, gains_ref, out_ref, turned_ref):
    normed = normalize(tokens_ref[...].astype(F32))[0] * gains_ref[0:1]
    out_ref[...] = normed.astype(BF)
    turned_ref[...] = normed.T.astype(BF)


def norm_tokens(tokens, gains):
    span = tokens.shape[0]
    steps = 4
    part = pl.BlockSpec((span // steps, D), lambda i: (i, 0))
    return pl.pallas_call(
        norm_body,
        grid=(steps,),
        in_specs=[part, pl.BlockSpec((2, D), lambda i: (0, 0))],
        out_specs=[part, pl.BlockSpec((D, span // steps), lambda i: (0, i))],
        out_shape=[jax.ShapeDtypeStruct((span, D), BF), jax.ShapeDtypeStruct((D, span), BF)],
        compiler_params=params(46),
        cost_estimate=cost(0, 3 * MIB),
        name="norm_tokens",
    )(tokens, gains)


def qkv_body(own_ref, other_ref, w_ref, own_out, other_out):
    step = pl.program_id(0)
    weight = join_tile(w_ref)
    own_out[...] = mul_nn(own_ref[...], weight).astype(BF)

    @pl.when(step >= D // COLS)
    def _():
        other_out[...] = mul_nn(other_ref[...], weight).astype(BF)


def project(own, other, weights):
    span = own.shape[0]
    skip = D // COLS
    once = pl.BlockSpec((span, D), lambda j: (0, 0))
    return pl.pallas_call(
        qkv_body,
        grid=(3 * D // COLS,),
        in_specs=[
            once,
            once,
            pl.BlockSpec((D // BLK, COLS // BLK, BLK, BLK), lambda j: (0, j, 0, 0)),
        ],
        out_specs=[
            pl.BlockSpec((span, COLS), lambda j: (0, j)),
            pl.BlockSpec((span, COLS), lambda j: (0, jnp.maximum(j - skip, 0))),
        ],
        out_shape=[
            jax.ShapeDtypeStruct((span, 3 * D), BF),
            jax.ShapeDtypeStruct((span, 2 * D), BF),
        ],
        compiler_params=params(),
        cost_estimate=cost(10 * span * D * D, 12 * MIB),
        name="qkv_projection",
    )(own, other, weights.reshape(-1, 3 * D // BLK, BLK, BLK))


def lane_masks(head):
    lane = lax.broadcasted_iota(jnp.int32, (1, BLK), 1)
    first = HD * (1 - head)
    keep = (lane // HD == head).astype(F32)
    dead_lane = (lane == first).astype(F32)
    terms = [(lane == first + 1 + i).astype(F32) for i in range(3)]
    return keep, dead_lane, terms


def three_terms(values):
    high = values.astype(BF).astype(F32)
    rest = values - high
    middle = rest.astype(BF).astype(F32)
    return high, middle, rest - middle


def key_bias(span, live_count):
    row = lax.broadcasted_iota(jnp.int32, (span, 1), 0)
    return jnp.where(row < live_count, 0.0, masked_score).astype(F32)


def attend_body(live_ref, q_ref, ko_ref, vo_ref, kx_ref, vx_ref, out_ref, aug_ref):
    span = q_ref.shape[0]
    bias_own = key_bias(span, live_ref[0])
    bias_other = key_bias(span, live_ref[1])
    queries = q_ref[...].astype(F32) * score_scale
    k_own, k_other = ko_ref[...].astype(F32), kx_ref[...].astype(F32)
    v_own_f, v_other_f = vo_ref[...].astype(F32), vx_ref[...].astype(F32)
    results, scores = [], []
    for head in range(2):
        keep, dead_lane, _ = lane_masks(head)
        q_head = (queries * keep + dead_lane).astype(BF)
        s_own = mul_nt(q_head, (k_own * keep + bias_own * dead_lane).astype(BF))
        s_other = mul_nt(q_head, (k_other * keep + bias_other * dead_lane).astype(BF))
        scores.append((q_head, s_own, s_other))
    for head in range(2):
        keep, _, terms = lane_masks(head)
        q_head, s_own, s_other = scores[head]
        top = jnp.max(jnp.maximum(s_own, s_other), -1, keepdims=True)
        p_own = jnp.exp(s_own - top)
        p_other = jnp.exp(s_other - top)
        v_own = (v_own_f * keep + (1.0 - keep)).astype(BF)
        v_other = (v_other_f * keep + (1.0 - keep)).astype(BF)
        mixed = mul_nn(p_own.astype(BF), v_own) + mul_nn(p_other.astype(BF), v_other)
        total = mixed[:, HD * (1 - head) : HD * (1 - head) + 1]
        results.append(mixed / total * keep)
        parts = three_terms(-(top + jnp.log(total)))
        stats = sum(part * lane for part, lane in zip(parts, terms))
        aug_ref[:, head * BLK : (head + 1) * BLK] = (q_head.astype(F32) + stats).astype(BF)
    out_ref[...] = (results[0] + results[1]).astype(BF)


def attend(live, own, other):
    span = own.shape[0]
    pairs = D // BLK
    col = lambda shift: pl.BlockSpec((span, BLK), lambda p: (0, p + shift))
    return pl.pallas_call(
        attend_body,
        grid=(pairs,),
        in_specs=[
            pl.BlockSpec(memory_space=pltpu.SMEM),
            col(0),
            col(pairs),
            col(2 * pairs),
            col(0),
            col(pairs),
        ],
        out_specs=[col(0), pl.BlockSpec((span, 2 * BLK), lambda p: (0, p))],
        out_shape=[
            jax.ShapeDtypeStruct((span, D), BF),
            jax.ShapeDtypeStruct((span, 2 * D), BF),
        ],
        compiler_params=params(),
        cost_estimate=cost(40 * span * span * D, 8 * MIB),
        name="attention",
    )(live, own, own, own, other, other)


def attend_back_body(
    live_ref, aug_ref, ko_ref, vo_ref, kx_ref, vx_ref, at_ref, g_ref, dq_ref, own_ref, other_ref
):
    span = at_ref.shape[0]
    grads = g_ref[...].astype(F32)
    product = grads * at_ref[...].astype(F32)
    keeps, g_augs, q_augs = [], [], []
    for head in range(2):
        keep, dead_lane, terms = lane_masks(head)
        delta = jnp.sum(product * keep, -1, keepdims=True)
        parts = three_terms(-delta)
        stats = sum(part * lane for part, lane in zip(parts, terms))
        g_augs.append((grads * keep + stats).astype(BF))
        q_augs.append(aug_ref[:, head * BLK : (head + 1) * BLK])
    d_query = [None, None]
    for k_ref, v_ref, out_ref, live in (
        (ko_ref, vo_ref, own_ref, live_ref[0]),
        (kx_ref, vx_ref, other_ref, live_ref[1]),
    ):
        bias = key_bias(span, live)
        keys = k_ref[...]
        keys_f, values_f = keys.astype(F32), v_ref[...].astype(F32)
        d_keys = d_values = None
        for head in range(2):
            keep, dead_lane, terms = lane_masks(head)
            ones = terms[0] + terms[1] + terms[2]
            k_aug = (keys_f * keep + (bias * dead_lane + ones)).astype(BF)
            v_aug = (values_f * keep + ones).astype(BF)
            probs = jnp.exp(mul_nt(k_aug, q_augs[head]))
            d_scores = (probs * mul_nt(v_aug, g_augs[head])).astype(BF)
            value_part = mul_nn(probs.astype(BF), g_augs[head]) * keep
            key_part = mul_nn(d_scores, q_augs[head]) * keep
            query_part = mul_tn(d_scores, keys) * (keep * score_scale)
            d_query[head] = query_part if d_query[head] is None else d_query[head] + query_part
            d_values = value_part if d_values is None else d_values + value_part
            d_keys = key_part if d_keys is None else d_keys + key_part
        out_ref[0] = d_keys.astype(out_ref.dtype)
        out_ref[1] = d_values.astype(out_ref.dtype)
    dq_ref[...] = (d_query[0] + d_query[1]).astype(BF)


def attend_back(live, aug, own, other, attended, grads):
    span = own.shape[0]
    pairs = D // BLK
    col = lambda shift: pl.BlockSpec((span, BLK), lambda p: (0, p + shift))
    pair_out = pl.BlockSpec((2, span, BLK), lambda p: (0, 0, p))
    return pl.pallas_call(
        attend_back_body,
        grid=(pairs,),
        in_specs=[
            pl.BlockSpec(memory_space=pltpu.SMEM),
            pl.BlockSpec((span, 2 * BLK), lambda p: (0, p)),
            col(pairs),
            col(2 * pairs),
            col(0),
            col(pairs),
            col(0),
            col(0),
        ],
        out_specs=[col(0), pair_out, pair_out],
        out_shape=[
            jax.ShapeDtypeStruct((span, D), BF),
            jax.ShapeDtypeStruct((2, span, D), BF),
            jax.ShapeDtypeStruct((2, span, D), BF),
        ],
        compiler_params=params(),
        cost_estimate=cost(60 * span * span * D, 12 * MIB),
        name="attention_backward",
    )(live, aug, own, own, other, other, attended, grads)


def feed_body(
    live_ref,
    tokens_ref,
    attended_ref,
    cot_ref,
    gains_ref,
    wo_ref,
    wu_ref,
    wd_ref,
    kept_ref,
    crossed_ref,
    rest_ref,
    gm_ref,
    ga_ref,
    gain_ref,
    unit,
    inv,
    normed,
    normed_t,
    top,
    acc_out,
    acc_back,
    up_stage,
    down_stage,
    out_stage,
    sems,
    out_sem,
):
    step = pl.program_id(0)
    place = step % 2
    side, width = up_stage.shape[1], up_stage.shape[2]
    per_tile = side * width
    up_first = side * side
    down_first = up_first + side * FF // BLK

    def drain(which):
        pltpu.make_async_copy(up_stage.at[which], up_stage.at[which], sems.at[0, which]).wait()
        pltpu.make_async_copy(down_stage.at[which], down_stage.at[which], sems.at[1, which]).wait()
    span = tokens_ref.shape[0]

    @pl.when(step == 0)
    def _():
        weight = join_tile(wo_ref)
        middle = tokens_ref[...].astype(F32) + mul_nn(attended_ref[...], weight)
        unit_vals, inv_std = normalize(middle)
        unit[...] = unit_vals
        inv[...] = inv_std
        normed_vals = unit_vals * gains_ref[1:2]
        normed[...] = normed_vals.astype(BF)
        normed_t[...] = normed_vals.T.astype(BF)
        row = lax.broadcasted_iota(jnp.int32, (span, 1), 0)
        top[...] = jnp.where(row < live_ref[2], cot_ref[...].astype(F32), 0.0).astype(BF)
        acc_out[...] = middle
        acc_back[...] = jnp.zeros_like(acc_back)

    w_up = join_tile(wu_ref)
    w_down = join_tile(wd_ref)
    hidden = mul_nn(normed[...], w_up)
    grad_act = mul_nt(top[...], w_down)
    share, slope_rest = gelu_parts(hidden)
    activated = (hidden * share).astype(BF)
    grad_hidden = (grad_act * (share + slope_rest)).astype(BF)
    acc_out[...] += mul_nn(activated, w_down)
    acc_back[...] += mul_nt(grad_hidden, w_up)

    @pl.when(step >= 2)
    def _():
        drain(place)

    split_flat(down_stage.at[place], mul_tn(activated, top[...]))
    dest = rest_ref.at[pl.ds(down_first + step * per_tile, per_tile)]
    pltpu.make_async_copy(down_stage.at[place], dest, sems.at[1, place]).start()
    split_tile(up_stage.at[place], mul_nn(normed_t[...], grad_hidden))
    for i in range(side):
        dest = rest_ref.at[pl.ds(up_first + i * (FF // BLK) + step * width, width)]
        pltpu.make_async_copy(up_stage.at[place, i], dest, sems.at[0, place]).start()

    @pl.when(step == pl.num_programs(0) - 1)
    def _():
        for flip in range(2):

            @pl.when(live_ref[3] == flip)
            def _():
                for ref, part in ((kept_ref, flip), (crossed_ref, 1 - flip)):
                    ref[...] = acc_out[part * (span // 2) : (part + 1) * (span // 2)].astype(BF)

        unit_vals = unit[...]
        back = acc_back[...]
        gain_ref[...] = jnp.sum(back * unit_vals, 0, keepdims=True)
        grad_middle = top[...].astype(F32) + norm_back(back * gains_ref[1:2], unit_vals, inv[...])
        gm_ref[...] = grad_middle
        back_middle = grad_middle.astype(BF)
        split_flat(out_stage, mul_tn(attended_ref[...], back_middle))
        out_copy = pltpu.make_async_copy(out_stage, rest_ref.at[pl.ds(0, up_first)], out_sem)
        out_copy.start()
        ga_ref[...] = mul_nt(back_middle, join_tile(wo_ref)).astype(BF)
        drain(1 - place)
        drain(place)
        out_copy.wait()


def feed(live, tokens, attended, cotangent, gains, weights):
    span = tokens.shape[0]
    side, width = D // BLK, COLS // BLK
    whole = lambda j: (0, 0)
    act = pl.BlockSpec((span, D), whole)
    once = pl.BlockSpec((span, D), whole, pipeline_mode=pl.Buffered(1))
    half_act = pl.BlockSpec((span // 2, D), whole)
    per_row = weights.reshape(-1, side, BLK, BLK)
    per_up = weights.reshape(-1, FF // BLK, BLK, BLK)
    out_row = (3 * side * side) // side // side
    up_row = 4 * side * side // (FF // BLK) // side
    down_row = (4 * side * side + side * FF // BLK) // side // width
    return pl.pallas_call(
        feed_body,
        grid=(FF // COLS,),
        in_specs=[
            pl.BlockSpec(memory_space=pltpu.SMEM),
            once,
            once,
            once,
            pl.BlockSpec((2, D), whole),
            pl.BlockSpec(
                (side, side, BLK, BLK),
                lambda j: (out_row, 0, 0, 0),
                pipeline_mode=pl.Buffered(1),
            ),
            pl.BlockSpec((side, width, BLK, BLK), lambda j: (up_row, j, 0, 0)),
            pl.BlockSpec((width, side, BLK, BLK), lambda j: (down_row + j, 0, 0, 0)),
        ],
        out_specs=[
            half_act,
            half_act,
            pl.BlockSpec(memory_space=pltpu.HBM),
            act,
            act,
            pl.BlockSpec((1, D), whole),
        ],
        out_shape=[
            jax.ShapeDtypeStruct((span // 2, D), BF),
            jax.ShapeDtypeStruct((span // 2, D), BF),
            jax.ShapeDtypeStruct((side * side + 2 * side * (FF // BLK), BLK, BLK), BF),
            jax.ShapeDtypeStruct((span, D), F32),
            jax.ShapeDtypeStruct((span, D), BF),
            jax.ShapeDtypeStruct((1, D), F32),
        ],
        scratch_shapes=[
            pltpu.VMEM((span, D), F32),
            pltpu.VMEM((span, 1), F32),
            pltpu.VMEM((span, D), BF),
            pltpu.VMEM((D, span), BF),
            pltpu.VMEM((span, D), BF),
            pltpu.VMEM((span, D), F32),
            pltpu.VMEM((span, D), F32),
            pltpu.VMEM((2, side, width, BLK, BLK), BF),
            pltpu.VMEM((2, side * width, BLK, BLK), BF),
            pltpu.VMEM((side * side, BLK, BLK), BF),
            pltpu.SemaphoreType.DMA((2, 2)),
            pltpu.SemaphoreType.DMA,
        ],
        compiler_params=params(),
        cost_estimate=cost(14 * span * D * FF, 50 * MIB),
        name="feed_forward",
    )(live, tokens, attended, cotangent, gains, per_row, per_up, per_row)


def query_body(normed_t, dq_ref, w_ref, grad_ref, acc_ref):
    step = pl.program_id(0)

    @pl.when(step == 0)
    def _():
        acc_ref[...] = jnp.zeros_like(acc_ref)

    grad = dq_ref[...]
    acc_ref[...] += mul_nt(grad, join_tile(w_ref))
    split_tile(grad_ref, mul_nn(normed_t[...], grad))


def query_back(normed1_t, d_query, weights):
    span = normed1_t.shape[1]
    side, width = D // BLK, COLS // BLK
    whole = lambda j: (0, 0)
    act = pl.BlockSpec((span, D), whole)
    tile = pl.BlockSpec((side, width, BLK, BLK), lambda j: (0, j, 0, 0))
    return pl.pallas_call(
        query_body,
        grid=(D // COLS,),
        in_specs=[
            pl.BlockSpec((D, span), whole),
            pl.BlockSpec((span, COLS), lambda j: (0, j)),
            tile,
        ],
        out_specs=[tile, act],
        out_shape=[
            jax.ShapeDtypeStruct((side, side, BLK, BLK), BF),
            jax.ShapeDtypeStruct((span, D), F32),
        ],
        compiler_params=params(),
        cost_estimate=cost(4 * span * D * D, 8 * MIB),
        name="query_backward",
    )(normed1_t, d_query, weights.reshape(-1, 3 * side, BLK, BLK))


def input_body(
    tokens_ref, gains_ref, normed_t, own_ref, recv_ref, acc_ref, gm_ref, w_ref, grad_ref, out_ref,
    gain_ref, acc
):
    step = pl.program_id(0)

    @pl.when(step == 0)
    def _():
        acc[...] = acc_ref[...]

    grad = (own_ref[0].astype(F32) + recv_ref[0].astype(F32)).astype(BF)
    acc[...] += mul_nt(grad, join_tile(w_ref))
    split_tile(grad_ref, mul_nn(normed_t[...], grad))

    @pl.when(step == pl.num_programs(0) - 1)
    def _():
        unit_vals, inv_std = normalize(tokens_ref[...].astype(F32))
        back = acc[...]
        gain_ref[...] = jnp.sum(back * unit_vals, 0, keepdims=True)
        out_ref[...] = (
            gm_ref[...] + norm_back(back * gains_ref[0:1], unit_vals, inv_std)
        ).astype(BF)


def input_back(tokens, gains, normed1_t, own, received, partial, grad_middle, weights):
    span = tokens.shape[0]
    side, width = D // BLK, COLS // BLK
    per = D // COLS
    whole = lambda j: (0, 0)
    act = pl.BlockSpec((span, D), whole)
    part = pl.BlockSpec((1, span, COLS), lambda j: (j // per, 0, j % per))
    return pl.pallas_call(
        input_body,
        grid=(2 * per,),
        in_specs=[
            act,
            pl.BlockSpec((2, D), whole),
            pl.BlockSpec((D, span), whole),
            part,
            part,
            act,
            act,
            pl.BlockSpec((side, width, BLK, BLK), lambda j: (0, j + per, 0, 0)),
        ],
        out_specs=[
            pl.BlockSpec((side, width, BLK, BLK), lambda j: (0, j, 0, 0)),
            act,
            pl.BlockSpec((1, D), whole),
        ],
        out_shape=[
            jax.ShapeDtypeStruct((side, 2 * side, BLK, BLK), BF),
            jax.ShapeDtypeStruct((span, D), BF),
            jax.ShapeDtypeStruct((1, D), F32),
        ],
        scratch_shapes=[pltpu.VMEM((span, D), F32)],
        compiler_params=params(),
        cost_estimate=cost(8 * span * D * D, 20 * MIB),
        name="input_backward",
    )(
        tokens, gains, normed1_t, own, received, partial, grad_middle,
        weights.reshape(-1, 3 * side, BLK, BLK),
    )


def source_numbers():
    side = D // BLK
    numbers = np.arange(3 * side * side + side * side + 2 * side * (FF // BLK), dtype=np.int32)
    row, col = np.divmod(numbers[: 3 * side * side], 3 * side)
    numbers[: 3 * side * side] = np.where(
        col < side, row * side + col, side * side + row * 2 * side + col - side
    )
    return numbers


def gather_body(first, bounds, table, *refs):
    sources = refs[:6]
    out_ref, stage, sems = refs[6:]
    step, steps = pl.program_id(0), pl.num_programs(0)
    count = stage.shape[1] // 2

    def fetch(which, slot):
        start = first + which * count
        for i in range(count):
            number = table[start + i]
            for low, high, own, other in zip(bounds, bounds[1:], sources[:3], sources[3:]):

                @pl.when((number >= low) & (number < high))
                def _():
                    for src, at in ((own, i), (other, count + i)):
                        pltpu.make_async_copy(
                            src.at[number - low], stage.at[slot, at], sems.at[slot]
                        ).start()

    @pl.when(step == 0)
    def _():
        fetch(0, 0)

    @pl.when(step + 1 < steps)
    def _():
        fetch(step + 1, (step + 1) % 2)

    slot = step % 2
    pltpu.make_async_copy(stage.at[slot], stage.at[slot], sems.at[slot]).wait()
    total = stage[slot, :count].astype(F32) + stage[slot, count:].astype(F32)
    out_ref[...] = total.astype(BF)


def gather_sums(table, first, count, own, other):
    hbm = pl.BlockSpec(memory_space=pltpu.HBM)
    steps = 4
    part = count // steps
    bounds = np.cumsum([0] + [src.shape[0] for src in own]).tolist()
    return pl.pallas_call(
        functools.partial(gather_body, first, bounds),
        grid=(steps,),
        in_specs=[pl.BlockSpec(memory_space=pltpu.SMEM)] + [hbm] * 6,
        out_specs=pl.BlockSpec((part, BLK, BLK), lambda i: (i, 0, 0)),
        out_shape=jax.ShapeDtypeStruct((count, BLK, BLK), BF),
        scratch_shapes=[
            pltpu.VMEM((2, 2 * part, BLK, BLK), BF),
            pltpu.SemaphoreType.DMA((2,)),
        ],
        compiler_params=params(46),
        cost_estimate=cost(0, 6 * count * BLK * BLK),
        name="gradient_sums",
    )(table, *own, *other)


def merge_body(first, second, passed, *refs):
    refs = list(refs)

    def total(count):
        return sum(refs.pop(0)[...].astype(F32) for _ in range(count))

    sums = [total(2), total(2)] if first else []
    if second:
        sums.append(total(3 if passed else 2))
    for ref, value in zip(refs, sums):
        ref[...] = value.astype(BF)


def merge_sums(low, came, kept, last, passed):
    steps = 3
    args, specs, shapes, outs = [], [], [], []

    def part(array, count, start):
        args.append(array)
        size = count // steps
        specs.append(pl.BlockSpec((size, BLK, BLK), lambda i: (i + start * steps, 0, 0)))

    def out(count):
        shapes.append(jax.ShapeDtypeStruct((count, BLK, BLK), BF))
        outs.append(pl.BlockSpec((count // steps, BLK, BLK), lambda i: (i, 0, 0)))

    if low is not None:
        count = low.shape[0] // 2
        for start in range(2):
            part(low, count, start)
            part(came, count, start)
            out(count)
    if kept is not None:
        for array in (kept, last) if passed is None else (kept, last, passed):
            part(array, kept.shape[0], 0)
        out(kept.shape[0])
    body = functools.partial(merge_body, low is not None, kept is not None, passed is not None)
    return pl.pallas_call(
        body,
        grid=(steps,),
        in_specs=specs,
        out_specs=outs,
        out_shape=shapes,
        compiler_params=params(46),
        cost_estimate=cost(0, 6 * MIB),
        name="merge_sums",
    )(*args)


def two_terms(values):
    high = values.astype(BF)
    return high, (values - high.astype(F32)).astype(BF)


def update_body(count, *refs):
    parts = refs[:count]
    m_ref, sl_ref, sr_ref, rl_ref, rr_ref, g_out, sl_out, sr_out, m_out = refs[count:]

    def long_left(terms, axis):
        return jnp.concatenate([terms[0], terms[0], terms[1]], axis)

    def long_right(terms, axis):
        return jnp.concatenate([terms[0], terms[1], terms[0]], axis)

    for i in range(g_out.shape[0]):
        total = sum(part[i].astype(F32) for part in parts)
        g_out[i] = total
        grad = two_terms(total)
        sl_out[i] = sl_ref[i] + mul_nt(long_left(grad, 1), long_right(grad, 1))
        tall = long_right(grad, 0)
        sr_out[i] = sr_ref[i] + mul_tn(long_left(grad, 0), tall)
        inner = mul_nn(long_left(two_terms(rl_ref[i]), 1), tall)
        direction = mul_nn(
            long_left(two_terms(inner), 1), long_right(two_terms(rr_ref[i]), 0)
        )
        master = m_ref[i]
        scale = jnp.sqrt(jnp.mean(master * master, keepdims=True) + 1e-06)
        scale = scale * lax.rsqrt(jnp.mean(direction * direction, keepdims=True) + 1e-06)
        m_out[i] = master - 0.3 * scale * direction


def update(parts, master, stat_left, stat_right, root_left, root_right):
    count = master.shape[0]
    group = 6 if count % 6 == 0 else 1
    block = pl.BlockSpec((group, BLK, BLK), lambda i: (i, 0, 0))
    shape = jax.ShapeDtypeStruct(master.shape, F32)
    return pl.pallas_call(
        functools.partial(update_body, len(parts)),
        grid=(count // group,),
        in_specs=[block] * (len(parts) + 5),
        out_specs=[block] * 4,
        out_shape=[shape] * 4,
        compiler_params=params(),
        cost_estimate=cost(48 * count * BLK**3, 15 * MIB),
        name="block_update",
    )(*parts, master, stat_left, stat_right, root_left, root_right)


def pair_moves():
    moves_same, moves_cross = [], []
    for z in range(4):
        for c in range(2):
            for moves, bit in ((moves_same, z % 2), (moves_cross, 1 - z % 2)):
                moves.append((z * 2 + c, (2 * c + bit) * 2 + z // 2))
    return moves_same, moves_cross


def row_part(values, which):
    return lax.dynamic_index_in_dim(values, which, 0, False)


def move_rows(values, crossed, back=False):
    moves = pair_moves()[crossed]
    return lax.ppermute(values, ("seq", "core"), [(b, a) for a, b in moves] if back else moves)


def in_order(kept, crossed, parity):
    return jnp.where(parity == 0, kept, crossed), jnp.where(parity == 0, crossed, kept)


def spread_rows(values, parity):
    kept = move_rows(row_part(values, parity), False)
    crossed = move_rows(row_part(values, 1 - parity), True)
    return jnp.concatenate(in_order(kept, crossed, parity), 0)


def swap_cores(values):
    return lax.ppermute(values, "core", [(0, 1), (1, 0)])


def chip_orders(chips):
    bits = [1 << i for i in range(chips.bit_length() - 1)]
    return bits, bits[::-1]


def offsets(order):
    result = [0]
    for bit in order:
        result = result + [o ^ bit for o in result]
    return result


def place_lists(chips, owned, planes):
    shape = (2, planes, chips, owned)
    by_core = np.array([offsets(order) for order in chip_orders(chips)], np.int32)
    grid = np.indices(shape).astype(np.int32).reshape(4, 2, -1)
    offset = np.broadcast_to(by_core[:, None, :, None], shape).reshape(2, -1)
    return grid[1, 0], offset, grid[3, 0]


def arrival_order(chips, owned, planes):
    per_plane, quarter = chips * owned, owned
    if chips != 4:
        return np.arange(planes * per_plane)
    pieces = [(0, 0)]
    for k in range(1, planes + 1):
        pieces += [(k, 0)] if k < planes else []
        pieces += [(k - 1, 1), (k - 1, 2)]
        pieces += [(k - 2, 3)] if k > 1 else []
    pieces.append((planes - 1, 3))
    starts = [k * per_plane + r * quarter for k, r in pieces]
    return np.concatenate([np.arange(start, start + quarter) for start in starts])


def swap_chips(values, bits):
    chips = lax.axis_size("chip")
    moves = [(i * 2 + c, (i ^ bits[c]) * 2 + c) for i in range(chips) for c in range(2)]
    return lax.ppermute(values, ("chip", "core"), moves)


def move_planes(values, shift):
    planes = lax.axis_size("seq")
    return lax.ppermute(values, "seq", [(i, (i + shift) % planes) for i in range(planes)])


def after(value, *deps):
    return lax.optimization_barrier((value, *deps))[0]


def together(*values):
    return lax.optimization_barrier(values)


def chip_steps():
    return list(zip(*chip_orders(lax.axis_size("chip"))))


def finish_pieces(pieces):
    for bits in chip_steps()[2:]:
        joined = jnp.concatenate(pieces, 0)
        pieces = [joined, swap_chips(joined, bits)]
    return pieces


def add_halves(kept, came):
    return (kept.astype(F32) + came.astype(F32)).astype(BF)


def pack_terms(values):
    high = lax.optimization_barrier(values.astype(BF))
    low = (values - high.astype(F32)).astype(BF)
    terms = jnp.stack([high, low]).reshape(-1, BLK)
    return jnp.pad(terms, ((0, BLK - terms.shape[0]), (0, 0)))[None]


def unpack_terms(blocks, shape):
    terms = blocks.reshape(-1, BLK, BLK)[:, : 2 * shape[0] * shape[1] // BLK]
    terms = terms.reshape(-1, 2, *shape).astype(F32)
    return terms[:, 0] + terms[:, 1]


def finish_sums(keep, send, riders):
    for bits in chip_steps()[::-1][1:-1]:
        count = keep.shape[0] // 2
        came = swap_chips(with_riders(send, riders), bits)
        riders = more_riders(riders, came, keep.shape[0])
        send = add_halves(keep[count:], came[count : 2 * count])
        keep = add_halves(keep[:count], came[:count])
    return keep, send, riders


def with_riders(send, riders):
    return send if riders is None else jnp.concatenate([send, riders], 0)


def more_riders(riders, came, count):
    return riders if riders is None else jnp.concatenate([riders, came[count:]], 0)


def by_chip(riders, me, core):
    chips = lax.axis_size("chip")
    ranks = np.array([np.argsort(offsets(order[::-1])) for order in chip_orders(chips)], np.int32)
    rank = jnp.asarray(ranks)[core][me ^ jnp.arange(chips, dtype=jnp.int32)]
    return riders.reshape(chips, -1, BLK, BLK)[rank]


def local(
    tokens,
    cotangent,
    lengths,
    owner_perm,
    master,
    norm_gains,
    stat_left,
    stat_right,
    root_left,
    root_right,
    moment_first,
    moment_second,
):
    core = lax.axis_index("core")
    place_z = lax.axis_index("seq")
    parity = place_z % 2
    block_count = owner_perm.shape[0]
    owned = master.shape[0]
    half = block_count // 2

    chips, planes = lax.axis_size("chip"), lax.axis_size("seq")
    me = lax.axis_index("chip")

    pair_lengths = jnp.stack([lengths, swap_cores(lengths)])
    pair_lengths = jnp.where(core == 0, pair_lengths, pair_lengths[::-1]).reshape(-1)
    length = lax.dynamic_index_in_dim(pair_lengths, place_z, 0, False)
    span = tokens.shape[0] * tokens.shape[1]
    live = jnp.stack([length - core * span, length - (1 - core) * span, length - core * span, parity])

    distance, offset, slot = place_lists(chips, owned, planes)
    offset = jnp.where(core == 0, offset, offset[::-1])
    device = ((place_z - distance) % planes * chips + (me ^ offset)) * 2
    device = device + jnp.stack([core, 1 - core])[:, None]
    table = owner_perm[(device * owned + slot).reshape(-1)]
    sums_table = jnp.asarray(source_numbers())[table[:half]]
    arrive = arrival_order(chips, owned, planes)
    near_slots, far_slots = device * owned + slot
    table = owner_perm[jnp.concatenate([near_slots[arrive], far_slots[arrive]])]

    shard = master.astype(BF)
    first_bits, second_bits = chip_steps()[:2]
    per_plane = chips * owned
    by_phase = chips == 4
    rows = (row_part(tokens, parity), row_part(tokens, 1 - parity))
    cross, held, weights, first = None, (), None, 0
    came, turned = swap_chips(shard, first_bits), swap_chips(shard, second_bits)
    next_shard = move_planes(shard, 1)
    pieces = [[shard, came, turned]]

    def place(parts, first, weights):
        others = [swap_cores(part) for part in parts]
        weights = place_blocks(table, first, parts, others, weights)
        return weights, first + sum(part.shape[0] for part in parts)

    for k in range(1, planes):
        ready = () if k == 1 else (cross, *held, live, table, sums_table)
        ready = ready if weights is None else (*ready, weights)
        this_shard, came, turned, row_a, row_b, *done = together(
            next_shard, came, turned, *rows, *ready
        )
        if k > 1:
            pieces[k - 2].append(done[0])
        cross = swap_chips(came, second_bits)
        arrived = [this_shard, came, turned, *(pieces[0][:1] if k == 1 else done[:1])]
        arrived = arrived[3:] + arrived[:3] if k == 1 else arrived
        pieces[k - 1][1:] = [came, turned]
        came, turned = swap_chips(this_shard, first_bits), swap_chips(this_shard, second_bits)
        pieces.append([this_shard, came, turned])
        if k < planes - 1:
            next_shard = move_planes(this_shard, 1)
        else:
            row_same = move_rows(row_a, False)
            row_cross = move_rows(after(row_b, row_same), True)
        if by_phase:
            if k > 1:
                weights, first = place(done[1:2], first, weights)
            held = (jnp.concatenate(arrived, 0),)
    came, turned, done, row_same, row_cross, *held = together(
        came, turned, cross, row_same, row_cross, *held, *([] if weights is None else [weights])
    )
    own_tokens = jnp.concatenate(in_order(row_same, row_cross, parity), 0)
    pieces[-2].append(done)
    pieces[-1][1:] = [came, turned, swap_chips(came, second_bits)]
    normed1, normed1_t = norm_tokens(own_tokens, norm_gains)
    if by_phase:
        weights, first = place(held[:1], first, weights)
        weights, first = place([came, turned, done], first, weights)
        last, normed1, *_ = together(pieces[-1][-1], normed1, weights)
        other_normed = swap_cores(normed1)
        weights, _ = place([last], first, weights)
    else:
        for each in pieces:
            each = [jnp.concatenate(finish_pieces(each), 0)]
            weights, first = place(each, first, weights)
        other_normed = swap_cores(normed1)
    own_cot = spread_rows(after(cotangent, weights), parity)

    own_qkv, other_kv = project(normed1, other_normed, weights)
    attended, q_aug = attend(live, own_qkv, other_kv)
    kept, crossed, g_rest, grad_middle, grad_attended, gain_second = feed(
        live, own_tokens, attended, own_cot, norm_gains, weights
    )
    other_rest = swap_cores(g_rest)
    kept, crossed = move_rows(kept, False, True), move_rows(crossed, True, True)
    layer_out = jnp.stack(in_order(kept, crossed, parity), 0)
    d_query, d_own, d_other = attend_back(live, q_aug, own_qkv, other_kv, attended, grad_attended)
    received = swap_cores(after(d_other, kept, crossed))
    flat = lambda g: g.reshape(-1, BLK, BLK)
    g_query, partial = query_back(normed1_t, d_query, weights)
    g_query = flat(g_query)
    other_query = swap_cores(g_query)
    g_kv, grad_in, gain_first = input_back(
        own_tokens, norm_gains, normed1_t, d_own, received, partial, grad_middle, weights
    )
    g_kv = flat(g_kv)
    gain_part = jnp.concatenate([gain_first, gain_second], 0)
    mine = pack_terms(gain_part)
    other_kv_grad = swap_cores(after(g_kv, other_query))
    theirs = swap_cores(mine)
    pair = jnp.concatenate([mine, theirs], 0)
    riders = jnp.where(core == 0, pair, pair[::-1])
    own_grads = (g_query, g_kv, g_rest)
    other_grads = (other_query, other_kv_grad, other_rest)
    half_plane = per_plane // 2
    last_bits, before_bits = chip_steps()[-1], chip_steps()[0]
    halves = grad_in.reshape(2, span // 2, D)
    rows = [row_part(halves, parity), row_part(halves, 1 - parity)]
    moved_rows, lows, sent, passed, riders_z = [], [], None, None, []

    def sums(k, part, held):
        first = k * per_plane + part * half_plane
        return gather_sums(held, first, half_plane, own_grads, other_grads)

    order = list(range(planes))[::-1]
    high = sums(order[0], 1, sums_table)
    held = sums_table
    held_riders = []
    for turn in range(planes + 1):
        group, moves = [], []
        if turn < planes:
            group.append(high)
            moves.append(lambda v: swap_chips(v, last_bits))
        if 1 <= turn <= planes:
            group.append(sent)
            moves.append(lambda v: swap_chips(v, before_bits))
        if 2 <= turn <= planes:
            group.append(part)
            moves.append(lambda v: move_planes(v, -1))
        if turn < 2:
            group.append(riders)
            bits = last_bits if turn == 0 else before_bits
            moves.append(lambda v: swap_chips(v, bits))
        if turn in (1, 2):
            group.append(rows[turn - 1])
            crossed = turn == 2
            moves.append(lambda v: move_rows(v, crossed, True))
        far_riders = [1, 2] if turn == planes - 1 else []
        group += [rider for _ in far_riders]
        moves += [functools.partial(move_planes, shift=-k) for k in far_riders]
        came = [move(value) for move, value in zip(moves, together(*group, *moved_rows, *held_riders))]
        if turn in (1, 2):
            moved_rows.append(came.pop())
        if turn < 2:
            riders = jnp.concatenate([riders, came.pop()], 0)
        count = len(came) - len(far_riders)
        riders_z, came = riders_z + came[count:], came[:count]
        if far_riders:
            riders_z += [move_planes(after(rider, *riders_z), -k) for k in range(3, planes)]
        if turn == planes:
            parts = [keep_before, *came]
            continue
        passed = came.pop() if turn >= 2 else None
        low = sums(order[turn], 0, after(held, high))
        if turn + 1 < planes:
            high = sums(order[turn + 1], 1, after(held, low))
        held = after(sums_table, *came)
        held_riders = [riders] if turn == 1 else []
        if turn == 1:
            plane_gain = by_chip(riders, me, core)
            plane_gain = jnp.sum(unpack_terms(plane_gain, gain_part.shape), 0)
            rider = pack_terms(plane_gain)
        second = (None, None, None) if turn == 0 else (keep_before, came[-1], passed)
        keep, sent, *part = merge_sums(low, came[0], *second)
        part = part[0] if part else None
        keep_before, sent, grown = finish_sums(keep, sent, riders if turn == 0 else None)
        riders = grown if turn == 0 else riders
    input_grad = jnp.stack(in_order(*moved_rows, parity), 0).astype(F32)
    planes_gain = [unpack_terms(each, gain_part.shape)[0] for each in (rider, *riders_z)]
    turned = (jnp.arange(planes, dtype=jnp.int32) - place_z) % planes
    gain_grad = jnp.sum(jnp.stack(planes_gain)[turned], 0)
    grad_blocks, stat_left_new, stat_right_new, master_new = update(
        parts, master, stat_left, stat_right, root_left, root_right
    )
    first_new = 0.9 * moment_first + 0.1 * gain_grad
    second_new = 0.999 * moment_second + 0.001 * gain_grad * gain_grad
    first_hat = first_new / (1.0 - 0.9**STEP)
    second_hat = second_new / (1.0 - 0.999**STEP)
    gains_new = norm_gains - 0.5 * first_hat / (jnp.sqrt(second_hat) + 1e-08)
    return (
        layer_out,
        input_grad,
        grad_blocks,
        stat_left_new,
        stat_right_new,
        master_new,
        first_new,
        second_new,
        gains_new,
    )


def solution(mesh):
    seq_size, rows_size = mesh.shape["seq"], mesh.shape["rows"]
    mesh = Mesh(mesh.devices.reshape(seq_size, rows_size // 2, 2), ("seq", "chip", "core"))
    activation = P(("chip", "core"), "seq", None)
    blocks = P(("seq", "chip", "core"), None, None)
    return jax.shard_map(
        local,
        mesh=mesh,
        in_specs=(
            activation, activation, P(("chip", "core")), P(), blocks, P(),
            blocks, blocks, blocks, blocks, P(), P(),
        ),
        out_specs=(activation, activation, blocks, blocks, blocks, blocks, P(), P(), P()),
        check_vma=False,
    )
```

```python
import functools
import jax
import jax.numpy as jnp
import numpy as np
from jax import lax
from jax.experimental import pallas as pl
from jax.experimental.pallas import tpu as pltpu
from jax.sharding import Mesh
from jax.sharding import PartitionSpec as P

D = 1024
HD = 64
FF = 4096
BLK = 128
STEP = 10
COLS = 1024
BF = jnp.bfloat16
F32 = jnp.float32
MIB = 1024 * 1024

norm_eps = 1e-05
score_scale = 0.125
masked_score = -1e30


def params(limit=56):
    return pltpu.CompilerParams(vmem_limit_bytes=limit * MIB)


def cost(flops, nbytes):
    return pl.CostEstimate(flops=int(flops), bytes_accessed=int(nbytes), transcendentals=0)


def mul_nn(left, right):
    return jnp.dot(left, right, preferred_element_type=F32)


def mul_nt(left, right):
    return lax.dot_general(left, right, (((1,), (1,)), ((), ())), preferred_element_type=F32)


def mul_tn(left, right):
    return lax.dot_general(left, right, (((0,), (0,)), ((), ())), preferred_element_type=F32)


def join_tile(ref):
    rows, cols = ref.shape[0], ref.shape[1]
    return jnp.concatenate([ref[:, j].reshape(rows * BLK, BLK) for j in range(cols)], axis=1)


def split_tile(ref, matrix):
    rows, cols = ref.shape[0], ref.shape[1]
    for j in range(cols):
        ref[:, j] = matrix[:, j * BLK : (j + 1) * BLK].reshape(rows, BLK, BLK).astype(ref.dtype)


def split_flat(ref, matrix):
    cols = matrix.shape[1] // BLK
    for i in range(matrix.shape[0] // BLK):
        for j in range(cols):
            block = matrix[i * BLK : (i + 1) * BLK, j * BLK : (j + 1) * BLK]
            ref[i * cols + j] = block.astype(ref.dtype)


def normalize(values):
    row_mean = jnp.mean(values, -1, keepdims=True)
    centered = values - row_mean
    row_var = jnp.mean(centered * centered, -1, keepdims=True)
    inv_std = lax.rsqrt(row_var + norm_eps)
    return centered * inv_std, inv_std


def gelu_parts(hidden):
    bell = jnp.exp(hidden * hidden * -0.5)
    t = 1.0 / (1.0 + jnp.abs(hidden) * (0.3275911 * 0.7071067811865476))
    poly = 1.061405429 * t - 1.453152027
    for term in (1.421413741, -0.284496736, 0.254829592):
        poly = poly * t + term
    tail = poly * t * 0.5 * bell
    return jnp.where(hidden < 0.0, tail, 1.0 - tail), hidden * bell * 0.3989422804014327


def norm_back(gradient, unit_vals, inv_std):
    grad_mean = jnp.mean(gradient, -1, keepdims=True)
    cross_mean = jnp.mean(gradient * unit_vals, -1, keepdims=True)
    return inv_std * (gradient - grad_mean - unit_vals * cross_mean)


def place_body(first, pieces, table, *refs):
    near, far = refs[:pieces], refs[pieces : 2 * pieces]
    out_ref, sem = refs[-2:]
    total = 0
    for start, sources in ((first, near), (table.shape[0] // 2 + first, far)):
        for src in sources:
            for slot in range(src.shape[0]):
                pltpu.make_async_copy(src.at[slot], out_ref.at[table[start + slot]], sem).start()
            start += src.shape[0]
            total += src.shape[0]
    done = out_ref.at[pl.ds(0, total)]
    pltpu.make_async_copy(done, done, sem).wait()


def place_blocks(table, first, near, far, kept):
    smem = pl.BlockSpec(memory_space=pltpu.SMEM)
    hbm = pl.BlockSpec(memory_space=pltpu.HBM)
    vmem = pl.BlockSpec(memory_space=pltpu.VMEM)
    kept = () if kept is None else (kept,)
    count = 2 * len(near)
    return pl.pallas_call(
        functools.partial(place_body, first, len(near)),
        out_shape=jax.ShapeDtypeStruct((table.shape[0], BLK, BLK), BF),
        in_specs=[smem] + [vmem] * count + [hbm] * len(kept),
        out_specs=hbm,
        scratch_shapes=[pltpu.SemaphoreType.DMA],
        input_output_aliases={1 + count: 0} if kept else {},
        compiler_params=params(46),
        cost_estimate=cost(0, 6 * MIB),
        name="place_weights",
    )(table, *near, *far, *kept)


def norm_body(tokens_ref, gains_ref, out_ref, turned_ref):
    normed = normalize(tokens_ref[...].astype(F32))[0] * gains_ref[0:1]
    out_ref[...] = normed.astype(BF)
    turned_ref[...] = normed.T.astype(BF)


def norm_tokens(tokens, gains):
    span = tokens.shape[0]
    steps = 4
    part = pl.BlockSpec((span // steps, D), lambda i: (i, 0))
    return pl.pallas_call(
        norm_body,
        grid=(steps,),
        in_specs=[part, pl.BlockSpec((2, D), lambda i: (0, 0))],
        out_specs=[part, pl.BlockSpec((D, span // steps), lambda i: (0, i))],
        out_shape=[jax.ShapeDtypeStruct((span, D), BF), jax.ShapeDtypeStruct((D, span), BF)],
        compiler_params=params(46),
        cost_estimate=cost(0, 3 * MIB),
        name="norm_tokens",
    )(tokens, gains)


def qkv_body(own_ref, other_ref, w_ref, own_out, other_out):
    step = pl.program_id(0)
    weight = join_tile(w_ref)
    own_out[...] = mul_nn(own_ref[...], weight).astype(BF)

    @pl.when(step >= D // COLS)
    def _():
        other_out[...] = mul_nn(other_ref[...], weight).astype(BF)


def project(own, other, weights):
    span = own.shape[0]
    skip = D // COLS
    once = pl.BlockSpec((span, D), lambda j: (0, 0))
    return pl.pallas_call(
        qkv_body,
        grid=(3 * D // COLS,),
        in_specs=[
            once,
            once,
            pl.BlockSpec((D // BLK, COLS // BLK, BLK, BLK), lambda j: (0, j, 0, 0)),
        ],
        out_specs=[
            pl.BlockSpec((span, COLS), lambda j: (0, j)),
            pl.BlockSpec((span, COLS), lambda j: (0, jnp.maximum(j - skip, 0))),
        ],
        out_shape=[
            jax.ShapeDtypeStruct((span, 3 * D), BF),
            jax.ShapeDtypeStruct((span, 2 * D), BF),
        ],
        compiler_params=params(),
        cost_estimate=cost(10 * span * D * D, 12 * MIB),
        name="qkv_projection",
    )(own, other, weights.reshape(-1, 3 * D // BLK, BLK, BLK))


def lane_masks(head):
    lane = lax.broadcasted_iota(jnp.int32, (1, BLK), 1)
    first = HD * (1 - head)
    keep = (lane // HD == head).astype(F32)
    dead_lane = (lane == first).astype(F32)
    terms = [(lane == first + 1 + i).astype(F32) for i in range(3)]
    return keep, dead_lane, terms


def three_terms(values):
    high = values.astype(BF).astype(F32)
    rest = values - high
    middle = rest.astype(BF).astype(F32)
    return high, middle, rest - middle


def key_bias(span, live_count):
    row = lax.broadcasted_iota(jnp.int32, (span, 1), 0)
    return jnp.where(row < live_count, 0.0, masked_score).astype(F32)


def attend_body(live_ref, q_ref, ko_ref, vo_ref, kx_ref, vx_ref, out_ref, aug_ref):
    span = q_ref.shape[0]
    bias_own = key_bias(span, live_ref[0])
    bias_other = key_bias(span, live_ref[1])
    queries = q_ref[...].astype(F32) * score_scale
    k_own, k_other = ko_ref[...].astype(F32), kx_ref[...].astype(F32)
    v_own_f, v_other_f = vo_ref[...].astype(F32), vx_ref[...].astype(F32)
    results, scores = [], []
    for head in range(2):
        keep, dead_lane, _ = lane_masks(head)
        q_head = (queries * keep + dead_lane).astype(BF)
        s_own = mul_nt(q_head, (k_own * keep + bias_own * dead_lane).astype(BF))
        s_other = mul_nt(q_head, (k_other * keep + bias_other * dead_lane).astype(BF))
        scores.append((q_head, s_own, s_other))
    for head in range(2):
        keep, _, terms = lane_masks(head)
        q_head, s_own, s_other = scores[head]
        top = jnp.max(jnp.maximum(s_own, s_other), -1, keepdims=True)
        p_own = jnp.exp(s_own - top)
        p_other = jnp.exp(s_other - top)
        v_own = (v_own_f * keep + (1.0 - keep)).astype(BF)
        v_other = (v_other_f * keep + (1.0 - keep)).astype(BF)
        mixed = mul_nn(p_own.astype(BF), v_own) + mul_nn(p_other.astype(BF), v_other)
        total = mixed[:, HD * (1 - head) : HD * (1 - head) + 1]
        results.append(mixed / total * keep)
        parts = three_terms(-(top + jnp.log(total)))
        stats = sum(part * lane for part, lane in zip(parts, terms))
        aug_ref[:, head * BLK : (head + 1) * BLK] = (q_head.astype(F32) + stats).astype(BF)
    out_ref[...] = (results[0] + results[1]).astype(BF)


def attend(live, own, other):
    span = own.shape[0]
    pairs = D // BLK
    col = lambda shift: pl.BlockSpec((span, BLK), lambda p: (0, p + shift))
    return pl.pallas_call(
        attend_body,
        grid=(pairs,),
        in_specs=[
            pl.BlockSpec(memory_space=pltpu.SMEM),
            col(0),
            col(pairs),
            col(2 * pairs),
            col(0),
            col(pairs),
        ],
        out_specs=[col(0), pl.BlockSpec((span, 2 * BLK), lambda p: (0, p))],
        out_shape=[
            jax.ShapeDtypeStruct((span, D), BF),
            jax.ShapeDtypeStruct((span, 2 * D), BF),
        ],
        compiler_params=params(),
        cost_estimate=cost(40 * span * span * D, 8 * MIB),
        name="attention",
    )(live, own, own, own, other, other)


def attend_back_body(
    live_ref, aug_ref, ko_ref, vo_ref, kx_ref, vx_ref, at_ref, g_ref, dq_ref, own_ref, other_ref
):
    span = at_ref.shape[0]
    grads = g_ref[...].astype(F32)
    product = grads * at_ref[...].astype(F32)
    keeps, g_augs, q_augs = [], [], []
    for head in range(2):
        keep, dead_lane, terms = lane_masks(head)
        delta = jnp.sum(product * keep, -1, keepdims=True)
        parts = three_terms(-delta)
        stats = sum(part * lane for part, lane in zip(parts, terms))
        g_augs.append((grads * keep + stats).astype(BF))
        q_augs.append(aug_ref[:, head * BLK : (head + 1) * BLK])
    d_query = [None, None]
    for k_ref, v_ref, out_ref, live in (
        (ko_ref, vo_ref, own_ref, live_ref[0]),
        (kx_ref, vx_ref, other_ref, live_ref[1]),
    ):
        bias = key_bias(span, live)
        keys = k_ref[...]
        keys_f, values_f = keys.astype(F32), v_ref[...].astype(F32)
        d_keys = d_values = None
        for head in range(2):
            keep, dead_lane, terms = lane_masks(head)
            ones = terms[0] + terms[1] + terms[2]
            k_aug = (keys_f * keep + (bias * dead_lane + ones)).astype(BF)
            v_aug = (values_f * keep + ones).astype(BF)
            probs = jnp.exp(mul_nt(k_aug, q_augs[head]))
            d_scores = (probs * mul_nt(v_aug, g_augs[head])).astype(BF)
            value_part = mul_nn(probs.astype(BF), g_augs[head]) * keep
            key_part = mul_nn(d_scores, q_augs[head]) * keep
            query_part = mul_tn(keys, d_scores)[head * HD : (head + 1) * HD]
            d_query[head] = query_part if d_query[head] is None else d_query[head] + query_part
            d_values = value_part if d_values is None else d_values + value_part
            d_keys = key_part if d_keys is None else d_keys + key_part
        out_ref[0] = d_keys.astype(out_ref.dtype)
        out_ref[1] = d_values.astype(out_ref.dtype)
    dq_ref[...] = (jnp.concatenate(d_query, 0).T * score_scale).astype(BF)


def attend_back(live, aug, own, other, attended, grads):
    span = own.shape[0]
    pairs = D // BLK
    col = lambda shift: pl.BlockSpec((span, BLK), lambda p: (0, p + shift))
    pair_out = pl.BlockSpec((2, span, BLK), lambda p: (0, 0, p))
    return pl.pallas_call(
        attend_back_body,
        grid=(pairs,),
        in_specs=[
            pl.BlockSpec(memory_space=pltpu.SMEM),
            pl.BlockSpec((span, 2 * BLK), lambda p: (0, p)),
            col(pairs),
            col(2 * pairs),
            col(0),
            col(pairs),
            col(0),
            col(0),
        ],
        out_specs=[col(0), pair_out, pair_out],
        out_shape=[
            jax.ShapeDtypeStruct((span, D), BF),
            jax.ShapeDtypeStruct((2, span, D), BF),
            jax.ShapeDtypeStruct((2, span, D), BF),
        ],
        compiler_params=params(),
        cost_estimate=cost(60 * span * span * D, 12 * MIB),
        name="attention_backward",
    )(live, aug, own, own, other, other, attended, grads)


def feed_body(
    live_ref,
    tokens_ref,
    attended_ref,
    cot_ref,
    gains_ref,
    wo_ref,
    wu_ref,
    wd_ref,
    kept_ref,
    crossed_ref,
    rest_ref,
    gm_ref,
    ga_ref,
    gain_ref,
    unit,
    inv,
    normed,
    normed_t,
    top,
    acc_out,
    acc_back,
    up_stage,
    down_stage,
    out_stage,
    sems,
    out_sem,
):
    step = pl.program_id(0)
    place = step % 2
    side, width = up_stage.shape[1], up_stage.shape[2]
    per_tile = side * width
    up_first = side * side
    down_first = up_first + side * FF // BLK

    def drain(which):
        pltpu.make_async_copy(up_stage.at[which], up_stage.at[which], sems.at[0, which]).wait()
        pltpu.make_async_copy(down_stage.at[which], down_stage.at[which], sems.at[1, which]).wait()
    span = tokens_ref.shape[0]

    @pl.when(step == 0)
    def _():
        weight = join_tile(wo_ref)
        middle = tokens_ref[...].astype(F32) + mul_nn(attended_ref[...], weight)
        unit_vals, inv_std = normalize(middle)
        unit[...] = unit_vals
        inv[...] = inv_std
        normed_vals = unit_vals * gains_ref[1:2]
        normed[...] = normed_vals.astype(BF)
        normed_t[...] = normed_vals.T.astype(BF)
        row = lax.broadcasted_iota(jnp.int32, (span, 1), 0)
        top[...] = jnp.where(row < live_ref[2], cot_ref[...].astype(F32), 0.0).astype(BF)
        acc_out[...] = middle
        acc_back[...] = jnp.zeros_like(acc_back)

    w_up = join_tile(wu_ref)
    w_down = join_tile(wd_ref)
    hidden = mul_nn(normed[...], w_up)
    grad_act = mul_nt(top[...], w_down)
    share, slope_rest = gelu_parts(hidden)
    activated = (hidden * share).astype(BF)
    grad_hidden = (grad_act * (share + slope_rest)).astype(BF)
    acc_out[...] += mul_nn(activated, w_down)
    acc_back[...] += mul_nt(grad_hidden, w_up)

    @pl.when(step >= 2)
    def _():
        drain(place)

    split_flat(down_stage.at[place], mul_tn(activated, top[...]))
    dest = rest_ref.at[pl.ds(down_first + step * per_tile, per_tile)]
    pltpu.make_async_copy(down_stage.at[place], dest, sems.at[1, place]).start()
    split_tile(up_stage.at[place], mul_nn(normed_t[...], grad_hidden))
    for i in range(side):
        dest = rest_ref.at[pl.ds(up_first + i * (FF // BLK) + step * width, width)]
        pltpu.make_async_copy(up_stage.at[place, i], dest, sems.at[0, place]).start()

    @pl.when(step == pl.num_programs(0) - 1)
    def _():
        for flip in range(2):

            @pl.when(live_ref[3] == flip)
            def _():
                for ref, part in ((kept_ref, flip), (crossed_ref, 1 - flip)):
                    ref[...] = acc_out[part * (span // 2) : (part + 1) * (span // 2)].astype(BF)

        unit_vals = unit[...]
        back = acc_back[...]
        gain_ref[...] = jnp.sum(back * unit_vals, 0, keepdims=True)
        grad_middle = top[...].astype(F32) + norm_back(back * gains_ref[1:2], unit_vals, inv[...])
        gm_ref[...] = grad_middle
        back_middle = grad_middle.astype(BF)
        split_flat(out_stage, mul_tn(attended_ref[...], back_middle))
        out_copy = pltpu.make_async_copy(out_stage, rest_ref.at[pl.ds(0, up_first)], out_sem)
        out_copy.start()
        ga_ref[...] = mul_nt(back_middle, join_tile(wo_ref)).astype(BF)
        drain(1 - place)
        drain(place)
        out_copy.wait()


def feed(live, tokens, attended, cotangent, gains, weights):
    span = tokens.shape[0]
    side, width = D // BLK, COLS // BLK
    whole = lambda j: (0, 0)
    act = pl.BlockSpec((span, D), whole)
    once = pl.BlockSpec((span, D), whole, pipeline_mode=pl.Buffered(1))
    half_act = pl.BlockSpec((span // 2, D), whole)
    per_row = weights.reshape(-1, side, BLK, BLK)
    per_up = weights.reshape(-1, FF // BLK, BLK, BLK)
    out_row = (3 * side * side) // side // side
    up_row = 4 * side * side // (FF // BLK) // side
    down_row = (4 * side * side + side * FF // BLK) // side // width
    return pl.pallas_call(
        feed_body,
        grid=(FF // COLS,),
        in_specs=[
            pl.BlockSpec(memory_space=pltpu.SMEM),
            once,
            once,
            once,
            pl.BlockSpec((2, D), whole),
            pl.BlockSpec(
                (side, side, BLK, BLK),
                lambda j: (out_row, 0, 0, 0),
                pipeline_mode=pl.Buffered(1),
            ),
            pl.BlockSpec((side, width, BLK, BLK), lambda j: (up_row, j, 0, 0)),
            pl.BlockSpec((width, side, BLK, BLK), lambda j: (down_row + j, 0, 0, 0)),
        ],
        out_specs=[
            half_act,
            half_act,
            pl.BlockSpec(memory_space=pltpu.HBM),
            act,
            act,
            pl.BlockSpec((1, D), whole),
        ],
        out_shape=[
            jax.ShapeDtypeStruct((span // 2, D), BF),
            jax.ShapeDtypeStruct((span // 2, D), BF),
            jax.ShapeDtypeStruct((side * side + 2 * side * (FF // BLK), BLK, BLK), BF),
            jax.ShapeDtypeStruct((span, D), F32),
            jax.ShapeDtypeStruct((span, D), BF),
            jax.ShapeDtypeStruct((1, D), F32),
        ],
        scratch_shapes=[
            pltpu.VMEM((span, D), F32),
            pltpu.VMEM((span, 1), F32),
            pltpu.VMEM((span, D), BF),
            pltpu.VMEM((D, span), BF),
            pltpu.VMEM((span, D), BF),
            pltpu.VMEM((span, D), F32),
            pltpu.VMEM((span, D), F32),
            pltpu.VMEM((2, side, width, BLK, BLK), BF),
            pltpu.VMEM((2, side * width, BLK, BLK), BF),
            pltpu.VMEM((side * side, BLK, BLK), BF),
            pltpu.SemaphoreType.DMA((2, 2)),
            pltpu.SemaphoreType.DMA,
        ],
        compiler_params=params(),
        cost_estimate=cost(14 * span * D * FF, 50 * MIB),
        name="feed_forward",
    )(live, tokens, attended, cotangent, gains, per_row, per_up, per_row)


def query_body(normed_t, dq_ref, w_ref, grad_ref, acc_ref):
    step = pl.program_id(0)

    @pl.when(step == 0)
    def _():
        acc_ref[...] = jnp.zeros_like(acc_ref)

    grad = dq_ref[...]
    acc_ref[...] += mul_nt(grad, join_tile(w_ref))
    split_tile(grad_ref, mul_nn(normed_t[...], grad))


def query_back(normed1_t, d_query, weights):
    span = normed1_t.shape[1]
    side, width = D // BLK, COLS // BLK
    whole = lambda j: (0, 0)
    act = pl.BlockSpec((span, D), whole)
    tile = pl.BlockSpec((side, width, BLK, BLK), lambda j: (0, j, 0, 0))
    return pl.pallas_call(
        query_body,
        grid=(D // COLS,),
        in_specs=[
            pl.BlockSpec((D, span), whole),
            pl.BlockSpec((span, COLS), lambda j: (0, j)),
            tile,
        ],
        out_specs=[tile, act],
        out_shape=[
            jax.ShapeDtypeStruct((side, side, BLK, BLK), BF),
            jax.ShapeDtypeStruct((span, D), F32),
        ],
        compiler_params=params(),
        cost_estimate=cost(4 * span * D * D, 8 * MIB),
        name="query_backward",
    )(normed1_t, d_query, weights.reshape(-1, 3 * side, BLK, BLK))


def input_body(
    tokens_ref, gains_ref, normed_t, own_ref, recv_ref, acc_ref, gm_ref, w_ref, grad_ref, out_ref,
    gain_ref, acc
):
    step = pl.program_id(0)

    @pl.when(step == 0)
    def _():
        acc[...] = acc_ref[...]

    grad = (own_ref[0].astype(F32) + recv_ref[0].astype(F32)).astype(BF)
    acc[...] += mul_nt(grad, join_tile(w_ref))
    split_tile(grad_ref, mul_nn(normed_t[...], grad))

    @pl.when(step == pl.num_programs(0) - 1)
    def _():
        unit_vals, inv_std = normalize(tokens_ref[...].astype(F32))
        back = acc[...]
        gain_ref[...] = jnp.sum(back * unit_vals, 0, keepdims=True)
        out_ref[...] = (
            gm_ref[...] + norm_back(back * gains_ref[0:1], unit_vals, inv_std)
        ).astype(BF)


def input_back(tokens, gains, normed1_t, own, received, partial, grad_middle, weights):
    span = tokens.shape[0]
    side, width = D // BLK, COLS // BLK
    per = D // COLS
    whole = lambda j: (0, 0)
    act = pl.BlockSpec((span, D), whole)
    part = pl.BlockSpec((1, span, COLS), lambda j: (j // per, 0, j % per))
    return pl.pallas_call(
        input_body,
        grid=(2 * per,),
        in_specs=[
            act,
            pl.BlockSpec((2, D), whole),
            pl.BlockSpec((D, span), whole),
            part,
            part,
            act,
            act,
            pl.BlockSpec((side, width, BLK, BLK), lambda j: (0, j + per, 0, 0)),
        ],
        out_specs=[
            pl.BlockSpec((side, width, BLK, BLK), lambda j: (0, j, 0, 0)),
            act,
            pl.BlockSpec((1, D), whole),
        ],
        out_shape=[
            jax.ShapeDtypeStruct((side, 2 * side, BLK, BLK), BF),
            jax.ShapeDtypeStruct((span, D), BF),
            jax.ShapeDtypeStruct((1, D), F32),
        ],
        scratch_shapes=[pltpu.VMEM((span, D), F32)],
        compiler_params=params(),
        cost_estimate=cost(8 * span * D * D, 20 * MIB),
        name="input_backward",
    )(
        tokens, gains, normed1_t, own, received, partial, grad_middle,
        weights.reshape(-1, 3 * side, BLK, BLK),
    )


def source_numbers():
    side = D // BLK
    numbers = np.arange(3 * side * side + side * side + 2 * side * (FF // BLK), dtype=np.int32)
    row, col = np.divmod(numbers[: 3 * side * side], 3 * side)
    numbers[: 3 * side * side] = np.where(
        col < side, row * side + col, side * side + row * 2 * side + col - side
    )
    return numbers


def gather_body(first, bounds, table, *refs):
    sources = refs[:6]
    out_ref, stage, sems = refs[6:]
    step, steps = pl.program_id(0), pl.num_programs(0)
    count = stage.shape[1] // 2

    def fetch(which, slot):
        start = first + which * count
        for i in range(count):
            number = table[start + i]
            for low, high, own, other in zip(bounds, bounds[1:], sources[:3], sources[3:]):

                @pl.when((number >= low) & (number < high))
                def _():
                    for src, at in ((own, i), (other, count + i)):
                        pltpu.make_async_copy(
                            src.at[number - low], stage.at[slot, at], sems.at[slot]
                        ).start()

    @pl.when(step == 0)
    def _():
        fetch(0, 0)

    @pl.when(step + 1 < steps)
    def _():
        fetch(step + 1, (step + 1) % 2)

    slot = step % 2
    pltpu.make_async_copy(stage.at[slot], stage.at[slot], sems.at[slot]).wait()
    total = stage[slot, :count].astype(F32) + stage[slot, count:].astype(F32)
    out_ref[...] = total.astype(BF)


def gather_sums(table, first, count, own, other):
    hbm = pl.BlockSpec(memory_space=pltpu.HBM)
    steps = 4
    part = count // steps
    bounds = np.cumsum([0] + [src.shape[0] for src in own]).tolist()
    return pl.pallas_call(
        functools.partial(gather_body, first, bounds),
        grid=(steps,),
        in_specs=[pl.BlockSpec(memory_space=pltpu.SMEM)] + [hbm] * 6,
        out_specs=pl.BlockSpec((part, BLK, BLK), lambda i: (i, 0, 0)),
        out_shape=jax.ShapeDtypeStruct((count, BLK, BLK), BF),
        scratch_shapes=[
            pltpu.VMEM((2, 2 * part, BLK, BLK), BF),
            pltpu.SemaphoreType.DMA((2,)),
        ],
        compiler_params=params(52),
        cost_estimate=cost(0, 6 * count * BLK * BLK),
        name="gradient_sums",
    )(table, *own, *other)


def merge_body(first, second, passed, *refs):
    refs = list(refs)

    def total(count):
        return sum(refs.pop(0)[...].astype(F32) for _ in range(count))

    sums = [total(2), total(2)] if first else []
    if second:
        sums.append(total(3 if passed else 2))
    for ref, value in zip(refs, sums):
        ref[...] = value.astype(BF)


def merge_sums(low, came, kept, last, passed):
    steps = 3
    args, specs, shapes, outs = [], [], [], []

    def part(array, count, start):
        args.append(array)
        size = count // steps
        specs.append(pl.BlockSpec((size, BLK, BLK), lambda i: (i + start * steps, 0, 0)))

    def out(count):
        shapes.append(jax.ShapeDtypeStruct((count, BLK, BLK), BF))
        outs.append(pl.BlockSpec((count // steps, BLK, BLK), lambda i: (i, 0, 0)))

    if low is not None:
        count = low.shape[0] // 2
        for start in range(2):
            part(low, count, start)
            part(came, count, start)
            out(count)
    if kept is not None:
        for array in (kept, last) if passed is None else (kept, last, passed):
            part(array, kept.shape[0], 0)
        out(kept.shape[0])
    body = functools.partial(merge_body, low is not None, kept is not None, passed is not None)
    return pl.pallas_call(
        body,
        grid=(steps,),
        in_specs=specs,
        out_specs=outs,
        out_shape=shapes,
        compiler_params=params(46),
        cost_estimate=cost(0, 6 * MIB),
        name="merge_sums",
    )(*args)


def two_terms(values):
    high = values.astype(BF)
    return high, (values - high.astype(F32)).astype(BF)


def update_body(count, *refs):
    parts = refs[:count]
    m_ref, sl_ref, sr_ref, rl_ref, rr_ref, g_out, sl_out, sr_out, m_out = refs[count:]

    def long_left(terms, axis):
        return jnp.concatenate([terms[0], terms[0], terms[1]], axis)

    def long_right(terms, axis):
        return jnp.concatenate([terms[0], terms[1], terms[0]], axis)

    count = range(g_out.shape[0])
    totals = [sum(part[i].astype(F32) for part in parts) for i in count]
    grads = [two_terms(total) for total in totals]
    talls = [long_right(grad, 0) for grad in grads]
    inners = [mul_nn(long_left(two_terms(rl_ref[i]), 1), talls[i]) for i in count]
    for i in count:
        g_out[i] = totals[i]
        sl_out[i] = sl_ref[i] + mul_nt(long_left(grads[i], 1), long_right(grads[i], 1))
    directions = [
        mul_nn(long_left(two_terms(inners[i]), 1), long_right(two_terms(rr_ref[i]), 0))
        for i in count
    ]
    for i in count:
        sr_out[i] = sr_ref[i] + mul_tn(long_left(grads[i], 0), talls[i])
    for i in count:
        master, direction = m_ref[i], directions[i]
        scale = jnp.sqrt(jnp.mean(master * master, keepdims=True) + 1e-06)
        scale = scale * lax.rsqrt(jnp.mean(direction * direction, keepdims=True) + 1e-06)
        m_out[i] = master - 0.3 * scale * direction


def update(parts, master, stat_left, stat_right, root_left, root_right):
    count = master.shape[0]
    group = 6 if count % 6 == 0 else 1
    block = pl.BlockSpec((group, BLK, BLK), lambda i: (i, 0, 0))
    shape = jax.ShapeDtypeStruct(master.shape, F32)
    return pl.pallas_call(
        functools.partial(update_body, len(parts)),
        grid=(count // group,),
        in_specs=[block] * (len(parts) + 5),
        out_specs=[block] * 4,
        out_shape=[shape] * 4,
        compiler_params=params(),
        cost_estimate=cost(48 * count * BLK**3, 15 * MIB),
        name="block_update",
    )(*parts, master, stat_left, stat_right, root_left, root_right)


def pair_moves():
    moves_same, moves_cross = [], []
    for z in range(4):
        for c in range(2):
            for moves, bit in ((moves_same, z % 2), (moves_cross, 1 - z % 2)):
                moves.append((z * 2 + c, (2 * c + bit) * 2 + z // 2))
    return moves_same, moves_cross


def row_part(values, which):
    return lax.dynamic_index_in_dim(values, which, 0, False)


def move_rows(values, crossed, back=False):
    moves = pair_moves()[crossed]
    return lax.ppermute(values, ("seq", "core"), [(b, a) for a, b in moves] if back else moves)


def in_order(kept, crossed, parity):
    return jnp.where(parity == 0, kept, crossed), jnp.where(parity == 0, crossed, kept)


def spread_rows(values, parity):
    kept = move_rows(row_part(values, parity), False)
    crossed = move_rows(row_part(values, 1 - parity), True)
    return jnp.concatenate(in_order(kept, crossed, parity), 0)


def swap_cores(values):
    return lax.ppermute(values, "core", [(0, 1), (1, 0)])


def chip_orders(chips):
    bits = [1 << i for i in range(chips.bit_length() - 1)]
    return bits, bits[::-1]


def offsets(order):
    result = [0]
    for bit in order:
        result = result + [o ^ bit for o in result]
    return result


def place_lists(chips, owned, planes):
    shape = (2, planes, chips, owned)
    by_core = np.array([offsets(order) for order in chip_orders(chips)], np.int32)
    grid = np.indices(shape).astype(np.int32).reshape(4, 2, -1)
    offset = np.broadcast_to(by_core[:, None, :, None], shape).reshape(2, -1)
    return grid[1, 0], offset, grid[3, 0]


def arrival_order(chips, owned, planes):
    per_plane, quarter = chips * owned, owned
    if chips != 4:
        return np.arange(planes * per_plane)
    pieces = [(0, 0)]
    for k in range(1, planes + 1):
        pieces += [(k, 0)] if k < planes else []
        pieces += [(k - 1, 1), (k - 1, 2)]
        pieces += [(k - 2, 3)] if k > 1 else []
    pieces.append((planes - 1, 3))
    starts = [k * per_plane + r * quarter for k, r in pieces]
    return np.concatenate([np.arange(start, start + quarter) for start in starts])


def swap_chips(values, bits):
    chips = lax.axis_size("chip")
    moves = [(i * 2 + c, (i ^ bits[c]) * 2 + c) for i in range(chips) for c in range(2)]
    return lax.ppermute(values, ("chip", "core"), moves)


def move_planes(values, shift):
    planes = lax.axis_size("seq")
    return lax.ppermute(values, "seq", [(i, (i + shift) % planes) for i in range(planes)])


def after(value, *deps):
    return lax.optimization_barrier((value, *deps))[0]


def together(*values):
    return lax.optimization_barrier(values)


def chip_steps():
    return list(zip(*chip_orders(lax.axis_size("chip"))))


def finish_pieces(pieces):
    for bits in chip_steps()[2:]:
        joined = jnp.concatenate(pieces, 0)
        pieces = [joined, swap_chips(joined, bits)]
    return pieces


def add_halves(kept, came):
    return (kept.astype(F32) + came.astype(F32)).astype(BF)


def pack_terms(values):
    high = lax.optimization_barrier(values.astype(BF))
    low = (values - high.astype(F32)).astype(BF)
    terms = jnp.stack([high, low]).reshape(-1, BLK)
    return jnp.pad(terms, ((0, BLK - terms.shape[0]), (0, 0)))[None]


def unpack_terms(blocks, shape):
    terms = blocks.reshape(-1, BLK, BLK)[:, : 2 * shape[0] * shape[1] // BLK]
    terms = terms.reshape(-1, 2, *shape).astype(F32)
    return terms[:, 0] + terms[:, 1]


def finish_sums(keep, send, riders):
    for bits in chip_steps()[::-1][1:-1]:
        count = keep.shape[0] // 2
        came = swap_chips(with_riders(send, riders), bits)
        riders = more_riders(riders, came, keep.shape[0])
        send = add_halves(keep[count:], came[count : 2 * count])
        keep = add_halves(keep[:count], came[:count])
    return keep, send, riders


def with_riders(send, riders):
    return send if riders is None else jnp.concatenate([send, riders], 0)


def more_riders(riders, came, count):
    return riders if riders is None else jnp.concatenate([riders, came[count:]], 0)


def by_chip(riders, me, core):
    chips = lax.axis_size("chip")
    ranks = np.array([np.argsort(offsets(order[::-1])) for order in chip_orders(chips)], np.int32)
    rank = jnp.asarray(ranks)[core][me ^ jnp.arange(chips, dtype=jnp.int32)]
    return riders.reshape(chips, -1, BLK, BLK)[rank]


def local(
    tokens,
    cotangent,
    lengths,
    owner_perm,
    master,
    norm_gains,
    stat_left,
    stat_right,
    root_left,
    root_right,
    moment_first,
    moment_second,
):
    core = lax.axis_index("core")
    place_z = lax.axis_index("seq")
    parity = place_z % 2
    block_count = owner_perm.shape[0]
    owned = master.shape[0]
    half = block_count // 2

    chips, planes = lax.axis_size("chip"), lax.axis_size("seq")
    me = lax.axis_index("chip")

    pair_lengths = jnp.stack([lengths, swap_cores(lengths)])
    pair_lengths = jnp.where(core == 0, pair_lengths, pair_lengths[::-1]).reshape(-1)
    length = lax.dynamic_index_in_dim(pair_lengths, place_z, 0, False)
    span = tokens.shape[0] * tokens.shape[1]
    live = jnp.stack([length - core * span, length - (1 - core) * span, length - core * span, parity])

    distance, offset, slot = place_lists(chips, owned, planes)
    offset = jnp.where(core == 0, offset, offset[::-1])
    device = ((place_z - distance) % planes * chips + (me ^ offset)) * 2
    device = device + jnp.stack([core, 1 - core])[:, None]
    table = owner_perm[(device * owned + slot).reshape(-1)]
    sums_table = jnp.asarray(source_numbers())[table[:half]]
    arrive = arrival_order(chips, owned, planes)
    near_slots, far_slots = device * owned + slot
    table = owner_perm[jnp.concatenate([near_slots[arrive], far_slots[arrive]])]

    shard = master.astype(BF)
    first_bits, second_bits = chip_steps()[:2]
    per_plane = chips * owned
    by_phase = chips == 4
    rows = (row_part(tokens, parity), row_part(tokens, 1 - parity))
    cross, held, weights, first = None, (), None, 0
    came, turned = swap_chips(shard, first_bits), swap_chips(shard, second_bits)
    next_shard = move_planes(shard, 1)
    pieces = [[shard, came, turned]]

    def place(parts, first, weights):
        others = [swap_cores(part) for part in parts]
        weights = place_blocks(table, first, parts, others, weights)
        return weights, first + sum(part.shape[0] for part in parts)

    for k in range(1, planes):
        ready = () if k == 1 else (cross, *held, live, table, sums_table)
        ready = ready if weights is None else (*ready, weights)
        this_shard, came, turned, row_a, row_b, *done = together(
            next_shard, came, turned, *rows, *ready
        )
        if k > 1:
            pieces[k - 2].append(done[0])
        cross = swap_chips(came, second_bits)
        arrived = [this_shard, came, turned, *(pieces[0][:1] if k == 1 else done[:1])]
        arrived = arrived[3:] + arrived[:3] if k == 1 else arrived
        pieces[k - 1][1:] = [came, turned]
        came, turned = swap_chips(this_shard, first_bits), swap_chips(this_shard, second_bits)
        pieces.append([this_shard, came, turned])
        if k < planes - 1:
            next_shard = move_planes(this_shard, 1)
        else:
            row_same = move_rows(row_a, False)
            row_cross = move_rows(after(row_b, row_same), True)
        if by_phase:
            if k > 1:
                weights, first = place(done[1:2], first, weights)
            held = (jnp.concatenate(arrived, 0),)
    came, turned, done, row_same, row_cross, *held = together(
        came, turned, cross, row_same, row_cross, *held, *([] if weights is None else [weights])
    )
    own_tokens = jnp.concatenate(in_order(row_same, row_cross, parity), 0)
    pieces[-2].append(done)
    pieces[-1][1:] = [came, turned, swap_chips(came, second_bits)]
    normed1, normed1_t = norm_tokens(own_tokens, norm_gains)
    if by_phase:
        weights, first = place(held[:1], first, weights)
        weights, first = place([came, turned, done], first, weights)
        last, normed1, *_ = together(pieces[-1][-1], normed1, weights)
        other_normed = swap_cores(normed1)
        weights, _ = place([last], first, weights)
    else:
        for each in pieces:
            each = [jnp.concatenate(finish_pieces(each), 0)]
            weights, first = place(each, first, weights)
        other_normed = swap_cores(normed1)
    own_cot = spread_rows(after(cotangent, weights), parity)

    own_qkv, other_kv = project(normed1, other_normed, weights)
    attended, q_aug = attend(live, own_qkv, other_kv)
    kept, crossed, g_rest, grad_middle, grad_attended, gain_second = feed(
        live, own_tokens, attended, own_cot, norm_gains, weights
    )
    other_rest = swap_cores(g_rest)
    kept, crossed = move_rows(kept, False, True), move_rows(crossed, True, True)
    layer_out = jnp.stack(in_order(kept, crossed, parity), 0)
    d_query, d_own, d_other = attend_back(live, q_aug, own_qkv, other_kv, attended, grad_attended)
    received = swap_cores(after(d_other, kept, crossed))
    flat = lambda g: g.reshape(-1, BLK, BLK)
    g_query, partial = query_back(normed1_t, d_query, weights)
    g_query = flat(g_query)
    other_query = swap_cores(g_query)
    g_kv, grad_in, gain_first = input_back(
        own_tokens, norm_gains, normed1_t, d_own, received, partial, grad_middle, weights
    )
    g_kv = flat(g_kv)
    gain_part = jnp.concatenate([gain_first, gain_second], 0)
    mine = pack_terms(gain_part)
    other_kv_grad = swap_cores(after(g_kv, other_query))
    theirs = swap_cores(mine)
    pair = jnp.concatenate([mine, theirs], 0)
    riders = jnp.where(core == 0, pair, pair[::-1])
    own_grads = (g_query, g_kv, g_rest)
    other_grads = (other_query, other_kv_grad, other_rest)
    half_plane = per_plane // 2
    last_bits, before_bits = chip_steps()[-1], chip_steps()[0]
    halves = grad_in.reshape(2, span // 2, D)
    rows = [row_part(halves, parity), row_part(halves, 1 - parity)]
    moved_rows, lows, sent, passed, riders_z = [], [], None, None, []

    def sums(k, part, held):
        first = k * per_plane + part * half_plane
        return gather_sums(held, first, half_plane, own_grads, other_grads)

    order = list(range(planes))[::-1]
    high = sums(order[0], 1, sums_table)
    held = sums_table
    held_riders = []
    for turn in range(planes + 1):
        group, moves = [], []
        if turn < planes:
            group.append(high)
            moves.append(lambda v: swap_chips(v, last_bits))
        if 1 <= turn <= planes:
            group.append(sent)
            moves.append(lambda v: swap_chips(v, before_bits))
        if 2 <= turn <= planes:
            group.append(part)
            moves.append(lambda v: move_planes(v, -1))
        if turn < 2:
            group.append(riders)
            bits = last_bits if turn == 0 else before_bits
            moves.append(lambda v: swap_chips(v, bits))
        if turn in (1, 2):
            group.append(rows[turn - 1])
            crossed = turn == 2
            moves.append(lambda v: move_rows(v, crossed, True))
        far_riders = [1, 2] if turn == planes - 1 else []
        group += [rider for _ in far_riders]
        moves += [functools.partial(move_planes, shift=-k) for k in far_riders]
        came = [move(value) for move, value in zip(moves, together(*group, *moved_rows, *held_riders))]
        if turn in (1, 2):
            moved_rows.append(came.pop())
        if turn < 2:
            riders = jnp.concatenate([riders, came.pop()], 0)
        count = len(came) - len(far_riders)
        riders_z, came = riders_z + came[count:], came[:count]
        if far_riders:
            riders_z += [move_planes(after(rider, *riders_z), -k) for k in range(3, planes)]
        if turn == planes:
            parts = [keep_before, *came]
            continue
        passed = came.pop() if turn >= 2 else None
        low = sums(order[turn], 0, after(held, high))
        if turn + 1 < planes:
            high = sums(order[turn + 1], 1, after(held, low))
        held = after(sums_table, *came)
        held_riders = [riders] if turn == 1 else []
        if turn == 1:
            plane_gain = by_chip(riders, me, core)
            plane_gain = jnp.sum(unpack_terms(plane_gain, gain_part.shape), 0)
            rider = pack_terms(plane_gain)
        second = (None, None, None) if turn == 0 else (keep_before, came[-1], passed)
        keep, sent, *part = merge_sums(low, came[0], *second)
        part = part[0] if part else None
        keep_before, sent, grown = finish_sums(keep, sent, riders if turn == 0 else None)
        riders = grown if turn == 0 else riders
    input_grad = jnp.stack(in_order(*moved_rows, parity), 0).astype(F32)
    planes_gain = [unpack_terms(each, gain_part.shape)[0] for each in (rider, *riders_z)]
    turned = (jnp.arange(planes, dtype=jnp.int32) - place_z) % planes
    gain_grad = jnp.sum(jnp.stack(planes_gain)[turned], 0)
    grad_blocks, stat_left_new, stat_right_new, master_new = update(
        parts, master, stat_left, stat_right, root_left, root_right
    )
    first_new = 0.9 * moment_first + 0.1 * gain_grad
    second_new = 0.999 * moment_second + 0.001 * gain_grad * gain_grad
    first_hat = first_new / (1.0 - 0.9**STEP)
    second_hat = second_new / (1.0 - 0.999**STEP)
    gains_new = norm_gains - 0.5 * first_hat / (jnp.sqrt(second_hat) + 1e-08)
    return (
        layer_out,
        input_grad,
        grad_blocks,
        stat_left_new,
        stat_right_new,
        master_new,
        first_new,
        second_new,
        gains_new,
    )


def solution(mesh):
    seq_size, rows_size = mesh.shape["seq"], mesh.shape["rows"]
    mesh = Mesh(mesh.devices.reshape(seq_size, rows_size // 2, 2), ("seq", "chip", "core"))
    activation = P(("chip", "core"), "seq", None)
    blocks = P(("seq", "chip", "core"), None, None)
    return jax.shard_map(
        local,
        mesh=mesh,
        in_specs=(
            activation, activation, P(("chip", "core")), P(), blocks, P(),
            blocks, blocks, blocks, blocks, P(), P(),
        ),
        out_specs=(activation, activation, blocks, blocks, blocks, blocks, P(), P(), P()),
        check_vma=False,
    )
```

```python
import functools
import jax
import jax.numpy as jnp
import numpy as np
from jax import lax
from jax.experimental import pallas as pl
from jax.experimental.pallas import tpu as pltpu
from jax.sharding import Mesh
from jax.sharding import PartitionSpec as P

D = 1024
HD = 64
FF = 4096
BLK = 128
STEP = 10
COLS = 1024
BF = jnp.bfloat16
F32 = jnp.float32
MIB = 1024 * 1024

norm_eps = 1e-05
score_scale = 0.125
masked_score = -1e30


def params(limit=56):
    return pltpu.CompilerParams(vmem_limit_bytes=limit * MIB)


def cost(flops, nbytes):
    return pl.CostEstimate(flops=int(flops), bytes_accessed=int(nbytes), transcendentals=0)


def mul_nn(left, right):
    return jnp.dot(left, right, preferred_element_type=F32)


def mul_nt(left, right):
    return lax.dot_general(left, right, (((1,), (1,)), ((), ())), preferred_element_type=F32)


def mul_tn(left, right):
    return lax.dot_general(left, right, (((0,), (0,)), ((), ())), preferred_element_type=F32)


def join_tile(ref):
    rows, cols = ref.shape[0], ref.shape[1]
    return jnp.concatenate([ref[:, j].reshape(rows * BLK, BLK) for j in range(cols)], axis=1)


def split_tile(ref, matrix):
    rows, cols = ref.shape[0], ref.shape[1]
    for j in range(cols):
        ref[:, j] = matrix[:, j * BLK : (j + 1) * BLK].reshape(rows, BLK, BLK).astype(ref.dtype)


def split_flat(ref, matrix):
    cols = matrix.shape[1] // BLK
    for i in range(matrix.shape[0] // BLK):
        for j in range(cols):
            block = matrix[i * BLK : (i + 1) * BLK, j * BLK : (j + 1) * BLK]
            ref[i * cols + j] = block.astype(ref.dtype)


def normalize(values):
    row_mean = jnp.mean(values, -1, keepdims=True)
    centered = values - row_mean
    row_var = jnp.mean(centered * centered, -1, keepdims=True)
    inv_std = lax.rsqrt(row_var + norm_eps)
    return centered * inv_std, inv_std


def gelu_parts(hidden):
    bell = jnp.exp(hidden * hidden * -0.5)
    t = 1.0 / (1.0 + jnp.abs(hidden) * (0.3275911 * 0.7071067811865476))
    poly = 1.061405429 * t - 1.453152027
    for term in (1.421413741, -0.284496736, 0.254829592):
        poly = poly * t + term
    tail = poly * t * 0.5 * bell
    return jnp.where(hidden < 0.0, tail, 1.0 - tail), hidden * bell * 0.3989422804014327


def norm_back(gradient, unit_vals, inv_std):
    grad_mean = jnp.mean(gradient, -1, keepdims=True)
    cross_mean = jnp.mean(gradient * unit_vals, -1, keepdims=True)
    return inv_std * (gradient - grad_mean - unit_vals * cross_mean)


def place_body(first, pieces, table, *refs):
    near, far = refs[:pieces], refs[pieces : 2 * pieces]
    out_ref, sem = refs[-2:]
    total = 0
    for start, sources in ((first, near), (table.shape[0] // 2 + first, far)):
        for src in sources:
            for slot in range(src.shape[0]):
                pltpu.make_async_copy(src.at[slot], out_ref.at[table[start + slot]], sem).start()
            start += src.shape[0]
            total += src.shape[0]
    done = out_ref.at[pl.ds(0, total)]
    pltpu.make_async_copy(done, done, sem).wait()


def place_blocks(table, first, near, far, kept):
    smem = pl.BlockSpec(memory_space=pltpu.SMEM)
    hbm = pl.BlockSpec(memory_space=pltpu.HBM)
    vmem = pl.BlockSpec(memory_space=pltpu.VMEM)
    kept = () if kept is None else (kept,)
    count = 2 * len(near)
    return pl.pallas_call(
        functools.partial(place_body, first, len(near)),
        out_shape=jax.ShapeDtypeStruct((table.shape[0], BLK, BLK), BF),
        in_specs=[smem] + [vmem] * count + [hbm] * len(kept),
        out_specs=hbm,
        scratch_shapes=[pltpu.SemaphoreType.DMA],
        input_output_aliases={1 + count: 0} if kept else {},
        compiler_params=params(46),
        cost_estimate=cost(0, 6 * MIB),
        name="place_weights",
    )(table, *near, *far, *kept)


def norm_body(tokens_ref, gains_ref, out_ref, turned_ref):
    normed = normalize(tokens_ref[...].astype(F32))[0] * gains_ref[0:1]
    out_ref[...] = normed.astype(BF)
    turned_ref[...] = normed.T.astype(BF)


def norm_tokens(tokens, gains):
    span = tokens.shape[0]
    steps = 4
    part = pl.BlockSpec((span // steps, D), lambda i: (i, 0))
    return pl.pallas_call(
        norm_body,
        grid=(steps,),
        in_specs=[part, pl.BlockSpec((2, D), lambda i: (0, 0))],
        out_specs=[part, pl.BlockSpec((D, span // steps), lambda i: (0, i))],
        out_shape=[jax.ShapeDtypeStruct((span, D), BF), jax.ShapeDtypeStruct((D, span), BF)],
        compiler_params=params(46),
        cost_estimate=cost(0, 3 * MIB),
        name="norm_tokens",
    )(tokens, gains)


def qkv_body(own_ref, other_ref, w_ref, own_out, other_out):
    step = pl.program_id(0)
    weight = join_tile(w_ref)
    own_out[...] = mul_nn(own_ref[...], weight).astype(BF)

    @pl.when(step >= D // COLS)
    def _():
        other_out[...] = mul_nn(other_ref[...], weight).astype(BF)


def project(own, other, weights):
    span = own.shape[0]
    skip = D // COLS
    once = pl.BlockSpec((span, D), lambda j: (0, 0))
    return pl.pallas_call(
        qkv_body,
        grid=(3 * D // COLS,),
        in_specs=[
            once,
            once,
            pl.BlockSpec((D // BLK, COLS // BLK, BLK, BLK), lambda j: (0, j, 0, 0)),
        ],
        out_specs=[
            pl.BlockSpec((span, COLS), lambda j: (0, j)),
            pl.BlockSpec((span, COLS), lambda j: (0, jnp.maximum(j - skip, 0))),
        ],
        out_shape=[
            jax.ShapeDtypeStruct((span, 3 * D), BF),
            jax.ShapeDtypeStruct((span, 2 * D), BF),
        ],
        compiler_params=params(),
        cost_estimate=cost(10 * span * D * D, 12 * MIB),
        name="qkv_projection",
    )(own, other, weights.reshape(-1, 3 * D // BLK, BLK, BLK))


def lane_masks(head):
    lane = lax.broadcasted_iota(jnp.int32, (1, BLK), 1)
    first = HD * (1 - head)
    keep = (lane // HD == head).astype(F32)
    dead_lane = (lane == first).astype(F32)
    terms = [(lane == first + 1 + i).astype(F32) for i in range(3)]
    return keep, dead_lane, terms


def three_terms(values):
    high = values.astype(BF).astype(F32)
    rest = values - high
    middle = rest.astype(BF).astype(F32)
    return high, middle, rest - middle


def key_bias(span, live_count):
    row = lax.broadcasted_iota(jnp.int32, (span, 1), 0)
    return jnp.where(row < live_count, 0.0, masked_score).astype(F32)


def attend_body(live_ref, q_ref, ko_ref, vo_ref, kx_ref, vx_ref, out_ref, aug_ref):
    span = q_ref.shape[0]
    bias_own = key_bias(span, live_ref[0])
    bias_other = key_bias(span, live_ref[1])
    queries = q_ref[...].astype(F32) * score_scale
    k_own, k_other = ko_ref[...].astype(F32), kx_ref[...].astype(F32)
    v_own_f, v_other_f = vo_ref[...].astype(F32), vx_ref[...].astype(F32)
    results, scores = [], []
    for head in range(2):
        keep, dead_lane, _ = lane_masks(head)
        q_head = (queries * keep + dead_lane).astype(BF)
        s_own = mul_nt(q_head, (k_own * keep + bias_own * dead_lane).astype(BF))
        s_other = mul_nt(q_head, (k_other * keep + bias_other * dead_lane).astype(BF))
        scores.append((q_head, s_own, s_other))
    for head in range(2):
        keep, _, terms = lane_masks(head)
        q_head, s_own, s_other = scores[head]
        top = jnp.max(jnp.maximum(s_own, s_other), -1, keepdims=True)
        p_own = jnp.exp(s_own - top)
        p_other = jnp.exp(s_other - top)
        v_own = (v_own_f * keep + (1.0 - keep)).astype(BF)
        v_other = (v_other_f * keep + (1.0 - keep)).astype(BF)
        mixed = mul_nn(p_own.astype(BF), v_own) + mul_nn(p_other.astype(BF), v_other)
        total = mixed[:, HD * (1 - head) : HD * (1 - head) + 1]
        results.append(mixed / total * keep)
        parts = three_terms(-(top + jnp.log(total)))
        stats = sum(part * lane for part, lane in zip(parts, terms))
        aug_ref[:, head * BLK : (head + 1) * BLK] = (q_head.astype(F32) + stats).astype(BF)
    out_ref[...] = (results[0] + results[1]).astype(BF)


def attend(live, own, other):
    span = own.shape[0]
    pairs = D // BLK
    col = lambda shift: pl.BlockSpec((span, BLK), lambda p: (0, p + shift))
    return pl.pallas_call(
        attend_body,
        grid=(pairs,),
        in_specs=[
            pl.BlockSpec(memory_space=pltpu.SMEM),
            col(0),
            col(pairs),
            col(2 * pairs),
            col(0),
            col(pairs),
        ],
        out_specs=[col(0), pl.BlockSpec((span, 2 * BLK), lambda p: (0, p))],
        out_shape=[
            jax.ShapeDtypeStruct((span, D), BF),
            jax.ShapeDtypeStruct((span, 2 * D), BF),
        ],
        compiler_params=params(),
        cost_estimate=cost(40 * span * span * D, 8 * MIB),
        name="attention",
    )(live, own, own, own, other, other)


def attend_back_body(
    live_ref, aug_ref, ko_ref, vo_ref, kx_ref, vx_ref, at_ref, g_ref, dq_ref, own_ref, other_ref
):
    span = at_ref.shape[0]
    grads = g_ref[...].astype(F32)
    product = grads * at_ref[...].astype(F32)
    keeps, g_augs, q_augs = [], [], []
    for head in range(2):
        keep, dead_lane, terms = lane_masks(head)
        delta = jnp.sum(product * keep, -1, keepdims=True)
        parts = three_terms(-delta)
        stats = sum(part * lane for part, lane in zip(parts, terms))
        g_augs.append((grads * keep + stats).astype(BF))
        q_augs.append(aug_ref[:, head * BLK : (head + 1) * BLK])
    d_query = [None, None]
    for k_ref, v_ref, out_ref, live in (
        (ko_ref, vo_ref, own_ref, live_ref[0]),
        (kx_ref, vx_ref, other_ref, live_ref[1]),
    ):
        bias = key_bias(span, live)
        keys = k_ref[...]
        keys_f, values_f = keys.astype(F32), v_ref[...].astype(F32)
        d_keys = d_values = None
        for head in range(2):
            keep, dead_lane, terms = lane_masks(head)
            ones = terms[0] + terms[1] + terms[2]
            k_aug = (keys_f * keep + (bias * dead_lane + ones)).astype(BF)
            v_aug = (values_f * keep + ones).astype(BF)
            probs = jnp.exp(mul_nt(k_aug, q_augs[head]))
            d_scores = (probs * mul_nt(v_aug, g_augs[head])).astype(BF)
            value_part = mul_nn(probs.astype(BF), g_augs[head]) * keep
            key_part = mul_nn(d_scores, q_augs[head]) * keep
            query_part = mul_tn(keys, d_scores)[head * HD : (head + 1) * HD]
            d_query[head] = query_part if d_query[head] is None else d_query[head] + query_part
            d_values = value_part if d_values is None else d_values + value_part
            d_keys = key_part if d_keys is None else d_keys + key_part
        out_ref[0] = d_keys.astype(out_ref.dtype)
        out_ref[1] = d_values.astype(out_ref.dtype)
    dq_ref[...] = (jnp.concatenate(d_query, 0).T * score_scale).astype(BF)


def attend_back(live, aug, own, other, attended, grads):
    span = own.shape[0]
    pairs = D // BLK
    col = lambda shift: pl.BlockSpec((span, BLK), lambda p: (0, p + shift))
    pair_out = pl.BlockSpec((2, span, BLK), lambda p: (0, 0, p))
    return pl.pallas_call(
        attend_back_body,
        grid=(pairs,),
        in_specs=[
            pl.BlockSpec(memory_space=pltpu.SMEM),
            pl.BlockSpec((span, 2 * BLK), lambda p: (0, p)),
            col(pairs),
            col(2 * pairs),
            col(0),
            col(pairs),
            col(0),
            col(0),
        ],
        out_specs=[col(0), pair_out, pair_out],
        out_shape=[
            jax.ShapeDtypeStruct((span, D), BF),
            jax.ShapeDtypeStruct((2, span, D), BF),
            jax.ShapeDtypeStruct((2, span, D), BF),
        ],
        compiler_params=params(),
        cost_estimate=cost(60 * span * span * D, 12 * MIB),
        name="attention_backward",
    )(live, aug, own, own, other, other, attended, grads)


def feed_body(
    live_ref,
    tokens_ref,
    attended_ref,
    cot_ref,
    gains_ref,
    wo_ref,
    wu_ref,
    wd_ref,
    kept_ref,
    crossed_ref,
    rest_ref,
    gm_ref,
    ga_ref,
    gain_ref,
    unit,
    inv,
    normed,
    normed_t,
    top,
    acc_out,
    acc_back,
    up_stage,
    down_stage,
    out_stage,
    sems,
    out_sem,
):
    step = pl.program_id(0)
    place = step % 2
    side, width = up_stage.shape[1], up_stage.shape[2]
    per_tile = side * width
    up_first = side * side
    down_first = up_first + side * FF // BLK

    def drain(which):
        pltpu.make_async_copy(up_stage.at[which], up_stage.at[which], sems.at[0, which]).wait()
        pltpu.make_async_copy(down_stage.at[which], down_stage.at[which], sems.at[1, which]).wait()
    span = tokens_ref.shape[0]

    @pl.when(step == 0)
    def _():
        weight = join_tile(wo_ref)
        middle = tokens_ref[...].astype(F32) + mul_nn(attended_ref[...], weight)
        unit_vals, inv_std = normalize(middle)
        unit[...] = unit_vals
        inv[...] = inv_std
        normed_vals = unit_vals * gains_ref[1:2]
        normed[...] = normed_vals.astype(BF)
        normed_t[...] = normed_vals.T.astype(BF)
        row = lax.broadcasted_iota(jnp.int32, (span, 1), 0)
        top[...] = jnp.where(row < live_ref[2], cot_ref[...].astype(F32), 0.0).astype(BF)
        acc_out[...] = middle
        acc_back[...] = jnp.zeros_like(acc_back)

    w_up = join_tile(wu_ref)
    w_down = join_tile(wd_ref)
    hidden = mul_nn(normed[...], w_up)
    grad_act = mul_nt(top[...], w_down)
    share, slope_rest = gelu_parts(hidden)
    activated = (hidden * share).astype(BF)
    grad_hidden = (grad_act * (share + slope_rest)).astype(BF)
    acc_out[...] += mul_nn(activated, w_down)
    acc_back[...] += mul_nt(grad_hidden, w_up)

    @pl.when(step >= 2)
    def _():
        drain(place)

    split_flat(down_stage.at[place], mul_tn(activated, top[...]))
    dest = rest_ref.at[pl.ds(down_first + step * per_tile, per_tile)]
    pltpu.make_async_copy(down_stage.at[place], dest, sems.at[1, place]).start()
    split_tile(up_stage.at[place], mul_nn(normed_t[...], grad_hidden))
    for i in range(side):
        dest = rest_ref.at[pl.ds(up_first + i * (FF // BLK) + step * width, width)]
        pltpu.make_async_copy(up_stage.at[place, i], dest, sems.at[0, place]).start()

    @pl.when(step == pl.num_programs(0) - 1)
    def _():
        for flip in range(2):

            @pl.when(live_ref[3] == flip)
            def _():
                for ref, part in ((kept_ref, flip), (crossed_ref, 1 - flip)):
                    ref[...] = acc_out[part * (span // 2) : (part + 1) * (span // 2)].astype(BF)

        unit_vals = unit[...]
        back = acc_back[...]
        gain_ref[...] = jnp.sum(back * unit_vals, 0, keepdims=True)
        grad_middle = top[...].astype(F32) + norm_back(back * gains_ref[1:2], unit_vals, inv[...])
        gm_ref[...] = grad_middle
        back_middle = grad_middle.astype(BF)
        split_flat(out_stage, mul_tn(attended_ref[...], back_middle))
        out_copy = pltpu.make_async_copy(out_stage, rest_ref.at[pl.ds(0, up_first)], out_sem)
        out_copy.start()
        ga_ref[...] = mul_nt(back_middle, join_tile(wo_ref)).astype(BF)
        drain(1 - place)
        drain(place)
        out_copy.wait()


def feed(live, tokens, attended, cotangent, gains, weights):
    span = tokens.shape[0]
    side, width = D // BLK, COLS // BLK
    whole = lambda j: (0, 0)
    act = pl.BlockSpec((span, D), whole)
    once = pl.BlockSpec((span, D), whole, pipeline_mode=pl.Buffered(1))
    half_act = pl.BlockSpec((span // 2, D), whole)
    per_row = weights.reshape(-1, side, BLK, BLK)
    per_up = weights.reshape(-1, FF // BLK, BLK, BLK)
    out_row = (3 * side * side) // side // side
    up_row = 4 * side * side // (FF // BLK) // side
    down_row = (4 * side * side + side * FF // BLK) // side // width
    return pl.pallas_call(
        feed_body,
        grid=(FF // COLS,),
        in_specs=[
            pl.BlockSpec(memory_space=pltpu.SMEM),
            once,
            once,
            once,
            pl.BlockSpec((2, D), whole),
            pl.BlockSpec(
                (side, side, BLK, BLK),
                lambda j: (out_row, 0, 0, 0),
                pipeline_mode=pl.Buffered(1),
            ),
            pl.BlockSpec((side, width, BLK, BLK), lambda j: (up_row, j, 0, 0)),
            pl.BlockSpec((width, side, BLK, BLK), lambda j: (down_row + j, 0, 0, 0)),
        ],
        out_specs=[
            half_act,
            half_act,
            pl.BlockSpec(memory_space=pltpu.HBM),
            act,
            act,
            pl.BlockSpec((1, D), whole),
        ],
        out_shape=[
            jax.ShapeDtypeStruct((span // 2, D), BF),
            jax.ShapeDtypeStruct((span // 2, D), BF),
            jax.ShapeDtypeStruct((side * side + 2 * side * (FF // BLK), BLK, BLK), BF),
            jax.ShapeDtypeStruct((span, D), F32),
            jax.ShapeDtypeStruct((span, D), BF),
            jax.ShapeDtypeStruct((1, D), F32),
        ],
        scratch_shapes=[
            pltpu.VMEM((span, D), F32),
            pltpu.VMEM((span, 1), F32),
            pltpu.VMEM((span, D), BF),
            pltpu.VMEM((D, span), BF),
            pltpu.VMEM((span, D), BF),
            pltpu.VMEM((span, D), F32),
            pltpu.VMEM((span, D), F32),
            pltpu.VMEM((2, side, width, BLK, BLK), BF),
            pltpu.VMEM((2, side * width, BLK, BLK), BF),
            pltpu.VMEM((side * side, BLK, BLK), BF),
            pltpu.SemaphoreType.DMA((2, 2)),
            pltpu.SemaphoreType.DMA,
        ],
        compiler_params=params(),
        cost_estimate=cost(14 * span * D * FF, 50 * MIB),
        name="feed_forward",
    )(live, tokens, attended, cotangent, gains, per_row, per_up, per_row)


def query_body(normed_t, dq_ref, w_ref, grad_ref, acc_ref):
    step = pl.program_id(0)

    @pl.when(step == 0)
    def _():
        acc_ref[...] = jnp.zeros_like(acc_ref)

    grad = dq_ref[...]
    acc_ref[...] += mul_nt(grad, join_tile(w_ref))
    split_tile(grad_ref, mul_nn(normed_t[...], grad))


def query_back(normed1_t, d_query, weights):
    span = normed1_t.shape[1]
    side, width = D // BLK, COLS // BLK
    whole = lambda j: (0, 0)
    act = pl.BlockSpec((span, D), whole)
    tile = pl.BlockSpec((side, width, BLK, BLK), lambda j: (0, j, 0, 0))
    return pl.pallas_call(
        query_body,
        grid=(D // COLS,),
        in_specs=[
            pl.BlockSpec((D, span), whole),
            pl.BlockSpec((span, COLS), lambda j: (0, j)),
            tile,
        ],
        out_specs=[tile, act],
        out_shape=[
            jax.ShapeDtypeStruct((side, side, BLK, BLK), BF),
            jax.ShapeDtypeStruct((span, D), F32),
        ],
        compiler_params=params(),
        cost_estimate=cost(4 * span * D * D, 8 * MIB),
        name="query_backward",
    )(normed1_t, d_query, weights.reshape(-1, 3 * side, BLK, BLK))


def input_body(normed_t, own_ref, recv_ref, acc_ref, w_ref, grad_ref, out_ref):
    step = pl.program_id(0)

    @pl.when(step == 0)
    def _():
        out_ref[...] = acc_ref[...]

    grad = (own_ref[0].astype(F32) + recv_ref[0].astype(F32)).astype(BF)
    out_ref[...] += mul_nt(grad, join_tile(w_ref))
    split_tile(grad_ref, mul_nn(normed_t[...], grad))


def input_back(normed1_t, own, received, partial, weights):
    span = normed1_t.shape[1]
    side, width = D // BLK, COLS // BLK
    per = D // COLS
    whole = lambda j: (0, 0)
    act = pl.BlockSpec((span, D), whole)
    part = pl.BlockSpec((1, span, COLS), lambda j: (j // per, 0, j % per))
    return pl.pallas_call(
        input_body,
        grid=(2 * per,),
        in_specs=[
            pl.BlockSpec((D, span), whole),
            part,
            part,
            act,
            pl.BlockSpec((side, width, BLK, BLK), lambda j: (0, j + per, 0, 0)),
        ],
        out_specs=[pl.BlockSpec((side, width, BLK, BLK), lambda j: (0, j, 0, 0)), act],
        out_shape=[
            jax.ShapeDtypeStruct((side, 2 * side, BLK, BLK), BF),
            jax.ShapeDtypeStruct((span, D), F32),
        ],
        compiler_params=params(),
        cost_estimate=cost(8 * span * D * D, 20 * MIB),
        name="input_backward",
    )(normed1_t, own, received, partial, weights.reshape(-1, 3 * side, BLK, BLK))


def input_end_body(live_ref, tokens_ref, gains_ref, back_ref, gm_ref, kept_ref, crossed_ref, gain_ref):
    step = pl.program_id(0)
    unit_vals, inv_std = normalize(tokens_ref[...].astype(F32))
    back = back_ref[...]

    @pl.when(step == 0)
    def _():
        gain_ref[...] = jnp.zeros_like(gain_ref)

    gain_ref[...] += jnp.sum(back * unit_vals, 0, keepdims=True)
    grad = (gm_ref[...] + norm_back(back * gains_ref[0:1], unit_vals, inv_std)).astype(BF)
    half = step // (pl.num_programs(0) // 2)
    rows = tokens_ref.shape[0]
    start = pl.multiple_of(step % (pl.num_programs(0) // 2) * rows, rows)

    @pl.when(half == live_ref[3])
    def _():
        kept_ref[pl.ds(start, rows)] = grad

    @pl.when(half != live_ref[3])
    def _():
        crossed_ref[pl.ds(start, rows)] = grad


def input_end(live, tokens, gains, back, grad_middle):
    span = tokens.shape[0]
    steps = 4
    part = pl.BlockSpec((span // steps, D), lambda i: (i, 0))
    half_act = pl.BlockSpec((span // 2, D), lambda i: (0, 0))
    row = lambda count: pl.BlockSpec((count, D), lambda i: (0, 0))
    return pl.pallas_call(
        input_end_body,
        grid=(steps,),
        in_specs=[pl.BlockSpec(memory_space=pltpu.SMEM), part, row(2), part, part],
        out_specs=[half_act, half_act, row(1)],
        out_shape=[
            jax.ShapeDtypeStruct((span // 2, D), BF),
            jax.ShapeDtypeStruct((span // 2, D), BF),
            jax.ShapeDtypeStruct((1, D), F32),
        ],
        compiler_params=params(46),
        cost_estimate=cost(0, 7 * MIB),
        name="input_gradient",
    )(live, tokens, gains, back, grad_middle)


def source_numbers():
    side = D // BLK
    numbers = np.arange(3 * side * side + side * side + 2 * side * (FF // BLK), dtype=np.int32)
    row, col = np.divmod(numbers[: 3 * side * side], 3 * side)
    numbers[: 3 * side * side] = np.where(
        col < side, row * side + col, side * side + row * 2 * side + col - side
    )
    return numbers


def gather_body(first, bounds, table, *refs):
    sources = refs[:6]
    out_ref, stage, sems = refs[6:]
    step, steps = pl.program_id(0), pl.num_programs(0)
    count = stage.shape[1] // 2

    def fetch(which, slot):
        start = first + which * count
        for i in range(count):
            number = table[start + i]
            for low, high, own, other in zip(bounds, bounds[1:], sources[:3], sources[3:]):

                @pl.when((number >= low) & (number < high))
                def _():
                    for src, at in ((own, i), (other, count + i)):
                        pltpu.make_async_copy(
                            src.at[number - low], stage.at[slot, at], sems.at[slot]
                        ).start()

    @pl.when(step == 0)
    def _():
        fetch(0, 0)

    @pl.when(step + 1 < steps)
    def _():
        fetch(step + 1, (step + 1) % 2)

    slot = step % 2
    pltpu.make_async_copy(stage.at[slot], stage.at[slot], sems.at[slot]).wait()
    total = stage[slot, :count].astype(F32) + stage[slot, count:].astype(F32)
    out_ref[...] = total.astype(BF)


def gather_sums(table, first, count, own, other):
    hbm = pl.BlockSpec(memory_space=pltpu.HBM)
    steps = 4
    part = count // steps
    bounds = np.cumsum([0] + [src.shape[0] for src in own]).tolist()
    return pl.pallas_call(
        functools.partial(gather_body, first, bounds),
        grid=(steps,),
        in_specs=[pl.BlockSpec(memory_space=pltpu.SMEM)] + [hbm] * 6,
        out_specs=pl.BlockSpec((part, BLK, BLK), lambda i: (i, 0, 0)),
        out_shape=jax.ShapeDtypeStruct((count, BLK, BLK), BF),
        scratch_shapes=[
            pltpu.VMEM((2, 2 * part, BLK, BLK), BF),
            pltpu.SemaphoreType.DMA((2,)),
        ],
        compiler_params=params(52),
        cost_estimate=cost(0, 6 * count * BLK * BLK),
        name="gradient_sums",
    )(table, *own, *other)


def merge_body(first, second, passed, *refs):
    refs = list(refs)

    def total(count):
        return sum(refs.pop(0)[...].astype(F32) for _ in range(count))

    sums = [total(2), total(2)] if first else []
    if second:
        sums.append(total(3 if passed else 2))
    for ref, value in zip(refs, sums):
        ref[...] = value.astype(BF)


def merge_sums(low, came, kept, last, passed):
    steps = 3
    args, specs, shapes, outs = [], [], [], []

    def part(array, count, start):
        args.append(array)
        size = count // steps
        specs.append(pl.BlockSpec((size, BLK, BLK), lambda i: (i + start * steps, 0, 0)))

    def out(count):
        shapes.append(jax.ShapeDtypeStruct((count, BLK, BLK), BF))
        outs.append(pl.BlockSpec((count // steps, BLK, BLK), lambda i: (i, 0, 0)))

    if low is not None:
        count = low.shape[0] // 2
        for start in range(2):
            part(low, count, start)
            part(came, count, start)
            out(count)
    if kept is not None:
        for array in (kept, last) if passed is None else (kept, last, passed):
            part(array, kept.shape[0], 0)
        out(kept.shape[0])
    body = functools.partial(merge_body, low is not None, kept is not None, passed is not None)
    return pl.pallas_call(
        body,
        grid=(steps,),
        in_specs=specs,
        out_specs=outs,
        out_shape=shapes,
        compiler_params=params(46),
        cost_estimate=cost(0, 6 * MIB),
        name="merge_sums",
    )(*args)


def two_terms(values):
    high = values.astype(BF)
    return high, (values - high.astype(F32)).astype(BF)


def update_body(count, *refs):
    parts = refs[:count]
    m_ref, sl_ref, sr_ref, rl_ref, rr_ref, g_out, sl_out, sr_out, m_out = refs[count:]

    def long_left(terms, axis):
        return jnp.concatenate([terms[0], terms[0], terms[1]], axis)

    def long_right(terms, axis):
        return jnp.concatenate([terms[0], terms[1], terms[0]], axis)

    count = range(g_out.shape[0])
    totals = [sum(part[i].astype(F32) for part in parts) for i in count]
    grads = [two_terms(total) for total in totals]
    talls = [long_right(grad, 0) for grad in grads]
    inners = [mul_nn(long_left(two_terms(rl_ref[i]), 1), talls[i]) for i in count]
    for i in count:
        g_out[i] = totals[i]
        sl_out[i] = sl_ref[i] + mul_nt(long_left(grads[i], 1), long_right(grads[i], 1))
    directions = [
        mul_nn(long_left(two_terms(inners[i]), 1), long_right(two_terms(rr_ref[i]), 0))
        for i in count
    ]
    for i in count:
        sr_out[i] = sr_ref[i] + mul_tn(long_left(grads[i], 0), talls[i])
    for i in count:
        master, direction = m_ref[i], directions[i]
        scale = jnp.sqrt(jnp.mean(master * master, keepdims=True) + 1e-06)
        scale = scale * lax.rsqrt(jnp.mean(direction * direction, keepdims=True) + 1e-06)
        m_out[i] = master - 0.3 * scale * direction


def update(parts, master, stat_left, stat_right, root_left, root_right):
    count = master.shape[0]
    group = 6 if count % 6 == 0 else 1
    block = pl.BlockSpec((group, BLK, BLK), lambda i: (i, 0, 0))
    shape = jax.ShapeDtypeStruct(master.shape, F32)
    return pl.pallas_call(
        functools.partial(update_body, len(parts)),
        grid=(count // group,),
        in_specs=[block] * (len(parts) + 5),
        out_specs=[block] * 4,
        out_shape=[shape] * 4,
        compiler_params=params(),
        cost_estimate=cost(48 * count * BLK**3, 15 * MIB),
        name="block_update",
    )(*parts, master, stat_left, stat_right, root_left, root_right)


def pair_moves():
    moves_same, moves_cross = [], []
    for z in range(4):
        for c in range(2):
            for moves, bit in ((moves_same, z % 2), (moves_cross, 1 - z % 2)):
                moves.append((z * 2 + c, (2 * c + bit) * 2 + z // 2))
    return moves_same, moves_cross


def row_part(values, which):
    return lax.dynamic_index_in_dim(values, which, 0, False)


def move_rows(values, crossed, back=False):
    moves = pair_moves()[crossed]
    return lax.ppermute(values, ("seq", "core"), [(b, a) for a, b in moves] if back else moves)


def in_order(kept, crossed, parity):
    return jnp.where(parity == 0, kept, crossed), jnp.where(parity == 0, crossed, kept)


def spread_rows(values, parity):
    kept = move_rows(row_part(values, parity), False)
    crossed = move_rows(row_part(values, 1 - parity), True)
    return jnp.concatenate(in_order(kept, crossed, parity), 0)


def swap_cores(values):
    return lax.ppermute(values, "core", [(0, 1), (1, 0)])


def chip_orders(chips):
    bits = [1 << i for i in range(chips.bit_length() - 1)]
    return bits, bits[::-1]


def offsets(order):
    result = [0]
    for bit in order:
        result = result + [o ^ bit for o in result]
    return result


def place_lists(chips, owned, planes):
    shape = (2, planes, chips, owned)
    by_core = np.array([offsets(order) for order in chip_orders(chips)], np.int32)
    grid = np.indices(shape).astype(np.int32).reshape(4, 2, -1)
    offset = np.broadcast_to(by_core[:, None, :, None], shape).reshape(2, -1)
    return grid[1, 0], offset, grid[3, 0]


def arrival_order(chips, owned, planes):
    per_plane, quarter = chips * owned, owned
    if chips != 4:
        return np.arange(planes * per_plane)
    pieces = [(0, 0)]
    for k in range(1, planes + 1):
        pieces += [(k, 0)] if k < planes else []
        pieces += [(k - 1, 1), (k - 1, 2)]
        pieces += [(k - 2, 3)] if k > 1 else []
    pieces.append((planes - 1, 3))
    starts = [k * per_plane + r * quarter for k, r in pieces]
    return np.concatenate([np.arange(start, start + quarter) for start in starts])


def swap_chips(values, bits):
    chips = lax.axis_size("chip")
    moves = [(i * 2 + c, (i ^ bits[c]) * 2 + c) for i in range(chips) for c in range(2)]
    return lax.ppermute(values, ("chip", "core"), moves)


def move_planes(values, shift):
    planes = lax.axis_size("seq")
    return lax.ppermute(values, "seq", [(i, (i + shift) % planes) for i in range(planes)])


def after(value, *deps):
    return lax.optimization_barrier((value, *deps))[0]


def together(*values):
    return lax.optimization_barrier(values)


def chip_steps():
    return list(zip(*chip_orders(lax.axis_size("chip"))))


def finish_pieces(pieces):
    for bits in chip_steps()[2:]:
        joined = jnp.concatenate(pieces, 0)
        pieces = [joined, swap_chips(joined, bits)]
    return pieces


def add_halves(kept, came):
    return (kept.astype(F32) + came.astype(F32)).astype(BF)


def pack_terms(values):
    high = lax.optimization_barrier(values.astype(BF))
    low = (values - high.astype(F32)).astype(BF)
    terms = jnp.stack([high, low]).reshape(-1, BLK)
    return jnp.pad(terms, ((0, BLK - terms.shape[0]), (0, 0)))[None]


def unpack_terms(blocks, shape):
    terms = blocks.reshape(-1, BLK, BLK)[:, : 2 * shape[0] * shape[1] // BLK]
    terms = terms.reshape(-1, 2, *shape).astype(F32)
    return terms[:, 0] + terms[:, 1]


def finish_sums(keep, send):
    for bits in chip_steps()[::-1][1:-1]:
        count = keep.shape[0] // 2
        came = swap_chips(send, bits)
        send = add_halves(keep[count:], came[count:])
        keep = add_halves(keep[:count], came[:count])
    return keep, send


def by_chip(riders, me, core):
    chips = lax.axis_size("chip")
    ranks = np.array([np.argsort(offsets(order[::-1])) for order in chip_orders(chips)], np.int32)
    rank = jnp.asarray(ranks)[core][me ^ jnp.arange(chips, dtype=jnp.int32)]
    return riders.reshape(chips, -1, BLK, BLK)[rank]


def local(
    tokens,
    cotangent,
    lengths,
    owner_perm,
    master,
    norm_gains,
    stat_left,
    stat_right,
    root_left,
    root_right,
    moment_first,
    moment_second,
):
    core = lax.axis_index("core")
    place_z = lax.axis_index("seq")
    parity = place_z % 2
    block_count = owner_perm.shape[0]
    owned = master.shape[0]
    half = block_count // 2

    chips, planes = lax.axis_size("chip"), lax.axis_size("seq")
    me = lax.axis_index("chip")

    pair_lengths = jnp.stack([lengths, swap_cores(lengths)])
    pair_lengths = jnp.where(core == 0, pair_lengths, pair_lengths[::-1]).reshape(-1)
    length = lax.dynamic_index_in_dim(pair_lengths, place_z, 0, False)
    span = tokens.shape[0] * tokens.shape[1]
    live = jnp.stack([length - core * span, length - (1 - core) * span, length - core * span, parity])

    distance, offset, slot = place_lists(chips, owned, planes)
    offset = jnp.where(core == 0, offset, offset[::-1])
    device = ((place_z - distance) % planes * chips + (me ^ offset)) * 2
    device = device + jnp.stack([core, 1 - core])[:, None]
    table = owner_perm[(device * owned + slot).reshape(-1)]
    sums_table = jnp.asarray(source_numbers())[table[:half]]
    arrive = arrival_order(chips, owned, planes)
    near_slots, far_slots = device * owned + slot
    table = owner_perm[jnp.concatenate([near_slots[arrive], far_slots[arrive]])]

    shard = master.astype(BF)
    first_bits, second_bits = chip_steps()[:2]
    per_plane = chips * owned
    by_phase = chips == 4
    rows = (row_part(tokens, parity), row_part(tokens, 1 - parity))
    cross, held, weights, first = None, (), None, 0
    came, turned = swap_chips(shard, first_bits), swap_chips(shard, second_bits)
    next_shard = move_planes(shard, 1)
    pieces = [[shard, came, turned]]

    def place(parts, first, weights):
        others = [swap_cores(part) for part in parts]
        weights = place_blocks(table, first, parts, others, weights)
        return weights, first + sum(part.shape[0] for part in parts)

    for k in range(1, planes):
        ready = () if k == 1 else (cross, *held, live, table, sums_table)
        ready = ready if weights is None else (*ready, weights)
        this_shard, came, turned, row_a, row_b, *done = together(
            next_shard, came, turned, *rows, *ready
        )
        if k > 1:
            pieces[k - 2].append(done[0])
        cross = swap_chips(came, second_bits)
        arrived = [this_shard, came, turned, *(pieces[0][:1] if k == 1 else done[:1])]
        arrived = arrived[3:] + arrived[:3] if k == 1 else arrived
        pieces[k - 1][1:] = [came, turned]
        came, turned = swap_chips(this_shard, first_bits), swap_chips(this_shard, second_bits)
        pieces.append([this_shard, came, turned])
        if k < planes - 1:
            next_shard = move_planes(this_shard, 1)
        else:
            row_same = move_rows(row_a, False)
            row_cross = move_rows(after(row_b, row_same), True)
        if by_phase:
            if k > 1:
                weights, first = place(done[1:2], first, weights)
            held = (jnp.concatenate(arrived, 0),)
    came, turned, done, row_same, row_cross, *held = together(
        came, turned, cross, row_same, row_cross, *held, *([] if weights is None else [weights])
    )
    own_tokens = jnp.concatenate(in_order(row_same, row_cross, parity), 0)
    pieces[-2].append(done)
    pieces[-1][1:] = [came, turned, swap_chips(came, second_bits)]
    normed1, normed1_t = norm_tokens(own_tokens, norm_gains)
    if by_phase:
        weights, first = place(held[:1], first, weights)
        parts = [came, turned, done]
        others = [swap_cores(part) for part in parts]
        last, normed1, *_ = together(pieces[-1][-1], normed1, weights, *others)
        weights = place_blocks(table, first, parts, others, weights)
        first += 3 * owned
        other_normed = swap_cores(normed1)
        weights, _ = place([last], first, weights)
    else:
        for each in pieces:
            each = [jnp.concatenate(finish_pieces(each), 0)]
            weights, first = place(each, first, weights)
        other_normed = swap_cores(normed1)
    own_cot = spread_rows(after(cotangent, weights), parity)

    own_qkv, other_kv = project(normed1, other_normed, weights)
    attended, q_aug = attend(live, own_qkv, other_kv)
    kept, crossed, g_rest, grad_middle, grad_attended, gain_second = feed(
        live, own_tokens, attended, own_cot, norm_gains, weights
    )
    other_rest = swap_cores(g_rest)
    kept, crossed = move_rows(kept, False, True), move_rows(crossed, True, True)
    layer_out = jnp.stack(in_order(kept, crossed, parity), 0)
    d_query, d_own, d_other = attend_back(live, q_aug, own_qkv, other_kv, attended, grad_attended)
    received = swap_cores(after(d_other, kept, crossed))
    flat = lambda g: g.reshape(-1, BLK, BLK)
    g_query, partial = query_back(normed1_t, d_query, weights)
    g_query = flat(g_query)
    other_query = swap_cores(g_query)
    g_kv, back = input_back(normed1_t, d_own, received, partial, weights)
    g_kv = flat(g_kv)
    other_kv_grad = swap_cores(after(g_kv, other_query))
    own_grads = (g_query, g_kv, g_rest)
    other_grads = (other_query, other_kv_grad, other_rest)
    half_plane = per_plane // 2
    last_bits, before_bits = chip_steps()[-1], chip_steps()[0]
    moved_rows, lows, sent, passed, riders_z = [], [], None, None, []

    def sums(k, part, held):
        first = k * per_plane + part * half_plane
        return gather_sums(held, first, half_plane, own_grads, other_grads)

    order = list(range(planes))[::-1]
    high = sums(order[0], 1, sums_table)
    held = sums_table
    held_riders = []
    for turn in range(planes + 1):
        group, moves = [], []
        if turn < planes:
            group.append(high)
            moves.append(lambda v: swap_chips(v, last_bits))
        if 1 <= turn <= planes:
            group.append(sent)
            moves.append(lambda v: swap_chips(v, before_bits))
        if 2 <= turn <= planes:
            group.append(part)
            moves.append(lambda v: move_planes(v, -1))
        if turn in (1, 2):
            group.append(riders)
            bits = last_bits if turn == 1 else before_bits
            moves.append(lambda v: swap_chips(v, bits))
        if turn in (1, 2):
            group.append(rows[turn - 1])
            crossed = turn == 2
            moves.append(lambda v: move_rows(v, crossed, True))
        far_riders = [1, 2] if turn == planes - 1 else []
        group += [rider for _ in far_riders]
        moves += [functools.partial(move_planes, shift=-k) for k in far_riders]
        came = [move(value) for move, value in zip(moves, together(*group, *moved_rows, *held_riders))]
        if turn in (1, 2):
            moved_rows.append(came.pop())
            riders = jnp.concatenate([riders, came.pop()], 0)
            for bits in chip_steps()[::-1][1:-1] if turn == 1 else ():
                riders = jnp.concatenate([riders, swap_chips(riders, bits)], 0)
        count = len(came) - len(far_riders)
        riders_z, came = riders_z + came[count:], came[:count]
        if far_riders:
            riders_z += [move_planes(after(rider, *riders_z), -k) for k in range(3, planes)]
        if turn == planes:
            parts = [keep_before, *came]
            continue
        passed = came.pop() if turn >= 2 else None
        low = sums(order[turn], 0, after(held, high))
        if turn + 1 < planes:
            high = sums(order[turn + 1], 1, after(held, low))
        held = after(sums_table, *came)
        held_riders = [riders] if turn == 2 else []
        if turn == 0:
            kept, crossed, gain_first = input_end(
                live, own_tokens, norm_gains, after(back, high), grad_middle
            )
            rows = [kept, crossed]
            gain_part = jnp.concatenate([gain_first, gain_second], 0)
            mine = pack_terms(gain_part)
            pair = jnp.concatenate([mine, swap_cores(mine)], 0)
            riders = jnp.where(core == 0, pair, pair[::-1])
        if turn == 2:
            plane_gain = by_chip(riders, me, core)
            plane_gain = jnp.sum(unpack_terms(plane_gain, gain_part.shape), 0)
            rider = pack_terms(plane_gain)
        second = (None, None, None) if turn == 0 else (keep_before, came[-1], passed)
        keep, sent, *part = merge_sums(low, came[0], *second)
        part = part[0] if part else None
        keep_before, sent = finish_sums(keep, sent)
    input_grad = jnp.stack(in_order(*moved_rows, parity), 0).astype(F32)
    planes_gain = [unpack_terms(each, gain_part.shape)[0] for each in (rider, *riders_z)]
    turned = (jnp.arange(planes, dtype=jnp.int32) - place_z) % planes
    gain_grad = jnp.sum(jnp.stack(planes_gain)[turned], 0)
    grad_blocks, stat_left_new, stat_right_new, master_new = update(
        parts, master, stat_left, stat_right, root_left, root_right
    )
    first_new = 0.9 * moment_first + 0.1 * gain_grad
    second_new = 0.999 * moment_second + 0.001 * gain_grad * gain_grad
    first_hat = first_new / (1.0 - 0.9**STEP)
    second_hat = second_new / (1.0 - 0.999**STEP)
    gains_new = norm_gains - 0.5 * first_hat / (jnp.sqrt(second_hat) + 1e-08)
    return (
        layer_out,
        input_grad,
        grad_blocks,
        stat_left_new,
        stat_right_new,
        master_new,
        first_new,
        second_new,
        gains_new,
    )


def solution(mesh):
    seq_size, rows_size = mesh.shape["seq"], mesh.shape["rows"]
    mesh = Mesh(mesh.devices.reshape(seq_size, rows_size // 2, 2), ("seq", "chip", "core"))
    activation = P(("chip", "core"), "seq", None)
    blocks = P(("seq", "chip", "core"), None, None)
    return jax.shard_map(
        local,
        mesh=mesh,
        in_specs=(
            activation, activation, P(("chip", "core")), P(), blocks, P(),
            blocks, blocks, blocks, blocks, P(), P(),
        ),
        out_specs=(activation, activation, blocks, blocks, blocks, blocks, P(), P(), P()),
        check_vma=False,
    )
```

```python
import functools
import jax
import jax.numpy as jnp
import numpy as np
from jax import lax
from jax.experimental import pallas as pl
from jax.experimental.pallas import tpu as pltpu
from jax.sharding import Mesh
from jax.sharding import PartitionSpec as P

D = 1024
HD = 64
FF = 4096
BLK = 128
STEP = 10
COLS = 1024
BF = jnp.bfloat16
F32 = jnp.float32
MIB = 1024 * 1024

norm_eps = 1e-05
score_scale = 0.125
masked_score = -1e30


def params(limit=56):
    return pltpu.CompilerParams(vmem_limit_bytes=limit * MIB)


def cost(flops, nbytes):
    return pl.CostEstimate(flops=int(flops), bytes_accessed=int(nbytes), transcendentals=0)


def mul_nn(left, right):
    return jnp.dot(left, right, preferred_element_type=F32)


def mul_nt(left, right):
    return lax.dot_general(left, right, (((1,), (1,)), ((), ())), preferred_element_type=F32)


def mul_tn(left, right):
    return lax.dot_general(left, right, (((0,), (0,)), ((), ())), preferred_element_type=F32)


def join_tile(ref):
    rows, cols = ref.shape[0], ref.shape[1]
    return jnp.concatenate([ref[:, j].reshape(rows * BLK, BLK) for j in range(cols)], axis=1)


def split_tile(ref, matrix):
    rows, cols = ref.shape[0], ref.shape[1]
    for j in range(cols):
        ref[:, j] = matrix[:, j * BLK : (j + 1) * BLK].reshape(rows, BLK, BLK).astype(ref.dtype)


def split_flat(ref, matrix):
    cols = matrix.shape[1] // BLK
    for i in range(matrix.shape[0] // BLK):
        for j in range(cols):
            block = matrix[i * BLK : (i + 1) * BLK, j * BLK : (j + 1) * BLK]
            ref[i * cols + j] = block.astype(ref.dtype)


def normalize(values):
    row_mean = jnp.mean(values, -1, keepdims=True)
    centered = values - row_mean
    row_var = jnp.mean(centered * centered, -1, keepdims=True)
    inv_std = lax.rsqrt(row_var + norm_eps)
    return centered * inv_std, inv_std


def gelu_parts(hidden):
    bell = jnp.exp(hidden * hidden * -0.5)
    t = 1.0 / (1.0 + jnp.abs(hidden) * (0.3275911 * 0.7071067811865476))
    poly = 1.061405429 * t - 1.453152027
    for term in (1.421413741, -0.284496736, 0.254829592):
        poly = poly * t + term
    tail = poly * t * 0.5 * bell
    return jnp.where(hidden < 0.0, tail, 1.0 - tail), hidden * bell * 0.3989422804014327


def norm_back(gradient, unit_vals, inv_std):
    grad_mean = jnp.mean(gradient, -1, keepdims=True)
    cross_mean = jnp.mean(gradient * unit_vals, -1, keepdims=True)
    return inv_std * (gradient - grad_mean - unit_vals * cross_mean)


def place_body(first, pieces, table, *refs):
    near, far = refs[:pieces], refs[pieces : 2 * pieces]
    out_ref, sem = refs[-2:]
    total = 0
    for start, sources in ((first, near), (table.shape[0] // 2 + first, far)):
        for src in sources:
            for slot in range(src.shape[0]):
                pltpu.make_async_copy(src.at[slot], out_ref.at[table[start + slot]], sem).start()
            start += src.shape[0]
            total += src.shape[0]
    done = out_ref.at[pl.ds(0, total)]
    pltpu.make_async_copy(done, done, sem).wait()


def place_blocks(table, first, near, far, kept):
    smem = pl.BlockSpec(memory_space=pltpu.SMEM)
    hbm = pl.BlockSpec(memory_space=pltpu.HBM)
    vmem = pl.BlockSpec(memory_space=pltpu.VMEM)
    kept = () if kept is None else (kept,)
    count = 2 * len(near)
    return pl.pallas_call(
        functools.partial(place_body, first, len(near)),
        out_shape=jax.ShapeDtypeStruct((table.shape[0], BLK, BLK), BF),
        in_specs=[smem] + [vmem] * count + [hbm] * len(kept),
        out_specs=hbm,
        scratch_shapes=[pltpu.SemaphoreType.DMA],
        input_output_aliases={1 + count: 0} if kept else {},
        compiler_params=params(46),
        cost_estimate=cost(0, 6 * MIB),
        name="place_weights",
    )(table, *near, *far, *kept)


def norm_body(tokens_ref, gains_ref, out_ref, turned_ref):
    normed = normalize(tokens_ref[...].astype(F32))[0] * gains_ref[0:1]
    out_ref[...] = normed.astype(BF)
    turned_ref[...] = normed.T.astype(BF)


def norm_tokens(tokens, gains):
    span = tokens.shape[0]
    steps = 4
    part = pl.BlockSpec((span // steps, D), lambda i: (i, 0))
    return pl.pallas_call(
        norm_body,
        grid=(steps,),
        in_specs=[part, pl.BlockSpec((2, D), lambda i: (0, 0))],
        out_specs=[part, pl.BlockSpec((D, span // steps), lambda i: (0, i))],
        out_shape=[jax.ShapeDtypeStruct((span, D), BF), jax.ShapeDtypeStruct((D, span), BF)],
        compiler_params=params(46),
        cost_estimate=cost(0, 3 * MIB),
        name="norm_tokens",
    )(tokens, gains)


def qkv_body(own_ref, other_ref, w_ref, own_out, other_out):
    step = pl.program_id(0)
    weight = join_tile(w_ref)
    own_out[...] = mul_nn(own_ref[...], weight).astype(BF)

    @pl.when(step >= D // COLS)
    def _():
        other_out[...] = mul_nn(other_ref[...], weight).astype(BF)


def project(own, other, weights):
    span = own.shape[0]
    skip = D // COLS
    once = pl.BlockSpec((span, D), lambda j: (0, 0))
    return pl.pallas_call(
        qkv_body,
        grid=(3 * D // COLS,),
        in_specs=[
            once,
            once,
            pl.BlockSpec((D // BLK, COLS // BLK, BLK, BLK), lambda j: (0, j, 0, 0)),
        ],
        out_specs=[
            pl.BlockSpec((span, COLS), lambda j: (0, j)),
            pl.BlockSpec((span, COLS), lambda j: (0, jnp.maximum(j - skip, 0))),
        ],
        out_shape=[
            jax.ShapeDtypeStruct((span, 3 * D), BF),
            jax.ShapeDtypeStruct((span, 2 * D), BF),
        ],
        compiler_params=params(),
        cost_estimate=cost(10 * span * D * D, 12 * MIB),
        name="qkv_projection",
    )(own, other, weights.reshape(-1, 3 * D // BLK, BLK, BLK))


def lane_masks(head):
    lane = lax.broadcasted_iota(jnp.int32, (1, BLK), 1)
    first = HD * (1 - head)
    keep = (lane // HD == head).astype(F32)
    dead_lane = (lane == first).astype(F32)
    terms = [(lane == first + 1 + i).astype(F32) for i in range(3)]
    return keep, dead_lane, terms


def three_terms(values):
    high = values.astype(BF).astype(F32)
    rest = values - high
    middle = rest.astype(BF).astype(F32)
    return high, middle, rest - middle


def key_bias(span, live_count):
    row = lax.broadcasted_iota(jnp.int32, (span, 1), 0)
    return jnp.where(row < live_count, 0.0, masked_score).astype(F32)


def attend_body(live_ref, q_ref, ko_ref, vo_ref, kx_ref, vx_ref, out_ref, aug_ref):
    span = q_ref.shape[0]
    bias_own = key_bias(span, live_ref[0])
    bias_other = key_bias(span, live_ref[1])
    queries = q_ref[...].astype(F32) * score_scale
    k_own, k_other = ko_ref[...].astype(F32), kx_ref[...].astype(F32)
    v_own_f, v_other_f = vo_ref[...].astype(F32), vx_ref[...].astype(F32)
    results, scores = [], []
    for head in range(2):
        keep, dead_lane, _ = lane_masks(head)
        q_head = (queries * keep + dead_lane).astype(BF)
        s_own = mul_nt(q_head, (k_own * keep + bias_own * dead_lane).astype(BF))
        s_other = mul_nt(q_head, (k_other * keep + bias_other * dead_lane).astype(BF))
        scores.append((q_head, s_own, s_other))
    for head in range(2):
        keep, _, terms = lane_masks(head)
        q_head, s_own, s_other = scores[head]
        top = jnp.max(jnp.maximum(s_own, s_other), -1, keepdims=True)
        p_own = jnp.exp(s_own - top)
        p_other = jnp.exp(s_other - top)
        v_own = (v_own_f * keep + (1.0 - keep)).astype(BF)
        v_other = (v_other_f * keep + (1.0 - keep)).astype(BF)
        mixed = mul_nn(p_own.astype(BF), v_own) + mul_nn(p_other.astype(BF), v_other)
        total = mixed[:, HD * (1 - head) : HD * (1 - head) + 1]
        results.append(mixed / total * keep)
        parts = three_terms(-(top + jnp.log(total)))
        stats = sum(part * lane for part, lane in zip(parts, terms))
        aug_ref[:, head * BLK : (head + 1) * BLK] = (q_head.astype(F32) + stats).astype(BF)
    out_ref[...] = (results[0] + results[1]).astype(BF)


def attend(live, own, other):
    span = own.shape[0]
    pairs = D // BLK
    col = lambda shift: pl.BlockSpec((span, BLK), lambda p: (0, p + shift))
    return pl.pallas_call(
        attend_body,
        grid=(pairs,),
        in_specs=[
            pl.BlockSpec(memory_space=pltpu.SMEM),
            col(0),
            col(pairs),
            col(2 * pairs),
            col(0),
            col(pairs),
        ],
        out_specs=[col(0), pl.BlockSpec((span, 2 * BLK), lambda p: (0, p))],
        out_shape=[
            jax.ShapeDtypeStruct((span, D), BF),
            jax.ShapeDtypeStruct((span, 2 * D), BF),
        ],
        compiler_params=params(),
        cost_estimate=cost(40 * span * span * D, 8 * MIB),
        name="attention",
    )(live, own, own, own, other, other)


def attend_back_body(
    live_ref, aug_ref, ko_ref, vo_ref, kx_ref, vx_ref, at_ref, g_ref, dq_ref, own_ref, other_ref
):
    span = at_ref.shape[0]
    grads = g_ref[...].astype(F32)
    product = grads * at_ref[...].astype(F32)
    keeps, g_augs, q_augs = [], [], []
    for head in range(2):
        keep, dead_lane, terms = lane_masks(head)
        delta = jnp.sum(product * keep, -1, keepdims=True)
        parts = three_terms(-delta)
        stats = sum(part * lane for part, lane in zip(parts, terms))
        g_augs.append((grads * keep + stats).astype(BF))
        q_augs.append(aug_ref[:, head * BLK : (head + 1) * BLK])
    d_query = [None, None]
    for k_ref, v_ref, out_ref, live in (
        (ko_ref, vo_ref, own_ref, live_ref[0]),
        (kx_ref, vx_ref, other_ref, live_ref[1]),
    ):
        bias = key_bias(span, live)
        keys = k_ref[...]
        keys_f, values_f = keys.astype(F32), v_ref[...].astype(F32)
        d_keys = d_values = None
        for head in range(2):
            keep, dead_lane, terms = lane_masks(head)
            ones = terms[0] + terms[1] + terms[2]
            k_aug = (keys_f * keep + (bias * dead_lane + ones)).astype(BF)
            v_aug = (values_f * keep + ones).astype(BF)
            probs = jnp.exp(mul_nt(k_aug, q_augs[head]))
            d_scores = (probs * mul_nt(v_aug, g_augs[head])).astype(BF)
            value_part = mul_nn(probs.astype(BF), g_augs[head]) * keep
            key_part = mul_nn(d_scores, q_augs[head]) * keep
            query_part = mul_tn(keys, d_scores)[head * HD : (head + 1) * HD]
            d_query[head] = query_part if d_query[head] is None else d_query[head] + query_part
            d_values = value_part if d_values is None else d_values + value_part
            d_keys = key_part if d_keys is None else d_keys + key_part
        out_ref[0] = d_keys.astype(out_ref.dtype)
        out_ref[1] = d_values.astype(out_ref.dtype)
    dq_ref[...] = (jnp.concatenate(d_query, 0).T * score_scale).astype(BF)


def attend_back(live, aug, own, other, attended, grads):
    span = own.shape[0]
    pairs = D // BLK
    col = lambda shift: pl.BlockSpec((span, BLK), lambda p: (0, p + shift))
    pair_out = pl.BlockSpec((2, span, BLK), lambda p: (0, 0, p))
    return pl.pallas_call(
        attend_back_body,
        grid=(pairs,),
        in_specs=[
            pl.BlockSpec(memory_space=pltpu.SMEM),
            pl.BlockSpec((span, 2 * BLK), lambda p: (0, p)),
            col(pairs),
            col(2 * pairs),
            col(0),
            col(pairs),
            col(0),
            col(0),
        ],
        out_specs=[col(0), pair_out, pair_out],
        out_shape=[
            jax.ShapeDtypeStruct((span, D), BF),
            jax.ShapeDtypeStruct((2, span, D), BF),
            jax.ShapeDtypeStruct((2, span, D), BF),
        ],
        compiler_params=params(),
        cost_estimate=cost(60 * span * span * D, 12 * MIB),
        name="attention_backward",
    )(live, aug, own, own, other, other, attended, grads)


def feed_body(
    live_ref,
    tokens_ref,
    attended_ref,
    kept_cot_ref,
    crossed_cot_ref,
    gains_ref,
    wo_ref,
    wu_ref,
    wd_ref,
    kept_ref,
    crossed_ref,
    rest_ref,
    gm_ref,
    ga_ref,
    gain_ref,
    unit,
    inv,
    normed,
    normed_t,
    top,
    acc_out,
    acc_back,
    up_stage,
    down_stage,
    out_stage,
    sems,
    out_sem,
):
    step = pl.program_id(0)
    place = step % 2
    side, width = up_stage.shape[1], up_stage.shape[2]
    per_tile = side * width
    up_first = side * side
    down_first = up_first + side * FF // BLK

    def drain(which):
        pltpu.make_async_copy(up_stage.at[which], up_stage.at[which], sems.at[0, which]).wait()
        pltpu.make_async_copy(down_stage.at[which], down_stage.at[which], sems.at[1, which]).wait()
    span = tokens_ref.shape[0]

    @pl.when(step == 0)
    def _():
        weight = join_tile(wo_ref)
        middle = tokens_ref[...].astype(F32) + mul_nn(attended_ref[...], weight)
        unit_vals, inv_std = normalize(middle)
        unit[...] = unit_vals
        inv[...] = inv_std
        normed_vals = unit_vals * gains_ref[1:2]
        normed[...] = normed_vals.astype(BF)
        normed_t[...] = normed_vals.T.astype(BF)
        half = span // 2
        row = lax.broadcasted_iota(jnp.int32, (half, 1), 0)
        for ref, crossed in ((kept_cot_ref, 0), (crossed_cot_ref, 1)):
            for flip in range(2):
                start = half * (flip ^ crossed)

                @pl.when(live_ref[3] == flip)
                def _():
                    keep = row + start < live_ref[2]
                    part = jnp.where(keep, ref[...].astype(F32), 0.0)
                    top[start : start + half] = part.astype(BF)

        acc_out[...] = middle
        acc_back[...] = jnp.zeros_like(acc_back)

    w_up = join_tile(wu_ref)
    w_down = join_tile(wd_ref)
    hidden = mul_nn(normed[...], w_up)
    grad_act = mul_nt(top[...], w_down)
    share, slope_rest = gelu_parts(hidden)
    activated = (hidden * share).astype(BF)
    grad_hidden = (grad_act * (share + slope_rest)).astype(BF)
    acc_out[...] += mul_nn(activated, w_down)
    acc_back[...] += mul_nt(grad_hidden, w_up)

    @pl.when(step >= 2)
    def _():
        drain(place)

    split_flat(down_stage.at[place], mul_tn(activated, top[...]))
    dest = rest_ref.at[pl.ds(down_first + step * per_tile, per_tile)]
    pltpu.make_async_copy(down_stage.at[place], dest, sems.at[1, place]).start()
    split_tile(up_stage.at[place], mul_nn(normed_t[...], grad_hidden))
    for i in range(side):
        dest = rest_ref.at[pl.ds(up_first + i * (FF // BLK) + step * width, width)]
        pltpu.make_async_copy(up_stage.at[place, i], dest, sems.at[0, place]).start()

    @pl.when(step == pl.num_programs(0) - 1)
    def _():
        for flip in range(2):

            @pl.when(live_ref[3] == flip)
            def _():
                for ref, part in ((kept_ref, flip), (crossed_ref, 1 - flip)):
                    ref[...] = acc_out[part * (span // 2) : (part + 1) * (span // 2)].astype(BF)

        unit_vals = unit[...]
        back = acc_back[...]
        gain_ref[...] = jnp.sum(back * unit_vals, 0, keepdims=True)
        grad_middle = top[...].astype(F32) + norm_back(back * gains_ref[1:2], unit_vals, inv[...])
        gm_ref[...] = grad_middle
        back_middle = grad_middle.astype(BF)
        split_flat(out_stage, mul_tn(attended_ref[...], back_middle))
        out_copy = pltpu.make_async_copy(out_stage, rest_ref.at[pl.ds(0, up_first)], out_sem)
        out_copy.start()
        ga_ref[...] = mul_nt(back_middle, join_tile(wo_ref)).astype(BF)
        drain(1 - place)
        drain(place)
        out_copy.wait()


def feed(live, tokens, attended, kept_cot, crossed_cot, gains, weights):
    span = tokens.shape[0]
    side, width = D // BLK, COLS // BLK
    whole = lambda j: (0, 0)
    act = pl.BlockSpec((span, D), whole)
    once = pl.BlockSpec((span, D), whole, pipeline_mode=pl.Buffered(1))
    half_act = pl.BlockSpec((span // 2, D), whole)
    per_row = weights.reshape(-1, side, BLK, BLK)
    per_up = weights.reshape(-1, FF // BLK, BLK, BLK)
    out_row = (3 * side * side) // side // side
    up_row = 4 * side * side // (FF // BLK) // side
    down_row = (4 * side * side + side * FF // BLK) // side // width
    return pl.pallas_call(
        feed_body,
        grid=(FF // COLS,),
        in_specs=[
            pl.BlockSpec(memory_space=pltpu.SMEM),
            once,
            once,
            half_act,
            half_act,
            pl.BlockSpec((2, D), whole),
            pl.BlockSpec(
                (side, side, BLK, BLK),
                lambda j: (out_row, 0, 0, 0),
                pipeline_mode=pl.Buffered(1),
            ),
            pl.BlockSpec((side, width, BLK, BLK), lambda j: (up_row, j, 0, 0)),
            pl.BlockSpec((width, side, BLK, BLK), lambda j: (down_row + j, 0, 0, 0)),
        ],
        out_specs=[
            half_act,
            half_act,
            pl.BlockSpec(memory_space=pltpu.HBM),
            act,
            act,
            pl.BlockSpec((1, D), whole),
        ],
        out_shape=[
            jax.ShapeDtypeStruct((span // 2, D), BF),
            jax.ShapeDtypeStruct((span // 2, D), BF),
            jax.ShapeDtypeStruct((side * side + 2 * side * (FF // BLK), BLK, BLK), BF),
            jax.ShapeDtypeStruct((span, D), F32),
            jax.ShapeDtypeStruct((span, D), BF),
            jax.ShapeDtypeStruct((1, D), F32),
        ],
        scratch_shapes=[
            pltpu.VMEM((span, D), F32),
            pltpu.VMEM((span, 1), F32),
            pltpu.VMEM((span, D), BF),
            pltpu.VMEM((D, span), BF),
            pltpu.VMEM((span, D), BF),
            pltpu.VMEM((span, D), F32),
            pltpu.VMEM((span, D), F32),
            pltpu.VMEM((2, side, width, BLK, BLK), BF),
            pltpu.VMEM((2, side * width, BLK, BLK), BF),
            pltpu.VMEM((side * side, BLK, BLK), BF),
            pltpu.SemaphoreType.DMA((2, 2)),
            pltpu.SemaphoreType.DMA,
        ],
        compiler_params=params(),
        cost_estimate=cost(14 * span * D * FF, 50 * MIB),
        name="feed_forward",
    )(live, tokens, attended, kept_cot, crossed_cot, gains, per_row, per_up, per_row)


def query_body(normed_t, dq_ref, w_ref, grad_ref, acc_ref):
    step = pl.program_id(0)

    @pl.when(step == 0)
    def _():
        acc_ref[...] = jnp.zeros_like(acc_ref)

    grad = dq_ref[...]
    acc_ref[...] += mul_nt(grad, join_tile(w_ref))
    split_tile(grad_ref, mul_nn(normed_t[...], grad))


def query_back(normed1_t, d_query, weights):
    span = normed1_t.shape[1]
    side, width = D // BLK, COLS // BLK
    whole = lambda j: (0, 0)
    act = pl.BlockSpec((span, D), whole)
    tile = pl.BlockSpec((side, width, BLK, BLK), lambda j: (0, j, 0, 0))
    return pl.pallas_call(
        query_body,
        grid=(D // COLS,),
        in_specs=[
            pl.BlockSpec((D, span), whole),
            pl.BlockSpec((span, COLS), lambda j: (0, j)),
            tile,
        ],
        out_specs=[tile, act],
        out_shape=[
            jax.ShapeDtypeStruct((side, side, BLK, BLK), BF),
            jax.ShapeDtypeStruct((span, D), F32),
        ],
        compiler_params=params(),
        cost_estimate=cost(4 * span * D * D, 8 * MIB),
        name="query_backward",
    )(normed1_t, d_query, weights.reshape(-1, 3 * side, BLK, BLK))


def input_body(normed_t, own_ref, recv_ref, acc_ref, w_ref, grad_ref, out_ref):
    step = pl.program_id(0)

    @pl.when(step == 0)
    def _():
        out_ref[...] = acc_ref[...]

    grad = (own_ref[0].astype(F32) + recv_ref[0].astype(F32)).astype(BF)
    out_ref[...] += mul_nt(grad, join_tile(w_ref))
    split_tile(grad_ref, mul_nn(normed_t[...], grad))


def input_back(normed1_t, own, received, partial, weights):
    span = normed1_t.shape[1]
    side, width = D // BLK, COLS // BLK
    per = D // COLS
    whole = lambda j: (0, 0)
    act = pl.BlockSpec((span, D), whole)
    part = pl.BlockSpec((1, span, COLS), lambda j: (j // per, 0, j % per))
    return pl.pallas_call(
        input_body,
        grid=(2 * per,),
        in_specs=[
            pl.BlockSpec((D, span), whole),
            part,
            part,
            act,
            pl.BlockSpec((side, width, BLK, BLK), lambda j: (0, j + per, 0, 0)),
        ],
        out_specs=[pl.BlockSpec((side, width, BLK, BLK), lambda j: (0, j, 0, 0)), act],
        out_shape=[
            jax.ShapeDtypeStruct((side, 2 * side, BLK, BLK), BF),
            jax.ShapeDtypeStruct((span, D), F32),
        ],
        compiler_params=params(),
        cost_estimate=cost(8 * span * D * D, 20 * MIB),
        name="input_backward",
    )(normed1_t, own, received, partial, weights.reshape(-1, 3 * side, BLK, BLK))


def input_end_body(live_ref, tokens_ref, gains_ref, back_ref, gm_ref, kept_ref, crossed_ref, gain_ref):
    step = pl.program_id(0)
    unit_vals, inv_std = normalize(tokens_ref[...].astype(F32))
    back = back_ref[...]

    @pl.when(step == 0)
    def _():
        gain_ref[...] = jnp.zeros_like(gain_ref)

    gain_ref[...] += jnp.sum(back * unit_vals, 0, keepdims=True)
    grad = (gm_ref[...] + norm_back(back * gains_ref[0:1], unit_vals, inv_std)).astype(BF)
    half = step // (pl.num_programs(0) // 2)
    rows = tokens_ref.shape[0]
    start = pl.multiple_of(step % (pl.num_programs(0) // 2) * rows, rows)

    @pl.when(half == live_ref[3])
    def _():
        kept_ref[pl.ds(start, rows)] = grad

    @pl.when(half != live_ref[3])
    def _():
        crossed_ref[pl.ds(start, rows)] = grad


def input_end(live, tokens, gains, back, grad_middle):
    span = tokens.shape[0]
    steps = 4
    part = pl.BlockSpec((span // steps, D), lambda i: (i, 0))
    half_act = pl.BlockSpec((span // 2, D), lambda i: (0, 0))
    row = lambda count: pl.BlockSpec((count, D), lambda i: (0, 0))
    return pl.pallas_call(
        input_end_body,
        grid=(steps,),
        in_specs=[pl.BlockSpec(memory_space=pltpu.SMEM), part, row(2), part, part],
        out_specs=[half_act, half_act, row(1)],
        out_shape=[
            jax.ShapeDtypeStruct((span // 2, D), BF),
            jax.ShapeDtypeStruct((span // 2, D), BF),
            jax.ShapeDtypeStruct((1, D), F32),
        ],
        compiler_params=params(46),
        cost_estimate=cost(0, 7 * MIB),
        name="input_gradient",
    )(live, tokens, gains, back, grad_middle)


def source_numbers():
    side = D // BLK
    numbers = np.arange(3 * side * side + side * side + 2 * side * (FF // BLK), dtype=np.int32)
    row, col = np.divmod(numbers[: 3 * side * side], 3 * side)
    numbers[: 3 * side * side] = np.where(
        col < side, row * side + col, side * side + row * 2 * side + col - side
    )
    return numbers


def gather_body(first, bounds, table, *refs):
    sources = refs[:6]
    out_ref, stage, sems = refs[6:]
    step, steps = pl.program_id(0), pl.num_programs(0)
    count = stage.shape[1] // 2

    def fetch(which, slot):
        start = first + which * count
        for i in range(count):
            number = table[start + i]
            for low, high, own, other in zip(bounds, bounds[1:], sources[:3], sources[3:]):

                @pl.when((number >= low) & (number < high))
                def _():
                    for src, at in ((own, i), (other, count + i)):
                        pltpu.make_async_copy(
                            src.at[number - low], stage.at[slot, at], sems.at[slot]
                        ).start()

    @pl.when(step == 0)
    def _():
        fetch(0, 0)

    @pl.when(step + 1 < steps)
    def _():
        fetch(step + 1, (step + 1) % 2)

    slot = step % 2
    pltpu.make_async_copy(stage.at[slot], stage.at[slot], sems.at[slot]).wait()
    total = stage[slot, :count].astype(F32) + stage[slot, count:].astype(F32)
    out_ref[...] = total.astype(BF)


def gather_sums(table, first, count, own, other):
    hbm = pl.BlockSpec(memory_space=pltpu.HBM)
    steps = 4
    part = count // steps
    bounds = np.cumsum([0] + [src.shape[0] for src in own]).tolist()
    return pl.pallas_call(
        functools.partial(gather_body, first, bounds),
        grid=(steps,),
        in_specs=[pl.BlockSpec(memory_space=pltpu.SMEM)] + [hbm] * 6,
        out_specs=pl.BlockSpec((part, BLK, BLK), lambda i: (i, 0, 0)),
        out_shape=jax.ShapeDtypeStruct((count, BLK, BLK), BF),
        scratch_shapes=[
            pltpu.VMEM((2, 2 * part, BLK, BLK), BF),
            pltpu.SemaphoreType.DMA((2,)),
        ],
        compiler_params=params(),
        cost_estimate=cost(0, 6 * count * BLK * BLK),
        name="gradient_sums",
    )(table, *own, *other)


def merge_body(first, second, passed, *refs):
    refs = list(refs)

    def total(count):
        return sum(refs.pop(0)[...].astype(F32) for _ in range(count))

    sums = [total(2), total(2)] if first else []
    if second:
        sums.append(total(3 if passed else 2))
    for ref, value in zip(refs, sums):
        ref[...] = value.astype(BF)


def merge_sums(low, came, kept, last, passed):
    steps = 3
    args, specs, shapes, outs = [], [], [], []

    def part(array, count, start):
        args.append(array)
        size = count // steps
        specs.append(pl.BlockSpec((size, BLK, BLK), lambda i: (i + start * steps, 0, 0)))

    def out(count):
        shapes.append(jax.ShapeDtypeStruct((count, BLK, BLK), BF))
        outs.append(pl.BlockSpec((count // steps, BLK, BLK), lambda i: (i, 0, 0)))

    if low is not None:
        count = low.shape[0] // 2
        for start in range(2):
            part(low, count, start)
            part(came, count, start)
            out(count)
    if kept is not None:
        for array in (kept, last) if passed is None else (kept, last, passed):
            part(array, kept.shape[0], 0)
        out(kept.shape[0])
    body = functools.partial(merge_body, low is not None, kept is not None, passed is not None)
    return pl.pallas_call(
        body,
        grid=(steps,),
        in_specs=specs,
        out_specs=outs,
        out_shape=shapes,
        compiler_params=params(44),
        cost_estimate=cost(0, 6 * MIB),
        name="merge_sums",
    )(*args)


def two_terms(values):
    high = values.astype(BF)
    return high, (values - high.astype(F32)).astype(BF)


def update_body(count, *refs):
    parts = refs[:count]
    m_ref, sl_ref, sr_ref, rl_ref, rr_ref, g_out, sl_out, sr_out, m_out = refs[count:]

    def long_left(terms, axis):
        return jnp.concatenate([terms[0], terms[0], terms[1]], axis)

    def long_right(terms, axis):
        return jnp.concatenate([terms[0], terms[1], terms[0]], axis)

    count = range(g_out.shape[0])
    totals = [sum(part[i].astype(F32) for part in parts) for i in count]
    grads = [two_terms(total) for total in totals]
    talls = [long_right(grad, 0) for grad in grads]
    inners = [mul_nn(long_left(two_terms(rl_ref[i]), 1), talls[i]) for i in count]
    for i in count:
        g_out[i] = totals[i]
        sl_out[i] = sl_ref[i] + mul_nt(long_left(grads[i], 1), long_right(grads[i], 1))
    directions = [
        mul_nn(long_left(two_terms(inners[i]), 1), long_right(two_terms(rr_ref[i]), 0))
        for i in count
    ]
    for i in count:
        sr_out[i] = sr_ref[i] + mul_tn(long_left(grads[i], 0), talls[i])
    for i in count:
        master, direction = m_ref[i], directions[i]
        scale = jnp.sqrt(jnp.mean(master * master, keepdims=True) + 1e-06)
        scale = scale * lax.rsqrt(jnp.mean(direction * direction, keepdims=True) + 1e-06)
        m_out[i] = master - 0.3 * scale * direction


def update(parts, master, stat_left, stat_right, root_left, root_right):
    count = master.shape[0]
    group = 6 if count % 6 == 0 else 1
    block = pl.BlockSpec((group, BLK, BLK), lambda i: (i, 0, 0))
    shape = jax.ShapeDtypeStruct(master.shape, F32)
    return pl.pallas_call(
        functools.partial(update_body, len(parts)),
        grid=(count // group,),
        in_specs=[block] * (len(parts) + 5),
        out_specs=[block] * 4,
        out_shape=[shape] * 4,
        compiler_params=params(),
        cost_estimate=cost(48 * count * BLK**3, 15 * MIB),
        name="block_update",
    )(*parts, master, stat_left, stat_right, root_left, root_right)


def pair_moves():
    moves_same, moves_cross = [], []
    for z in range(4):
        for c in range(2):
            for moves, bit in ((moves_same, z % 2), (moves_cross, 1 - z % 2)):
                moves.append((z * 2 + c, (2 * c + bit) * 2 + z // 2))
    return moves_same, moves_cross


def row_part(values, which):
    return lax.dynamic_index_in_dim(values, which, 0, False)


def move_rows(values, crossed, back=False):
    moves = pair_moves()[crossed]
    return lax.ppermute(values, ("seq", "core"), [(b, a) for a, b in moves] if back else moves)


def in_order(kept, crossed, parity):
    return jnp.where(parity == 0, kept, crossed), jnp.where(parity == 0, crossed, kept)


def swap_cores(values):
    return lax.ppermute(values, "core", [(0, 1), (1, 0)])


def chip_orders(chips):
    bits = [1 << i for i in range(chips.bit_length() - 1)]
    return bits, bits[::-1]


def offsets(order):
    result = [0]
    for bit in order:
        result = result + [o ^ bit for o in result]
    return result


def place_lists(chips, owned, planes):
    shape = (2, planes, chips, owned)
    by_core = np.array([offsets(order) for order in chip_orders(chips)], np.int32)
    grid = np.indices(shape).astype(np.int32).reshape(4, 2, -1)
    offset = np.broadcast_to(by_core[:, None, :, None], shape).reshape(2, -1)
    return grid[1, 0], offset, grid[3, 0]


def arrival_order(chips, owned, planes):
    per_plane, quarter = chips * owned, owned
    if chips != 4:
        return np.arange(planes * per_plane)
    pieces = [(0, 0)]
    for k in range(1, planes + 1):
        pieces += [(k, 0)] if k < planes else []
        pieces += [(k - 1, 1), (k - 1, 2)]
        pieces += [(k - 2, 3)] if k > 1 else []
    pieces.append((planes - 1, 3))
    starts = [k * per_plane + r * quarter for k, r in pieces]
    return np.concatenate([np.arange(start, start + quarter) for start in starts])


def swap_chips(values, bits):
    chips = lax.axis_size("chip")
    moves = [(i * 2 + c, (i ^ bits[c]) * 2 + c) for i in range(chips) for c in range(2)]
    return lax.ppermute(values, ("chip", "core"), moves)


def move_planes(values, shift):
    planes = lax.axis_size("seq")
    return lax.ppermute(values, "seq", [(i, (i + shift) % planes) for i in range(planes)])


def after(value, *deps):
    return lax.optimization_barrier((value, *deps))[0]


def together(*values):
    return lax.optimization_barrier(values)


def chip_steps():
    return list(zip(*chip_orders(lax.axis_size("chip"))))


def finish_pieces(pieces):
    for bits in chip_steps()[2:]:
        joined = jnp.concatenate(pieces, 0)
        pieces = [joined, swap_chips(joined, bits)]
    return pieces


def add_halves(kept, came):
    return (kept.astype(F32) + came.astype(F32)).astype(BF)


def pack_terms(values):
    high = lax.optimization_barrier(values.astype(BF))
    low = (values - high.astype(F32)).astype(BF)
    terms = jnp.stack([high, low]).reshape(-1, BLK)
    return jnp.pad(terms, ((0, BLK - terms.shape[0]), (0, 0)))[None]


def unpack_terms(blocks, shape):
    terms = blocks.reshape(-1, BLK, BLK)[:, : 2 * shape[0] * shape[1] // BLK]
    terms = terms.reshape(-1, 2, *shape).astype(F32)
    return terms[:, 0] + terms[:, 1]


def finish_sums(keep, send):
    for bits in chip_steps()[::-1][1:-1]:
        count = keep.shape[0] // 2
        came = swap_chips(send, bits)
        send = add_halves(keep[count:], came[count:])
        keep = add_halves(keep[:count], came[:count])
    return keep, send


def by_chip(riders, me, core):
    chips = lax.axis_size("chip")
    ranks = np.array([np.argsort(offsets(order[::-1])) for order in chip_orders(chips)], np.int32)
    rank = jnp.asarray(ranks)[core][me ^ jnp.arange(chips, dtype=jnp.int32)]
    return riders.reshape(chips, -1, BLK, BLK)[rank]


def local(
    tokens,
    cotangent,
    lengths,
    owner_perm,
    master,
    norm_gains,
    stat_left,
    stat_right,
    root_left,
    root_right,
    moment_first,
    moment_second,
):
    core = lax.axis_index("core")
    place_z = lax.axis_index("seq")
    parity = place_z % 2
    block_count = owner_perm.shape[0]
    owned = master.shape[0]
    half = block_count // 2

    chips, planes = lax.axis_size("chip"), lax.axis_size("seq")
    me = lax.axis_index("chip")

    pair_lengths = jnp.stack([lengths, swap_cores(lengths)])
    pair_lengths = jnp.where(core == 0, pair_lengths, pair_lengths[::-1]).reshape(-1)
    length = lax.dynamic_index_in_dim(pair_lengths, place_z, 0, False)
    span = tokens.shape[0] * tokens.shape[1]
    live = jnp.stack([length - core * span, length - (1 - core) * span, length - core * span, parity])

    distance, offset, slot = place_lists(chips, owned, planes)
    offset = jnp.where(core == 0, offset, offset[::-1])
    device = ((place_z - distance) % planes * chips + (me ^ offset)) * 2
    device = device + jnp.stack([core, 1 - core])[:, None]
    table = owner_perm[(device * owned + slot).reshape(-1)]
    sums_table = jnp.asarray(source_numbers())[table[:half]]
    arrive = arrival_order(chips, owned, planes)
    near_slots, far_slots = device * owned + slot
    table = owner_perm[jnp.concatenate([near_slots[arrive], far_slots[arrive]])]

    shard = master.astype(BF)
    first_bits, second_bits = chip_steps()[:2]
    per_plane = chips * owned
    by_phase = chips == 4
    rows = (row_part(tokens, parity), row_part(tokens, 1 - parity))
    cross, held, weights, first = None, (), None, 0
    came, turned = swap_chips(shard, first_bits), swap_chips(shard, second_bits)
    next_shard = move_planes(shard, 1)
    pieces = [[shard, came, turned]]

    def place(parts, first, weights):
        others = [swap_cores(part) for part in parts]
        weights = place_blocks(table, first, parts, others, weights)
        return weights, first + sum(part.shape[0] for part in parts)

    for k in range(1, planes):
        ready = () if k == 1 else (cross, *held, live, table, sums_table)
        ready = ready if weights is None else (*ready, weights)
        this_shard, came, turned, row_a, row_b, *done = together(
            next_shard, came, turned, *rows, *ready
        )
        if k > 1:
            pieces[k - 2].append(done[0])
        cross = swap_chips(came, second_bits)
        arrived = [this_shard, came, turned, *(pieces[0][:1] if k == 1 else done[:1])]
        arrived = arrived[3:] + arrived[:3] if k == 1 else arrived
        pieces[k - 1][1:] = [came, turned]
        came, turned = swap_chips(this_shard, first_bits), swap_chips(this_shard, second_bits)
        pieces.append([this_shard, came, turned])
        if k < planes - 1:
            next_shard = move_planes(this_shard, 1)
        else:
            row_same = move_rows(row_a, False)
            row_cross = move_rows(after(row_b, row_same), True)
        if by_phase:
            if k > 1:
                weights, first = place(done[1:2], first, weights)
            held = (jnp.concatenate(arrived, 0),)
    came, turned, done, row_same, row_cross, *held = together(
        came, turned, cross, row_same, row_cross, *held, *([] if weights is None else [weights])
    )
    own_tokens = jnp.concatenate(in_order(row_same, row_cross, parity), 0)
    pieces[-2].append(done)
    pieces[-1][1:] = [came, turned, swap_chips(came, second_bits)]
    normed1, normed1_t = norm_tokens(own_tokens, norm_gains)
    if by_phase:
        weights, first = place(held[:1], first, weights)
        parts = [came, turned, done]
        others = [swap_cores(part) for part in parts]
        last, normed1, *_ = together(pieces[-1][-1], normed1, weights, *others)
        weights = place_blocks(table, first, parts, others, weights)
        first += 3 * owned
        other_normed = swap_cores(normed1)
        weights, _ = place([last], first, weights)
    else:
        for each in pieces:
            each = [jnp.concatenate(finish_pieces(each), 0)]
            weights, first = place(each, first, weights)
        other_normed = swap_cores(normed1)
    cotangent = after(cotangent, weights)
    cot_rows = [move_rows(row_part(cotangent, abs(i - parity)), i == 1) for i in range(2)]

    own_qkv, other_kv = project(normed1, other_normed, weights)
    attended, q_aug = attend(live, own_qkv, other_kv)
    kept, crossed, g_rest, grad_middle, grad_attended, gain_second = feed(
        live, own_tokens, attended, *cot_rows, norm_gains, weights
    )
    other_rest = swap_cores(g_rest)
    kept, crossed = move_rows(kept, False, True), move_rows(crossed, True, True)
    layer_out = jnp.stack(in_order(kept, crossed, parity), 0)
    d_query, d_own, d_other = attend_back(live, q_aug, own_qkv, other_kv, attended, grad_attended)
    received = swap_cores(after(d_other, kept, crossed))
    flat = lambda g: g.reshape(-1, BLK, BLK)
    g_query, partial = query_back(normed1_t, d_query, weights)
    g_query = flat(g_query)
    other_query = swap_cores(g_query)
    g_kv, back = input_back(normed1_t, d_own, received, partial, weights)
    g_kv = flat(g_kv)
    other_kv_grad = swap_cores(after(g_kv, other_query))
    own_grads = (g_query, g_kv, g_rest)
    other_grads = (other_query, other_kv_grad, other_rest)
    half_plane = per_plane // 2
    last_bits, before_bits = chip_steps()[-1], chip_steps()[0]
    moved_rows, lows, sent, passed, riders_z = [], [], None, None, []

    def sums(k, part, held):
        first = k * per_plane + part * half_plane
        return gather_sums(held, first, half_plane, own_grads, other_grads)

    order = list(range(planes))[::-1]
    high = sums(order[0], 1, sums_table)
    held = sums_table
    held_riders = []
    for turn in range(planes + 1):
        group, moves = [], []
        if turn < planes:
            group.append(high)
            moves.append(lambda v: swap_chips(v, last_bits))
        if 1 <= turn <= planes:
            group.append(sent)
            moves.append(lambda v: swap_chips(v, before_bits))
        if 2 <= turn <= planes:
            group.append(part)
            moves.append(lambda v: move_planes(v, -1))
        if turn in (1, 2):
            group.append(riders)
            bits = last_bits if turn == 1 else before_bits
            moves.append(lambda v: swap_chips(v, bits))
        if turn in (1, 2):
            group.append(rows[turn - 1])
            crossed = turn == 2
            moves.append(lambda v: move_rows(v, crossed, True))
        far_riders = [1, 2] if turn == planes - 1 else []
        group += [rider for _ in far_riders]
        moves += [functools.partial(move_planes, shift=-k) for k in far_riders]
        came = [move(value) for move, value in zip(moves, together(*group, *moved_rows, *held_riders))]
        if turn in (1, 2):
            moved_rows.append(came.pop())
            riders = jnp.concatenate([riders, came.pop()], 0)
            for bits in chip_steps()[::-1][1:-1] if turn == 1 else ():
                riders = jnp.concatenate([riders, swap_chips(riders, bits)], 0)
        count = len(came) - len(far_riders)
        riders_z, came = riders_z + came[count:], came[:count]
        if far_riders:
            riders_z += [move_planes(after(rider, *riders_z), -k) for k in range(3, planes)]
        if turn == planes:
            parts = [keep_before, *came]
            continue
        passed = came.pop() if turn >= 2 else None
        low = sums(order[turn], 0, after(held, high))
        if turn + 1 < planes:
            high = sums(order[turn + 1], 1, after(held, low))
        held = after(sums_table, *came)
        held_riders = [riders] if turn == 2 else []
        if turn == 0:
            kept, crossed, gain_first = input_end(
                live, own_tokens, norm_gains, after(back, high), grad_middle
            )
            rows = [kept, crossed]
            gain_part = jnp.concatenate([gain_first, gain_second], 0)
            mine = pack_terms(gain_part)
            pair = jnp.concatenate([mine, swap_cores(mine)], 0)
            riders = jnp.where(core == 0, pair, pair[::-1])
        if turn == 2:
            plane_gain = by_chip(riders, me, core)
            plane_gain = jnp.sum(unpack_terms(plane_gain, gain_part.shape), 0)
            rider = pack_terms(plane_gain)
        second = (None, None, None) if turn == 0 else (keep_before, came[-1], passed)
        keep, sent, *part = merge_sums(low, came[0], *second)
        part = part[0] if part else None
        keep_before, sent = finish_sums(keep, sent)
    input_grad = jnp.stack(in_order(*moved_rows, parity), 0).astype(F32)
    planes_gain = [unpack_terms(each, gain_part.shape)[0] for each in (rider, *riders_z)]
    turned = (jnp.arange(planes, dtype=jnp.int32) - place_z) % planes
    gain_grad = jnp.sum(jnp.stack(planes_gain)[turned], 0)
    grad_blocks, stat_left_new, stat_right_new, master_new = update(
        parts, master, stat_left, stat_right, root_left, root_right
    )
    first_new = 0.9 * moment_first + 0.1 * gain_grad
    second_new = 0.999 * moment_second + 0.001 * gain_grad * gain_grad
    first_hat = first_new / (1.0 - 0.9**STEP)
    second_hat = second_new / (1.0 - 0.999**STEP)
    gains_new = norm_gains - 0.5 * first_hat / (jnp.sqrt(second_hat) + 1e-08)
    return (
        layer_out,
        input_grad,
        grad_blocks,
        stat_left_new,
        stat_right_new,
        master_new,
        first_new,
        second_new,
        gains_new,
    )


def solution(mesh):
    seq_size, rows_size = mesh.shape["seq"], mesh.shape["rows"]
    mesh = Mesh(mesh.devices.reshape(seq_size, rows_size // 2, 2), ("seq", "chip", "core"))
    activation = P(("chip", "core"), "seq", None)
    blocks = P(("seq", "chip", "core"), None, None)
    return jax.shard_map(
        local,
        mesh=mesh,
        in_specs=(
            activation, activation, P(("chip", "core")), P(), blocks, P(),
            blocks, blocks, blocks, blocks, P(), P(),
        ),
        out_specs=(activation, activation, blocks, blocks, blocks, blocks, P(), P(), P()),
        check_vma=False,
    )
```

```python
import functools
import jax
import jax.numpy as jnp
import numpy as np
from jax import lax
from jax.experimental import pallas as pl
from jax.experimental.pallas import tpu as pltpu
from jax.sharding import Mesh
from jax.sharding import PartitionSpec as P

D = 1024
HD = 64
FF = 4096
BLK = 128
STEP = 10
COLS = 1024
BF = jnp.bfloat16
F32 = jnp.float32
MIB = 1024 * 1024

norm_eps = 1e-05
score_scale = 0.125
masked_score = -1e30


def params(limit=56):
    return pltpu.CompilerParams(vmem_limit_bytes=limit * MIB)


def cost(flops, nbytes):
    return pl.CostEstimate(flops=int(flops), bytes_accessed=int(nbytes), transcendentals=0)


def mul_nn(left, right):
    return jnp.dot(left, right, preferred_element_type=F32)


def mul_nt(left, right):
    return lax.dot_general(left, right, (((1,), (1,)), ((), ())), preferred_element_type=F32)


def mul_tn(left, right):
    return lax.dot_general(left, right, (((0,), (0,)), ((), ())), preferred_element_type=F32)


def join_tile(ref):
    rows, cols = ref.shape[0], ref.shape[1]
    return jnp.concatenate([ref[:, j].reshape(rows * BLK, BLK) for j in range(cols)], axis=1)


def split_tile(ref, matrix):
    rows, cols = ref.shape[0], ref.shape[1]
    for j in range(cols):
        ref[:, j] = matrix[:, j * BLK : (j + 1) * BLK].reshape(rows, BLK, BLK).astype(ref.dtype)


def split_flat(ref, matrix):
    cols = matrix.shape[1] // BLK
    for i in range(matrix.shape[0] // BLK):
        for j in range(cols):
            block = matrix[i * BLK : (i + 1) * BLK, j * BLK : (j + 1) * BLK]
            ref[i * cols + j] = block.astype(ref.dtype)


def normalize(values):
    row_mean = jnp.mean(values, -1, keepdims=True)
    centered = values - row_mean
    row_var = jnp.mean(centered * centered, -1, keepdims=True)
    inv_std = lax.rsqrt(row_var + norm_eps)
    return centered * inv_std, inv_std


def gelu_parts(hidden):
    bell = jnp.exp(hidden * hidden * -0.5)
    t = 1.0 / (1.0 + jnp.abs(hidden) * (0.3275911 * 0.7071067811865476))
    poly = 1.061405429 * t - 1.453152027
    for term in (1.421413741, -0.284496736, 0.254829592):
        poly = poly * t + term
    tail = poly * t * 0.5 * bell
    return jnp.where(hidden < 0.0, tail, 1.0 - tail), hidden * bell * 0.3989422804014327


def norm_back(gradient, unit_vals, inv_std):
    grad_mean = jnp.mean(gradient, -1, keepdims=True)
    cross_mean = jnp.mean(gradient * unit_vals, -1, keepdims=True)
    return inv_std * (gradient - grad_mean - unit_vals * cross_mean)


def place_body(first, pieces, table, *refs):
    near, far = refs[:pieces], refs[pieces : 2 * pieces]
    out_ref, sem = refs[-2:]
    total = 0
    for start, sources in ((first, near), (table.shape[0] // 2 + first, far)):
        for src in sources:
            for slot in range(src.shape[0]):
                pltpu.make_async_copy(src.at[slot], out_ref.at[table[start + slot]], sem).start()
            start += src.shape[0]
            total += src.shape[0]
    done = out_ref.at[pl.ds(0, total)]
    pltpu.make_async_copy(done, done, sem).wait()


def place_blocks(table, first, near, far, kept):
    smem = pl.BlockSpec(memory_space=pltpu.SMEM)
    hbm = pl.BlockSpec(memory_space=pltpu.HBM)
    vmem = pl.BlockSpec(memory_space=pltpu.VMEM)
    kept = () if kept is None else (kept,)
    count = 2 * len(near)
    return pl.pallas_call(
        functools.partial(place_body, first, len(near)),
        out_shape=jax.ShapeDtypeStruct((table.shape[0], BLK, BLK), BF),
        in_specs=[smem] + [vmem] * count + [hbm] * len(kept),
        out_specs=hbm,
        scratch_shapes=[pltpu.SemaphoreType.DMA],
        input_output_aliases={1 + count: 0} if kept else {},
        compiler_params=params(46),
        cost_estimate=cost(0, 6 * MIB),
        name="place_weights",
    )(table, *near, *far, *kept)


def norm_body(tokens_ref, gains_ref, out_ref, turned_ref):
    normed = normalize(tokens_ref[...].astype(F32))[0] * gains_ref[0:1]
    out_ref[...] = normed.astype(BF)
    turned_ref[...] = normed.T.astype(BF)


def norm_tokens(tokens, gains):
    span = tokens.shape[0]
    steps = 4
    part = pl.BlockSpec((span // steps, D), lambda i: (i, 0))
    return pl.pallas_call(
        norm_body,
        grid=(steps,),
        in_specs=[part, pl.BlockSpec((2, D), lambda i: (0, 0))],
        out_specs=[part, pl.BlockSpec((D, span // steps), lambda i: (0, i))],
        out_shape=[jax.ShapeDtypeStruct((span, D), BF), jax.ShapeDtypeStruct((D, span), BF)],
        compiler_params=params(46),
        cost_estimate=cost(0, 3 * MIB),
        name="norm_tokens",
    )(tokens, gains)


def qkv_body(own_ref, other_ref, w_ref, own_out, other_out):
    step = pl.program_id(0)
    weight = join_tile(w_ref)
    own_out[...] = mul_nn(own_ref[...], weight).astype(BF)

    @pl.when(step >= D // COLS)
    def _():
        other_out[...] = mul_nn(other_ref[...], weight).astype(BF)


def project(own, other, weights):
    span = own.shape[0]
    skip = D // COLS
    once = pl.BlockSpec((span, D), lambda j: (0, 0))
    return pl.pallas_call(
        qkv_body,
        grid=(3 * D // COLS,),
        in_specs=[
            once,
            once,
            pl.BlockSpec((D // BLK, COLS // BLK, BLK, BLK), lambda j: (0, j, 0, 0)),
        ],
        out_specs=[
            pl.BlockSpec((span, COLS), lambda j: (0, j)),
            pl.BlockSpec((span, COLS), lambda j: (0, jnp.maximum(j - skip, 0))),
        ],
        out_shape=[
            jax.ShapeDtypeStruct((span, 3 * D), BF),
            jax.ShapeDtypeStruct((span, 2 * D), BF),
        ],
        compiler_params=params(),
        cost_estimate=cost(10 * span * D * D, 12 * MIB),
        name="qkv_projection",
    )(own, other, weights.reshape(-1, 3 * D // BLK, BLK, BLK))


def lane_masks(head):
    lane = lax.broadcasted_iota(jnp.int32, (1, BLK), 1)
    first = HD * (1 - head)
    keep = (lane // HD == head).astype(F32)
    dead_lane = (lane == first).astype(F32)
    terms = [(lane == first + 1 + i).astype(F32) for i in range(3)]
    return keep, dead_lane, terms


def three_terms(values):
    high = values.astype(BF).astype(F32)
    rest = values - high
    middle = rest.astype(BF).astype(F32)
    return high, middle, rest - middle


def key_bias(span, live_count):
    row = lax.broadcasted_iota(jnp.int32, (span, 1), 0)
    return jnp.where(row < live_count, 0.0, masked_score).astype(F32)


def attend_body(live_ref, q_ref, ko_ref, vo_ref, kx_ref, vx_ref, out_ref, aug_ref):
    span = q_ref.shape[0]
    bias_own = key_bias(span, live_ref[0])
    bias_other = key_bias(span, live_ref[1])
    queries = q_ref[...].astype(F32) * score_scale
    k_own, k_other = ko_ref[...].astype(F32), kx_ref[...].astype(F32)
    v_own_f, v_other_f = vo_ref[...].astype(F32), vx_ref[...].astype(F32)
    results, scores = [], []
    for head in range(2):
        keep, dead_lane, _ = lane_masks(head)
        q_head = (queries * keep + dead_lane).astype(BF)
        s_own = mul_nt(q_head, (k_own * keep + bias_own * dead_lane).astype(BF))
        s_other = mul_nt(q_head, (k_other * keep + bias_other * dead_lane).astype(BF))
        scores.append((q_head, s_own, s_other))
    for head in range(2):
        keep, _, terms = lane_masks(head)
        q_head, s_own, s_other = scores[head]
        top = jnp.max(jnp.maximum(s_own, s_other), -1, keepdims=True)
        p_own = jnp.exp(s_own - top)
        p_other = jnp.exp(s_other - top)
        v_own = (v_own_f * keep + (1.0 - keep)).astype(BF)
        v_other = (v_other_f * keep + (1.0 - keep)).astype(BF)
        mixed = mul_nn(p_own.astype(BF), v_own) + mul_nn(p_other.astype(BF), v_other)
        total = mixed[:, HD * (1 - head) : HD * (1 - head) + 1]
        results.append(mixed / total * keep)
        parts = three_terms(-(top + jnp.log(total)))
        stats = sum(part * lane for part, lane in zip(parts, terms))
        aug_ref[:, head * BLK : (head + 1) * BLK] = (q_head.astype(F32) + stats).astype(BF)
    out_ref[...] = (results[0] + results[1]).astype(BF)


def attend(live, own, other):
    span = own.shape[0]
    pairs = D // BLK
    col = lambda shift: pl.BlockSpec((span, BLK), lambda p: (0, p + shift))
    return pl.pallas_call(
        attend_body,
        grid=(pairs,),
        in_specs=[
            pl.BlockSpec(memory_space=pltpu.SMEM),
            col(0),
            col(pairs),
            col(2 * pairs),
            col(0),
            col(pairs),
        ],
        out_specs=[col(0), pl.BlockSpec((span, 2 * BLK), lambda p: (0, p))],
        out_shape=[
            jax.ShapeDtypeStruct((span, D), BF),
            jax.ShapeDtypeStruct((span, 2 * D), BF),
        ],
        compiler_params=params(),
        cost_estimate=cost(40 * span * span * D, 8 * MIB),
        name="attention",
    )(live, own, own, own, other, other)


def attend_back_body(
    live_ref, aug_ref, ko_ref, vo_ref, kx_ref, vx_ref, at_ref, g_ref, dq_ref, own_ref, other_ref
):
    span = at_ref.shape[0]
    grads = g_ref[...].astype(F32)
    product = grads * at_ref[...].astype(F32)
    keeps, g_augs, q_augs = [], [], []
    for head in range(2):
        keep, dead_lane, terms = lane_masks(head)
        delta = jnp.sum(product * keep, -1, keepdims=True)
        parts = three_terms(-delta)
        stats = sum(part * lane for part, lane in zip(parts, terms))
        g_augs.append((grads * keep + stats).astype(BF))
        q_augs.append(aug_ref[:, head * BLK : (head + 1) * BLK])
    d_query = [None, None]
    for k_ref, v_ref, out_ref, live in (
        (ko_ref, vo_ref, own_ref, live_ref[0]),
        (kx_ref, vx_ref, other_ref, live_ref[1]),
    ):
        bias = key_bias(span, live)
        keys = k_ref[...]
        keys_f, values_f = keys.astype(F32), v_ref[...].astype(F32)
        d_keys = d_values = None
        for head in range(2):
            keep, dead_lane, terms = lane_masks(head)
            ones = terms[0] + terms[1] + terms[2]
            k_aug = (keys_f * keep + (bias * dead_lane + ones)).astype(BF)
            v_aug = (values_f * keep + ones).astype(BF)
            probs = jnp.exp(mul_nt(k_aug, q_augs[head]))
            d_scores = (probs * mul_nt(v_aug, g_augs[head])).astype(BF)
            value_part = mul_nn(probs.astype(BF), g_augs[head]) * keep
            key_part = mul_nn(d_scores, q_augs[head]) * keep
            query_part = mul_tn(keys, d_scores)[head * HD : (head + 1) * HD]
            d_query[head] = query_part if d_query[head] is None else d_query[head] + query_part
            d_values = value_part if d_values is None else d_values + value_part
            d_keys = key_part if d_keys is None else d_keys + key_part
        out_ref[0] = d_keys.astype(out_ref.dtype)
        out_ref[1] = d_values.astype(out_ref.dtype)
    dq_ref[...] = (jnp.concatenate(d_query, 0).T * score_scale).astype(BF)


def attend_back(live, aug, own, other, attended, grads):
    span = own.shape[0]
    pairs = D // BLK
    col = lambda shift: pl.BlockSpec((span, BLK), lambda p: (0, p + shift))
    pair_out = pl.BlockSpec((2, span, BLK), lambda p: (0, 0, p))
    return pl.pallas_call(
        attend_back_body,
        grid=(pairs,),
        in_specs=[
            pl.BlockSpec(memory_space=pltpu.SMEM),
            pl.BlockSpec((span, 2 * BLK), lambda p: (0, p)),
            col(pairs),
            col(2 * pairs),
            col(0),
            col(pairs),
            col(0),
            col(0),
        ],
        out_specs=[col(0), pair_out, pair_out],
        out_shape=[
            jax.ShapeDtypeStruct((span, D), BF),
            jax.ShapeDtypeStruct((2, span, D), BF),
            jax.ShapeDtypeStruct((2, span, D), BF),
        ],
        compiler_params=params(),
        cost_estimate=cost(60 * span * span * D, 12 * MIB),
        name="attention_backward",
    )(live, aug, own, own, other, other, attended, grads)


def feed_body(
    live_ref,
    tokens_ref,
    attended_ref,
    cot_ref,
    gains_ref,
    wo_ref,
    wu_ref,
    wd_ref,
    kept_ref,
    crossed_ref,
    rest_ref,
    gm_ref,
    ga_ref,
    gain_ref,
    unit,
    inv,
    normed,
    normed_t,
    top,
    acc_out,
    acc_back,
    up_stage,
    down_stage,
    out_stage,
    sems,
    out_sem,
):
    step = pl.program_id(0)
    place = step % 2
    side, width = up_stage.shape[1], up_stage.shape[2]
    per_tile = side * width
    up_first = side * side
    down_first = up_first + side * FF // BLK

    def drain(which):
        pltpu.make_async_copy(up_stage.at[which], up_stage.at[which], sems.at[0, which]).wait()
        pltpu.make_async_copy(down_stage.at[which], down_stage.at[which], sems.at[1, which]).wait()
    span = tokens_ref.shape[0]

    @pl.when(step == 0)
    def _():
        weight = join_tile(wo_ref)
        middle = tokens_ref[...].astype(F32) + mul_nn(attended_ref[...], weight)
        unit_vals, inv_std = normalize(middle)
        unit[...] = unit_vals
        inv[...] = inv_std
        normed_vals = unit_vals * gains_ref[1:2]
        normed[...] = normed_vals.astype(BF)
        normed_t[...] = normed_vals.T.astype(BF)
        row = lax.broadcasted_iota(jnp.int32, (span, 1), 0)
        top[...] = jnp.where(row < live_ref[2], cot_ref[...].astype(F32), 0.0).astype(BF)
        acc_out[...] = middle
        acc_back[...] = jnp.zeros_like(acc_back)

    w_up = join_tile(wu_ref)
    w_down = join_tile(wd_ref)
    hidden = mul_nn(normed[...], w_up)
    grad_act = mul_nt(top[...], w_down)
    share, slope_rest = gelu_parts(hidden)
    activated = (hidden * share).astype(BF)
    grad_hidden = (grad_act * (share + slope_rest)).astype(BF)
    acc_out[...] += mul_nn(activated, w_down)
    acc_back[...] += mul_nt(grad_hidden, w_up)

    @pl.when(step >= 2)
    def _():
        drain(place)

    split_flat(down_stage.at[place], mul_tn(activated, top[...]))
    dest = rest_ref.at[pl.ds(down_first + step * per_tile, per_tile)]
    pltpu.make_async_copy(down_stage.at[place], dest, sems.at[1, place]).start()
    split_tile(up_stage.at[place], mul_nn(normed_t[...], grad_hidden))
    for i in range(side):
        dest = rest_ref.at[pl.ds(up_first + i * (FF // BLK) + step * width, width)]
        pltpu.make_async_copy(up_stage.at[place, i], dest, sems.at[0, place]).start()

    @pl.when(step == pl.num_programs(0) - 1)
    def _():
        for flip in range(2):

            @pl.when(live_ref[3] == flip)
            def _():
                for ref, part in ((kept_ref, flip), (crossed_ref, 1 - flip)):
                    ref[...] = acc_out[part * (span // 2) : (part + 1) * (span // 2)].astype(BF)

        unit_vals = unit[...]
        back = acc_back[...]
        gain_ref[...] = jnp.sum(back * unit_vals, 0, keepdims=True)
        grad_middle = top[...].astype(F32) + norm_back(back * gains_ref[1:2], unit_vals, inv[...])
        gm_ref[...] = grad_middle
        back_middle = grad_middle.astype(BF)
        split_flat(out_stage, mul_tn(attended_ref[...], back_middle))
        out_copy = pltpu.make_async_copy(out_stage, rest_ref.at[pl.ds(0, up_first)], out_sem)
        out_copy.start()
        ga_ref[...] = mul_nt(back_middle, join_tile(wo_ref)).astype(BF)
        drain(1 - place)
        drain(place)
        out_copy.wait()


def feed(live, tokens, attended, cotangent, gains, weights):
    span = tokens.shape[0]
    side, width = D // BLK, COLS // BLK
    whole = lambda j: (0, 0)
    act = pl.BlockSpec((span, D), whole)
    once = pl.BlockSpec((span, D), whole, pipeline_mode=pl.Buffered(1))
    half_act = pl.BlockSpec((span // 2, D), whole)
    per_row = weights.reshape(-1, side, BLK, BLK)
    per_up = weights.reshape(-1, FF // BLK, BLK, BLK)
    out_row = (3 * side * side) // side // side
    up_row = 4 * side * side // (FF // BLK) // side
    down_row = (4 * side * side + side * FF // BLK) // side // width
    return pl.pallas_call(
        feed_body,
        grid=(FF // COLS,),
        in_specs=[
            pl.BlockSpec(memory_space=pltpu.SMEM),
            once,
            once,
            once,
            pl.BlockSpec((2, D), whole),
            pl.BlockSpec(
                (side, side, BLK, BLK),
                lambda j: (out_row, 0, 0, 0),
                pipeline_mode=pl.Buffered(1),
            ),
            pl.BlockSpec((side, width, BLK, BLK), lambda j: (up_row, j, 0, 0)),
            pl.BlockSpec((width, side, BLK, BLK), lambda j: (down_row + j, 0, 0, 0)),
        ],
        out_specs=[
            half_act,
            half_act,
            pl.BlockSpec(memory_space=pltpu.HBM),
            act,
            act,
            pl.BlockSpec((1, D), whole),
        ],
        out_shape=[
            jax.ShapeDtypeStruct((span // 2, D), BF),
            jax.ShapeDtypeStruct((span // 2, D), BF),
            jax.ShapeDtypeStruct((side * side + 2 * side * (FF // BLK), BLK, BLK), BF),
            jax.ShapeDtypeStruct((span, D), F32),
            jax.ShapeDtypeStruct((span, D), BF),
            jax.ShapeDtypeStruct((1, D), F32),
        ],
        scratch_shapes=[
            pltpu.VMEM((span, D), F32),
            pltpu.VMEM((span, 1), F32),
            pltpu.VMEM((span, D), BF),
            pltpu.VMEM((D, span), BF),
            pltpu.VMEM((span, D), BF),
            pltpu.VMEM((span, D), F32),
            pltpu.VMEM((span, D), F32),
            pltpu.VMEM((2, side, width, BLK, BLK), BF),
            pltpu.VMEM((2, side * width, BLK, BLK), BF),
            pltpu.VMEM((side * side, BLK, BLK), BF),
            pltpu.SemaphoreType.DMA((2, 2)),
            pltpu.SemaphoreType.DMA,
        ],
        compiler_params=params(),
        cost_estimate=cost(14 * span * D * FF, 50 * MIB),
        name="feed_forward",
    )(live, tokens, attended, cotangent, gains, per_row, per_up, per_row)


def query_body(normed_t, dq_ref, w_ref, grad_ref, acc_ref):
    step = pl.program_id(0)

    @pl.when(step == 0)
    def _():
        acc_ref[...] = jnp.zeros_like(acc_ref)

    grad = dq_ref[...]
    acc_ref[...] += mul_nt(grad, join_tile(w_ref))
    split_tile(grad_ref, mul_nn(normed_t[...], grad))


def query_back(normed1_t, d_query, weights):
    span = normed1_t.shape[1]
    side, width = D // BLK, COLS // BLK
    whole = lambda j: (0, 0)
    act = pl.BlockSpec((span, D), whole)
    tile = pl.BlockSpec((side, width, BLK, BLK), lambda j: (0, j, 0, 0))
    return pl.pallas_call(
        query_body,
        grid=(D // COLS,),
        in_specs=[
            pl.BlockSpec((D, span), whole),
            pl.BlockSpec((span, COLS), lambda j: (0, j)),
            tile,
        ],
        out_specs=[tile, act],
        out_shape=[
            jax.ShapeDtypeStruct((side, side, BLK, BLK), BF),
            jax.ShapeDtypeStruct((span, D), F32),
        ],
        compiler_params=params(),
        cost_estimate=cost(4 * span * D * D, 8 * MIB),
        name="query_backward",
    )(normed1_t, d_query, weights.reshape(-1, 3 * side, BLK, BLK))


def input_body(normed_t, own_ref, recv_ref, acc_ref, w_ref, grad_ref, out_ref):
    step = pl.program_id(0)

    @pl.when(step == 0)
    def _():
        out_ref[...] = acc_ref[...]

    grad = (own_ref[0].astype(F32) + recv_ref[0].astype(F32)).astype(BF)
    out_ref[...] += mul_nt(grad, join_tile(w_ref))
    split_tile(grad_ref, mul_nn(normed_t[...], grad))


def input_back(normed1_t, own, received, partial, weights):
    span = normed1_t.shape[1]
    side, width = D // BLK, COLS // BLK
    per = D // COLS
    whole = lambda j: (0, 0)
    act = pl.BlockSpec((span, D), whole)
    part = pl.BlockSpec((1, span, COLS), lambda j: (j // per, 0, j % per))
    return pl.pallas_call(
        input_body,
        grid=(2 * per,),
        in_specs=[
            pl.BlockSpec((D, span), whole),
            part,
            part,
            act,
            pl.BlockSpec((side, width, BLK, BLK), lambda j: (0, j + per, 0, 0)),
        ],
        out_specs=[pl.BlockSpec((side, width, BLK, BLK), lambda j: (0, j, 0, 0)), act],
        out_shape=[
            jax.ShapeDtypeStruct((side, 2 * side, BLK, BLK), BF),
            jax.ShapeDtypeStruct((span, D), F32),
        ],
        compiler_params=params(),
        cost_estimate=cost(8 * span * D * D, 20 * MIB),
        name="input_backward",
    )(normed1_t, own, received, partial, weights.reshape(-1, 3 * side, BLK, BLK))


def input_end_body(live_ref, tokens_ref, gains_ref, back_ref, gm_ref, kept_ref, crossed_ref, gain_ref):
    step = pl.program_id(0)
    unit_vals, inv_std = normalize(tokens_ref[...].astype(F32))
    back = back_ref[...]

    @pl.when(step == 0)
    def _():
        gain_ref[...] = jnp.zeros_like(gain_ref)

    gain_ref[...] += jnp.sum(back * unit_vals, 0, keepdims=True)
    grad = (gm_ref[...] + norm_back(back * gains_ref[0:1], unit_vals, inv_std)).astype(BF)
    half = step // (pl.num_programs(0) // 2)
    rows = tokens_ref.shape[0]
    start = pl.multiple_of(step % (pl.num_programs(0) // 2) * rows, rows)

    @pl.when(half == live_ref[3])
    def _():
        kept_ref[pl.ds(start, rows)] = grad

    @pl.when(half != live_ref[3])
    def _():
        crossed_ref[pl.ds(start, rows)] = grad


def input_end(live, tokens, gains, back, grad_middle):
    span = tokens.shape[0]
    steps = 4
    part = pl.BlockSpec((span // steps, D), lambda i: (i, 0))
    half_act = pl.BlockSpec((span // 2, D), lambda i: (0, 0))
    row = lambda count: pl.BlockSpec((count, D), lambda i: (0, 0))
    return pl.pallas_call(
        input_end_body,
        grid=(steps,),
        in_specs=[pl.BlockSpec(memory_space=pltpu.SMEM), part, row(2), part, part],
        out_specs=[half_act, half_act, row(1)],
        out_shape=[
            jax.ShapeDtypeStruct((span // 2, D), BF),
            jax.ShapeDtypeStruct((span // 2, D), BF),
            jax.ShapeDtypeStruct((1, D), F32),
        ],
        compiler_params=params(46),
        cost_estimate=cost(0, 7 * MIB),
        name="input_gradient",
    )(live, tokens, gains, back, grad_middle)


def source_numbers():
    side = D // BLK
    numbers = np.arange(3 * side * side + side * side + 2 * side * (FF // BLK), dtype=np.int32)
    row, col = np.divmod(numbers[: 3 * side * side], 3 * side)
    numbers[: 3 * side * side] = np.where(
        col < side, row * side + col, side * side + row * 2 * side + col - side
    )
    return numbers


def gather_body(first, bounds, table, *refs):
    sources = refs[:6]
    out_ref, stage, sems = refs[6:]
    step, steps = pl.program_id(0), pl.num_programs(0)
    count = stage.shape[1] // 2

    def copy_pair(number, which, i, slot):
        for src, at in ((sources[which], i), (sources[3 + which], count + i)):
            source = src.at[number - bounds[which]]
            pltpu.make_async_copy(source, stage.at[slot, at], sems.at[slot]).start()

    def fetch(which, slot):
        start = first + which * count
        for i in range(count):
            number = table[start + i]
            common = number >= bounds[2]

            @pl.when(common)
            def _():
                copy_pair(number, 2, i, slot)

            @pl.when(jnp.logical_not(common))
            def _():
                @pl.when(number >= bounds[1])
                def _():
                    copy_pair(number, 1, i, slot)

                @pl.when(number < bounds[1])
                def _():
                    copy_pair(number, 0, i, slot)

    @pl.when(step == 0)
    def _():
        fetch(0, 0)

    @pl.when(step + 1 < steps)
    def _():
        fetch(step + 1, (step + 1) % 2)

    slot = step % 2
    pltpu.make_async_copy(stage.at[slot], stage.at[slot], sems.at[slot]).wait()
    total = stage[slot, :count].astype(F32) + stage[slot, count:].astype(F32)
    out_ref[...] = total.astype(BF)


def gather_sums(table, first, count, own, other):
    hbm = pl.BlockSpec(memory_space=pltpu.HBM)
    steps = 4
    part = count // steps
    bounds = np.cumsum([0] + [src.shape[0] for src in own]).tolist()
    return pl.pallas_call(
        functools.partial(gather_body, first, bounds),
        grid=(steps,),
        in_specs=[pl.BlockSpec(memory_space=pltpu.SMEM)] + [hbm] * 6,
        out_specs=pl.BlockSpec((part, BLK, BLK), lambda i: (i, 0, 0)),
        out_shape=jax.ShapeDtypeStruct((count, BLK, BLK), BF),
        scratch_shapes=[
            pltpu.VMEM((2, 2 * part, BLK, BLK), BF),
            pltpu.SemaphoreType.DMA((2,)),
        ],
        compiler_params=params(52),
        cost_estimate=cost(0, 6 * count * BLK * BLK),
        name="gradient_sums",
    )(table, *own, *other)


def merge_body(first, second, passed, *refs):
    refs = list(refs)

    def total(count):
        return sum(refs.pop(0)[...].astype(F32) for _ in range(count))

    sums = [total(2), total(2)] if first else []
    if second:
        sums.append(total(3 if passed else 2))
    for ref, value in zip(refs, sums):
        ref[...] = value.astype(BF)


def merge_sums(low, came, kept, last, passed):
    steps = 3
    args, specs, shapes, outs = [], [], [], []

    def part(array, count, start):
        args.append(array)
        size = count // steps
        specs.append(pl.BlockSpec((size, BLK, BLK), lambda i: (i + start * steps, 0, 0)))

    def out(count):
        shapes.append(jax.ShapeDtypeStruct((count, BLK, BLK), BF))
        outs.append(pl.BlockSpec((count // steps, BLK, BLK), lambda i: (i, 0, 0)))

    if low is not None:
        count = low.shape[0] // 2
        for start in range(2):
            part(low, count, start)
            part(came, count, start)
            out(count)
    if kept is not None:
        for array in (kept, last) if passed is None else (kept, last, passed):
            part(array, kept.shape[0], 0)
        out(kept.shape[0])
    body = functools.partial(merge_body, low is not None, kept is not None, passed is not None)
    return pl.pallas_call(
        body,
        grid=(steps,),
        in_specs=specs,
        out_specs=outs,
        out_shape=shapes,
        compiler_params=params(46),
        cost_estimate=cost(0, 6 * MIB),
        name="merge_sums",
    )(*args)


def two_terms(values):
    high = values.astype(BF)
    return high, (values - high.astype(F32)).astype(BF)


def update_body(count, *refs):
    parts = refs[:count]
    m_ref, sl_ref, sr_ref, rl_ref, rr_ref, g_out, sl_out, sr_out, m_out = refs[count:]

    def long_left(terms, axis):
        return jnp.concatenate([terms[0], terms[0], terms[1]], axis)

    def long_right(terms, axis):
        return jnp.concatenate([terms[0], terms[1], terms[0]], axis)

    count = range(g_out.shape[0])
    totals = [sum(part[i].astype(F32) for part in parts) for i in count]
    grads = [two_terms(total) for total in totals]
    talls = [long_right(grad, 0) for grad in grads]
    inners = [mul_nn(long_left(two_terms(rl_ref[i]), 1), talls[i]) for i in count]
    for i in count:
        g_out[i] = totals[i]
        sl_out[i] = sl_ref[i] + mul_nt(long_left(grads[i], 1), long_right(grads[i], 1))
    directions = [
        mul_nn(long_left(two_terms(inners[i]), 1), long_right(two_terms(rr_ref[i]), 0))
        for i in count
    ]
    for i in count:
        sr_out[i] = sr_ref[i] + mul_tn(long_left(grads[i], 0), talls[i])
    for i in count:
        master, direction = m_ref[i], directions[i]
        scale = jnp.sqrt(jnp.mean(master * master, keepdims=True) + 1e-06)
        scale = scale * lax.rsqrt(jnp.mean(direction * direction, keepdims=True) + 1e-06)
        m_out[i] = master - 0.3 * scale * direction


def update(parts, master, stat_left, stat_right, root_left, root_right):
    count = master.shape[0]
    group = 6 if count % 6 == 0 else 1
    block = pl.BlockSpec((group, BLK, BLK), lambda i: (i, 0, 0))
    shape = jax.ShapeDtypeStruct(master.shape, F32)
    return pl.pallas_call(
        functools.partial(update_body, len(parts)),
        grid=(count // group,),
        in_specs=[block] * (len(parts) + 5),
        out_specs=[block] * 4,
        out_shape=[shape] * 4,
        compiler_params=params(),
        cost_estimate=cost(48 * count * BLK**3, 15 * MIB),
        name="block_update",
    )(*parts, master, stat_left, stat_right, root_left, root_right)


def pair_moves():
    moves_same, moves_cross = [], []
    for z in range(4):
        for c in range(2):
            for moves, bit in ((moves_same, z % 2), (moves_cross, 1 - z % 2)):
                moves.append((z * 2 + c, (2 * c + bit) * 2 + z // 2))
    return moves_same, moves_cross


def row_part(values, which):
    return lax.dynamic_index_in_dim(values, which, 0, False)


def move_rows(values, crossed, back=False):
    moves = pair_moves()[crossed]
    return lax.ppermute(values, ("seq", "core"), [(b, a) for a, b in moves] if back else moves)


def in_order(kept, crossed, parity):
    return jnp.where(parity == 0, kept, crossed), jnp.where(parity == 0, crossed, kept)


def spread_rows(values, parity):
    kept = move_rows(row_part(values, parity), False)
    crossed = move_rows(row_part(values, 1 - parity), True)
    return jnp.concatenate(in_order(kept, crossed, parity), 0)


def swap_cores(values):
    return lax.ppermute(values, "core", [(0, 1), (1, 0)])


def chip_orders(chips):
    bits = [1 << i for i in range(chips.bit_length() - 1)]
    return bits, bits[::-1]


def offsets(order):
    result = [0]
    for bit in order:
        result = result + [o ^ bit for o in result]
    return result


def place_lists(chips, owned, planes):
    shape = (2, planes, chips, owned)
    by_core = np.array([offsets(order) for order in chip_orders(chips)], np.int32)
    grid = np.indices(shape).astype(np.int32).reshape(4, 2, -1)
    offset = np.broadcast_to(by_core[:, None, :, None], shape).reshape(2, -1)
    return grid[1, 0], offset, grid[3, 0]


def arrival_order(chips, owned, planes):
    per_plane, quarter = chips * owned, owned
    if chips != 4:
        return np.arange(planes * per_plane)
    pieces = [(0, 0)]
    for k in range(1, planes + 1):
        pieces += [(k, 0)] if k < planes else []
        pieces += [(k - 1, 1), (k - 1, 2)]
        pieces += [(k - 2, 3)] if k > 1 else []
    pieces.append((planes - 1, 3))
    starts = [k * per_plane + r * quarter for k, r in pieces]
    return np.concatenate([np.arange(start, start + quarter) for start in starts])


def swap_chips(values, bits):
    chips = lax.axis_size("chip")
    moves = [(i * 2 + c, (i ^ bits[c]) * 2 + c) for i in range(chips) for c in range(2)]
    return lax.ppermute(values, ("chip", "core"), moves)


def move_planes(values, shift):
    planes = lax.axis_size("seq")
    return lax.ppermute(values, "seq", [(i, (i + shift) % planes) for i in range(planes)])


def after(value, *deps):
    return lax.optimization_barrier((value, *deps))[0]


def together(*values):
    return lax.optimization_barrier(values)


def chip_steps():
    return list(zip(*chip_orders(lax.axis_size("chip"))))


def finish_pieces(pieces):
    for bits in chip_steps()[2:]:
        joined = jnp.concatenate(pieces, 0)
        pieces = [joined, swap_chips(joined, bits)]
    return pieces


def add_halves(kept, came):
    return (kept.astype(F32) + came.astype(F32)).astype(BF)


def pack_terms(values):
    high = lax.optimization_barrier(values.astype(BF))
    low = (values - high.astype(F32)).astype(BF)
    terms = jnp.stack([high, low]).reshape(-1, BLK)
    return jnp.pad(terms, ((0, BLK - terms.shape[0]), (0, 0)))[None]


def unpack_terms(blocks, shape):
    terms = blocks.reshape(-1, BLK, BLK)[:, : 2 * shape[0] * shape[1] // BLK]
    terms = terms.reshape(-1, 2, *shape).astype(F32)
    return terms[:, 0] + terms[:, 1]


def finish_sums(keep, send):
    for bits in chip_steps()[::-1][1:-1]:
        count = keep.shape[0] // 2
        came = swap_chips(send, bits)
        send = add_halves(keep[count:], came[count:])
        keep = add_halves(keep[:count], came[:count])
    return keep, send


def by_chip(riders, me, core):
    chips = lax.axis_size("chip")
    ranks = np.array([np.argsort(offsets(order[::-1])) for order in chip_orders(chips)], np.int32)
    rank = jnp.asarray(ranks)[core][me ^ jnp.arange(chips, dtype=jnp.int32)]
    return riders.reshape(chips, -1, BLK, BLK)[rank]


def local(
    tokens,
    cotangent,
    lengths,
    owner_perm,
    master,
    norm_gains,
    stat_left,
    stat_right,
    root_left,
    root_right,
    moment_first,
    moment_second,
):
    core = lax.axis_index("core")
    place_z = lax.axis_index("seq")
    parity = place_z % 2
    block_count = owner_perm.shape[0]
    owned = master.shape[0]
    half = block_count // 2

    chips, planes = lax.axis_size("chip"), lax.axis_size("seq")
    me = lax.axis_index("chip")

    pair_lengths = jnp.stack([lengths, swap_cores(lengths)])
    pair_lengths = jnp.where(core == 0, pair_lengths, pair_lengths[::-1]).reshape(-1)
    length = lax.dynamic_index_in_dim(pair_lengths, place_z, 0, False)
    span = tokens.shape[0] * tokens.shape[1]
    live = jnp.stack([length - core * span, length - (1 - core) * span, length - core * span, parity])

    distance, offset, slot = place_lists(chips, owned, planes)
    offset = jnp.where(core == 0, offset, offset[::-1])
    device = ((place_z - distance) % planes * chips + (me ^ offset)) * 2
    device = device + jnp.stack([core, 1 - core])[:, None]
    table = owner_perm[(device * owned + slot).reshape(-1)]
    sums_table = jnp.asarray(source_numbers())[table[:half]]
    arrive = arrival_order(chips, owned, planes)
    near_slots, far_slots = device * owned + slot
    table = owner_perm[jnp.concatenate([near_slots[arrive], far_slots[arrive]])]

    shard = master.astype(BF)
    first_bits, second_bits = chip_steps()[:2]
    per_plane = chips * owned
    by_phase = chips == 4
    rows = (row_part(tokens, parity), row_part(tokens, 1 - parity))
    cross, held, weights, first = None, (), None, 0
    came, turned = swap_chips(shard, first_bits), swap_chips(shard, second_bits)
    next_shard = move_planes(shard, 1)
    pieces = [[shard, came, turned]]

    def place(parts, first, weights):
        others = [swap_cores(part) for part in parts]
        weights = place_blocks(table, first, parts, others, weights)
        return weights, first + sum(part.shape[0] for part in parts)

    for k in range(1, planes):
        ready = () if k == 1 else (cross, *held, live, table, sums_table)
        ready = ready if weights is None else (*ready, weights)
        this_shard, came, turned, row_a, row_b, *done = together(
            next_shard, came, turned, *rows, *ready
        )
        if k > 1:
            pieces[k - 2].append(done[0])
        cross = swap_chips(came, second_bits)
        arrived = [this_shard, came, turned, *(pieces[0][:1] if k == 1 else done[:1])]
        arrived = arrived[3:] + arrived[:3] if k == 1 else arrived
        pieces[k - 1][1:] = [came, turned]
        came, turned = swap_chips(this_shard, first_bits), swap_chips(this_shard, second_bits)
        pieces.append([this_shard, came, turned])
        if k < planes - 1:
            next_shard = move_planes(this_shard, 1)
        else:
            row_same = move_rows(row_a, False)
            row_cross = move_rows(after(row_b, row_same), True)
        if by_phase:
            if k > 1:
                weights, first = place(done[1:2], first, weights)
            held = (jnp.concatenate(arrived, 0),)
    came, turned, done, row_same, row_cross, *held = together(
        came, turned, cross, row_same, row_cross, *held, *([] if weights is None else [weights])
    )
    own_tokens = jnp.concatenate(in_order(row_same, row_cross, parity), 0)
    pieces[-2].append(done)
    pieces[-1][1:] = [came, turned, swap_chips(came, second_bits)]
    normed1, normed1_t = norm_tokens(own_tokens, norm_gains)
    if by_phase:
        weights, first = place(held[:1], first, weights)
        parts = [came, turned, done]
        others = [swap_cores(part) for part in parts]
        last, normed1, *_ = together(pieces[-1][-1], normed1, weights, *others)
        weights = place_blocks(table, first, parts, others, weights)
        first += 3 * owned
        other_normed = swap_cores(normed1)
        weights, _ = place([last], first, weights)
    else:
        for each in pieces:
            each = [jnp.concatenate(finish_pieces(each), 0)]
            weights, first = place(each, first, weights)
        other_normed = swap_cores(normed1)
    own_cot = spread_rows(after(cotangent, weights), parity)

    own_qkv, other_kv = project(normed1, other_normed, weights)
    attended, q_aug = attend(live, own_qkv, other_kv)
    kept, crossed, g_rest, grad_middle, grad_attended, gain_second = feed(
        live, own_tokens, attended, own_cot, norm_gains, weights
    )
    other_rest = swap_cores(g_rest)
    kept, crossed = move_rows(kept, False, True), move_rows(crossed, True, True)
    layer_out = jnp.stack(in_order(kept, crossed, parity), 0)
    d_query, d_own, d_other = attend_back(live, q_aug, own_qkv, other_kv, attended, grad_attended)
    received = swap_cores(after(d_other, kept, crossed))
    flat = lambda g: g.reshape(-1, BLK, BLK)
    g_query, partial = query_back(normed1_t, d_query, weights)
    g_query = flat(g_query)
    other_query = swap_cores(g_query)
    g_kv, back = input_back(normed1_t, d_own, received, partial, weights)
    g_kv = flat(g_kv)
    other_kv_grad = swap_cores(after(g_kv, other_query))
    own_grads = (g_query, g_kv, g_rest)
    other_grads = (other_query, other_kv_grad, other_rest)
    half_plane = per_plane // 2
    last_bits, before_bits = chip_steps()[-1], chip_steps()[0]
    moved_rows, lows, sent, passed, riders_z = [], [], None, None, []

    def sums(k, part, held):
        first = k * per_plane + part * half_plane
        return gather_sums(held, first, half_plane, own_grads, other_grads)

    order = list(range(planes))[::-1]
    high = sums(order[0], 1, sums_table)
    held = sums_table
    held_riders = []
    for turn in range(planes + 1):
        group, moves = [], []
        if turn < planes:
            group.append(high)
            moves.append(lambda v: swap_chips(v, last_bits))
        if 1 <= turn <= planes:
            group.append(sent)
            moves.append(lambda v: swap_chips(v, before_bits))
        if 2 <= turn <= planes:
            group.append(part)
            moves.append(lambda v: move_planes(v, -1))
        if turn in (1, 2):
            group.append(riders)
            bits = last_bits if turn == 1 else before_bits
            moves.append(lambda v: swap_chips(v, bits))
        if turn in (1, 2):
            group.append(rows[turn - 1])
            crossed = turn == 2
            moves.append(lambda v: move_rows(v, crossed, True))
        far_riders = [1, 2] if turn == planes - 1 else []
        group += [rider for _ in far_riders]
        moves += [functools.partial(move_planes, shift=-k) for k in far_riders]
        came = [move(value) for move, value in zip(moves, together(*group, *moved_rows, *held_riders))]
        if turn in (1, 2):
            moved_rows.append(came.pop())
            riders = jnp.concatenate([riders, came.pop()], 0)
            for bits in chip_steps()[::-1][1:-1] if turn == 1 else ():
                riders = jnp.concatenate([riders, swap_chips(riders, bits)], 0)
        count = len(came) - len(far_riders)
        riders_z, came = riders_z + came[count:], came[:count]
        if far_riders:
            riders_z += [move_planes(after(rider, *riders_z), -k) for k in range(3, planes)]
        if turn == planes:
            parts = [keep_before, *came]
            continue
        passed = came.pop() if turn >= 2 else None
        low = sums(order[turn], 0, after(held, high))
        if turn + 1 < planes:
            high = sums(order[turn + 1], 1, after(held, low))
        held = after(sums_table, *came)
        held_riders = [riders] if turn == 2 else []
        if turn == 0:
            kept, crossed, gain_first = input_end(
                live, own_tokens, norm_gains, after(back, high), grad_middle
            )
            rows = [kept, crossed]
            gain_part = jnp.concatenate([gain_first, gain_second], 0)
            mine = pack_terms(gain_part)
            pair = jnp.concatenate([mine, swap_cores(mine)], 0)
            riders = jnp.where(core == 0, pair, pair[::-1])
        if turn == 2:
            plane_gain = by_chip(riders, me, core)
            plane_gain = jnp.sum(unpack_terms(plane_gain, gain_part.shape), 0)
            rider = pack_terms(plane_gain)
        second = (None, None, None) if turn == 0 else (keep_before, came[-1], passed)
        keep, sent, *part = merge_sums(low, came[0], *second)
        part = part[0] if part else None
        keep_before, sent = finish_sums(keep, sent)
    input_grad = jnp.stack(in_order(*moved_rows, parity), 0).astype(F32)
    planes_gain = [unpack_terms(each, gain_part.shape)[0] for each in (rider, *riders_z)]
    turned = (jnp.arange(planes, dtype=jnp.int32) - place_z) % planes
    gain_grad = jnp.sum(jnp.stack(planes_gain)[turned], 0)
    grad_blocks, stat_left_new, stat_right_new, master_new = update(
        parts, master, stat_left, stat_right, root_left, root_right
    )
    first_new = 0.9 * moment_first + 0.1 * gain_grad
    second_new = 0.999 * moment_second + 0.001 * gain_grad * gain_grad
    first_hat = first_new / (1.0 - 0.9**STEP)
    second_hat = second_new / (1.0 - 0.999**STEP)
    gains_new = norm_gains - 0.5 * first_hat / (jnp.sqrt(second_hat) + 1e-08)
    return (
        layer_out,
        input_grad,
        grad_blocks,
        stat_left_new,
        stat_right_new,
        master_new,
        first_new,
        second_new,
        gains_new,
    )


def solution(mesh):
    seq_size, rows_size = mesh.shape["seq"], mesh.shape["rows"]
    mesh = Mesh(mesh.devices.reshape(seq_size, rows_size // 2, 2), ("seq", "chip", "core"))
    activation = P(("chip", "core"), "seq", None)
    blocks = P(("seq", "chip", "core"), None, None)
    return jax.shard_map(
        local,
        mesh=mesh,
        in_specs=(
            activation, activation, P(("chip", "core")), P(), blocks, P(),
            blocks, blocks, blocks, blocks, P(), P(),
        ),
        out_specs=(activation, activation, blocks, blocks, blocks, blocks, P(), P(), P()),
        check_vma=False,
    )
```

```python
import functools
import jax
import jax.numpy as jnp
import numpy as np
from jax import lax
from jax.experimental import pallas as pl
from jax.experimental.pallas import tpu as pltpu
from jax.sharding import Mesh
from jax.sharding import PartitionSpec as P

D = 1024
HD = 64
FF = 4096
BLK = 128
STEP = 10
COLS = 1024
BF = jnp.bfloat16
F32 = jnp.float32
MIB = 1024 * 1024

norm_eps = 1e-05
score_scale = 0.125
masked_score = -1e30


def params(limit=56):
    return pltpu.CompilerParams(vmem_limit_bytes=limit * MIB)


def cost(flops, nbytes):
    return pl.CostEstimate(flops=int(flops), bytes_accessed=int(nbytes), transcendentals=0)


def mul_nn(left, right):
    return jnp.dot(left, right, preferred_element_type=F32)


def mul_nt(left, right):
    return lax.dot_general(left, right, (((1,), (1,)), ((), ())), preferred_element_type=F32)


def mul_tn(left, right):
    return lax.dot_general(left, right, (((0,), (0,)), ((), ())), preferred_element_type=F32)


def join_tile(ref):
    rows, cols = ref.shape[0], ref.shape[1]
    return jnp.concatenate([ref[:, j].reshape(rows * BLK, BLK) for j in range(cols)], axis=1)


def split_tile(ref, matrix):
    rows, cols = ref.shape[0], ref.shape[1]
    for j in range(cols):
        ref[:, j] = matrix[:, j * BLK : (j + 1) * BLK].reshape(rows, BLK, BLK).astype(ref.dtype)


def split_flat(ref, matrix):
    cols = matrix.shape[1] // BLK
    for i in range(matrix.shape[0] // BLK):
        for j in range(cols):
            block = matrix[i * BLK : (i + 1) * BLK, j * BLK : (j + 1) * BLK]
            ref[i * cols + j] = block.astype(ref.dtype)


def normalize(values):
    row_mean = jnp.mean(values, -1, keepdims=True)
    centered = values - row_mean
    row_var = jnp.mean(centered * centered, -1, keepdims=True)
    inv_std = lax.rsqrt(row_var + norm_eps)
    return centered * inv_std, inv_std


def gelu_parts(hidden):
    bell = jnp.exp(hidden * hidden * -0.5)
    t = 1.0 / (1.0 + jnp.abs(hidden) * (0.3275911 * 0.7071067811865476))
    poly = 1.061405429 * t - 1.453152027
    for term in (1.421413741, -0.284496736, 0.254829592):
        poly = poly * t + term
    tail = poly * t * 0.5 * bell
    return jnp.where(hidden < 0.0, tail, 1.0 - tail), hidden * bell * 0.3989422804014327


def norm_back(gradient, unit_vals, inv_std):
    grad_mean = jnp.mean(gradient, -1, keepdims=True)
    cross_mean = jnp.mean(gradient * unit_vals, -1, keepdims=True)
    return inv_std * (gradient - grad_mean - unit_vals * cross_mean)


def place_body(first, pieces, table, *refs):
    near, far = refs[:pieces], refs[pieces : 2 * pieces]
    out_ref, sem = refs[-2:]
    total = 0
    for start, sources in ((first, near), (table.shape[0] // 2 + first, far)):
        for src in sources:
            for slot in range(src.shape[0]):
                pltpu.make_async_copy(src.at[slot], out_ref.at[table[start + slot]], sem).start()
            start += src.shape[0]
            total += src.shape[0]
    done = out_ref.at[pl.ds(0, total)]
    pltpu.make_async_copy(done, done, sem).wait()


def place_blocks(table, first, near, far, kept):
    smem = pl.BlockSpec(memory_space=pltpu.SMEM)
    hbm = pl.BlockSpec(memory_space=pltpu.HBM)
    vmem = pl.BlockSpec(memory_space=pltpu.VMEM)
    kept = () if kept is None else (kept,)
    count = 2 * len(near)
    return pl.pallas_call(
        functools.partial(place_body, first, len(near)),
        out_shape=jax.ShapeDtypeStruct((table.shape[0], BLK, BLK), BF),
        in_specs=[smem] + [vmem] * count + [hbm] * len(kept),
        out_specs=hbm,
        scratch_shapes=[pltpu.SemaphoreType.DMA],
        input_output_aliases={1 + count: 0} if kept else {},
        compiler_params=params(46),
        cost_estimate=cost(0, 6 * MIB),
        name="place_weights",
    )(table, *near, *far, *kept)


def norm_body(tokens_ref, gains_ref, out_ref, turned_ref):
    normed = normalize(tokens_ref[...].astype(F32))[0] * gains_ref[0:1]
    out_ref[...] = normed.astype(BF)
    turned_ref[...] = normed.T.astype(BF)


def norm_tokens(tokens, gains):
    span = tokens.shape[0]
    steps = 4
    part = pl.BlockSpec((span // steps, D), lambda i: (i, 0))
    return pl.pallas_call(
        norm_body,
        grid=(steps,),
        in_specs=[part, pl.BlockSpec((2, D), lambda i: (0, 0))],
        out_specs=[part, pl.BlockSpec((D, span // steps), lambda i: (0, i))],
        out_shape=[jax.ShapeDtypeStruct((span, D), BF), jax.ShapeDtypeStruct((D, span), BF)],
        compiler_params=params(46),
        cost_estimate=cost(0, 3 * MIB),
        name="norm_tokens",
    )(tokens, gains)


def qkv_body(own_ref, other_ref, w_ref, own_out, other_out):
    step = pl.program_id(0)
    weight = join_tile(w_ref)
    own_out[...] = mul_nn(own_ref[...], weight).astype(BF)

    @pl.when(step >= D // COLS)
    def _():
        other_out[...] = mul_nn(other_ref[...], weight).astype(BF)


def project(own, other, weights):
    span = own.shape[0]
    skip = D // COLS
    once = pl.BlockSpec((span, D), lambda j: (0, 0))
    return pl.pallas_call(
        qkv_body,
        grid=(3 * D // COLS,),
        in_specs=[
            once,
            once,
            pl.BlockSpec((D // BLK, COLS // BLK, BLK, BLK), lambda j: (0, j, 0, 0)),
        ],
        out_specs=[
            pl.BlockSpec((span, COLS), lambda j: (0, j)),
            pl.BlockSpec((span, COLS), lambda j: (0, jnp.maximum(j - skip, 0))),
        ],
        out_shape=[
            jax.ShapeDtypeStruct((span, 3 * D), BF),
            jax.ShapeDtypeStruct((span, 2 * D), BF),
        ],
        compiler_params=params(),
        cost_estimate=cost(10 * span * D * D, 12 * MIB),
        name="qkv_projection",
    )(own, other, weights.reshape(-1, 3 * D // BLK, BLK, BLK))


def lane_masks(head):
    lane = lax.broadcasted_iota(jnp.int32, (1, BLK), 1)
    first = HD * (1 - head)
    keep = (lane // HD == head).astype(F32)
    dead_lane = (lane == first).astype(F32)
    terms = [(lane == first + 1 + i).astype(F32) for i in range(3)]
    return keep, dead_lane, terms


def three_terms(values):
    high = values.astype(BF).astype(F32)
    rest = values - high
    middle = rest.astype(BF).astype(F32)
    return high, middle, rest - middle


def key_bias(span, live_count):
    row = lax.broadcasted_iota(jnp.int32, (span, 1), 0)
    return jnp.where(row < live_count, 0.0, masked_score).astype(F32)


def attend_body(live_ref, q_ref, ko_ref, vo_ref, kx_ref, vx_ref, out_ref, aug_ref):
    span = q_ref.shape[0]
    bias_own = key_bias(span, live_ref[0])
    bias_other = key_bias(span, live_ref[1])
    queries = q_ref[...].astype(F32) * score_scale
    k_own, k_other = ko_ref[...].astype(F32), kx_ref[...].astype(F32)
    v_own_f, v_other_f = vo_ref[...].astype(F32), vx_ref[...].astype(F32)
    results, scores = [], []
    for head in range(2):
        keep, dead_lane, _ = lane_masks(head)
        q_head = (queries * keep + dead_lane).astype(BF)
        s_own = mul_nt(q_head, (k_own * keep + bias_own * dead_lane).astype(BF))
        s_other = mul_nt(q_head, (k_other * keep + bias_other * dead_lane).astype(BF))
        scores.append((q_head, s_own, s_other))
    for head in range(2):
        keep, _, terms = lane_masks(head)
        q_head, s_own, s_other = scores[head]
        top = jnp.max(jnp.maximum(s_own, s_other), -1, keepdims=True)
        p_own = jnp.exp(s_own - top)
        p_other = jnp.exp(s_other - top)
        v_own = (v_own_f * keep + (1.0 - keep)).astype(BF)
        v_other = (v_other_f * keep + (1.0 - keep)).astype(BF)
        mixed = mul_nn(p_own.astype(BF), v_own) + mul_nn(p_other.astype(BF), v_other)
        total = mixed[:, HD * (1 - head) : HD * (1 - head) + 1]
        results.append(mixed / total * keep)
        parts = three_terms(-(top + jnp.log(total)))
        stats = sum(part * lane for part, lane in zip(parts, terms))
        aug_ref[:, head * BLK : (head + 1) * BLK] = (q_head.astype(F32) + stats).astype(BF)
    out_ref[...] = (results[0] + results[1]).astype(BF)


def attend(live, own, other):
    span = own.shape[0]
    pairs = D // BLK
    col = lambda shift: pl.BlockSpec((span, BLK), lambda p: (0, p + shift))
    return pl.pallas_call(
        attend_body,
        grid=(pairs,),
        in_specs=[
            pl.BlockSpec(memory_space=pltpu.SMEM),
            col(0),
            col(pairs),
            col(2 * pairs),
            col(0),
            col(pairs),
        ],
        out_specs=[col(0), pl.BlockSpec((span, 2 * BLK), lambda p: (0, p))],
        out_shape=[
            jax.ShapeDtypeStruct((span, D), BF),
            jax.ShapeDtypeStruct((span, 2 * D), BF),
        ],
        compiler_params=params(),
        cost_estimate=cost(40 * span * span * D, 8 * MIB),
        name="attention",
    )(live, own, own, own, other, other)


def attend_back_body(
    live_ref, aug_ref, ko_ref, vo_ref, kx_ref, vx_ref, at_ref, g_ref, dq_ref, own_ref, other_ref
):
    span = at_ref.shape[0]
    grads = g_ref[...].astype(F32)
    product = grads * at_ref[...].astype(F32)
    keeps, g_augs, q_augs = [], [], []
    for head in range(2):
        keep, dead_lane, terms = lane_masks(head)
        delta = jnp.sum(product * keep, -1, keepdims=True)
        parts = three_terms(-delta)
        stats = sum(part * lane for part, lane in zip(parts, terms))
        g_augs.append((grads * keep + stats).astype(BF))
        q_augs.append(aug_ref[:, head * BLK : (head + 1) * BLK])
    d_query = [None, None]
    for k_ref, v_ref, out_ref, live in (
        (ko_ref, vo_ref, own_ref, live_ref[0]),
        (kx_ref, vx_ref, other_ref, live_ref[1]),
    ):
        bias = key_bias(span, live)
        keys = k_ref[...]
        keys_f, values_f = keys.astype(F32), v_ref[...].astype(F32)
        d_keys = d_values = None
        for head in range(2):
            keep, dead_lane, terms = lane_masks(head)
            ones = terms[0] + terms[1] + terms[2]
            k_aug = (keys_f * keep + (bias * dead_lane + ones)).astype(BF)
            v_aug = (values_f * keep + ones).astype(BF)
            probs = jnp.exp(mul_nt(k_aug, q_augs[head]))
            d_scores = (probs * mul_nt(v_aug, g_augs[head])).astype(BF)
            value_part = mul_nn(probs.astype(BF), g_augs[head]) * keep
            key_part = mul_nn(d_scores, q_augs[head]) * keep
            query_part = mul_tn(keys, d_scores)[head * HD : (head + 1) * HD]
            d_query[head] = query_part if d_query[head] is None else d_query[head] + query_part
            d_values = value_part if d_values is None else d_values + value_part
            d_keys = key_part if d_keys is None else d_keys + key_part
        out_ref[0] = d_keys.astype(out_ref.dtype)
        out_ref[1] = d_values.astype(out_ref.dtype)
    dq_ref[...] = (jnp.concatenate(d_query, 0).T * score_scale).astype(BF)


def attend_back(live, aug, own, other, attended, grads):
    span = own.shape[0]
    pairs = D // BLK
    col = lambda shift: pl.BlockSpec((span, BLK), lambda p: (0, p + shift))
    pair_out = pl.BlockSpec((2, span, BLK), lambda p: (0, 0, p))
    return pl.pallas_call(
        attend_back_body,
        grid=(pairs,),
        in_specs=[
            pl.BlockSpec(memory_space=pltpu.SMEM),
            pl.BlockSpec((span, 2 * BLK), lambda p: (0, p)),
            col(pairs),
            col(2 * pairs),
            col(0),
            col(pairs),
            col(0),
            col(0),
        ],
        out_specs=[col(0), pair_out, pair_out],
        out_shape=[
            jax.ShapeDtypeStruct((span, D), BF),
            jax.ShapeDtypeStruct((2, span, D), BF),
            jax.ShapeDtypeStruct((2, span, D), BF),
        ],
        compiler_params=params(),
        cost_estimate=cost(60 * span * span * D, 12 * MIB),
        name="attention_backward",
    )(live, aug, own, own, other, other, attended, grads)


def feed_body(
    live_ref,
    tokens_ref,
    attended_ref,
    cot_ref,
    gains_ref,
    wo_ref,
    wu_ref,
    wd_ref,
    kept_ref,
    crossed_ref,
    rest_ref,
    gm_ref,
    ga_ref,
    gain_ref,
    unit,
    inv,
    normed,
    normed_t,
    top,
    acc_out,
    acc_back,
    up_stage,
    down_stage,
    out_stage,
    sems,
    out_sem,
):
    step = pl.program_id(0)
    place = step % 2
    side, width = up_stage.shape[1], up_stage.shape[2]
    per_tile = side * width
    up_first = side * side
    down_first = up_first + side * FF // BLK

    def drain(which):
        pltpu.make_async_copy(up_stage.at[which], up_stage.at[which], sems.at[0, which]).wait()
        pltpu.make_async_copy(down_stage.at[which], down_stage.at[which], sems.at[1, which]).wait()
    span = tokens_ref.shape[0]

    @pl.when(step == 0)
    def _():
        weight = join_tile(wo_ref)
        middle = tokens_ref[...].astype(F32) + mul_nn(attended_ref[...], weight)
        unit_vals, inv_std = normalize(middle)
        unit[...] = unit_vals
        inv[...] = inv_std
        normed_vals = unit_vals * gains_ref[1:2]
        normed[...] = normed_vals.astype(BF)
        normed_t[...] = normed_vals.T.astype(BF)
        row = lax.broadcasted_iota(jnp.int32, (span, 1), 0)
        top[...] = jnp.where(row < live_ref[2], cot_ref[...].astype(F32), 0.0).astype(BF)
        acc_out[...] = middle
        acc_back[...] = jnp.zeros_like(acc_back)

    w_up = join_tile(wu_ref)
    w_down = join_tile(wd_ref)
    hidden = mul_nn(normed[...], w_up)
    grad_act = mul_nt(top[...], w_down)
    share, slope_rest = gelu_parts(hidden)
    activated = (hidden * share).astype(BF)
    grad_hidden = (grad_act * (share + slope_rest)).astype(BF)
    acc_out[...] += mul_nn(activated, w_down)
    acc_back[...] += mul_nt(grad_hidden, w_up)

    @pl.when(step >= 2)
    def _():
        drain(place)

    split_flat(down_stage.at[place], mul_tn(activated, top[...]))
    dest = rest_ref.at[pl.ds(down_first + step * per_tile, per_tile)]
    pltpu.make_async_copy(down_stage.at[place], dest, sems.at[1, place]).start()
    split_tile(up_stage.at[place], mul_nn(normed_t[...], grad_hidden))
    for i in range(side):
        dest = rest_ref.at[pl.ds(up_first + i * (FF // BLK) + step * width, width)]
        pltpu.make_async_copy(up_stage.at[place, i], dest, sems.at[0, place]).start()

    @pl.when(step == pl.num_programs(0) - 1)
    def _():
        for flip in range(2):

            @pl.when(live_ref[3] == flip)
            def _():
                for ref, part in ((kept_ref, flip), (crossed_ref, 1 - flip)):
                    ref[...] = acc_out[part * (span // 2) : (part + 1) * (span // 2)].astype(BF)

        unit_vals = unit[...]
        back = acc_back[...]
        gain_ref[...] = jnp.sum(back * unit_vals, 0, keepdims=True)
        grad_middle = top[...].astype(F32) + norm_back(back * gains_ref[1:2], unit_vals, inv[...])
        gm_ref[...] = grad_middle
        back_middle = grad_middle.astype(BF)
        split_flat(out_stage, mul_tn(attended_ref[...], back_middle))
        out_copy = pltpu.make_async_copy(out_stage, rest_ref.at[pl.ds(0, up_first)], out_sem)
        out_copy.start()
        ga_ref[...] = mul_nt(back_middle, join_tile(wo_ref)).astype(BF)
        drain(1 - place)
        drain(place)
        out_copy.wait()


def feed(live, tokens, attended, cotangent, gains, weights):
    span = tokens.shape[0]
    side, width = D // BLK, COLS // BLK
    whole = lambda j: (0, 0)
    act = pl.BlockSpec((span, D), whole)
    once = pl.BlockSpec((span, D), whole, pipeline_mode=pl.Buffered(1))
    half_act = pl.BlockSpec((span // 2, D), whole)
    per_row = weights.reshape(-1, side, BLK, BLK)
    per_up = weights.reshape(-1, FF // BLK, BLK, BLK)
    out_row = (3 * side * side) // side // side
    up_row = 4 * side * side // (FF // BLK) // side
    down_row = (4 * side * side + side * FF // BLK) // side // width
    return pl.pallas_call(
        feed_body,
        grid=(FF // COLS,),
        in_specs=[
            pl.BlockSpec(memory_space=pltpu.SMEM),
            once,
            once,
            once,
            pl.BlockSpec((2, D), whole),
            pl.BlockSpec(
                (side, side, BLK, BLK),
                lambda j: (out_row, 0, 0, 0),
                pipeline_mode=pl.Buffered(1),
            ),
            pl.BlockSpec((side, width, BLK, BLK), lambda j: (up_row, j, 0, 0)),
            pl.BlockSpec((width, side, BLK, BLK), lambda j: (down_row + j, 0, 0, 0)),
        ],
        out_specs=[
            half_act,
            half_act,
            pl.BlockSpec(memory_space=pltpu.HBM),
            act,
            act,
            pl.BlockSpec((1, D), whole),
        ],
        out_shape=[
            jax.ShapeDtypeStruct((span // 2, D), BF),
            jax.ShapeDtypeStruct((span // 2, D), BF),
            jax.ShapeDtypeStruct((side * side + 2 * side * (FF // BLK), BLK, BLK), BF),
            jax.ShapeDtypeStruct((span, D), F32),
            jax.ShapeDtypeStruct((span, D), BF),
            jax.ShapeDtypeStruct((1, D), F32),
        ],
        scratch_shapes=[
            pltpu.VMEM((span, D), F32),
            pltpu.VMEM((span, 1), F32),
            pltpu.VMEM((span, D), BF),
            pltpu.VMEM((D, span), BF),
            pltpu.VMEM((span, D), BF),
            pltpu.VMEM((span, D), F32),
            pltpu.VMEM((span, D), F32),
            pltpu.VMEM((2, side, width, BLK, BLK), BF),
            pltpu.VMEM((2, side * width, BLK, BLK), BF),
            pltpu.VMEM((side * side, BLK, BLK), BF),
            pltpu.SemaphoreType.DMA((2, 2)),
            pltpu.SemaphoreType.DMA,
        ],
        compiler_params=params(),
        cost_estimate=cost(14 * span * D * FF, 50 * MIB),
        name="feed_forward",
    )(live, tokens, attended, cotangent, gains, per_row, per_up, per_row)


def query_body(normed_t, dq_ref, w_ref, grad_ref, acc_ref):
    step = pl.program_id(0)

    @pl.when(step == 0)
    def _():
        acc_ref[...] = jnp.zeros_like(acc_ref)

    grad = dq_ref[...]
    acc_ref[...] += mul_nt(grad, join_tile(w_ref))
    split_tile(grad_ref, mul_nn(normed_t[...], grad))


def query_back(normed1_t, d_query, weights):
    span = normed1_t.shape[1]
    side, width = D // BLK, COLS // BLK
    whole = lambda j: (0, 0)
    act = pl.BlockSpec((span, D), whole)
    tile = pl.BlockSpec((side, width, BLK, BLK), lambda j: (0, j, 0, 0))
    return pl.pallas_call(
        query_body,
        grid=(D // COLS,),
        in_specs=[
            pl.BlockSpec((D, span), whole),
            pl.BlockSpec((span, COLS), lambda j: (0, j)),
            tile,
        ],
        out_specs=[tile, act],
        out_shape=[
            jax.ShapeDtypeStruct((side, side, BLK, BLK), BF),
            jax.ShapeDtypeStruct((span, D), F32),
        ],
        compiler_params=params(),
        cost_estimate=cost(4 * span * D * D, 8 * MIB),
        name="query_backward",
    )(normed1_t, d_query, weights.reshape(-1, 3 * side, BLK, BLK))


def input_body(normed_t, own_ref, recv_ref, acc_ref, w_ref, grad_ref, out_ref):
    step = pl.program_id(0)

    @pl.when(step == 0)
    def _():
        out_ref[...] = acc_ref[...]

    grad = (own_ref[0].astype(F32) + recv_ref[0].astype(F32)).astype(BF)
    out_ref[...] += mul_nt(grad, join_tile(w_ref))
    split_tile(grad_ref, mul_nn(normed_t[...], grad))


def input_back(normed1_t, own, received, partial, weights):
    span = normed1_t.shape[1]
    side, width = D // BLK, COLS // BLK
    per = D // COLS
    whole = lambda j: (0, 0)
    act = pl.BlockSpec((span, D), whole)
    part = pl.BlockSpec((1, span, COLS), lambda j: (j // per, 0, j % per))
    return pl.pallas_call(
        input_body,
        grid=(2 * per,),
        in_specs=[
            pl.BlockSpec((D, span), whole),
            part,
            part,
            act,
            pl.BlockSpec((side, width, BLK, BLK), lambda j: (0, j + per, 0, 0)),
        ],
        out_specs=[pl.BlockSpec((side, width, BLK, BLK), lambda j: (0, j, 0, 0)), act],
        out_shape=[
            jax.ShapeDtypeStruct((side, 2 * side, BLK, BLK), BF),
            jax.ShapeDtypeStruct((span, D), F32),
        ],
        compiler_params=params(),
        cost_estimate=cost(8 * span * D * D, 20 * MIB),
        name="input_backward",
    )(normed1_t, own, received, partial, weights.reshape(-1, 3 * side, BLK, BLK))


def input_end_body(live_ref, tokens_ref, gains_ref, back_ref, gm_ref, kept_ref, crossed_ref, gain_ref):
    step = pl.program_id(0)
    unit_vals, inv_std = normalize(tokens_ref[...].astype(F32))
    back = back_ref[...]

    @pl.when(step == 0)
    def _():
        gain_ref[...] = jnp.zeros_like(gain_ref)

    gain_ref[...] += jnp.sum(back * unit_vals, 0, keepdims=True)
    grad = (gm_ref[...] + norm_back(back * gains_ref[0:1], unit_vals, inv_std)).astype(BF)
    half = step // (pl.num_programs(0) // 2)
    rows = tokens_ref.shape[0]
    start = pl.multiple_of(step % (pl.num_programs(0) // 2) * rows, rows)

    @pl.when(half == live_ref[3])
    def _():
        kept_ref[pl.ds(start, rows)] = grad

    @pl.when(half != live_ref[3])
    def _():
        crossed_ref[pl.ds(start, rows)] = grad


def input_end(live, tokens, gains, back, grad_middle):
    span = tokens.shape[0]
    steps = 4
    part = pl.BlockSpec((span // steps, D), lambda i: (i, 0))
    half_act = pl.BlockSpec((span // 2, D), lambda i: (0, 0))
    row = lambda count: pl.BlockSpec((count, D), lambda i: (0, 0))
    return pl.pallas_call(
        input_end_body,
        grid=(steps,),
        in_specs=[pl.BlockSpec(memory_space=pltpu.SMEM), part, row(2), part, part],
        out_specs=[half_act, half_act, row(1)],
        out_shape=[
            jax.ShapeDtypeStruct((span // 2, D), BF),
            jax.ShapeDtypeStruct((span // 2, D), BF),
            jax.ShapeDtypeStruct((1, D), F32),
        ],
        compiler_params=params(46),
        cost_estimate=cost(0, 7 * MIB),
        name="input_gradient",
    )(live, tokens, gains, back, grad_middle)


def source_numbers():
    side = D // BLK
    numbers = np.arange(3 * side * side + side * side + 2 * side * (FF // BLK), dtype=np.int32)
    row, col = np.divmod(numbers[: 3 * side * side], 3 * side)
    numbers[: 3 * side * side] = np.where(
        col < side, row * side + col, side * side + row * 2 * side + col - side
    )
    return numbers


def gather_body(first, bounds, table, *refs):
    sources = refs[:6]
    out_ref, stage, sems = refs[6:]
    step = pl.program_id(0)
    count = stage.shape[1] // 2

    def fetch(which, slot):
        start = first + which * count
        for i in range(count):
            number = table[start + i]
            for low, high, own, other in zip(bounds, bounds[1:], sources[:3], sources[3:]):

                @pl.when((number >= low) & (number < high))
                def _():
                    for src, at in ((own, i), (other, count + i)):
                        pltpu.make_async_copy(
                            src.at[number - low], stage.at[slot, at], sems.at[slot]
                        ).start()

    @pl.when(step == 0)
    def _():
        for which in range(stage.shape[0]):
            fetch(which, which)

    slot = step
    pltpu.make_async_copy(stage.at[slot], stage.at[slot], sems.at[slot]).wait()
    total = stage[slot, :count].astype(F32) + stage[slot, count:].astype(F32)
    out_ref[...] = total.astype(BF)


def gather_sums(table, first, count, own, other):
    hbm = pl.BlockSpec(memory_space=pltpu.HBM)
    steps = 4
    part = count // steps
    bounds = np.cumsum([0] + [src.shape[0] for src in own]).tolist()
    return pl.pallas_call(
        functools.partial(gather_body, first, bounds),
        grid=(steps,),
        in_specs=[pl.BlockSpec(memory_space=pltpu.SMEM)] + [hbm] * 6,
        out_specs=pl.BlockSpec((part, BLK, BLK), lambda i: (i, 0, 0)),
        out_shape=jax.ShapeDtypeStruct((count, BLK, BLK), BF),
        scratch_shapes=[
            pltpu.VMEM((steps, 2 * part, BLK, BLK), BF),
            pltpu.SemaphoreType.DMA((steps,)),
        ],
        compiler_params=params(52),
        cost_estimate=cost(0, 6 * count * BLK * BLK),
        name="gradient_sums",
    )(table, *own, *other)


def merge_body(first, second, passed, *refs):
    refs = list(refs)

    def total(count):
        return sum(refs.pop(0)[...].astype(F32) for _ in range(count))

    sums = [total(2), total(2)] if first else []
    if second:
        sums.append(total(3 if passed else 2))
    for ref, value in zip(refs, sums):
        ref[...] = value.astype(BF)


def merge_sums(low, came, kept, last, passed):
    steps = 3
    args, specs, shapes, outs = [], [], [], []

    def part(array, count, start):
        args.append(array)
        size = count // steps
        specs.append(pl.BlockSpec((size, BLK, BLK), lambda i: (i + start * steps, 0, 0)))

    def out(count):
        shapes.append(jax.ShapeDtypeStruct((count, BLK, BLK), BF))
        outs.append(pl.BlockSpec((count // steps, BLK, BLK), lambda i: (i, 0, 0)))

    if low is not None:
        count = low.shape[0] // 2
        for start in range(2):
            part(low, count, start)
            part(came, count, start)
            out(count)
    if kept is not None:
        for array in (kept, last) if passed is None else (kept, last, passed):
            part(array, kept.shape[0], 0)
        out(kept.shape[0])
    body = functools.partial(merge_body, low is not None, kept is not None, passed is not None)
    return pl.pallas_call(
        body,
        grid=(steps,),
        in_specs=specs,
        out_specs=outs,
        out_shape=shapes,
        compiler_params=params(46),
        cost_estimate=cost(0, 6 * MIB),
        name="merge_sums",
    )(*args)


def two_terms(values):
    high = values.astype(BF)
    return high, (values - high.astype(F32)).astype(BF)


def update_body(count, *refs):
    parts = refs[:count]
    m_ref, sl_ref, sr_ref, rl_ref, rr_ref, g_out, sl_out, sr_out, m_out = refs[count:]

    def long_left(terms, axis):
        return jnp.concatenate([terms[0], terms[0], terms[1]], axis)

    def long_right(terms, axis):
        return jnp.concatenate([terms[0], terms[1], terms[0]], axis)

    count = range(g_out.shape[0])
    totals = [sum(part[i].astype(F32) for part in parts) for i in count]
    grads = [two_terms(total) for total in totals]
    talls = [long_right(grad, 0) for grad in grads]
    inners = [mul_nn(long_left(two_terms(rl_ref[i]), 1), talls[i]) for i in count]
    for i in count:
        g_out[i] = totals[i]
        sl_out[i] = sl_ref[i] + mul_nt(long_left(grads[i], 1), long_right(grads[i], 1))
    directions = [
        mul_nn(long_left(two_terms(inners[i]), 1), long_right(two_terms(rr_ref[i]), 0))
        for i in count
    ]
    for i in count:
        sr_out[i] = sr_ref[i] + mul_tn(long_left(grads[i], 0), talls[i])
    for i in count:
        master, direction = m_ref[i], directions[i]
        scale = jnp.sqrt(jnp.mean(master * master, keepdims=True) + 1e-06)
        scale = scale * lax.rsqrt(jnp.mean(direction * direction, keepdims=True) + 1e-06)
        m_out[i] = master - 0.3 * scale * direction


def update(parts, master, stat_left, stat_right, root_left, root_right):
    count = master.shape[0]
    group = 6 if count % 6 == 0 else 1
    block = pl.BlockSpec((group, BLK, BLK), lambda i: (i, 0, 0))
    shape = jax.ShapeDtypeStruct(master.shape, F32)
    return pl.pallas_call(
        functools.partial(update_body, len(parts)),
        grid=(count // group,),
        in_specs=[block] * (len(parts) + 5),
        out_specs=[block] * 4,
        out_shape=[shape] * 4,
        compiler_params=params(),
        cost_estimate=cost(48 * count * BLK**3, 15 * MIB),
        name="block_update",
    )(*parts, master, stat_left, stat_right, root_left, root_right)


def pair_moves():
    moves_same, moves_cross = [], []
    for z in range(4):
        for c in range(2):
            for moves, bit in ((moves_same, z % 2), (moves_cross, 1 - z % 2)):
                moves.append((z * 2 + c, (2 * c + bit) * 2 + z // 2))
    return moves_same, moves_cross


def row_part(values, which):
    return lax.dynamic_index_in_dim(values, which, 0, False)


def move_rows(values, crossed, back=False):
    moves = pair_moves()[crossed]
    return lax.ppermute(values, ("seq", "core"), [(b, a) for a, b in moves] if back else moves)


def in_order(kept, crossed, parity):
    return jnp.where(parity == 0, kept, crossed), jnp.where(parity == 0, crossed, kept)


def spread_rows(values, parity):
    kept = move_rows(row_part(values, parity), False)
    crossed = move_rows(row_part(values, 1 - parity), True)
    return jnp.concatenate(in_order(kept, crossed, parity), 0)


def swap_cores(values):
    return lax.ppermute(values, "core", [(0, 1), (1, 0)])


def chip_orders(chips):
    bits = [1 << i for i in range(chips.bit_length() - 1)]
    return bits, bits[::-1]


def offsets(order):
    result = [0]
    for bit in order:
        result = result + [o ^ bit for o in result]
    return result


def place_lists(chips, owned, planes):
    shape = (2, planes, chips, owned)
    by_core = np.array([offsets(order) for order in chip_orders(chips)], np.int32)
    grid = np.indices(shape).astype(np.int32).reshape(4, 2, -1)
    offset = np.broadcast_to(by_core[:, None, :, None], shape).reshape(2, -1)
    return grid[1, 0], offset, grid[3, 0]


def arrival_order(chips, owned, planes):
    per_plane, quarter = chips * owned, owned
    if chips != 4:
        return np.arange(planes * per_plane)
    pieces = [(0, 0)]
    for k in range(1, planes + 1):
        pieces += [(k, 0)] if k < planes else []
        pieces += [(k - 1, 1), (k - 1, 2)]
        pieces += [(k - 2, 3)] if k > 1 else []
    pieces.append((planes - 1, 3))
    starts = [k * per_plane + r * quarter for k, r in pieces]
    return np.concatenate([np.arange(start, start + quarter) for start in starts])


def swap_chips(values, bits):
    chips = lax.axis_size("chip")
    moves = [(i * 2 + c, (i ^ bits[c]) * 2 + c) for i in range(chips) for c in range(2)]
    return lax.ppermute(values, ("chip", "core"), moves)


def move_planes(values, shift):
    planes = lax.axis_size("seq")
    return lax.ppermute(values, "seq", [(i, (i + shift) % planes) for i in range(planes)])


def after(value, *deps):
    return lax.optimization_barrier((value, *deps))[0]


def together(*values):
    return lax.optimization_barrier(values)


def chip_steps():
    return list(zip(*chip_orders(lax.axis_size("chip"))))


def finish_pieces(pieces):
    for bits in chip_steps()[2:]:
        joined = jnp.concatenate(pieces, 0)
        pieces = [joined, swap_chips(joined, bits)]
    return pieces


def add_halves(kept, came):
    return (kept.astype(F32) + came.astype(F32)).astype(BF)


def pack_terms(values):
    high = lax.optimization_barrier(values.astype(BF))
    low = (values - high.astype(F32)).astype(BF)
    terms = jnp.stack([high, low]).reshape(-1, BLK)
    return jnp.pad(terms, ((0, BLK - terms.shape[0]), (0, 0)))[None]


def unpack_terms(blocks, shape):
    terms = blocks.reshape(-1, BLK, BLK)[:, : 2 * shape[0] * shape[1] // BLK]
    terms = terms.reshape(-1, 2, *shape).astype(F32)
    return terms[:, 0] + terms[:, 1]


def finish_sums(keep, send):
    for bits in chip_steps()[::-1][1:-1]:
        count = keep.shape[0] // 2
        came = swap_chips(send, bits)
        send = add_halves(keep[count:], came[count:])
        keep = add_halves(keep[:count], came[:count])
    return keep, send


def by_chip(riders, me, core):
    chips = lax.axis_size("chip")
    ranks = np.array([np.argsort(offsets(order[::-1])) for order in chip_orders(chips)], np.int32)
    rank = jnp.asarray(ranks)[core][me ^ jnp.arange(chips, dtype=jnp.int32)]
    return riders.reshape(chips, -1, BLK, BLK)[rank]


def local(
    tokens,
    cotangent,
    lengths,
    owner_perm,
    master,
    norm_gains,
    stat_left,
    stat_right,
    root_left,
    root_right,
    moment_first,
    moment_second,
):
    core = lax.axis_index("core")
    place_z = lax.axis_index("seq")
    parity = place_z % 2
    block_count = owner_perm.shape[0]
    owned = master.shape[0]
    half = block_count // 2

    chips, planes = lax.axis_size("chip"), lax.axis_size("seq")
    me = lax.axis_index("chip")

    pair_lengths = jnp.stack([lengths, swap_cores(lengths)])
    pair_lengths = jnp.where(core == 0, pair_lengths, pair_lengths[::-1]).reshape(-1)
    length = lax.dynamic_index_in_dim(pair_lengths, place_z, 0, False)
    span = tokens.shape[0] * tokens.shape[1]
    live = jnp.stack([length - core * span, length - (1 - core) * span, length - core * span, parity])

    distance, offset, slot = place_lists(chips, owned, planes)
    offset = jnp.where(core == 0, offset, offset[::-1])
    device = ((place_z - distance) % planes * chips + (me ^ offset)) * 2
    device = device + jnp.stack([core, 1 - core])[:, None]
    table = owner_perm[(device * owned + slot).reshape(-1)]
    sums_table = jnp.asarray(source_numbers())[table[:half]]
    arrive = arrival_order(chips, owned, planes)
    near_slots, far_slots = device * owned + slot
    table = owner_perm[jnp.concatenate([near_slots[arrive], far_slots[arrive]])]

    shard = master.astype(BF)
    first_bits, second_bits = chip_steps()[:2]
    per_plane = chips * owned
    by_phase = chips == 4
    rows = (row_part(tokens, parity), row_part(tokens, 1 - parity))
    cross, held, weights, first = None, (), None, 0
    came, turned = swap_chips(shard, first_bits), swap_chips(shard, second_bits)
    next_shard = move_planes(shard, 1)
    pieces = [[shard, came, turned]]

    def place(parts, first, weights):
        others = [swap_cores(part) for part in parts]
        weights = place_blocks(table, first, parts, others, weights)
        return weights, first + sum(part.shape[0] for part in parts)

    for k in range(1, planes):
        ready = () if k == 1 else (cross, *held, live, table, sums_table)
        ready = ready if weights is None else (*ready, weights)
        this_shard, came, turned, row_a, row_b, *done = together(
            next_shard, came, turned, *rows, *ready
        )
        if k > 1:
            pieces[k - 2].append(done[0])
        cross = swap_chips(came, second_bits)
        arrived = [this_shard, came, turned, *(pieces[0][:1] if k == 1 else done[:1])]
        arrived = arrived[3:] + arrived[:3] if k == 1 else arrived
        pieces[k - 1][1:] = [came, turned]
        came, turned = swap_chips(this_shard, first_bits), swap_chips(this_shard, second_bits)
        pieces.append([this_shard, came, turned])
        if k < planes - 1:
            next_shard = move_planes(this_shard, 1)
        else:
            row_same = move_rows(row_a, False)
            row_cross = move_rows(after(row_b, row_same), True)
        if by_phase:
            if k > 1:
                weights, first = place(done[1:2], first, weights)
            held = (jnp.concatenate(arrived, 0),)
    came, turned, done, row_same, row_cross, *held = together(
        came, turned, cross, row_same, row_cross, *held, *([] if weights is None else [weights])
    )
    own_tokens = jnp.concatenate(in_order(row_same, row_cross, parity), 0)
    pieces[-2].append(done)
    pieces[-1][1:] = [came, turned, swap_chips(came, second_bits)]
    normed1, normed1_t = norm_tokens(own_tokens, norm_gains)
    if by_phase:
        weights, first = place(held[:1], first, weights)
        parts = [came, turned, done]
        others = [swap_cores(part) for part in parts]
        last, normed1, *_ = together(pieces[-1][-1], normed1, weights, *others)
        weights = place_blocks(table, first, parts, others, weights)
        first += 3 * owned
        other_normed = swap_cores(normed1)
        weights, _ = place([last], first, weights)
    else:
        for each in pieces:
            each = [jnp.concatenate(finish_pieces(each), 0)]
            weights, first = place(each, first, weights)
        other_normed = swap_cores(normed1)
    own_cot = spread_rows(after(cotangent, weights), parity)

    own_qkv, other_kv = project(normed1, other_normed, weights)
    attended, q_aug = attend(live, own_qkv, other_kv)
    kept, crossed, g_rest, grad_middle, grad_attended, gain_second = feed(
        live, own_tokens, attended, own_cot, norm_gains, weights
    )
    other_rest = swap_cores(g_rest)
    kept, crossed = move_rows(kept, False, True), move_rows(crossed, True, True)
    layer_out = jnp.stack(in_order(kept, crossed, parity), 0)
    d_query, d_own, d_other = attend_back(live, q_aug, own_qkv, other_kv, attended, grad_attended)
    received = swap_cores(after(d_other, kept, crossed))
    flat = lambda g: g.reshape(-1, BLK, BLK)
    g_query, partial = query_back(normed1_t, d_query, weights)
    g_query = flat(g_query)
    other_query = swap_cores(g_query)
    g_kv, back = input_back(normed1_t, d_own, received, partial, weights)
    g_kv = flat(g_kv)
    other_kv_grad = swap_cores(after(g_kv, other_query))
    own_grads = (g_query, g_kv, g_rest)
    other_grads = (other_query, other_kv_grad, other_rest)
    half_plane = per_plane // 2
    last_bits, before_bits = chip_steps()[-1], chip_steps()[0]
    moved_rows, lows, sent, passed, riders_z = [], [], None, None, []

    def sums(k, part, held):
        first = k * per_plane + part * half_plane
        return gather_sums(held, first, half_plane, own_grads, other_grads)

    order = list(range(planes))[::-1]
    high = sums(order[0], 1, sums_table)
    held = sums_table
    held_riders = []
    for turn in range(planes + 1):
        group, moves = [], []
        if turn < planes:
            group.append(high)
            moves.append(lambda v: swap_chips(v, last_bits))
        if 1 <= turn <= planes:
            group.append(sent)
            moves.append(lambda v: swap_chips(v, before_bits))
        if 2 <= turn <= planes:
            group.append(part)
            moves.append(lambda v: move_planes(v, -1))
        if turn in (1, 2):
            group.append(riders)
            bits = last_bits if turn == 1 else before_bits
            moves.append(lambda v: swap_chips(v, bits))
        if turn in (1, 2):
            group.append(rows[turn - 1])
            crossed = turn == 2
            moves.append(lambda v: move_rows(v, crossed, True))
        far_riders = [1, 2] if turn == planes - 1 else []
        group += [rider for _ in far_riders]
        moves += [functools.partial(move_planes, shift=-k) for k in far_riders]
        came = [move(value) for move, value in zip(moves, together(*group, *moved_rows, *held_riders))]
        if turn in (1, 2):
            moved_rows.append(came.pop())
            riders = jnp.concatenate([riders, came.pop()], 0)
            for bits in chip_steps()[::-1][1:-1] if turn == 1 else ():
                riders = jnp.concatenate([riders, swap_chips(riders, bits)], 0)
        count = len(came) - len(far_riders)
        riders_z, came = riders_z + came[count:], came[:count]
        if far_riders:
            riders_z += [move_planes(after(rider, *riders_z), -k) for k in range(3, planes)]
        if turn == planes:
            parts = [keep_before, *came]
            continue
        passed = came.pop() if turn >= 2 else None
        low = sums(order[turn], 0, after(held, high))
        if turn + 1 < planes:
            high = sums(order[turn + 1], 1, after(held, low))
        held = after(sums_table, *came)
        held_riders = [riders] if turn == 2 else []
        if turn == 0:
            kept, crossed, gain_first = input_end(
                live, own_tokens, norm_gains, after(back, high), grad_middle
            )
            rows = [kept, crossed]
            gain_part = jnp.concatenate([gain_first, gain_second], 0)
            mine = pack_terms(gain_part)
            pair = jnp.concatenate([mine, swap_cores(mine)], 0)
            riders = jnp.where(core == 0, pair, pair[::-1])
        if turn == 2:
            plane_gain = by_chip(riders, me, core)
            plane_gain = jnp.sum(unpack_terms(plane_gain, gain_part.shape), 0)
            rider = pack_terms(plane_gain)
        second = (None, None, None) if turn == 0 else (keep_before, came[-1], passed)
        keep, sent, *part = merge_sums(low, came[0], *second)
        part = part[0] if part else None
        keep_before, sent = finish_sums(keep, sent)
    input_grad = jnp.stack(in_order(*moved_rows, parity), 0).astype(F32)
    planes_gain = [unpack_terms(each, gain_part.shape)[0] for each in (rider, *riders_z)]
    turned = (jnp.arange(planes, dtype=jnp.int32) - place_z) % planes
    gain_grad = jnp.sum(jnp.stack(planes_gain)[turned], 0)
    grad_blocks, stat_left_new, stat_right_new, master_new = update(
        parts, master, stat_left, stat_right, root_left, root_right
    )
    first_new = 0.9 * moment_first + 0.1 * gain_grad
    second_new = 0.999 * moment_second + 0.001 * gain_grad * gain_grad
    first_hat = first_new / (1.0 - 0.9**STEP)
    second_hat = second_new / (1.0 - 0.999**STEP)
    gains_new = norm_gains - 0.5 * first_hat / (jnp.sqrt(second_hat) + 1e-08)
    return (
        layer_out,
        input_grad,
        grad_blocks,
        stat_left_new,
        stat_right_new,
        master_new,
        first_new,
        second_new,
        gains_new,
    )


def solution(mesh):
    seq_size, rows_size = mesh.shape["seq"], mesh.shape["rows"]
    mesh = Mesh(mesh.devices.reshape(seq_size, rows_size // 2, 2), ("seq", "chip", "core"))
    activation = P(("chip", "core"), "seq", None)
    blocks = P(("seq", "chip", "core"), None, None)
    return jax.shard_map(
        local,
        mesh=mesh,
        in_specs=(
            activation, activation, P(("chip", "core")), P(), blocks, P(),
            blocks, blocks, blocks, blocks, P(), P(),
        ),
        out_specs=(activation, activation, blocks, blocks, blocks, blocks, P(), P(), P()),
        check_vma=False,
    )
```
